32 devices in a mesh: dp: 8 (over y, x, core), section: 4 (over z).
Axes of the slice: x: 2, y: 2, z: 4, core: 2. Of those that a mesh axis runs over, the one named last changes fastest.
Arguments:
- block_input: bfloat16 [16, 1536, 512], P('dp'), may hold values from -6 to 6
- known_genes: int32 [16, 1536], P('dp'), may hold values 0 or 1
- attn_proj: bfloat16 [2, 512, 1536], replicated, may hold values from -0.25 to 0.25
- attn_out: bfloat16 [2, 512, 512], replicated, may hold values from -2 to 2
- query_bias: float32 [2, 512], replicated, may hold values from -1.5 to 1.5
- value_bias: float32 [2, 512], replicated, may hold values from -0.15 to 0.15
- out_bias: float32 [2, 512], replicated, may hold values from -1.5 to 1.5
- ff_in: bfloat16 [2, 512, 512], replicated, may hold values from -0.25 to 0.25
- ff_out: bfloat16 [2, 512, 512], replicated, may hold values from -0.25 to 0.25
- ff_bias_in: float32 [2, 512], replicated, may hold values from -1.5 to 1.5
- ff_bias_out: float32 [2, 512], replicated, may hold values from -1.5 to 1.5
- norm_gain: float32 [2, 2, 512], replicated, may hold values from 0.1 to 1.9
- norm_shift: float32 [2, 2, 512], replicated, may hold values from -1.5 to 1.5
- cotangent: bfloat16 [16, 1536, 512], P('dp'), may hold values from -6 to 6
Outputs:
- section_outputs: bfloat16 [4, 16, 1536, 512], P('section', 'dp')
- section_input_grads: bfloat16 [4, 16, 1536, 512], P('section', 'dp')
- grad_attn_proj: float32 [2, 512, 1536], P(None, ('dp', 'section'))
- grad_attn_out: float32 [2, 512, 512], P(None, ('dp', 'section'))
- grad_query_bias: float32 [2, 512], P(None, ('dp', 'section'))
- grad_value_bias: float32 [2, 512], P(None, ('dp', 'section'))
- grad_out_bias: float32 [2, 512], P(None, ('dp', 'section'))
- grad_ff_in: float32 [2, 512, 512], P(None, ('dp', 'section'))
- grad_ff_out: float32 [2, 512, 512], P(None, ('dp', 'section'))
- grad_ff_bias_in: float32 [2, 512], P(None, ('dp', 'section'))
- grad_ff_bias_out: float32 [2, 512], P(None, ('dp', 'section'))
- grad_norm_gain: float32 [2, 2, 512], P(None, None, ('dp', 'section'))
- grad_norm_shift: float32 [2, 2, 512], P(None, None, ('dp', 'section'))
The draws below stay inside these ranges and needn't reach their ends.
All inputs are finite; a program needn't handle non-finite values. No bound on the sum of `known_genes` on one device may be relied on, other than what follows from the above.
Results may differ from the reference program's by a relative error of at most 0.02.
Values may be sent and summed in bfloat16 or wider, within the bound.
No kernel may reach another device: no remote copies, remote signals or barrier semaphores. Data moves between devices by JAX's collectives and lax.ppermute only.
A program may use at most 256 MiB of HBM per device.

```python
import jax
import jax.numpy as jnp
from jax import lax

D = 512
HEADS = 8
HEAD_DIM = 64
FF = 512
LAYERS = 2
LONG = 1024
SHORT = 512
ROWS = 16
TOKENS_ROW = 1536


def place_ends(drawn, own_key, least, high):
    longest = drawn.shape.index(max(drawn.shape))
    spots = []
    for shift in (0, 1):
        where = [jax.random.randint(jax.random.fold_in(own_key, axis), (), 0, length) for axis, length in enumerate(drawn.shape)]
        where[longest] = (where[longest] + shift) % drawn.shape[longest]
        spots.append(tuple(where))
    return drawn.at[spots[0]].set(least).at[spots[1]].set(high)


def raised(values, rng, source, target, shards_of, factor):
    def block_of(axis_at):
        return (jnp.arange(values.shape[axis_at]) // (values.shape[axis_at] // shards_of)).reshape((-1,) + (1,) * (values.ndim - 1 - axis_at))

    first = jax.random.permutation(rng, shards_of)[block_of(target)]
    far = (block_of(target) + shards_of // 2) % shards_of
    return jnp.where((block_of(source) == first) | (block_of(source) == far), factor * values, values)


def block_levels(key, extent, shards, least, largest):
    level = 1.0
    for dim, parts in shards:
        draws = jax.random.uniform(jax.random.fold_in(jax.random.fold_in(key, 6), dim), (parts,), jnp.float32, least / len(shards), largest / len(shards))
        level = level * jnp.repeat(jnp.exp(draws), extent[dim] // parts).reshape((-1,) + (1,) * (len(extent) - 1 - dim))
    return level


def bell_draw(stream_key, extent, width, most, cuts=(), dtype=jnp.bfloat16):
    gain = block_levels(stream_key, extent, cuts, -0.22, 0.18) if cuts else 1.0
    values = jax.random.normal(stream_key, extent, jnp.float32) * width * gain
    return jnp.minimum(jnp.maximum(values, -most), most).astype(dtype)


def gaussian_with(key, extent, deviation, reach, shards, heavy, kind=jnp.bfloat16):
    entries = deviation * jax.random.normal(key, extent, jnp.float32)
    if shards:
        entries = entries * block_levels(key, extent, shards, -0.22, 0.18)
    return jnp.clip(raised(entries, jax.random.fold_in(key, 3), *heavy), -reach, reach).astype(kind)


def setup_inputs(seed: int = 0) -> dict:
    streams_of = jax.random.split(jax.random.key(seed), 15)
    return {
        "block_input": bell_draw(streams_of[0], (ROWS, TOKENS_ROW, D), 1.0, 6.0, ((0, 8),)),
        "known_genes": place_ends((jax.random.randint(streams_of[1], (ROWS, TOKENS_ROW), 0, 2) < 1).astype(jnp.int32), jax.random.fold_in(streams_of[1], 1), 0, 1),
        "attn_proj": bell_draw(streams_of[2], (LAYERS, D, 3 * D), D ** -0.5, 0.25),
        "attn_out": bell_draw(streams_of[3], (LAYERS, D, D), 8 ** -0.5, 2.0),
        "query_bias": bell_draw(streams_of[4], (LAYERS, D), 0.3, 1.5, (), jnp.float32),
        "value_bias": bell_draw(streams_of[5], (LAYERS, D), 0.03, 0.15, (), jnp.float32),
        "out_bias": bell_draw(streams_of[6], (LAYERS, D), 0.3, 1.5, (), jnp.float32),
        "ff_in": bell_draw(streams_of[7], (LAYERS, D, FF), D ** -0.5, 0.25),
        "ff_out": bell_draw(streams_of[8], (LAYERS, FF, D), FF ** -0.5, 0.25),
        "ff_bias_in": bell_draw(streams_of[9], (LAYERS, FF), 0.3, 1.5, (), jnp.float32),
        "ff_bias_out": bell_draw(streams_of[10], (LAYERS, D), 0.3, 1.5, (), jnp.float32),
        "norm_gain": jnp.clip(1.0 + 0.18 * jax.random.normal(streams_of[11], (LAYERS, 2, D), jnp.float32), 0.1, 1.9),
        "norm_shift": bell_draw(streams_of[12], (LAYERS, 2, D), 0.3, 1.5, (), jnp.float32),
        "cotangent": gaussian_with(streams_of[13], (ROWS, TOKENS_ROW, D), 1.0, 6.0, ((0, 8),), (0, 2, 8, 2.0)),
    }


@jax.custom_vjp
def low(v):
    return lax.optimization_barrier(v.astype(jnp.bfloat16)).astype(jnp.float32)

@jax.custom_vjp
def low_back(v):
    return v

def low_keep(v):
    return (low(v), None)

def low_pass(kept, grad):
    return (grad,)

def back_keep(v):
    return (v, None)

def back_low(kept, grad):
    return (low(grad),)
low.defvjp(low_keep, low_pass)
low_back.defvjp(back_keep, back_low)
highest_precision = lax.Precision.HIGHEST
eps_norm = 1e-05
masked_fill = -1e+30

def norm_rows(residual, gain_row, shift_row):
    center = residual - lax.optimization_barrier(jnp.mean(residual, axis=-1, keepdims=True))
    variance = lax.optimization_barrier(jnp.mean(center * center, axis=-1, keepdims=True))
    return center * lax.rsqrt(variance + eps_norm) * gain_row + shift_row

def split_heads(matrix):
    return matrix.reshape(matrix.shape[0], HEADS, HEAD_DIM)

def attend_cell(query_cell, key_cell, value_cell, known_cell):
    length = query_cell.shape[0]
    scores = jnp.einsum('qhd,khd->hqk', split_heads(query_cell), split_heads(key_cell), precision=highest_precision)
    scores = low_back(scores * HEAD_DIM ** (-0.5))
    row_ids = lax.iota(jnp.int32, length)
    allowed = (known_cell[None, :] == 1) | (row_ids[:, None] == row_ids[None, :])
    masked = jnp.where(allowed[None], scores, masked_fill)
    exp_scores = jnp.exp(masked - lax.optimization_barrier(jnp.max(masked, axis=-1, keepdims=True)))
    soft_probs = low(exp_scores / lax.optimization_barrier(jnp.sum(exp_scores, axis=-1, keepdims=True)))
    mixed_heads = jnp.einsum('hqk,khd->qhd', soft_probs, split_heads(value_cell), precision=highest_precision)
    return mixed_heads.reshape(length, D)

def attention_layer(section_in, known_row, w_qkv, w_mix, bias_query, bias_value, bias_mix, gain_row, shift_row):
    projected = low_back(jnp.dot(section_in, w_qkv, precision=highest_precision))
    query_all = low(projected[:, :D] + bias_query)
    key_all = low(projected[:, D:2 * D])
    value_all = low(projected[:, 2 * D:] + bias_value)
    pieces = []
    for cell_start, cell_len in ((0, LONG), (LONG, SHORT)):
        pieces.append(attend_cell(query_all[cell_start:cell_start + cell_len], key_all[cell_start:cell_start + cell_len], value_all[cell_start:cell_start + cell_len], known_row[cell_start:cell_start + cell_len]))
    attn_mix = low_back(low(jnp.concatenate(pieces, axis=0)))
    branch = low_back(jnp.dot(attn_mix, w_mix, precision=highest_precision)) + bias_mix
    return low(norm_rows(section_in + branch, gain_row, shift_row))

def feed_layer(section_in, w_up, w_down, bias_up, bias_down, gain_row, shift_row):
    pre_act = low_back(jnp.dot(section_in, w_up, precision=highest_precision)) + bias_up
    hidden = low(jax.nn.gelu(pre_act, approximate=False))
    branch = low_back(jnp.dot(hidden, w_down, precision=highest_precision)) + bias_down
    return low(norm_rows(section_in + branch, gain_row, shift_row))

def stack_forward(params, probes, row_input, known_row):
    attn_proj, attn_out, query_bias, value_bias, out_bias, ff_in, ff_out, ff_bias_in, ff_bias_out, norm_gain, norm_shift = params
    current = row_input
    outputs = []
    for section_num in range(2 * LAYERS):
        layer_num = section_num // 2
        current = low_back(current + probes[section_num])
        if section_num % 2 == 0:
            current = attention_layer(current, known_row, attn_proj[layer_num], attn_out[layer_num], query_bias[layer_num], value_bias[layer_num], out_bias[layer_num], norm_gain[layer_num, 0], norm_shift[layer_num, 0])
        else:
            current = feed_layer(current, ff_in[layer_num], ff_out[layer_num], ff_bias_in[layer_num], ff_bias_out[layer_num], norm_gain[layer_num, 1], norm_shift[layer_num, 1])
        outputs.append(current)
    return (current, jnp.stack(outputs))

def reference(block_input, known_genes, attn_proj, attn_out, query_bias, value_bias, out_bias, ff_in, ff_out, ff_bias_in, ff_bias_out, norm_gain, norm_shift, cotangent):
    params = tuple((tensor.astype(jnp.float32) for tensor in (attn_proj, attn_out, query_bias, value_bias, out_bias, ff_in, ff_out, ff_bias_in, ff_bias_out, norm_gain, norm_shift)))
    probe_zero = jnp.zeros((2 * LAYERS, LONG + SHORT, D), jnp.float32)

    def one_row(totals, row_data):
        row_input, known_row, row_cot = row_data

        def forward_fn(param_set, probe_set):
            return stack_forward(param_set, probe_set, row_input.astype(jnp.float32), known_row)
        final_out, pullback, section_acts = jax.vjp(forward_fn, params, probe_zero, has_aux=True)
        param_grads, probe_grads = pullback(row_cot.astype(jnp.float32))
        totals = jax.tree.map(jnp.add, totals, param_grads)
        return (totals, (section_acts.astype(jnp.bfloat16), probe_grads.astype(jnp.bfloat16)))
    zero_totals = jax.tree.map(jnp.zeros_like, params)
    totals, (section_acts, probe_grads) = lax.scan(one_row, zero_totals, (block_input, known_genes, cotangent))
    section_outputs = jnp.swapaxes(section_acts, 0, 1)
    section_input_grads = jnp.swapaxes(probe_grads, 0, 1)
    return (section_outputs, section_input_grads, totals[0], totals[1], totals[2], totals[3], totals[4], totals[5], totals[6], totals[7], totals[8], totals[9], totals[10])
```

```python
import jax
import jax.numpy as jnp
from jax import lax
from jax.experimental import pallas as pl
from jax.experimental.pallas import tpu as pltpu
from jax.sharding import PartitionSpec as P

D = 512
HEADS = 8
HEAD_DIM = 64
LONG = 1024
SHORT = 512
EPS = 1e-05
FILL = -1e30
SCALE = HEAD_DIM ** (-0.5)
LOG2E = 1.4426950408889634
SOFT = SCALE * LOG2E
BF = jnp.bfloat16
F32 = jnp.float32
VAUG = HEAD_DIM + 16


def nn(a, b):
    return lax.dot_general(a, b, (((1,), (0,)), ((), ())), preferred_element_type=F32)


def nt(a, b):
    return lax.dot_general(a, b, (((1,), (1,)), ((), ())), preferred_element_type=F32)


def tn(a, b):
    return lax.dot_general(a, b, (((0,), (0,)), ((), ())), preferred_element_type=F32)


def key_counts(length):
    return (length // 2 + length // 8, length)


def by_count(known_count, length, run):
    low = 0
    for size in key_counts(length):
        if low == 0:
            inside = known_count <= size
        elif size == length:
            inside = known_count > low
        else:
            inside = (known_count > low) & (known_count <= size)
        pl.when(inside)(lambda size=size: run(size))
        low = size


def norm_rows(residual):
    center = residual - jnp.mean(residual, axis=-1, keepdims=True)
    inv_std = lax.rsqrt(jnp.mean(center * center, axis=-1, keepdims=True) + EPS)
    return center * inv_std, inv_std


def one_hot_rows(rank_row, size, length):
    return (lax.broadcasted_iota(jnp.int32, (size, length), 0) == rank_row).astype(F32).astype(BF)


def one_hot_cols(rank_col, size):
    length = rank_col.shape[0]
    return (lax.broadcasted_iota(jnp.int32, (length, size), 1) == rank_col).astype(F32).astype(BF)


def put_masked(dst, src, tokens):
    zeros = jnp.zeros((HEAD_DIM, tokens), BF)
    for head in range(HEADS):
        part = (head % 2) * HEAD_DIM
        dst[head, part : part + HEAD_DIM, :] = src[head * HEAD_DIM : (head + 1) * HEAD_DIM, :]
        dst[head, HEAD_DIM - part : 2 * HEAD_DIM - part, :] = zeros


def head_sums(a, b):
    out = []
    for head in range(HEADS):
        rows = slice(head * HEAD_DIM, (head + 1) * HEAD_DIM)
        out.append(jnp.sum(a[rows, :].astype(F32) * b[rows, :].astype(F32), axis=0, keepdims=True))
    return out


def forward_kernel(
    scal, rank_row, unk, u_own, u_oth, w_t, bcol, w_mix, vecs, ff_in, ff_out,
    s_even, s_odd, q_t, ko_t, vo_t, u_c, k_c, mix_t, lse, nrm0, inv0, gp, hid, nrm1, inv1,
    qm, vaug, kb, sd,
):
    half = u_own.shape[0]
    length = 2 * half
    count = scal[1]
    uo = u_own[...]
    own_t = nt(w_t[...], uo)
    q_t[...] = (own_t[:D] + bcol[:, 0:1]).astype(BF)
    ko_t[...] = own_t[D : 2 * D].astype(BF)
    vo_t[...] = (own_t[2 * D :] + bcol[:, 1:2]).astype(BF)
    put_masked(qm, q_t, half)
    for head, row in enumerate(head_sums(q_t, ko_t)):
        sd[head] = row + unk[...]
    ones_rows = (lax.broadcasted_iota(jnp.int32, (16, length), 0) == 0).astype(F32).astype(BF)
    for head in range(HEADS):
        vaug[head * VAUG + HEAD_DIM : (head + 1) * VAUG, :] = ones_rows
    block = min(half, 256)

    def run(size):
        pick = one_hot_rows(rank_row[...], size, length)
        uc = (nn(pick[:, :half], uo) + nn(pick[:, half:], u_oth[...])).astype(BF)
        u_c[:size, :] = uc
        k_c[:size, :] = nt(uc, w_t[D : 2 * D, :]).astype(BF)
        vct = (nt(w_t[2 * D :, :], uc) + bcol[:, 1:2]).astype(BF)
        for head in range(HEADS):
            vaug[head * VAUG : head * VAUG + HEAD_DIM, :size] = vct[head * HEAD_DIM : (head + 1) * HEAD_DIM, :]
        kb[:size, :] = jnp.where(lax.broadcasted_iota(jnp.int32, (size, 128), 0) < count, 0.0, FILL)

        def pair(p, carry):
            kcp = k_c[:size, pl.ds(pl.multiple_of(p * 128, 128), 128)]
            for e in range(2):
                head = 2 * p + e
                vrows = vaug[pl.ds(pl.multiple_of(head * VAUG, 16), VAUG), :size]
                for start in range(0, half, block):
                    cols = slice(start, start + block)
                    scores = nn(kcp, qm[head, :, cols])
                    sdr = sd[head, :, cols]
                    tops, probs = [], []
                    for t in range(0, block, 128):
                        part = scores[:, t : t + 128] + kb[:size, :]
                        top = jnp.maximum(jnp.max(part, axis=0, keepdims=True), sdr[:, t : t + 128])
                        tops.append(top)
                        probs.append(jnp.exp2((part - top) * SOFT).astype(BF))
                    top = jnp.concatenate(tops, axis=1)
                    mixed = nn(vrows, jnp.concatenate(probs, axis=1))
                    pd = jnp.exp2((sdr - top) * SOFT)
                    total = mixed[HEAD_DIM : HEAD_DIM + 1] + pd
                    rows = pl.ds(pl.multiple_of(head * HEAD_DIM, HEAD_DIM), HEAD_DIM)
                    own = vo_t[rows, cols].astype(F32)
                    mix_t[rows, cols] = ((mixed[:HEAD_DIM] + pd * own) / total).astype(BF)
                    lse[head, :, cols] = top * SOFT + jnp.log2(total)
            return carry

        lax.fori_loop(0, HEADS // 2, pair, 0)

    by_count(count, length, run)

    def tail(i, carry):
        rows = pl.ds(pl.multiple_of(i * 128, 128), 128)
        res = u_own[rows, :].astype(F32) + tn(mix_t[:, rows], w_mix[...]) + vecs[0:1, :]
        normed, inv = norm_rows(res)
        nrm0[rows, :] = normed.astype(BF)
        inv0[rows, :] = inv
        even = (normed * vecs[1:2, :] + vecs[2:3, :]).astype(BF)
        s_even[rows, :] = even
        pre = nn(even, ff_in[...]) + vecs[3:4, :]
        cdf = 0.5 + 0.5 * lax.erf(pre * 0.7071067811865476)
        hidden = (pre * cdf).astype(BF)
        hid[rows, :] = hidden
        gp[rows, :] = (cdf + pre * (0.3989422804014327 * jnp.exp(-0.5 * pre * pre))).astype(BF)
        res = even.astype(F32) + nn(hidden, ff_out[...]) + vecs[4:5, :]
        normed, inv = norm_rows(res)
        nrm1[rows, :] = normed.astype(BF)
        inv1[rows, :] = inv
        s_odd[rows, :] = (normed * vecs[5:6, :] + vecs[6:7, :]).astype(BF)
        return carry

    lax.fori_loop(0, half // 128, tail, 0)


def norm_back(grad, normed, inv, gain):
    e = grad * gain
    return inv * (
        e - jnp.mean(e, axis=-1, keepdims=True) - normed * jnp.mean(e * normed, axis=-1, keepdims=True)
    )


def backward_kernel(
    scal, rank_col, unk, g_own, g_oth, s_even, u_own, q_t, ko_t, vo_t, u_c, k_c, mix_t, lse, nrm0, inv0,
    gp, hid, nrm1, inv1, w_t, bvrow, w_mix, vecs, ff_in, ff_out,
    g_in, g_odd, dx_own, dx_oth, d_qkv, d_mix, d_in, d_out, d_vec, d_col,
    db, dpre, dr, qm, dmm, dm_t, delta, kc_t, vc, kb, dq_t, dk_c, dxs,
):
    half = u_own.shape[0]
    length = 2 * half
    count = scal[1]
    d_vec[...] = jnp.zeros_like(d_vec)

    def add_row(slot, value):
        d_vec[slot : slot + 1, :] += jnp.sum(value, axis=0, keepdims=True)

    def head_part(i, carry):
        rows = pl.ds(pl.multiple_of(i * 128, 128), 128)
        grad = g_own[rows, :].astype(F32)
        if g_oth is not None:
            grad = grad + g_oth[rows, :].astype(F32)
            low = grad.astype(BF)
            g_in[rows, :] = low
            grad = low.astype(F32)
        normed = nrm1[rows, :].astype(F32)
        add_row(5, grad * normed)
        add_row(6, grad)
        dres = norm_back(grad, normed, inv1[rows, :], vecs[5:6, :])
        add_row(4, dres)
        low = dres.astype(BF)
        db[rows, :] = low
        dp = nt(low, ff_out[...]) * gp[rows, :].astype(F32)
        add_row(3, dp)
        low = dp.astype(BF)
        dpre[rows, :] = low
        low = (dres + nt(low, ff_in[...])).astype(BF)
        g_odd[rows, :] = low
        grad = low.astype(F32)
        normed = nrm0[rows, :].astype(F32)
        add_row(1, grad * normed)
        add_row(2, grad)
        dres = norm_back(grad, normed, inv0[rows, :], vecs[1:2, :])
        add_row(0, dres)
        dr[rows, :] = dres
        return carry

    lax.fori_loop(0, half // 128, head_part, 0)
    d_out[...] = tn(hid[...], db[...])
    d_in[...] = tn(s_even[...], dpre[...])
    db[...] = dr[...].astype(BF)
    d_mix[...] = nn(mix_t[...], db[...])
    dmt = nt(w_mix[...], db[...])
    dm_t[...] = dmt.astype(BF)
    d_col[:, 1:2] = jnp.sum(dm_t[...].astype(F32), axis=1, keepdims=True)
    put_masked(qm, q_t, half)
    put_masked(dmm, dm_t, half)
    for head, row in enumerate(head_sums(dm_t, mix_t)):
        delta[head] = row
    block = min(half, 256)

    def run(size):
        uc = u_c[:size, :]
        kc_t[:, :size] = nt(w_t[D : 2 * D, :], uc).astype(BF)
        vc[:size, :] = (nt(uc, w_t[2 * D :, :]) + bvrow[...]).astype(BF)
        kb[:size, :] = jnp.where(lax.broadcasted_iota(jnp.int32, (size, 128), 0) < count, 0.0, FILL)

        def pair(p, carry):
            lanes = pl.ds(pl.multiple_of(p * 128, 128), 128)
            kcp = k_c[:size, lanes]
            vcp = vc[:size, lanes]
            dk = jnp.zeros((size, 128), F32)
            dv = jnp.zeros((size, 128), F32)
            for e in range(2):
                head = 2 * p + e
                rows = pl.ds(pl.multiple_of(head * HEAD_DIM, HEAD_DIM), HEAD_DIM)
                for start in range(0, half, block):
                    cols = slice(start, start + block)
                    qtm = qm[head, :, cols]
                    dmh = dmm[head, :, cols]
                    scores = nn(kcp, qtm)
                    dprob = nn(vcp, dmh)
                    lser = lse[head, :, cols]
                    delr = delta[head, :, cols]
                    lows, grads = [], []
                    for t in range(0, block, 128):
                        tile = slice(t, t + 128)
                        prob = jnp.exp2(jnp.minimum(scores[:, tile] * SOFT - lser[:, tile], kb[:size, :]))
                        lows.append(prob.astype(BF))
                        grads.append((prob * (dprob[:, tile] - delr[:, tile])).astype(BF))
                    low = jnp.concatenate(lows, axis=1)
                    ds = jnp.concatenate(grads, axis=1)
                    dv = dv + nt(low, dmh)
                    dk = dk + nt(ds, qtm)
                    dq_t[rows, cols] = nn(kc_t[rows, :size], ds) * SCALE
            dk_c[:size, lanes] = (dk * SCALE).astype(BF)
            dk_c[:size, pl.ds(pl.multiple_of(D + p * 128, 128), 128)] = dv.astype(BF)
            return carry

        lax.fori_loop(0, HEADS // 2, pair, 0)
        dkv = dk_c[:size, :]
        d_qkv[:, D:] = tn(uc, dkv)
        dxc = nn(dkv, w_t[D:, :]).astype(BF)
        dxs[...] = nn(one_hot_cols(rank_col[:half, :], size), dxc)
        dx_oth[...] = nn(one_hot_cols(rank_col[half:, :], size), dxc).astype(BF)

    by_count(count, length, run)

    dp_t = dmm_rows = None
    sds = head_sums(q_t, ko_t)
    dps = head_sums(dm_t, vo_t)
    dk_parts, dv_parts, dq_parts = [], [], []
    for head in range(HEADS):
        rows = slice(head * HEAD_DIM, (head + 1) * HEAD_DIM)
        prob = jnp.exp2(jnp.minimum(sds[head] * SOFT - lse[head], unk[...]))
        ds = (prob * (dps[head] - delta[head])).astype(BF).astype(F32) * SCALE
        low = prob.astype(BF).astype(F32)
        dq_parts.append(dq_t[rows, :] + ds * ko_t[rows, :].astype(F32))
        dk_parts.append((ds * q_t[rows, :].astype(F32)).astype(BF))
        dv_parts.append((low * dm_t[rows, :].astype(F32)).astype(BF))
    dq = jnp.concatenate(dq_parts, axis=0)
    d_col[:, 0:1] = jnp.sum(dq, axis=1, keepdims=True)
    dp_t = jnp.concatenate([dq.astype(BF)] + dk_parts + dv_parts, axis=0)
    u_t = u_own[...].T
    dw = nt(u_t, dp_t)
    d_qkv[:, :D] = dw[:, :D]
    d_qkv[:, D:] += dw[:, D:]
    dx_own[...] = dr[...] + dxs[...] + tn(dp_t, w_t[...])


def full(shape):
    zeros = (0,) * len(shape)
    return pl.BlockSpec(shape, lambda i, s: zeros)


def shape_of(shape, dtype=BF):
    return jax.ShapeDtypeStruct(shape, dtype)


VMEM_LIMIT = 56 * 1024 * 1024


def call(kernel, scal, ins, in_specs, outs, scratch, flops):
    return pl.pallas_call(
        kernel,
        grid_spec=pltpu.PrefetchScalarGridSpec(
            num_scalar_prefetch=1,
            grid=(1,),
            in_specs=in_specs,
            out_specs=[full(o.shape) for o in outs],
            scratch_shapes=scratch,
        ),
        out_shape=outs,
        compiler_params=pltpu.CompilerParams(vmem_limit_bytes=VMEM_LIMIT),
        cost_estimate=pl.CostEstimate(flops=flops, bytes_accessed=12 * 2**20, transcendentals=2**20),
    )(scal, *ins)


def forward_layer(scal, rank_row, unk, u_own, u_oth, weights, half, own_spec=None, oth_spec=None):
    length = 2 * half
    w_t, bcol, bvrow, w_mix, vecs, ff_in, ff_out = weights
    ins = [rank_row, unk, u_own, u_oth, w_t, bcol, w_mix, vecs, ff_in, ff_out]
    specs = [full(x.shape) for x in ins]
    if own_spec is not None:
        specs[2], specs[3] = own_spec, oth_spec
    tok = shape_of((half, D))
    feat = shape_of((D, half))
    col = shape_of((half, 1), F32)
    outs = [
        tok, tok, feat, feat, feat, shape_of((length, D)), shape_of((length, D)), feat,
        shape_of((HEADS, 1, half), F32), tok, col, tok, tok, tok, col,
    ]
    scratch = [
        pltpu.VMEM((HEADS, 128, half), BF),
        pltpu.VMEM((HEADS * VAUG, length), BF),
        pltpu.VMEM((length, 128), F32),
        pltpu.VMEM((HEADS, 1, half), F32),
    ]
    return call(forward_kernel, scal, ins, specs, outs, scratch, half * 2**23)


def backward_layer(scal, rank_col, unk, g_own, g_oth, u_own, saved, weights, half, u_spec=None):
    length = 2 * half
    w_t, bcol, bvrow, w_mix, vecs, ff_in, ff_out = weights
    s_even, s_odd, q_t, ko_t, vo_t, u_c, k_c, mix_t, lse, nrm0, inv0, gp, hid, nrm1, inv1 = saved
    ins = [
        rank_col, unk, g_own, g_oth, s_even, u_own, q_t, ko_t, vo_t, u_c, k_c, mix_t, lse, nrm0, inv0,
        gp, hid, nrm1, inv1, w_t, bvrow, w_mix, vecs, ff_in, ff_out,
    ]
    tok = shape_of((half, D))
    square = shape_of((D, D), F32)
    outs = [tok, tok, shape_of((half, D), F32), tok, shape_of((D, 3 * D), F32), square, square, square,
            shape_of((8, D), F32), shape_of((D, 2), F32)]
    specs = [None if x is None else full(x.shape) for x in ins]
    if u_spec is not None:
        specs[5] = u_spec
    kernel = backward_kernel
    if g_oth is None:
        del ins[3], specs[3], outs[0]

        def kernel(scal, rank_col, unk, g_own, *rest):
            saved_refs, out_refs = rest[:21], rest[21:]
            backward_kernel(scal, rank_col, unk, g_own, None, *saved_refs, None, *out_refs)

    scratch = [
        pltpu.VMEM((half, D), BF),
        pltpu.VMEM((half, D), BF),
        pltpu.VMEM((half, D), F32),
        pltpu.VMEM((HEADS, 128, half), BF),
        pltpu.VMEM((HEADS, 128, half), BF),
        pltpu.VMEM((D, half), BF),
        pltpu.VMEM((HEADS, 1, half), F32),
        pltpu.VMEM((D, length), BF),
        pltpu.VMEM((length, D), BF),
        pltpu.VMEM((length, 128), F32),
        pltpu.VMEM((D, half), F32),
        pltpu.VMEM((length, 2 * D), BF),
        pltpu.VMEM((half, D), F32),
    ]
    out = call(kernel, scal, ins, specs, outs, scratch, half * 2**24)
    return ([None] + list(out)) if g_oth is None else out


def make_per_device(dp_count, section_count):
    both = ("dp", "section")

    def index(dp, section):
        return dp * section_count + section

    mate_pairs = [
        (index(d, s), index(d ^ 1, s)) for d in range(dp_count) for s in range(section_count)
    ]
    fetch_pairs = [
        (index(d, s), index(d ^ 1, s))
        for d in range(dp_count)
        for s in range(section_count)
        if d % 2 == s // 2
    ]

    def per_device(
        block_input, known_genes, attn_proj, attn_out, query_bias, value_bias, out_bias, ff_in, ff_out,
        ff_bias_in, ff_bias_out, norm_gain, norm_shift, cotangent,
    ):
        core = lax.axis_index("dp") % 2
        section = lax.axis_index("section")
        owner = section // 2
        slot = section % 2

        def row_of(array):
            local = lax.dynamic_index_in_dim(array, slot, 0, keepdims=False)
            sent = lax.ppermute(local, both, fetch_pairs)
            return jnp.where(core == owner, local, sent)

        known = row_of(known_genes)
        row = row_of(block_input)
        cot = row_of(cotangent)

        layers = []
        w_t_all = jnp.swapaxes(attn_proj, 1, 2)
        bcols = jnp.stack([query_bias, value_bias], axis=2)
        zero = jnp.zeros((2, D), F32)
        vecs_all = jnp.stack(
            [out_bias, norm_gain[:, 0], norm_shift[:, 0], ff_bias_in, ff_bias_out, norm_gain[:, 1], norm_shift[:, 1], zero],
            axis=1,
        )
        for layer in range(2):
            layers.append(
                (w_t_all[layer], bcols[layer], value_bias[layer][None], attn_out[layer], vecs_all[layer], ff_in[layer], ff_out[layer])
            )

        cells = []
        for start, length in ((0, LONG), (LONG, SHORT)):
            half = length // 2
            parts = known[start : start + length].reshape(2, half)
            own = lax.dynamic_index_in_dim(parts, core, 0, keepdims=False)
            oth = lax.dynamic_index_in_dim(parts, 1 - core, 0, keepdims=False)
            order = jnp.concatenate([own, oth])
            ids = lax.iota(jnp.int32, length)
            rank = jnp.sum(jnp.where(ids[None, :] <= ids[:, None], order[None, :], 0), axis=1) - 1
            rank = jnp.where(order == 1, rank, -1)
            unk = jnp.where(own == 1, FILL, 0.0).astype(F32)[None]
            scal = jnp.stack([core, jnp.sum(order)]).astype(jnp.int32)
            base = start // half
            blocks = row.reshape(-1, half, D)
            own_spec = pl.BlockSpec((None, half, D), lambda i, s, base=base: (base + s[0], 0, 0))
            oth_spec = pl.BlockSpec((None, half, D), lambda i, s, base=base: (base + 1 - s[0], 0, 0))
            cells.append(dict(half=half, scal=scal, row=rank[None], col=rank[:, None], unk=unk, blocks=blocks,
                              own=own_spec, oth=oth_spec, start=start))

        def mate(x):
            return lax.ppermute(x, both, mate_pairs)

        for cell in cells:
            cell["f0"] = forward_layer(cell["scal"], cell["row"], cell["unk"], cell["blocks"], cell["blocks"], layers[0],
                                       cell["half"], cell["own"], cell["oth"])
            cell["x1"] = cell["f0"][1]
            cell["x1o"] = mate(cell["x1"])
        for cell in cells:
            cell["f1"] = forward_layer(cell["scal"], cell["row"], cell["unk"], cell["x1"], cell["x1o"], layers[1], cell["half"])
        for cell in cells:
            half = cell["half"]
            cots = lax.dynamic_index_in_dim(
                cot[cell["start"] : cell["start"] + 2 * half].reshape(2, half, D), core, 0, keepdims=False
            )
            cell["b1"] = backward_layer(cell["scal"], cell["col"], cell["unk"], cots, None, cell["x1"], cell["f1"], layers[1], half)
            cell["b1o"] = mate(cell["b1"][3])
        for cell in cells:
            half = cell["half"]
            cell["b0"] = backward_layer(cell["scal"], cell["col"], cell["unk"], cell["b1"][2], cell["b1o"], cell["blocks"], cell["f0"],
                                        layers[0], half, cell["own"])
            cell["b0o"] = mate(cell["b0"][3])
            cell["g0"] = (cell["b0"][2] + cell["b0o"].astype(F32)).astype(BF)

        def place(parts):
            got = lax.all_to_all(parts, "section", 0, 0)
            mine = lax.dynamic_slice_in_dim(got, 2 * core, 2, 0)
            theirs = mate(lax.dynamic_slice_in_dim(got, 2 - 2 * core, 2, 0))
            first = jnp.where(core == 0, mine, theirs)
            second = jnp.where(core == 0, theirs, mine)
            lh, sh = LONG // 2, SHORT // 2
            return jnp.concatenate([first[:, :lh], second[:, :lh], first[:, lh:], second[:, lh:]], axis=1)[None]

        outs = jnp.stack([
            jnp.concatenate([cells[0][f][k], cells[1][f][k]], axis=0) for f, k in (("f0", 0), ("f0", 1), ("f1", 0), ("f1", 1))
        ])
        grads = jnp.stack([
            jnp.concatenate(p, axis=0)
            for p in (
                [c["g0"] for c in cells], [c["b0"][1] for c in cells], [c["b0"][0] for c in cells], [c["b1"][1] for c in cells],
            )
        ])
        section_outputs = place(outs)
        section_grads = place(grads)

        def both_layers(k):
            return jnp.stack([sum(c[b][k] for c in cells) for b in ("b0", "b1")])

        tot_qkv, tot_mix, tot_in, tot_out, tot_vec, tot_col = [both_layers(k) for k in range(4, 10)]
        vec = [tot_vec[:, k] for k in range(7)] + [tot_col[:, :, 0], tot_col[:, :, 1]]
        total = dp_count * section_count

        def blocks(x, width):
            return jnp.moveaxis(x.reshape(2, total, -1), 1, 0).reshape(total, 2 * width)

        size = D // total
        widths = [size * 3 * D] + [size * D] * 3 + [size] * 9
        packed = jnp.concatenate(
            [blocks(x, w) for x, w in zip([tot_qkv, tot_mix, tot_in, tot_out] + vec, widths)], axis=1
        ).astype(BF)
        width = packed.shape[1]
        held = packed.reshape(dp_count, section_count, width)
        me = lax.axis_index("dp")
        bits = dp_count.bit_length() - 1
        kept = held.reshape((2,) * bits + (section_count, width))
        for bit in range(bits):
            axis = bits - 1 - bit
            mine = (me >> bit) & 1
            keep = lax.dynamic_index_in_dim(kept, mine, axis, keepdims=True)
            send = lax.dynamic_index_in_dim(kept, 1 - mine, axis, keepdims=True)
            pairs = [
                (index(d, s), index(d ^ (1 << bit), s)) for d in range(dp_count) for s in range(section_count)
            ]
            kept = (keep.astype(F32) + lax.ppermute(send, both, pairs).astype(F32)).astype(BF)
        kept = kept.reshape(section_count, width)
        final = jnp.sum(lax.all_to_all(kept, "section", 0, 0).astype(F32), axis=0)
        pieces, at = [], 0
        for w in widths:
            pieces.append(final[at : at + 2 * w])
            at += 2 * w
        g_qkv = pieces[0].reshape(2, size, 3 * D)
        g_mix, g_in, g_out = [x.reshape(2, size, D) for x in pieces[1:4]]
        v = [x.reshape(2, size) for x in pieces[4:]]
        return (
            section_outputs, section_grads, g_qkv, g_mix, v[7], v[8], v[0], g_in, g_out, v[3], v[4],
            jnp.stack([v[1], v[5]], axis=1), jnp.stack([v[2], v[6]], axis=1),
        )

    return per_device


def solution(mesh):
    rows = P("dp", None, None)
    placed = (rows, P("dp", None)) + (P(),) * 11 + (rows,)
    sections = P("section", "dp", None, None)
    matrix = P(None, ("dp", "section"), None)
    vector = P(None, ("dp", "section"))
    pairs = P(None, None, ("dp", "section"))
    return jax.shard_map(
        make_per_device(mesh.shape["dp"], mesh.shape["section"]),
        mesh=mesh,
        in_specs=placed,
        out_specs=(
            sections, sections, matrix, matrix, vector, vector, vector, matrix, matrix, vector, vector, pairs, pairs,
        ),
        check_vma=False,
    )
```

```python
from types import SimpleNamespace

import jax
import jax.numpy as jnp
from jax import lax
from jax.experimental import pallas as pl
from jax.experimental.pallas import tpu as pltpu
from jax.sharding import PartitionSpec as P

D = 512
HEADS = 8
HEAD_DIM = 64
LONG = 1024
SHORT = 512
ROW = LONG + SHORT
EPS = 1e-05
FILL = -1e30
SCALE = HEAD_DIM ** (-0.5)
LOG2E = 1.4426950408889634
LN2 = 0.6931471805599453
SOFT = SCALE * LOG2E
BF = jnp.bfloat16
F32 = jnp.float32
VAUG = HEAD_DIM + 16
PACK = 3 * D + 3 * D + 128
SMALLEST, LARGEST = 2.0 ** -60, 2.0 ** 90
VMEM_LIMIT = 48 * 1024 * 1024
LAYER_PARAMS = (
    "attn_proj", "attn_out", "ff_in", "ff_out",
    "query_bias", "value_bias", "out_bias", "ff_bias_in", "ff_bias_out", "norm_gain", "norm_shift",
)
MATRICES = LAYER_PARAMS[:4]


def nn(a, b):
    return lax.dot_general(a, b, (((1,), (0,)), ((), ())), preferred_element_type=F32)


def nt(a, b):
    return lax.dot_general(a, b, (((1,), (1,)), ((), ())), preferred_element_type=F32)


def tn(a, b):
    return lax.dot_general(a, b, (((0,), (0,)), ((), ())), preferred_element_type=F32)


def call(body, ins, outs, scratch, flops=2**30, aliases=None, sems=32):
    names = list(ins) + list(outs) + list(scratch) + ["sems"]

    def kernel(*refs):
        body(SimpleNamespace(**dict(zip(names, refs))))

    in_names, out_names = list(ins), list(outs)
    result = pl.pallas_call(
        kernel,
        in_specs=[pl.BlockSpec(memory_space=space) for _, space in ins.values()],
        out_specs=[pl.BlockSpec(memory_space=space) for _, _, space in outs.values()],
        out_shape=[jax.ShapeDtypeStruct(shape, dtype) for shape, dtype, _ in outs.values()],
        scratch_shapes=[pltpu.VMEM(shape, dtype) for shape, dtype in scratch.values()] + [pltpu.SemaphoreType.DMA((sems,))],
        input_output_aliases={in_names.index(a): out_names.index(b) for a, b in (aliases or {}).items()},
        compiler_params=pltpu.CompilerParams(vmem_limit_bytes=VMEM_LIMIT),
        cost_estimate=pl.CostEstimate(flops=flops, bytes_accessed=12 * 2**20, transcendentals=2**20),
    )(*[array for array, _ in ins.values()])
    return dict(zip(out_names, result))


class Copies:
    def __init__(self, sems):
        self.sems, self.used, self.ends = sems, 0, []

    def start(self, src, dst):
        copy = pltpu.make_async_copy(src, dst, self.sems.at[self.used])
        self.used += 1
        copy.start()
        return copy

    def either(self, first, src_a, src_b, dst):
        sem = self.sems.at[self.used]
        self.used += 1
        pl.when(first)(lambda: pltpu.make_async_copy(src_a, dst, sem).start())
        pl.when(jnp.logical_not(first))(lambda: pltpu.make_async_copy(src_b, dst, sem).start())
        return pltpu.make_async_copy(src_a, dst, sem)

    def one_of(self, src, dsts, which):
        sem = self.sems.at[self.used]
        self.used += 1
        for at, dst in enumerate(dsts):
            pl.when(which == at)(lambda dst=dst: pltpu.make_async_copy(src, dst, sem).start())
        self.ends.append(pltpu.make_async_copy(src, dsts[0], sem))

    def out(self, src, dst):
        self.ends.append(self.start(src, dst))

    def finish(self):
        for copy in self.ends:
            copy.wait()


def norm_rows(residual):
    center = residual - jnp.mean(residual, axis=-1, keepdims=True)
    inv_std = lax.rsqrt(jnp.mean(center * center, axis=-1, keepdims=True) + EPS)
    return center * inv_std, inv_std


def norm_back(grad, normed, inv, gain):
    e = grad * gain
    return inv * (
        e - jnp.mean(e, axis=-1, keepdims=True) - normed * jnp.mean(e * normed, axis=-1, keepdims=True)
    )


def one_hot_rows(rank_row, size, length):
    return (lax.broadcasted_iota(jnp.int32, (size, length), 0) == rank_row).astype(F32).astype(BF)


def one_hot_cols(rank_col, size):
    length = rank_col.shape[0]
    return (lax.broadcasted_iota(jnp.int32, (length, size), 1) == rank_col).astype(F32).astype(BF)


def put_masked(dst, src, tokens):
    zeros = jnp.zeros((HEAD_DIM, tokens), BF)
    for head in range(HEADS):
        part = (head % 2) * HEAD_DIM
        dst[head, part : part + HEAD_DIM, :] = src[head * HEAD_DIM : (head + 1) * HEAD_DIM, :]
        dst[head, HEAD_DIM - part : 2 * HEAD_DIM - part, :] = zeros


def head_sums(a, b):
    out = []
    for head in range(HEADS):
        rows = slice(head * HEAD_DIM, (head + 1) * HEAD_DIM)
        out.append(jnp.sum(a[rows, :].astype(F32) * b[rows, :].astype(F32), axis=0, keepdims=True))
    return out


def rank_tokens(known, length):
    upto = lax.broadcasted_iota(jnp.int32, (length, length), 0) <= lax.broadcasted_iota(jnp.int32, (length, length), 1)
    low = jnp.broadcast_to(known.astype(F32), (8, length))
    place = nn(low.astype(BF), upto.astype(F32).astype(BF))
    return jnp.where(low > 0.5, place - 1.0, -1.0).astype(jnp.int32)


def small_count(length):
    return length // 2 + length // 8


def param_row(ref, layer, kind=None):
    return ref[pl.ds(layer, 1), :] if kind is None else ref[layer, pl.ds(kind, 1), :]


def forward_body(r, half, start, layer):
    length = 2 * half
    core, slot_ship = r.scal[0], r.scal[3]
    copies = Copies(r.sems)
    if layer == 0:
        mine, slot = r.scal[1] == 1, r.scal[2]
        own_rows = pl.ds(pl.multiple_of(start + core * half, half), half)
        oth_rows = pl.ds(pl.multiple_of(start + (1 - core) * half, half), half)
        u_own_in = copies.either(mine, r.x_here.at[slot, own_rows], r.x_there.at[slot, own_rows], r.u_own)
        u_oth_in = copies.either(mine, r.x_here.at[slot, oth_rows], r.x_there.at[slot, oth_rows], r.u_oth)
    else:
        u_own_in = copies.start(r.x_own, r.u_own)
        u_oth_in = copies.start(r.x_oth, r.u_oth)
    w_in = copies.start(r.attn_proj.at[layer], r.w)
    late = [
        copies.start(r.attn_out.at[layer], r.w_mix),
        copies.start(r.ff_in.at[layer], r.w_up),
        copies.start(r.ff_out.at[layer], r.w_down),
    ]
    if layer == 0:
        here = r.known_here[pl.ds(slot, 1), :]
        there = r.known_there[pl.ds(slot, 1), :]
        known = jnp.where(mine, here, there)[:, start : start + length]
        first, second = known[:, :half], known[:, half:]
        known = jnp.concatenate([jnp.where(core == 0, first, second), jnp.where(core == 0, second, first)], axis=1)
        rank = rank_tokens(known, length)
        r.rank[...] = rank
    else:
        rank = r.rank[...]
    rank_row = rank[0:1, :]
    count = jnp.max(rank_row) + 1
    unk = jnp.where(rank_row[:, :half] >= 0, FILL, 0.0)

    u_own_in.wait()
    w_in.wait()
    own = nn(r.u_own[...], r.w[...])
    r.q_t[...] = (own[:, :D] + param_row(r.query_bias, layer)).astype(BF).T
    r.ko_t[...] = (own[:, D : 2 * D] * SOFT).astype(BF).T
    r.vo_t[...] = (own[:, 2 * D :] + param_row(r.value_bias, layer)).astype(BF).T
    put_masked(r.qm, r.q_t, half)
    for head, row in enumerate(head_sums(r.q_t, r.ko_t)):
        r.sd[head] = row + unk
        r.total[head] = jnp.zeros_like(row)
        r.top[head] = jnp.zeros_like(row)
    u_oth_in.wait()
    block = min(half, 256)

    def keys(size):
        pick = one_hot_rows(rank_row, size, length)
        uc = (nn(pick[:, :half], r.u_own[...]) + nn(pick[:, half:], r.u_oth[...])).astype(BF)
        r.uc[:size, :] = uc
        kv = nn(uc, r.w[:, D:])
        r.k_c[:size, :] = (kv[:, :D] * SOFT).astype(BF)
        inside = lax.broadcasted_iota(jnp.int32, (size, D), 0) < count
        vc = jnp.where(inside, kv[:, D:] + param_row(r.value_bias, layer), 0.0).astype(BF)
        r.v_c[:size, :] = vc
        vct = vc.T
        ones = lax.broadcasted_iota(jnp.int32, (16, size), 1) < count
        ones = (ones & (lax.broadcasted_iota(jnp.int32, (16, size), 0) == 0)).astype(F32).astype(BF)
        for head in range(HEADS):
            r.vaug[head * VAUG : head * VAUG + HEAD_DIM, :size] = vct[head * HEAD_DIM : (head + 1) * HEAD_DIM, :]
            r.vaug[head * VAUG + HEAD_DIM : (head + 1) * VAUG, :size] = ones

    def attend(size, safe):
        if safe:
            r.kb[...] = jnp.where(lax.broadcasted_iota(jnp.int32, (size, 128), 0) < count, 0.0, FILL)

        def pair(p, carry):
            kcp = r.k_c[:size, pl.ds(pl.multiple_of(p * 128, 128), 128)]
            for e in range(2):
                head = 2 * p + e
                vrows = r.vaug[pl.ds(pl.multiple_of(head * VAUG, 16), VAUG), :size]
                rows = pl.ds(pl.multiple_of(head * HEAD_DIM, HEAD_DIM), HEAD_DIM)
                for at in range(0, half, block):
                    cols = slice(at, at + block)
                    scores = nn(kcp, r.qm[head, :, cols])
                    own_score = r.sd[head, :, cols]
                    if safe:
                        tops, probs = [], []
                        for t in range(0, block, 128):
                            part = scores[:, t : t + 128] + r.kb[...]
                            top = jnp.maximum(jnp.max(part, axis=0, keepdims=True), own_score[:, t : t + 128])
                            tops.append(top)
                            probs.append(jnp.exp2(part - top).astype(BF))
                        top = jnp.concatenate(tops, axis=1)
                        low = jnp.concatenate(probs, axis=1)
                        r.top[head, :, cols] = top
                        own_score = own_score - top
                    else:
                        low = jnp.exp2(scores).astype(BF)
                    mixed = nn(vrows, low)
                    own_prob = jnp.exp2(own_score)
                    total = mixed[HEAD_DIM : HEAD_DIM + 1] + own_prob
                    r.total[head, :, cols] = total
                    mixed = mixed[:HEAD_DIM] + own_prob * r.vo_t[rows, cols].astype(F32)
                    r.mix_t[rows, cols] = (mixed * (1.0 / total)).astype(BF)
            return carry

        lax.fori_loop(0, HEADS // 2, pair, 0)

    def quick():
        keys(small_count(length))
        attend(small_count(length), False)

    pl.when(count <= small_count(length))(quick)
    totals = r.total[...]
    fine = jnp.min(jnp.where((totals > SMALLEST) & (totals < LARGEST), 1, 0)) == 1

    def careful():
        keys(length)
        attend(length, True)

    pl.when(jnp.logical_not(fine))(careful)
    for copy in late:
        copy.wait()

    for at in range(0, half, 256):
        rows = slice(at, at + 256)
        res = r.u_own[rows, :].astype(F32) + tn(r.mix_t[:, rows], r.w_mix[...]) + param_row(r.out_bias, layer)
        normed, inv0 = norm_rows(res)
        r.nrm0[rows, :] = normed.astype(BF)
        even = (normed * param_row(r.norm_gain, layer, 0) + param_row(r.norm_shift, layer, 0)).astype(BF)
        r.even[rows, :] = even
        pre = nn(even, r.w_up[...]) + param_row(r.ff_bias_in, layer)
        cdf = 0.5 + 0.5 * lax.erf(pre * 0.7071067811865476)
        hidden = (pre * cdf).astype(BF)
        r.hid[rows, :] = hidden
        r.gp[rows, :] = (cdf + pre * (0.3989422804014327 * jnp.exp(-0.5 * pre * pre))).astype(BF)
        res = even.astype(F32) + nn(hidden, r.w_down[...]) + param_row(r.ff_bias_out, layer)
        normed, inv1 = norm_rows(res)
        r.nrm1[rows, :] = normed.astype(BF)
        r.odd[rows, :] = (normed * param_row(r.norm_gain, layer, 1) + param_row(r.norm_shift, layer, 1)).astype(BF)
        r.inv[rows, :] = jnp.where(lax.broadcasted_iota(jnp.int32, (256, 128), 1) == 0, inv0, inv1)

    for name in SAVED:
        copies.out(getattr(r, name), getattr(r, name + "_out"))
    copies.out(r.odd, r.odd_out)
    base = 0 if start == 0 else LONG // 2
    sends = [s.at[pl.ds(base, half)] for s in (r.send0, r.send1, r.send2, r.send3)]
    copies.one_of(r.even, sends, slot_ship ^ (2 * layer))
    copies.one_of(r.odd, sends, slot_ship ^ (2 * layer + 1))
    copies.finish()


SAVED = ("even", "q_t", "ko_t", "vo_t", "uc", "k_c", "v_c", "mix_t", "nrm0", "nrm1", "gp", "hid", "inv", "top", "total")


def buffers(half):
    length = 2 * half
    tok, feat, keys = ((half, D), BF), ((D, half), BF), ((length, D), BF)
    rows = ((HEADS, 1, half), F32)
    return dict(
        even=tok, q_t=feat, ko_t=feat, vo_t=feat, uc=keys, k_c=keys, v_c=keys, mix_t=feat, nrm0=tok, nrm1=tok, gp=tok,
        hid=tok, inv=((half, 128), F32), top=rows, total=rows,
    )


def weight_buffers():
    square = ((D, D), BF)
    return dict(w=((D, 3 * D), BF), w_mix=square, w_up=square, w_down=square)


def param_inputs(params):
    return {name: (params[name], pl.ANY if name in MATRICES else pltpu.VMEM) for name in LAYER_PARAMS}


def forward_layer(layer, half, start, scal, params, inputs, sends):
    length = 2 * half
    saved = buffers(half)
    ins = {"scal": (scal, pltpu.SMEM), **param_inputs(params), **inputs}
    outs = {name + "_out": (*saved[name], pl.ANY) for name in SAVED}
    outs["odd_out"] = ((half, D), BF, pl.ANY)
    aliases = {}
    for t in range(4):
        outs[f"send{t}"] = ((ROW // 2, D), BF, pl.ANY)
        if sends is not None:
            ins[f"sent{t}"] = (sends[t], pl.ANY)
            aliases[f"sent{t}"] = f"send{t}"
    if layer == 0:
        outs["rank"] = ((8, length), jnp.int32, pltpu.VMEM)
    scratch = {
        **saved, **weight_buffers(), "u_own": ((half, D), BF), "u_oth": ((half, D), BF), "odd": ((half, D), BF),
        "qm": ((HEADS, 128, half), BF), "vaug": ((HEADS * VAUG, length), BF), "kb": ((length, 128), F32),
        "sd": ((HEADS, 1, half), F32),
    }
    out = call(lambda r: forward_body(r, half, start, layer), ins, outs, scratch, half * 2**23, aliases)
    return out, [out[f"send{t}"] for t in range(4)]


def backward_body(r, half, start, layer, last):
    length = 2 * half
    core, slot_ship = r.scal[0], r.scal[3]
    copies = Copies(r.sems)
    u_rows = pl.ds(pl.multiple_of(start + core * half, half), half)
    mine, slot = r.scal[1] == 1, r.scal[2]
    if layer == 1:
        g_in = [copies.either(mine, r.c_here.at[slot, u_rows], r.c_there.at[slot, u_rows], r.g)]
        u_in = copies.start(r.x_own, r.u_own)
    else:
        g_in = [copies.start(r.dx_own, r.dx), copies.start(r.dx_oth, r.g)]
        u_in = copies.either(mine, r.x_here.at[slot, u_rows], r.x_there.at[slot, u_rows], r.u_own)
    loads = {}
    for name in ("nrm1", "inv", "gp", "nrm0", "hid", "even", "mix_t", "q_t", "k_c", "v_c", "top", "total", "ko_t", "vo_t", "uc"):
        loads[name] = copies.start(getattr(r, name + "_in"), getattr(r, name))
        if name == "inv":
            loads["w_down"] = copies.start(r.ff_out.at[layer], r.w_down)
            loads["w_up"] = copies.start(r.ff_in.at[layer], r.w_up)
        if name == "mix_t":
            loads["w_mix"] = copies.start(r.attn_out.at[layer], r.w_mix)
    loads["w"] = copies.start(r.attn_proj.at[layer], r.w)
    if last:
        loads["prev"] = copies.start(r.prev_pack, r.prev)

    def need(*names):
        for name in names:
            loads.pop(name).wait()

    sums = [jnp.zeros((1, D), F32) for _ in range(7)]

    def add(slot, value):
        sums[slot] = sums[slot] + jnp.sum(value, axis=0, keepdims=True)

    for copy in g_in:
        copy.wait()
    need("nrm1", "inv", "w_down", "w_up", "gp", "nrm0")
    for at in range(0, half, 256):
        rows = slice(at, at + 256)
        if layer == 1:
            grad = r.g[rows, :].astype(F32)
        else:
            low = (r.dx[rows, :] + r.g[rows, :].astype(F32)).astype(BF)
            r.g[rows, :] = low
            grad = low.astype(F32)
        normed = r.nrm1[rows, :].astype(F32)
        add(5, grad * normed)
        add(6, grad)
        dres = norm_back(grad, normed, r.inv[rows, 1:2], param_row(r.norm_gain, layer, 1))
        add(4, dres)
        low = dres.astype(BF)
        r.db1[rows, :] = low
        dp = nt(low, r.w_down[...]) * r.gp[rows, :].astype(F32)
        add(3, dp)
        low = dp.astype(BF)
        r.dpre[rows, :] = low
        low = (dres + nt(low, r.w_up[...])).astype(BF)
        r.g_odd[rows, :] = low
        grad = low.astype(F32)
        normed = r.nrm0[rows, :].astype(F32)
        add(1, grad * normed)
        add(2, grad)
        dres = norm_back(grad, normed, r.inv[rows, 0:1], param_row(r.norm_gain, layer, 0))
        add(0, dres)
        r.dr[rows, :] = dres
        r.db0[rows, :] = dres.astype(BF)

    sends = (r.send0, r.send1, r.send2, r.send3)
    copies.one_of(r.g_odd, sends, slot_ship ^ (2 * layer + 1))
    if layer == 0:
        copies.one_of(r.g, sends, slot_ship ^ 2)

    if last:
        need("prev")

    def put(cols, value):
        if last:
            value = value + r.prev[:, cols].astype(F32)
        r.pack[:, cols] = value.astype(BF)

    need("hid", "even", "mix_t", "w_mix")
    put(slice(5 * D, 6 * D), tn(r.hid[...], r.db1[...]))
    put(slice(4 * D, 5 * D), tn(r.even[...], r.dpre[...]))
    put(slice(3 * D, 4 * D), nn(r.mix_t[...], r.db0[...]))
    dm_t = nt(r.w_mix[...], r.db0[...]).astype(BF)
    r.dm_t[...] = dm_t
    dm_sum = jnp.sum(dm_t.astype(F32), axis=1, keepdims=True)
    need("q_t", "top", "total", "ko_t", "vo_t")
    put_masked(r.qm, r.q_t, half)
    zeros = jnp.zeros((HEAD_DIM, half), BF)
    deltas = head_sums(r.dm_t, r.mix_t)
    for head in range(HEADS):
        rows = slice(head * HEAD_DIM, (head + 1) * HEAD_DIM)
        part = (head % 2) * HEAD_DIM
        inv_total = 1.0 / r.total[head]
        r.total[head] = inv_total
        r.delta[head] = deltas[head] * inv_total
        r.dmm[head, part : part + HEAD_DIM, :] = (r.dm_t[rows, :].astype(F32) * inv_total).astype(BF)
        r.dmm[head, HEAD_DIM - part : 2 * HEAD_DIM - part, :] = zeros
    block = min(half, 256)
    need("k_c", "v_c", "uc", "w")
    rank = r.rank[...]
    count = jnp.max(rank[0:1, :]) + 1
    rank_col = rank.astype(F32).T[:, 0:1].astype(jnp.int32)
    quick_ok = (count <= small_count(length)) & (jnp.max(jnp.abs(r.top[...])) == 0.0)

    def run(size, safe):
        r.kc_t[:, :size] = r.k_c[:size, :].T
        if safe:
            r.kb[...] = jnp.where(lax.broadcasted_iota(jnp.int32, (size, 128), 0) < count, 0.0, FILL)

        def pair(p, carry):
            lanes = pl.ds(pl.multiple_of(p * 128, 128), 128)
            kcp = r.k_c[:size, lanes]
            vcp = r.v_c[:size, lanes]
            dk = jnp.zeros((size, 128), F32)
            dv = jnp.zeros((size, 128), F32)
            for e in range(2):
                head = 2 * p + e
                rows = pl.ds(pl.multiple_of(head * HEAD_DIM, HEAD_DIM), HEAD_DIM)
                for at in range(0, half, block):
                    cols = slice(at, at + block)
                    qtm = r.qm[head, :, cols]
                    dmh = r.dmm[head, :, cols]
                    scores = nn(kcp, qtm)
                    dprob = nn(vcp, dmh)
                    delta = r.delta[head, :, cols]
                    if safe:
                        top = r.top[head, :, cols]
                        lows, grads = [], []
                        for t in range(0, block, 128):
                            tile = slice(t, t + 128)
                            prob = jnp.exp2(jnp.minimum(scores[:, tile] - top[:, tile], r.kb[...]))
                            lows.append(prob.astype(BF))
                            grads.append((prob * (dprob[:, tile] - delta[:, tile])).astype(BF))
                        low = jnp.concatenate(lows, axis=1)
                        ds = jnp.concatenate(grads, axis=1)
                    else:
                        prob = jnp.exp2(scores)
                        low = prob.astype(BF)
                        ds = (prob * (dprob - delta)).astype(BF)
                    dv = dv + nt(low, dmh)
                    dk = dk + nt(ds, qtm)
                    r.dq_t[rows, cols] = nn(r.kc_t[rows, :size], ds) * LN2
            r.dkv[:size, lanes] = (dk * SCALE).astype(BF)
            r.dkv[:size, pl.ds(pl.multiple_of(D + p * 128, 128), 128)] = dv.astype(BF)
            return carry

        lax.fori_loop(0, HEADS // 2, pair, 0)
        dkv = r.dkv[:size, :]
        r.dw_kv[...] = tn(r.uc[:size, :], dkv)
        dxc = nt(dkv, r.w[:, D:]).astype(BF)
        r.dr[...] += nn(one_hot_cols(rank_col[:half, :], size), dxc)
        r.dxo[...] = nn(one_hot_cols(rank_col[half:, :], size), dxc).astype(BF)

    pl.when(quick_ok)(lambda: run(small_count(length), False))
    pl.when(jnp.logical_not(quick_ok))(lambda: run(length, True))
    copies.out(r.dxo, r.dx_oth_out)

    unk = jnp.where(rank[0:1, :half] >= 0, FILL, 0.0)
    own_scores = head_sums(r.q_t, r.ko_t)
    own_dprobs = head_sums(r.dm_t, r.vo_t)
    dq_parts, dk_parts, dv_parts = [], [], []
    for head in range(HEADS):
        rows = slice(head * HEAD_DIM, (head + 1) * HEAD_DIM)
        inv_total = r.total[head]
        prob = jnp.exp2(own_scores[head] + unk - r.top[head]) * inv_total
        ds = (prob * own_dprobs[head] - prob * (r.delta[head] / inv_total)).astype(BF).astype(F32)
        low = prob.astype(BF).astype(F32)
        dq_parts.append(r.dq_t[rows, :] + (ds * LN2) * r.ko_t[rows, :].astype(F32))
        dk_parts.append(((ds * SCALE) * r.q_t[rows, :].astype(F32)).astype(BF))
        dv_parts.append((low * r.dm_t[rows, :].astype(F32)).astype(BF))
    dq = jnp.concatenate(dq_parts, axis=0)
    dq_sum = jnp.sum(dq, axis=1, keepdims=True)
    dp = jnp.concatenate([dq.astype(BF)] + dk_parts + dv_parts, axis=0).T
    u_in.wait()
    dw = tn(r.u_own[...], dp)
    put(slice(0, D), dw[:, :D])
    put(slice(D, 3 * D), dw[:, D:] + r.dw_kv[...])
    r.dr[...] += nt(dp, r.w[...])
    copies.out(r.dr, r.dx_own_out)
    vectors = jnp.concatenate(sums + [jnp.zeros((121, D), F32)], axis=0).T
    lane = lax.broadcasted_iota(jnp.int32, (D, 128), 1)
    vectors = jnp.where(lane == 7, dq_sum, jnp.where(lane == 8, dm_sum, vectors))
    put(slice(6 * D, 6 * D + 128), vectors)
    copies.out(r.pack, r.pack_out)
    copies.finish()


def backward_layer(layer, half, start, scal, params, saved, inputs, rank, sends, prev):
    length = 2 * half
    shapes = buffers(half)
    tok = ((half, D), BF)
    ins = {"scal": (scal, pltpu.SMEM), **param_inputs(params), **inputs, "rank": (rank, pltpu.VMEM)}
    for name in SAVED:
        ins[name + "_in"] = (saved[name + "_out"], pl.ANY)
    outs = {
        "dx_own_out": ((half, D), F32, pl.ANY), "dx_oth_out": (*tok, pl.ANY), "pack_out": ((D, PACK), BF, pl.ANY),
    }
    aliases = {}
    for t in range(4):
        outs[f"send{t}"] = (*tok, pl.ANY)
        if sends is not None:
            ins[f"sent{t}"] = (sends[t], pl.ANY)
            aliases[f"sent{t}"] = f"send{t}"
    scratch = {
        **shapes, **weight_buffers(), "u_own": tok, "g": tok, "g_odd": tok, "db0": tok, "db1": tok, "dpre": tok, "dxo": tok,
        "dr": ((half, D), F32), "qm": ((HEADS, 128, half), BF), "dmm": ((HEADS, 128, half), BF), "dm_t": ((D, half), BF),
        "delta": ((HEADS, 1, half), F32), "kc_t": ((D, length), BF), "kb": ((length, 128), F32), "dq_t": ((D, half), F32),
        "dkv": ((length, 2 * D), BF), "dw_kv": ((D, 2 * D), F32), "pack": ((D, PACK), BF),
    }
    if layer == 0:
        scratch["dx"] = ((half, D), F32)
    if prev is not None:
        ins["prev_pack"] = (prev, pl.ANY)
        scratch["prev"] = ((D, PACK), BF)
    out = call(
        lambda r: backward_body(r, half, start, layer, prev is not None), ins, outs, scratch, half * 2**24, aliases, 40
    )
    return out, [out[f"send{t}"] for t in range(4)]


def first_grads(half, scal, dx_own, dx_oth, sends):
    def body(r):
        copies = Copies(r.sems)
        r.total[...] = (r.own[...] + r.oth[...].astype(F32)).astype(BF)
        copies.one_of(r.total, (r.send0, r.send1, r.send2, r.send3), r.scal[3])
        copies.finish()

    tok = ((half, D), BF)
    ins = {"scal": (scal, pltpu.SMEM), "own": (dx_own, pltpu.VMEM), "oth": (dx_oth, pltpu.VMEM)}
    for t in range(4):
        ins[f"sent{t}"] = (sends[t], pl.ANY)
    outs = {f"send{t}": (*tok, pl.ANY) for t in range(4)}
    out = call(body, ins, outs, {"total": tok}, 2**20, {f"sent{t}": f"send{t}" for t in range(4)}, 4)
    return [out[f"send{t}"] for t in range(4)]


def assemble(scal, sets):
    def body(r):
        copies = Copies(r.sems)
        section = r.scal[4]
        for t in range(4):
            which = section ^ t
            slot, core = which // 2, which % 2
            for n, (pieces, start, half, base) in enumerate(sets):
                src = getattr(r, f"p{n}_{t}").at[pl.ds(base, half)]
                copies.out(src, r.out.at[0, slot, pl.ds(pl.multiple_of(start + core * half, half), half)])
        copies.finish()

    ins = {"scal": (scal, pltpu.SMEM)}
    for n, (pieces, _, _, _) in enumerate(sets):
        for t in range(4):
            ins[f"p{n}_{t}"] = (pieces[t], pl.ANY)
    return call(body, ins, {"out": ((1, 2, ROW, D), BF, pl.ANY)}, {}, 2**20, None, 4 * len(sets))["out"]


def unpack(packs, size):
    wide = ((2, size, 3 * D), F32, pltpu.VMEM)
    square = ((2, size, D), F32, pltpu.VMEM)
    vec = ((2, size), F32, pltpu.VMEM)
    pair = ((2, 2, size), F32, pltpu.VMEM)
    outs = dict(
        proj=wide, out=square, qb=vec, vb=vec, ob=vec, up=square, down=square, ub=vec, db=vec, gain=pair, shift=pair
    )

    def body(r):
        for layer in range(2):
            pack = getattr(r, f"pack{layer}")
            r.proj[layer] = pack[:, : 3 * D].astype(F32)
            r.out[layer] = pack[:, 3 * D : 4 * D].astype(F32)
            r.up[layer] = pack[:, 4 * D : 5 * D].astype(F32)
            r.down[layer] = pack[:, 5 * D : 6 * D].astype(F32)
            cols = pack[:, 6 * D : 6 * D + 128].astype(F32).T
            for ref, k in ((r.ob, 0), (r.ub, 3), (r.db, 4), (r.qb, 7), (r.vb, 8)):
                ref[layer : layer + 1, :] = cols[k : k + 1, :]
            for kind in range(2):
                r.gain[layer, kind : kind + 1, :] = cols[4 * kind + 1 : 4 * kind + 2, :]
                r.shift[layer, kind : kind + 1, :] = cols[4 * kind + 2 : 4 * kind + 3, :]

    ins = {f"pack{layer}": (packs[layer], pltpu.VMEM) for layer in range(2)}
    return list(call(body, ins, outs, {}, 2**20, None, 1).values())


def make_per_device(dp_count, section_count):
    both = ("dp", "section")

    def index(dp, section):
        return dp * section_count + section

    everyone = [(d, s) for d in range(dp_count) for s in range(section_count)]
    mate_pairs = [(index(d, s), index(d ^ 1, s)) for d, s in everyone]
    fetch_pairs = [(index(d, s), index(d ^ 1, s)) for d, s in everyone if d % 2 == s // 2]

    def round_pairs(t, sections):
        pairs = []
        for d, z in everyone:
            to = (2 * (z % 2) + d % 2) ^ t
            if to in sections:
                pairs.append((index(d, z), index(d - d % 2 + z // 2, to)))
        return pairs

    def ship(sends, sections=(0, 1, 2, 3)):
        return [lax.ppermute(sends[t], both, round_pairs(t, sections)) for t in range(4)]

    def mate(x):
        return lax.ppermute(x, both, mate_pairs)

    def per_device(
        block_input, known_genes, attn_proj, attn_out, query_bias, value_bias, out_bias, ff_in, ff_out,
        ff_bias_in, ff_bias_out, norm_gain, norm_shift, cotangent,
    ):
        params = dict(
            attn_proj=attn_proj, attn_out=attn_out, query_bias=query_bias, value_bias=value_bias, out_bias=out_bias,
            ff_in=ff_in, ff_out=ff_out, ff_bias_in=ff_bias_in, ff_bias_out=ff_bias_out, norm_gain=norm_gain,
            norm_shift=norm_shift,
        )
        core = lax.axis_index("dp") % 2
        section = lax.axis_index("section")
        mine = (core == section // 2).astype(jnp.int32)
        scal = jnp.stack([core, mine, section % 2, 2 * (section % 2) + core, section]).astype(jnp.int32)

        known_there = lax.ppermute(known_genes, both, fetch_pairs)
        x_there = lax.ppermute(block_input, both, fetch_pairs)
        c_there = lax.ppermute(cotangent, both, fetch_pairs)
        x_in = {"x_here": (block_input, pl.ANY), "x_there": (x_there, pl.ANY)}
        c_in = {"c_here": (cotangent, pl.ANY), "c_there": (c_there, pl.ANY)}
        known_in = {"known_here": (known_genes, pltpu.VMEM), "known_there": (known_there, pltpu.VMEM)}

        cells = ((LONG // 2, 0), (SHORT // 2, LONG))
        f0, f1, x_own, x_oth = {}, {}, {}, {}
        sends = None
        for half, start in cells:
            f0[half], sends = forward_layer(0, half, start, scal, params, {**x_in, **known_in}, sends)
            x_own[half] = f0[half]["odd_out"]
            x_oth[half] = mate(x_own[half])
        got_low = ship(sends, (0, 1))
        sends = None
        for half, start in cells:
            ins = {"x_own": (x_own[half], pl.ANY), "x_oth": (x_oth[half], pl.ANY), "rank": (f0[half]["rank"], pltpu.VMEM)}
            f1[half], sends = forward_layer(1, half, start, scal, params, ins, sends)
        got_high = ship(sends, (2, 3))

        prev = [None, None]
        got_grads = []
        for half, start in cells:
            rank = f0[half]["rank"]
            ins = {**c_in, "x_own": (x_own[half], pl.ANY)}
            b1, sends = backward_layer(1, half, start, scal, params, f1[half], ins, rank, None, prev[1])
            prev[1] = b1["pack_out"]
            ins = {**x_in, "dx_own": (b1["dx_own_out"], pl.ANY), "dx_oth": (mate(b1["dx_oth_out"]), pl.ANY)}
            b0, sends = backward_layer(0, half, start, scal, params, f0[half], ins, rank, sends, prev[0])
            prev[0] = b0["pack_out"]
            sends = first_grads(half, scal, b0["dx_own_out"], mate(b0["dx_oth_out"]), sends)
            got_grads.append(ship(sends))

        low = section < 2
        got = [jnp.where(low, a, b) for a, b in zip(got_low, got_high)]
        section_outputs = assemble(scal, [(got, 0, LONG // 2, 0), (got, LONG, SHORT // 2, LONG // 2)])
        section_grads = assemble(
            scal, [(got_grads[n], start, half, 0) for n, (half, start) in enumerate(cells)]
        )
        packs = []
        for layer in range(2):
            part = lax.psum_scatter(prev[layer], "dp", scatter_dimension=0, tiled=True)
            packs.append(lax.psum_scatter(part, "section", scatter_dimension=0, tiled=True))
        grads = unpack(packs, D // (dp_count * section_count))
        return (section_outputs, section_grads, *grads)

    return per_device


def solution(mesh):
    rows = P("dp", None, None)
    placed = (rows, P("dp", None)) + (P(),) * 11 + (rows,)
    sections = P("section", "dp", None, None)
    matrix = P(None, ("dp", "section"), None)
    vector = P(None, ("dp", "section"))
    pairs = P(None, None, ("dp", "section"))
    return jax.shard_map(
        make_per_device(mesh.shape["dp"], mesh.shape["section"]),
        mesh=mesh,
        in_specs=placed,
        out_specs=(
            sections, sections, matrix, matrix, vector, vector, vector, matrix, matrix, vector, vector, pairs, pairs,
        ),
        check_vma=False,
    )
```

```python
from types import SimpleNamespace

import jax
import jax.numpy as jnp
from jax import lax
from jax.experimental import pallas as pl
from jax.experimental.pallas import tpu as pltpu
from jax.sharding import PartitionSpec as P

D = 512
HEADS = 8
HEAD_DIM = 64
LONG = 1024
SHORT = 512
ROW = LONG + SHORT
EPS = 1e-05
FILL = -1e30
SCALE = HEAD_DIM ** (-0.5)
LOG2E = 1.4426950408889634
LN2 = 0.6931471805599453
SOFT = SCALE * LOG2E
BF = jnp.bfloat16
F32 = jnp.float32
VAUG = HEAD_DIM + 16
PACK = 3 * D + 3 * D + 128
SMALLEST, LARGEST = 2.0 ** -60, 2.0 ** 90
VMEM_LIMIT = 63 * 1024 * 1024
LAYER_PARAMS = (
    "attn_proj", "attn_out", "ff_in", "ff_out",
    "query_bias", "value_bias", "out_bias", "ff_bias_in", "ff_bias_out", "norm_gain", "norm_shift",
)
MATRICES = LAYER_PARAMS[:4]


def nn(a, b):
    return lax.dot_general(a, b, (((1,), (0,)), ((), ())), preferred_element_type=F32)


def nt(a, b):
    return lax.dot_general(a, b, (((1,), (1,)), ((), ())), preferred_element_type=F32)


def tn(a, b):
    return lax.dot_general(a, b, (((0,), (0,)), ((), ())), preferred_element_type=F32)


def call(body, ins, outs, scratch, aliases=None, sems=48):
    names = list(ins) + list(outs) + list(scratch) + ["sems"]

    def kernel(*refs):
        body(SimpleNamespace(**dict(zip(names, refs))))

    in_names, out_names = list(ins), list(outs)
    result = pl.pallas_call(
        kernel,
        in_specs=[pl.BlockSpec(memory_space=space) for _, space in ins.values()],
        out_specs=[pl.BlockSpec(memory_space=space) for _, _, space in outs.values()],
        out_shape=[jax.ShapeDtypeStruct(shape, dtype) for shape, dtype, _ in outs.values()],
        scratch_shapes=[pltpu.VMEM(shape, dtype) for shape, dtype in scratch.values()] + [pltpu.SemaphoreType.DMA((sems,))],
        input_output_aliases={in_names.index(a): out_names.index(b) for a, b in (aliases or {}).items()},
        compiler_params=pltpu.CompilerParams(vmem_limit_bytes=VMEM_LIMIT),
        cost_estimate=pl.CostEstimate(flops=2**20, bytes_accessed=2**12, transcendentals=0),
    )(*[array for array, _ in ins.values()])
    return dict(zip(out_names, result))


class Copies:
    def __init__(self, sems):
        self.sems, self.used, self.ends = sems, 0, []

    def start(self, src, dst):
        copy = pltpu.make_async_copy(src, dst, self.sems.at[self.used])
        self.used += 1
        copy.start()
        return copy

    def either(self, first, src_a, src_b, dst):
        sem = self.sems.at[self.used]
        self.used += 1
        pl.when(first)(lambda: pltpu.make_async_copy(src_a, dst, sem).start())
        pl.when(jnp.logical_not(first))(lambda: pltpu.make_async_copy(src_b, dst, sem).start())
        return pltpu.make_async_copy(src_a, dst, sem)

    def one_of(self, src, dsts, which):
        sem = self.sems.at[self.used]
        self.used += 1
        for at, dst in enumerate(dsts):
            pl.when(which == at)(lambda dst=dst: pltpu.make_async_copy(src, dst, sem).start())
        self.ends.append(pltpu.make_async_copy(src, dsts[0], sem))

    def out(self, src, dst):
        self.ends.append(self.start(src, dst))

    def finish(self):
        for copy in self.ends:
            copy.wait()


def norm_rows(residual):
    center = residual - jnp.mean(residual, axis=-1, keepdims=True)
    inv_std = lax.rsqrt(jnp.mean(center * center, axis=-1, keepdims=True) + EPS)
    return center * inv_std, inv_std


def norm_back(grad, normed, inv, gain):
    e = grad * gain
    return inv * (
        e - jnp.mean(e, axis=-1, keepdims=True) - normed * jnp.mean(e * normed, axis=-1, keepdims=True)
    )


def one_hot_rows(rank_row, size, length):
    return (lax.broadcasted_iota(jnp.int32, (size, length), 0) == rank_row).astype(F32).astype(BF)


def one_hot_cols(rank_col, size):
    length = rank_col.shape[0]
    return (lax.broadcasted_iota(jnp.int32, (length, size), 1) == rank_col).astype(F32).astype(BF)


def put_masked(dst, src, tokens):
    zeros = jnp.zeros((HEAD_DIM, tokens), BF)
    for head in range(HEADS):
        part = (head % 2) * HEAD_DIM
        dst[head, part : part + HEAD_DIM, :] = src[head * HEAD_DIM : (head + 1) * HEAD_DIM, :]
        dst[head, HEAD_DIM - part : 2 * HEAD_DIM - part, :] = zeros


def head_sums(a, b):
    out = []
    for head in range(HEADS):
        rows = slice(head * HEAD_DIM, (head + 1) * HEAD_DIM)
        out.append(jnp.sum(a[rows, :].astype(F32) * b[rows, :].astype(F32), axis=0, keepdims=True))
    return out


def rank_tokens(known, length):
    upto = lax.broadcasted_iota(jnp.int32, (length, length), 0) <= lax.broadcasted_iota(jnp.int32, (length, length), 1)
    low = jnp.broadcast_to(known.astype(F32), (8, length))
    place = nn(low.astype(BF), upto.astype(F32).astype(BF))
    return jnp.where(low > 0.5, place - 1.0, -1.0).astype(jnp.int32)


def small_count(length):
    return length // 2 + length // 8


def param_row(ref, layer, kind=None):
    return ref[pl.ds(layer, 1), :] if kind is None else ref[layer, pl.ds(kind, 1), :]


def forward_body(r, half, start, layer):
    length = 2 * half
    core, slot_ship = r.scal[0], r.scal[3]
    copies = Copies(r.sems)
    if layer == 0:
        mine, slot = r.scal[1] == 1, r.scal[2]
        own_rows = pl.ds(pl.multiple_of(start + core * half, half), half)
        oth_rows = pl.ds(pl.multiple_of(start + (1 - core) * half, half), half)
        u_own_in = copies.either(mine, r.x_here.at[slot, own_rows], r.x_there.at[slot, own_rows], r.u_own)
        u_oth_in = copies.either(mine, r.x_here.at[slot, oth_rows], r.x_there.at[slot, oth_rows], r.u_oth)
    else:
        rank_in = copies.start(r.rank_in, r.rank)
        u_own_in = copies.start(r.x_own, r.u_own)
        u_oth_in = copies.start(r.x_oth, r.u_oth)
    w_in = copies.start(r.attn_proj_in.at[layer], r.w)
    late = [
        copies.start(r.attn_out_in.at[layer], r.w_mix),
        copies.start(r.ff_in_in.at[layer], r.w_up),
        copies.start(r.ff_out_in.at[layer], r.w_down),
    ]
    small = start_params(copies, r)
    if layer == 0:
        known_in = copies.either(mine, r.known_here, r.known_there, r.known)
        known_in.wait()
        known = r.known[pl.ds(slot, 1), :][:, start : start + length]
        first, second = known[:, :half], known[:, half:]
        known = jnp.concatenate([jnp.where(core == 0, first, second), jnp.where(core == 0, second, first)], axis=1)
        rank = rank_tokens(known, length)
        r.rank[...] = rank
        copies.out(r.rank, r.rank_out)
    else:
        rank_in.wait()
        rank = r.rank[...]
    rank_row = rank[0:1, :]
    count = jnp.max(rank_row) + 1
    unk = jnp.where(rank_row[:, :half] >= 0, FILL, 0.0)

    for copy in small:
        copy.wait()

    def save(*names):
        for name in names:
            copies.out(getattr(r, name), getattr(r, name + "_out"))

    u_own_in.wait()
    w_in.wait()
    own = nn(r.u_own[...], r.w[...])
    r.q_t[...] = (own[:, :D] + param_row(r.query_bias, layer)).astype(BF).T
    r.ko_t[...] = (own[:, D : 2 * D] * SOFT).astype(BF).T
    r.vo_t[...] = (own[:, 2 * D :] + param_row(r.value_bias, layer)).astype(BF).T
    save("q_t", "ko_t", "vo_t")
    put_masked(r.qm, r.q_t, half)
    for head, row in enumerate(head_sums(r.q_t, r.ko_t)):
        r.sd[head] = row + unk
        r.total[head] = jnp.zeros_like(row)
        r.top[head] = jnp.zeros_like(row)
    u_oth_in.wait()
    block = min(half, 256)

    def keys(size):
        pick = one_hot_rows(rank_row, size, length)
        uc = (nn(pick[:, :half], r.u_own[...]) + nn(pick[:, half:], r.u_oth[...])).astype(BF)
        r.uc[:size, :] = uc
        kv = nn(uc, r.w[:, D:])
        r.k_c[:size, :] = (kv[:, :D] * SOFT).astype(BF)
        inside = lax.broadcasted_iota(jnp.int32, (size, D), 0) < count
        vc = jnp.where(inside, kv[:, D:] + param_row(r.value_bias, layer), 0.0).astype(BF)
        r.v_c[:size, :] = vc
        vct = vc.T
        ones = lax.broadcasted_iota(jnp.int32, (16, size), 1) < count
        ones = (ones & (lax.broadcasted_iota(jnp.int32, (16, size), 0) == 0)).astype(F32).astype(BF)
        for head in range(HEADS):
            r.vaug[head * VAUG : head * VAUG + HEAD_DIM, :size] = vct[head * HEAD_DIM : (head + 1) * HEAD_DIM, :]
            r.vaug[head * VAUG + HEAD_DIM : (head + 1) * VAUG, :size] = ones

    def attend(size, safe):
        if safe:
            r.kb[...] = jnp.where(lax.broadcasted_iota(jnp.int32, (size, 128), 0) < count, 0.0, FILL)

        def pair(p, carry):
            kcp = r.k_c[:size, pl.ds(pl.multiple_of(p * 128, 128), 128)]
            for e in range(2):
                head = 2 * p + e
                vrows = r.vaug[pl.ds(pl.multiple_of(head * VAUG, 16), VAUG), :size]
                rows = pl.ds(pl.multiple_of(head * HEAD_DIM, HEAD_DIM), HEAD_DIM)
                for at in range(0, half, block):
                    cols = slice(at, at + block)
                    scores = nn(kcp, r.qm[head, :, cols])
                    own_score = r.sd[head, :, cols]
                    if safe:
                        tops, probs = [], []
                        for t in range(0, block, 128):
                            part = scores[:, t : t + 128] + r.kb[...]
                            top = jnp.maximum(jnp.max(part, axis=0, keepdims=True), own_score[:, t : t + 128])
                            tops.append(top)
                            probs.append(jnp.exp2(part - top).astype(BF))
                        top = jnp.concatenate(tops, axis=1)
                        low = jnp.concatenate(probs, axis=1)
                        r.top[head, :, cols] = top
                        own_score = own_score - top
                    else:
                        low = jnp.exp2(scores).astype(BF)
                    mixed = nn(vrows, low)
                    own_prob = jnp.exp2(own_score)
                    total = mixed[HEAD_DIM : HEAD_DIM + 1] + own_prob
                    r.total[head, :, cols] = total
                    mixed = mixed[:HEAD_DIM] + own_prob * r.vo_t[rows, cols].astype(F32)
                    r.mix_t[rows, cols] = (mixed * (1.0 / total)).astype(BF)
            return carry

        lax.fori_loop(0, HEADS // 2, pair, 0)

    def quick():
        keys(small_count(length))
        attend(small_count(length), False)

    pl.when(count <= small_count(length))(quick)
    totals = r.total[...]
    fine = jnp.min(jnp.where((totals > SMALLEST) & (totals < LARGEST), 1, 0)) == 1

    def careful():
        keys(length)
        attend(length, True)

    pl.when(jnp.logical_not(fine))(careful)
    save("uc", "k_c", "v_c", "mix_t", "top", "total")
    for copy in late:
        copy.wait()

    for at in range(0, half, 256):
        rows = slice(at, at + 256)
        res = r.u_own[rows, :].astype(F32) + tn(r.mix_t[:, rows], r.w_mix[...]) + param_row(r.out_bias, layer)
        normed, inv0 = norm_rows(res)
        r.nrm0[rows, :] = normed.astype(BF)
        even = (normed * param_row(r.norm_gain, layer, 0) + param_row(r.norm_shift, layer, 0)).astype(BF)
        r.even[rows, :] = even
        pre = nn(even, r.w_up[...]) + param_row(r.ff_bias_in, layer)
        cdf = 0.5 + 0.5 * lax.erf(pre * 0.7071067811865476)
        hidden = (pre * cdf).astype(BF)
        r.hid[rows, :] = hidden
        r.gp[rows, :] = (cdf + pre * (0.3989422804014327 * jnp.exp(-0.5 * pre * pre))).astype(BF)
        res = even.astype(F32) + nn(hidden, r.w_down[...]) + param_row(r.ff_bias_out, layer)
        normed, inv1 = norm_rows(res)
        r.nrm1[rows, :] = normed.astype(BF)
        r.odd[rows, :] = (normed * param_row(r.norm_gain, layer, 1) + param_row(r.norm_shift, layer, 1)).astype(BF)
        r.inv[rows, :] = jnp.where(lax.broadcasted_iota(jnp.int32, (256, 128), 1) == 0, inv0, inv1)

    copies.out(r.odd, r.odd_out)
    save("even", "nrm0", "nrm1", "gp", "hid", "inv")
    base = 0 if start == 0 else LONG // 2
    sends = [s.at[pl.ds(base, half)] for s in (r.send0, r.send1, r.send2, r.send3)]
    copies.one_of(r.even, sends, slot_ship ^ (2 * layer))
    copies.one_of(r.odd, sends, slot_ship ^ (2 * layer + 1))
    copies.finish()


SAVED = ("even", "q_t", "ko_t", "vo_t", "uc", "k_c", "v_c", "mix_t", "nrm0", "nrm1", "gp", "hid", "inv", "top", "total")


def buffers(half):
    length = 2 * half
    tok, feat, keys = ((half, D), BF), ((D, half), BF), ((length, D), BF)
    rows = ((HEADS, 1, half), F32)
    return dict(
        even=tok, q_t=feat, ko_t=feat, vo_t=feat, uc=keys, k_c=keys, v_c=keys, mix_t=feat, nrm0=tok, nrm1=tok, gp=tok,
        hid=tok, inv=((half, 128), F32), top=rows, total=rows,
    )


def weight_buffers():
    square = ((D, D), BF)
    return dict(w=((D, 3 * D), BF), w_mix=square, w_up=square, w_down=square)


def param_inputs(params):
    return {name + "_in": (params[name], pl.ANY) for name in LAYER_PARAMS}


def param_buffers():
    pairs = {name: ((2, 2, D) if name.startswith("norm") else (2, D), F32) for name in LAYER_PARAMS[4:]}
    return {**pairs, **weight_buffers()}


def start_params(copies, r):
    return [copies.start(getattr(r, name + "_in"), getattr(r, name)) for name in LAYER_PARAMS[4:]]


def forward_layer(layer, half, start, scal, params, inputs, sends):
    length = 2 * half
    saved = buffers(half)
    ins = {"scal": (scal, pltpu.SMEM), **param_inputs(params), **inputs}
    outs = {name + "_out": (*saved[name], pl.ANY) for name in SAVED}
    outs["odd_out"] = ((half, D), BF, pl.ANY)
    aliases = {}
    for t in range(4):
        outs[f"send{t}"] = ((ROW // 2, D), BF, pl.ANY)
        if sends is not None:
            ins[f"sent{t}"] = (sends[t], pl.ANY)
            aliases[f"sent{t}"] = f"send{t}"
    if layer == 0:
        outs["rank_out"] = ((8, length), jnp.int32, pl.ANY)
    scratch = {
        **saved, **param_buffers(), "u_own": ((half, D), BF), "u_oth": ((half, D), BF), "odd": ((half, D), BF),
        "qm": ((HEADS, 128, half), BF), "vaug": ((HEADS * VAUG, length), BF), "kb": ((length, 128), F32),
        "sd": ((HEADS, 1, half), F32), "rank": ((8, length), jnp.int32),
    }
    if layer == 0:
        scratch["known"] = ((2, ROW), jnp.int32)
    out = call(lambda r: forward_body(r, half, start, layer), ins, outs, scratch, aliases)
    return out, [out[f"send{t}"] for t in range(4)]


def backward_body(r, half, start, layer, last):
    length = 2 * half
    core, slot_ship = r.scal[0], r.scal[3]
    copies = Copies(r.sems)
    u_rows = pl.ds(pl.multiple_of(start + core * half, half), half)
    mine, slot = r.scal[1] == 1, r.scal[2]
    if layer == 1:
        g_in = [copies.either(mine, r.c_here.at[slot, u_rows], r.c_there.at[slot, u_rows], r.g)]
        u_in = copies.start(r.x_own, r.u_own)
    else:
        g_in = [copies.start(r.dx_own, r.dx), copies.start(r.dx_oth, r.g)]
        u_in = copies.either(mine, r.x_here.at[slot, u_rows], r.x_there.at[slot, u_rows], r.u_own)
    loads = {}
    for name in ("nrm1", "inv", "gp", "nrm0", "hid", "even", "mix_t", "q_t", "k_c", "v_c", "top", "total", "ko_t", "vo_t", "uc"):
        loads[name] = copies.start(getattr(r, name + "_in"), getattr(r, name))
        if name == "inv":
            loads["w_down"] = copies.start(r.ff_out_in.at[layer], r.w_down)
            loads["w_up"] = copies.start(r.ff_in_in.at[layer], r.w_up)
        if name == "mix_t":
            loads["w_mix"] = copies.start(r.attn_out_in.at[layer], r.w_mix)
    loads["rank"] = copies.start(r.rank_in, r.rank)
    small = start_params(copies, r)
    loads["w"] = copies.start(r.attn_proj_in.at[layer], r.w)
    if last:
        loads["prev"] = copies.start(r.prev_pack, r.prev)

    def need(*names):
        for name in names:
            loads.pop(name).wait()

    sums = [jnp.zeros((1, D), F32) for _ in range(7)]

    def add(slot, value):
        sums[slot] = sums[slot] + jnp.sum(value, axis=0, keepdims=True)

    for copy in g_in + small:
        copy.wait()
    need("nrm1", "inv", "w_down", "w_up", "gp", "nrm0")
    for at in range(0, half, 256):
        rows = slice(at, at + 256)
        if layer == 1:
            grad = r.g[rows, :].astype(F32)
        else:
            low = (r.dx[rows, :] + r.g[rows, :].astype(F32)).astype(BF)
            r.g[rows, :] = low
            grad = low.astype(F32)
        normed = r.nrm1[rows, :].astype(F32)
        add(5, grad * normed)
        add(6, grad)
        dres = norm_back(grad, normed, r.inv[rows, 1:2], param_row(r.norm_gain, layer, 1))
        add(4, dres)
        low = dres.astype(BF)
        r.db1[rows, :] = low
        dp = nt(low, r.w_down[...]) * r.gp[rows, :].astype(F32)
        add(3, dp)
        low = dp.astype(BF)
        r.dpre[rows, :] = low
        low = (dres + nt(low, r.w_up[...])).astype(BF)
        r.g_odd[rows, :] = low
        grad = low.astype(F32)
        normed = r.nrm0[rows, :].astype(F32)
        add(1, grad * normed)
        add(2, grad)
        dres = norm_back(grad, normed, r.inv[rows, 0:1], param_row(r.norm_gain, layer, 0))
        add(0, dres)
        r.dr[rows, :] = dres
        r.db0[rows, :] = dres.astype(BF)

    sends = (r.send0, r.send1, r.send2, r.send3)
    copies.one_of(r.g_odd, sends, slot_ship ^ (2 * layer + 1))
    if layer == 0:
        copies.one_of(r.g, sends, slot_ship ^ 2)

    if last:
        need("prev")

    def put(cols, value):
        if last:
            value = value + r.prev[:, cols].astype(F32)
        r.pack[:, cols] = value.astype(BF)

    need("hid", "even", "mix_t", "w_mix")
    put(slice(5 * D, 6 * D), tn(r.hid[...], r.db1[...]))
    put(slice(4 * D, 5 * D), tn(r.even[...], r.dpre[...]))
    put(slice(3 * D, 4 * D), nn(r.mix_t[...], r.db0[...]))
    dm_t = nt(r.w_mix[...], r.db0[...]).astype(BF)
    r.dm_t[...] = dm_t
    dm_sum = jnp.sum(dm_t.astype(F32), axis=1, keepdims=True)
    need("q_t", "top", "total", "ko_t", "vo_t")
    put_masked(r.qm, r.q_t, half)
    zeros = jnp.zeros((HEAD_DIM, half), BF)
    deltas = head_sums(r.dm_t, r.mix_t)
    for head in range(HEADS):
        rows = slice(head * HEAD_DIM, (head + 1) * HEAD_DIM)
        part = (head % 2) * HEAD_DIM
        inv_total = 1.0 / r.total[head]
        r.total[head] = inv_total
        r.delta[head] = deltas[head] * inv_total
        r.dmm[head, part : part + HEAD_DIM, :] = (r.dm_t[rows, :].astype(F32) * inv_total).astype(BF)
        r.dmm[head, HEAD_DIM - part : 2 * HEAD_DIM - part, :] = zeros
    block = min(half, 256)
    need("k_c", "v_c", "uc", "w", "rank")
    rank = r.rank[...]
    count = jnp.max(rank[0:1, :]) + 1
    rank_col = rank.astype(F32).T[:, 0:1].astype(jnp.int32)
    quick_ok = (count <= small_count(length)) & (jnp.max(jnp.abs(r.top[...])) == 0.0)

    def run(size, safe):
        r.kc_t[:, :size] = r.k_c[:size, :].T
        if safe:
            r.kb[...] = jnp.where(lax.broadcasted_iota(jnp.int32, (size, 128), 0) < count, 0.0, FILL)

        def pair(p, carry):
            lanes = pl.ds(pl.multiple_of(p * 128, 128), 128)
            kcp = r.k_c[:size, lanes]
            vcp = r.v_c[:size, lanes]
            dk = jnp.zeros((size, 128), F32)
            dv = jnp.zeros((size, 128), F32)
            for e in range(2):
                head = 2 * p + e
                rows = pl.ds(pl.multiple_of(head * HEAD_DIM, HEAD_DIM), HEAD_DIM)
                for at in range(0, half, block):
                    cols = slice(at, at + block)
                    qtm = r.qm[head, :, cols]
                    dmh = r.dmm[head, :, cols]
                    scores = nn(kcp, qtm)
                    dprob = nn(vcp, dmh)
                    delta = r.delta[head, :, cols]
                    if safe:
                        top = r.top[head, :, cols]
                        lows, grads = [], []
                        for t in range(0, block, 128):
                            tile = slice(t, t + 128)
                            prob = jnp.exp2(jnp.minimum(scores[:, tile] - top[:, tile], r.kb[...]))
                            lows.append(prob.astype(BF))
                            grads.append((prob * (dprob[:, tile] - delta[:, tile])).astype(BF))
                        low = jnp.concatenate(lows, axis=1)
                        ds = jnp.concatenate(grads, axis=1)
                    else:
                        prob = jnp.exp2(scores)
                        low = prob.astype(BF)
                        ds = (prob * (dprob - delta)).astype(BF)
                    dv = dv + nt(low, dmh)
                    dk = dk + nt(ds, qtm)
                    r.dq_t[rows, cols] = nn(r.kc_t[rows, :size], ds) * LN2
            r.dkv[:size, lanes] = (dk * SCALE).astype(BF)
            r.dkv[:size, pl.ds(pl.multiple_of(D + p * 128, 128), 128)] = dv.astype(BF)
            return carry

        lax.fori_loop(0, HEADS // 2, pair, 0)
        dkv = r.dkv[:size, :]
        r.dw_kv[...] = tn(r.uc[:size, :], dkv)
        dxc = nt(dkv, r.w[:, D:]).astype(BF)
        r.dr[...] += nn(one_hot_cols(rank_col[:half, :], size), dxc)
        r.dxo[...] = nn(one_hot_cols(rank_col[half:, :], size), dxc).astype(BF)

    pl.when(quick_ok)(lambda: run(small_count(length), False))
    pl.when(jnp.logical_not(quick_ok))(lambda: run(length, True))
    copies.out(r.dxo, r.dx_oth_out)

    unk = jnp.where(rank[0:1, :half] >= 0, FILL, 0.0)
    own_scores = head_sums(r.q_t, r.ko_t)
    own_dprobs = head_sums(r.dm_t, r.vo_t)
    dq_parts, dk_parts, dv_parts = [], [], []
    for head in range(HEADS):
        rows = slice(head * HEAD_DIM, (head + 1) * HEAD_DIM)
        inv_total = r.total[head]
        prob = jnp.exp2(own_scores[head] + unk - r.top[head]) * inv_total
        ds = (prob * own_dprobs[head] - prob * (r.delta[head] / inv_total)).astype(BF).astype(F32)
        low = prob.astype(BF).astype(F32)
        dq_parts.append(r.dq_t[rows, :] + (ds * LN2) * r.ko_t[rows, :].astype(F32))
        dk_parts.append(((ds * SCALE) * r.q_t[rows, :].astype(F32)).astype(BF))
        dv_parts.append((low * r.dm_t[rows, :].astype(F32)).astype(BF))
    dq = jnp.concatenate(dq_parts, axis=0)
    dq_sum = jnp.sum(dq, axis=1, keepdims=True)
    dp = jnp.concatenate([dq.astype(BF)] + dk_parts + dv_parts, axis=0).T
    u_in.wait()
    dw = tn(r.u_own[...], dp)
    put(slice(0, D), dw[:, :D])
    put(slice(D, 3 * D), dw[:, D:] + r.dw_kv[...])
    r.dr[...] += nt(dp, r.w[...])
    copies.out(r.dr, r.dx_own_out)
    vectors = jnp.concatenate(sums + [jnp.zeros((121, D), F32)], axis=0).T
    lane = lax.broadcasted_iota(jnp.int32, (D, 128), 1)
    vectors = jnp.where(lane == 7, dq_sum, jnp.where(lane == 8, dm_sum, vectors))
    put(slice(6 * D, 6 * D + 128), vectors)
    copies.out(r.pack, r.pack_out)
    copies.finish()


def backward_layer(layer, half, start, scal, params, saved, inputs, rank, sends, prev):
    length = 2 * half
    shapes = buffers(half)
    tok = ((half, D), BF)
    ins = {"scal": (scal, pltpu.SMEM), **param_inputs(params), **inputs, "rank_in": (rank, pl.ANY)}
    for name in SAVED:
        ins[name + "_in"] = (saved[name + "_out"], pl.ANY)
    outs = {
        "dx_own_out": ((half, D), F32, pl.ANY), "dx_oth_out": (*tok, pl.ANY), "pack_out": ((D, PACK), BF, pl.ANY),
    }
    aliases = {}
    for t in range(4):
        outs[f"send{t}"] = (*tok, pl.ANY)
        if sends is not None:
            ins[f"sent{t}"] = (sends[t], pl.ANY)
            aliases[f"sent{t}"] = f"send{t}"
    scratch = {
        **shapes, **param_buffers(), "u_own": tok, "g": tok, "g_odd": tok, "db0": tok, "db1": tok, "dpre": tok, "dxo": tok,
        "dr": ((half, D), F32), "qm": ((HEADS, 128, half), BF), "dmm": ((HEADS, 128, half), BF), "dm_t": ((D, half), BF),
        "delta": ((HEADS, 1, half), F32), "kc_t": ((D, length), BF), "kb": ((length, 128), F32), "dq_t": ((D, half), F32),
        "dkv": ((length, 2 * D), BF), "dw_kv": ((D, 2 * D), F32), "pack": ((D, PACK), BF),
        "rank": ((8, length), jnp.int32),
    }
    if layer == 0:
        scratch["dx"] = ((half, D), F32)
    if prev is not None:
        ins["prev_pack"] = (prev, pl.ANY)
        scratch["prev"] = ((D, PACK), BF)
    out = call(
        lambda r: backward_body(r, half, start, layer, prev is not None), ins, outs, scratch, aliases
    )
    return out, [out[f"send{t}"] for t in range(4)]


def first_grads(half, scal, dx_own, dx_oth, sends):
    def body(r):
        copies = Copies(r.sems)
        r.total[...] = (r.own[...] + r.oth[...].astype(F32)).astype(BF)
        copies.one_of(r.total, (r.send0, r.send1, r.send2, r.send3), r.scal[3])
        copies.finish()

    tok = ((half, D), BF)
    ins = {"scal": (scal, pltpu.SMEM), "own": (dx_own, pltpu.VMEM), "oth": (dx_oth, pltpu.VMEM)}
    for t in range(4):
        ins[f"sent{t}"] = (sends[t], pl.ANY)
    outs = {f"send{t}": (*tok, pl.ANY) for t in range(4)}
    out = call(body, ins, outs, {"total": tok}, {f"sent{t}": f"send{t}" for t in range(4)}, 4)
    return [out[f"send{t}"] for t in range(4)]


def assemble(scal, sets):
    def body(r):
        copies = Copies(r.sems)
        section = r.scal[4]
        for t in range(4):
            which = section ^ t
            slot, core = which // 2, which % 2
            for n, (pieces, start, half, base) in enumerate(sets):
                src = getattr(r, f"p{n}_{t}").at[pl.ds(base, half)]
                copies.out(src, r.out.at[0, slot, pl.ds(pl.multiple_of(start + core * half, half), half)])
        copies.finish()

    ins = {"scal": (scal, pltpu.SMEM)}
    for n, (pieces, _, _, _) in enumerate(sets):
        for t in range(4):
            ins[f"p{n}_{t}"] = (pieces[t], pl.ANY)
    return call(body, ins, {"out": ((1, 2, ROW, D), BF, pl.ANY)}, {}, None, 4 * len(sets))["out"]


def unpack(packs, size):
    wide = ((2, size, 3 * D), F32, pltpu.VMEM)
    square = ((2, size, D), F32, pltpu.VMEM)
    vec = ((2, size), F32, pltpu.VMEM)
    pair = ((2, 2, size), F32, pltpu.VMEM)
    outs = dict(
        proj=wide, out=square, qb=vec, vb=vec, ob=vec, up=square, down=square, ub=vec, db=vec, gain=pair, shift=pair
    )

    def body(r):
        for layer in range(2):
            pack = getattr(r, f"pack{layer}")
            r.proj[layer] = pack[:, : 3 * D].astype(F32)
            r.out[layer] = pack[:, 3 * D : 4 * D].astype(F32)
            r.up[layer] = pack[:, 4 * D : 5 * D].astype(F32)
            r.down[layer] = pack[:, 5 * D : 6 * D].astype(F32)
            cols = pack[:, 6 * D : 6 * D + 128].astype(F32).T
            for ref, k in ((r.ob, 0), (r.ub, 3), (r.db, 4), (r.qb, 7), (r.vb, 8)):
                ref[layer : layer + 1, :] = cols[k : k + 1, :]
            for kind in range(2):
                r.gain[layer, kind : kind + 1, :] = cols[4 * kind + 1 : 4 * kind + 2, :]
                r.shift[layer, kind : kind + 1, :] = cols[4 * kind + 2 : 4 * kind + 3, :]

    ins = {f"pack{layer}": (packs[layer], pltpu.VMEM) for layer in range(2)}
    return list(call(body, ins, outs, {}, None, 1).values())


def make_per_device(dp_count, section_count):
    both = ("dp", "section")

    def index(dp, section):
        return dp * section_count + section

    everyone = [(d, s) for d in range(dp_count) for s in range(section_count)]
    mate_pairs = [(index(d, s), index(d ^ 1, s)) for d, s in everyone]
    fetch_pairs = [(index(d, s), index(d ^ 1, s)) for d, s in everyone if d % 2 == s // 2]

    def round_pairs(t, sections):
        pairs = []
        for d, z in everyone:
            to = (2 * (z % 2) + d % 2) ^ t
            if to in sections:
                pairs.append((index(d, z), index(d - d % 2 + z // 2, to)))
        return pairs

    def ship(sends, sections=(0, 1, 2, 3)):
        return [lax.ppermute(sends[t], both, round_pairs(t, sections)) for t in range(4)]

    def mate(x):
        return lax.ppermute(x, both, mate_pairs)

    def per_device(
        block_input, known_genes, attn_proj, attn_out, query_bias, value_bias, out_bias, ff_in, ff_out,
        ff_bias_in, ff_bias_out, norm_gain, norm_shift, cotangent,
    ):
        params = dict(
            attn_proj=attn_proj, attn_out=attn_out, query_bias=query_bias, value_bias=value_bias, out_bias=out_bias,
            ff_in=ff_in, ff_out=ff_out, ff_bias_in=ff_bias_in, ff_bias_out=ff_bias_out, norm_gain=norm_gain,
            norm_shift=norm_shift,
        )
        core = lax.axis_index("dp") % 2
        section = lax.axis_index("section")
        mine = (core == section // 2).astype(jnp.int32)
        scal = jnp.stack([core, mine, section % 2, 2 * (section % 2) + core, section]).astype(jnp.int32)

        known_there = lax.ppermute(known_genes, both, fetch_pairs)
        x_there = lax.ppermute(block_input, both, fetch_pairs)
        c_there = lax.ppermute(cotangent, both, fetch_pairs)
        x_in = {"x_here": (block_input, pl.ANY), "x_there": (x_there, pl.ANY)}
        c_in = {"c_here": (cotangent, pl.ANY), "c_there": (c_there, pl.ANY)}
        known_in = {"known_here": (known_genes, pl.ANY), "known_there": (known_there, pl.ANY)}

        cells = ((LONG // 2, 0), (SHORT // 2, LONG))
        f0, f1, x_own, x_oth = {}, {}, {}, {}

        def after(value, *earlier):
            return lax.optimization_barrier((value, earlier))[0]

        sends = None
        for half, start in cells:
            f0[half], sends = forward_layer(0, half, start, scal, params, {**x_in, **known_in}, sends)
            x_own[half] = f0[half]["odd_out"]
            x_oth[half] = mate(x_own[half])
        got_low = ship(sends, (0, 1))
        sends = None
        for half, start in cells:
            ins = {"x_own": (x_own[half], pl.ANY), "x_oth": (x_oth[half], pl.ANY), "rank_in": (f0[half]["rank_out"], pl.ANY)}
            f1[half], sends = forward_layer(1, half, start, scal, params, ins, sends)
        got_high = ship(sends, (2, 3))

        prev = [None, None]
        got_grads = []
        order = scal
        for n, (half, start) in enumerate(cells):
            rank = f0[half]["rank_out"]
            ins = {**c_in, "x_own": (x_own[half], pl.ANY)}
            b1, sends = backward_layer(1, half, start, order, params, f1[half], ins, rank, None, prev[1])
            prev[1] = b1["pack_out"]
            dx_oth = mate(b1["dx_oth_out"])
            if n == 0:
                order = after(order, got_low)
            ins = {**x_in, "dx_own": (b1["dx_own_out"], pl.ANY), "dx_oth": (dx_oth, pl.ANY)}
            b0, sends = backward_layer(0, half, start, order, params, f0[half], ins, rank, sends, prev[0])
            prev[0] = b0["pack_out"]
            sends = first_grads(half, scal, b0["dx_own_out"], mate(b0["dx_oth_out"]), sends)
            got_grads.append(ship(sends))
            if n == 0:
                order = after(order, sends, got_high)

        low = section < 2
        got = [jnp.where(low, a, b) for a, b in zip(got_low, got_high)]
        section_outputs = assemble(scal, [(got, 0, LONG // 2, 0), (got, LONG, SHORT // 2, LONG // 2)])
        section_grads = assemble(
            scal, [(got_grads[n], start, half, 0) for n, (half, start) in enumerate(cells)]
        )
        packs = []
        for layer in range(2):
            part = lax.psum_scatter(prev[layer], "dp", scatter_dimension=0, tiled=True)
            packs.append(lax.psum_scatter(part, "section", scatter_dimension=0, tiled=True))
        grads = unpack(packs, D // (dp_count * section_count))
        return (section_outputs, section_grads, *grads)

    return per_device


def solution(mesh):
    rows = P("dp", None, None)
    placed = (rows, P("dp", None)) + (P(),) * 11 + (rows,)
    sections = P("section", "dp", None, None)
    matrix = P(None, ("dp", "section"), None)
    vector = P(None, ("dp", "section"))
    pairs = P(None, None, ("dp", "section"))
    return jax.shard_map(
        make_per_device(mesh.shape["dp"], mesh.shape["section"]),
        mesh=mesh,
        in_specs=placed,
        out_specs=(
            sections, sections, matrix, matrix, vector, vector, vector, matrix, matrix, vector, vector, pairs, pairs,
        ),
        check_vma=False,
    )
```

```python
from types import SimpleNamespace

import jax
import jax.numpy as jnp
from jax import lax
from jax.experimental import pallas as pl
from jax.experimental.pallas import tpu as pltpu
from jax.sharding import PartitionSpec as P

D = 512
HEADS = 8
HEAD_DIM = 64
LONG = 1024
SHORT = 512
ROW = LONG + SHORT
EPS = 1e-05
FILL = -1e30
SCALE = HEAD_DIM ** (-0.5)
LOG2E = 1.4426950408889634
LN2 = 0.6931471805599453
SOFT = SCALE * LOG2E
BF = jnp.bfloat16
F32 = jnp.float32
VAUG = HEAD_DIM + 16
ATT_PACK = 4 * D + 128
FF_PACK = 2 * D + 128
PACK = ATT_PACK + FF_PACK
OWN = ROW // 2
CELLS = ((0, LONG, 0, LONG // 2), (LONG, SHORT, LONG // 2, SHORT // 2))
SMALLEST, LARGEST = 2.0 ** -60, 2.0 ** 90
VMEM_LIMIT = 63 * 1024 * 1024
LAYER_PARAMS = (
    "attn_proj", "attn_out", "ff_in", "ff_out",
    "query_bias", "value_bias", "out_bias", "ff_bias_in", "ff_bias_out", "norm_gain", "norm_shift",
)
MATRICES = LAYER_PARAMS[:4]


def nn(a, b):
    return lax.dot_general(a, b, (((1,), (0,)), ((), ())), preferred_element_type=F32)


def nt(a, b):
    return lax.dot_general(a, b, (((1,), (1,)), ((), ())), preferred_element_type=F32)


def tn(a, b):
    return lax.dot_general(a, b, (((0,), (0,)), ((), ())), preferred_element_type=F32)


def call(body, ins, outs, scratch, aliases=None, sems=48, micros=0.001):
    names = list(ins) + list(outs) + list(scratch) + ["sems"]

    def kernel(*refs):
        body(SimpleNamespace(**dict(zip(names, refs))))

    in_names, out_names = list(ins), list(outs)
    result = pl.pallas_call(
        kernel,
        in_specs=[pl.BlockSpec(memory_space=space) for _, space in ins.values()],
        out_specs=[pl.BlockSpec(memory_space=space) for _, _, space in outs.values()],
        out_shape=[jax.ShapeDtypeStruct(shape, dtype) for shape, dtype, _ in outs.values()],
        scratch_shapes=[pltpu.VMEM(shape, dtype) for shape, dtype in scratch.values()] + [pltpu.SemaphoreType.DMA((sems,))],
        input_output_aliases={in_names.index(a): out_names.index(b) for a, b in (aliases or {}).items()},
        compiler_params=pltpu.CompilerParams(vmem_limit_bytes=VMEM_LIMIT),
        cost_estimate=pl.CostEstimate(flops=int(micros * 1150000000), bytes_accessed=2**12, transcendentals=0),
    )(*[array for array, _ in ins.values()])
    return dict(zip(out_names, result))


class Copies:
    def __init__(self, sems):
        self.sems, self.used, self.ends = sems, 0, []

    def start(self, src, dst):
        copy = pltpu.make_async_copy(src, dst, self.sems.at[self.used])
        self.used += 1
        copy.start()
        return copy

    def either(self, first, src_a, src_b, dst, out=False):
        sem = self.sems.at[self.used]
        self.used += 1
        pl.when(first)(lambda: pltpu.make_async_copy(src_a, dst, sem).start())
        pl.when(jnp.logical_not(first))(lambda: pltpu.make_async_copy(src_b, dst, sem).start())
        copy = pltpu.make_async_copy(src_a, dst, sem)
        if out:
            self.ends.append(copy)
        return copy

    def out(self, src, dst):
        self.ends.append(self.start(src, dst))

    def finish(self):
        for copy in self.ends:
            copy.wait()


def norm_rows(residual):
    center = residual - jnp.mean(residual, axis=-1, keepdims=True)
    inv_std = lax.rsqrt(jnp.mean(center * center, axis=-1, keepdims=True) + EPS)
    return center * inv_std, inv_std


def norm_back(grad, normed, inv, gain):
    e = grad * gain
    return inv * (
        e - jnp.mean(e, axis=-1, keepdims=True) - normed * jnp.mean(e * normed, axis=-1, keepdims=True)
    )


def one_hot_rows(rank_row, size, length):
    return (lax.broadcasted_iota(jnp.int32, (size, length), 0) == rank_row).astype(F32).astype(BF)


def one_hot_cols(rank_col, size):
    length = rank_col.shape[0]
    return (lax.broadcasted_iota(jnp.int32, (length, size), 1) == rank_col).astype(F32).astype(BF)


def put_masked(dst, src, tokens):
    zeros = jnp.zeros((HEAD_DIM, tokens), BF)
    for head in range(HEADS):
        part = (head % 2) * HEAD_DIM
        dst[head, part : part + HEAD_DIM, :] = src[head * HEAD_DIM : (head + 1) * HEAD_DIM, :]
        dst[head, HEAD_DIM - part : 2 * HEAD_DIM - part, :] = zeros


def head_sums(a, b):
    out = []
    for head in range(HEADS):
        rows = slice(head * HEAD_DIM, (head + 1) * HEAD_DIM)
        out.append(jnp.sum(a[rows, :].astype(F32) * b[rows, :].astype(F32), axis=0, keepdims=True))
    return out


def rank_tokens(known, length):
    upto = lax.broadcasted_iota(jnp.int32, (length, length), 0) <= lax.broadcasted_iota(jnp.int32, (length, length), 1)
    low = jnp.broadcast_to(known.astype(F32), (8, length))
    place = nn(low.astype(BF), upto.astype(F32).astype(BF))
    return jnp.where(low > 0.5, place - 1.0, -1.0).astype(jnp.int32)


def small_count(length):
    return length // 2 + length // 8


def param_row(ref, layer, kind=None):
    return ref[pl.ds(layer, 1), :] if kind is None else ref[layer, pl.ds(kind, 1), :]


def key_rows(quick):
    sizes = [small_count(length) if quick else length for _, length, _, _ in CELLS]
    return ((0, sizes[0]), (sizes[0], sizes[1])), sum(sizes)


def split_rank(r):
    ranks = [r.rank[:, start : start + length] for start, length, _, _ in CELLS]
    return ranks, [jnp.max(rank[0:1, :]) + 1 for rank in ranks]


def units():
    out = []
    for cell, (_, _, first, count) in enumerate(CELLS):
        for at in range(first, first + count, 256):
            out.append((cell, slice(at, at + 256)))
    return out


def small_counts(counts):
    ok = counts[0] <= small_count(CELLS[0][1])
    for count, (_, length, _, _) in zip(counts[1:], CELLS[1:]):
        ok = ok & (count <= small_count(length))
    return ok


def put_key_bias(r, rows, counts):
    for (first, size), count in zip(rows, counts):
        inside = lax.broadcasted_iota(jnp.int32, (size, 128), 0) < count
        r.kb[first : first + size, :] = jnp.where(inside, 0.0, FILL)


def own_rows_of(core, other=False):
    place = 1 - core if other else core
    return [pl.ds(pl.multiple_of(start + place * count, count), count) for start, _, _, count in CELLS]


def forward_body(r, layer):
    core = r.scal[0]
    copies = Copies(r.sems)
    mine, slot = r.scal[1] == 1, r.scal[2]
    if layer == 0:
        known_in = copies.either(mine, r.known_here, r.known_there, r.known)
        u_in = []
        for buffer, other in ((r.u_own, False), (r.u_oth, True)):
            for rows, (_, _, first, count) in zip(own_rows_of(core, other), CELLS):
                u_in.append(
                    copies.either(
                        mine, r.x_here.at[slot, rows], r.x_there.at[slot, rows], buffer.at[pl.ds(first, count)]
                    )
                )
        u_own_in, u_oth_in = u_in[:2], u_in[2:]
    else:
        rank_in = copies.start(r.rank_in, r.rank)
        u_own_in, u_oth_in = [copies.start(r.x_own.at[1], r.u_own)], [copies.start(r.x_oth.at[1], r.u_oth)]
    w_in = copies.start(r.attn_proj_in.at[layer], r.w)
    small = start_params(copies, r)
    late = [
        copies.start(r.attn_out_in.at[layer], r.w_mix),
        copies.start(r.ff_in_in.at[layer], r.w_up),
        copies.start(r.ff_out_in.at[layer], r.w_down),
    ]

    def save(*names):
        for name in names:
            copies.out(getattr(r, name), getattr(r, name + "_out"))

    if layer == 0:
        known_in.wait()
        for start, length, _, count in CELLS:
            known = r.known[pl.ds(slot, 1), :][:, start : start + length]
            first, second = known[:, :count], known[:, count:]
            known = jnp.concatenate([jnp.where(core == 0, first, second), jnp.where(core == 0, second, first)], axis=1)
            r.rank[:, start : start + length] = rank_tokens(known, length)
        save("rank")
    else:
        rank_in.wait()
    ranks, counts = split_rank(r)
    for copy in small + u_own_in:
        copy.wait()
    w_in.wait()
    own = nn(r.u_own[...], r.w[...])
    r.q_t[...] = (own[:, :D] + param_row(r.query_bias, layer)).astype(BF).T
    r.ko_t[...] = (own[:, D : 2 * D] * SOFT).astype(BF).T
    r.vo_t[...] = (own[:, 2 * D :] + param_row(r.value_bias, layer)).astype(BF).T
    save("q_t", "ko_t", "vo_t")
    put_masked(r.qm, r.q_t, OWN)
    unk = jnp.concatenate(
        [jnp.where(rank[0:1, :count] >= 0, FILL, 0.0) for rank, (_, _, _, count) in zip(ranks, CELLS)], axis=1
    )
    for head, row in enumerate(head_sums(r.q_t, r.ko_t)):
        r.sd[head] = row + unk
        r.total[head] = jnp.zeros_like(row)
        r.top[head] = jnp.zeros_like(row)
    for copy in u_oth_in:
        copy.wait()

    def keys(quick):
        rows, total = key_rows(quick)
        for rank, (_, length, own_first, count), (first, size) in zip(ranks, CELLS, rows):
            pick = one_hot_rows(rank[0:1, :], size, length)
            tokens = slice(own_first, own_first + count)
            uc = nn(pick[:, :count], r.u_own[tokens, :]) + nn(pick[:, count:], r.u_oth[tokens, :])
            r.uc[first : first + size, :] = uc.astype(BF)
        kv = nn(r.uc[:total, :], r.w[:, D:])
        r.k_c[:total, :] = (kv[:, :D] * SOFT).astype(BF)
        ones = []
        for (first, size), known in zip(rows, counts):
            inside = lax.broadcasted_iota(jnp.int32, (size, D), 0) < known
            vc = kv[first : first + size, D:] + param_row(r.value_bias, layer)
            r.v_c[first : first + size, :] = jnp.where(inside, vc, 0.0).astype(BF)
            lane = lax.broadcasted_iota(jnp.int32, (16, size), 1)
            ones.append(((lane < known) & (lax.broadcasted_iota(jnp.int32, (16, size), 0) == 0)).astype(F32))
        vct = r.v_c[:total, :].T
        ones = jnp.concatenate(ones, axis=1).astype(BF)
        for head in range(HEADS):
            r.vaug[head * VAUG : head * VAUG + HEAD_DIM, :total] = vct[head * HEAD_DIM : (head + 1) * HEAD_DIM, :]
            r.vaug[head * VAUG + HEAD_DIM : (head + 1) * VAUG, :total] = ones

    def attend(quick):
        rows_of, _ = key_rows(quick)
        if not quick:
            put_key_bias(r, rows_of, counts)

        def pair(p, carry):
            lanes = pl.ds(pl.multiple_of(p * 128, 128), 128)
            for e in range(2):
                head = 2 * p + e
                feats = pl.ds(pl.multiple_of(head * HEAD_DIM, HEAD_DIM), HEAD_DIM)
                for cell, cols in units():
                    keys_at = slice(rows_of[cell][0], rows_of[cell][0] + rows_of[cell][1])
                    vrows = r.vaug[pl.ds(pl.multiple_of(head * VAUG, 16), VAUG), keys_at]
                    scores = nn(r.k_c[keys_at, lanes], r.qm[head, :, cols])
                    own_score = r.sd[head, :, cols]
                    if quick:
                        low = jnp.exp2(scores).astype(BF)
                    else:
                        tops, probs = [], []
                        for t in range(0, 256, 128):
                            part = scores[:, t : t + 128] + r.kb[keys_at, :]
                            top = jnp.maximum(jnp.max(part, axis=0, keepdims=True), own_score[:, t : t + 128])
                            tops.append(top)
                            probs.append(jnp.exp2(part - top).astype(BF))
                        top = jnp.concatenate(tops, axis=1)
                        low = jnp.concatenate(probs, axis=1)
                        r.top[head, :, cols] = top
                        own_score = own_score - top
                    mixed = nn(vrows, low)
                    own_prob = jnp.exp2(own_score)
                    total = mixed[HEAD_DIM : HEAD_DIM + 1] + own_prob
                    r.total[head, :, cols] = total
                    mixed = mixed[:HEAD_DIM] + own_prob * r.vo_t[feats, cols].astype(F32)
                    r.mix_t[feats, cols] = (mixed * (1.0 / total)).astype(BF)
            return carry

        lax.fori_loop(0, HEADS // 2, pair, 0)

    def run(quick):
        keys(quick)
        attend(quick)

    pl.when(small_counts(counts))(lambda: run(True))
    totals = r.total[...]
    fine = jnp.min(jnp.where((totals > SMALLEST) & (totals < LARGEST), 1, 0)) == 1
    pl.when(jnp.logical_not(fine))(lambda: run(False))
    save("uc", "k_c", "v_c", "mix_t", "top", "total")
    for copy in late:
        copy.wait()

    for at in range(0, OWN, 256):
        rows = slice(at, at + 256)
        res = r.u_own[rows, :].astype(F32) + tn(r.mix_t[:, rows], r.w_mix[...]) + param_row(r.out_bias, layer)
        normed, inv0 = norm_rows(res)
        r.nrm0[rows, :] = normed.astype(BF)
        even = (normed * param_row(r.norm_gain, layer, 0) + param_row(r.norm_shift, layer, 0)).astype(BF)
        r.even[rows, :] = even
        pre = nn(even, r.w_up[...]) + param_row(r.ff_bias_in, layer)
        cdf = 0.5 + 0.5 * lax.erf(pre * 0.7071067811865476)
        hidden = (pre * cdf).astype(BF)
        r.hid[rows, :] = hidden
        r.gp[rows, :] = (cdf + pre * (0.3989422804014327 * jnp.exp(-0.5 * pre * pre))).astype(BF)
        res = even.astype(F32) + nn(hidden, r.w_down[...]) + param_row(r.ff_bias_out, layer)
        normed, inv1 = norm_rows(res)
        r.nrm1[rows, :] = normed.astype(BF)
        r.odd[rows, :] = (normed * param_row(r.norm_gain, layer, 1) + param_row(r.norm_shift, layer, 1)).astype(BF)
        r.inv[rows, :] = jnp.where(lax.broadcasted_iota(jnp.int32, (256, 128), 1) == 0, inv0, inv1)

    copies.out(r.even, r.pair_out.at[0])
    copies.out(r.odd, r.pair_out.at[1])
    if layer == 0:
        copies.either(core == 0, r.even, r.odd, r.ship_out.at[core], True)
    else:
        copies.out(r.even, r.ship_out.at[core])
    save("nrm0", "nrm1", "gp", "hid", "inv")
    copies.finish()


TOK = ((OWN, D), BF)
FEAT = ((D, OWN), BF)
KEYS = ((ROW, D), BF)
HEAD_ROWS = ((HEADS, 1, OWN), F32)
RANK = ((8, ROW), jnp.int32)
SAVED = dict(
    even=TOK, q_t=FEAT, ko_t=FEAT, vo_t=FEAT, uc=KEYS, k_c=KEYS, v_c=KEYS, mix_t=FEAT, nrm0=TOK, nrm1=TOK, gp=TOK, hid=TOK,
    inv=((OWN, 128), F32), top=HEAD_ROWS, total=HEAD_ROWS,
)
FF_SAVED = ("nrm1", "inv", "gp", "nrm0", "hid", "even")
ATT_SAVED = ("mix_t", "q_t", "k_c", "v_c", "top", "total", "ko_t", "vo_t", "uc")
BOTH = ((2, OWN, D), BF)


def weight_buffers():
    square = ((D, D), BF)
    return dict(w=((D, 3 * D), BF), w_mix=square, w_up=square, w_down=square)


def param_inputs(params):
    return {name + "_in": (params[name], pl.ANY) for name in LAYER_PARAMS}


def param_buffers():
    pairs = {name: ((2, 2, D) if name.startswith("norm") else (2, D), F32) for name in LAYER_PARAMS[4:]}
    return {**pairs, **weight_buffers()}


def start_params(copies, r):
    return [copies.start(getattr(r, name + "_in"), getattr(r, name)) for name in LAYER_PARAMS[4:]]


def any_inputs(**arrays):
    return {name: (array, pl.ANY) for name, array in arrays.items()}


def forward_layer(layer, scal, params, inputs):
    ins = {"scal": (scal, pltpu.SMEM), **param_inputs(params), **inputs}
    outs = {name + "_out": (*spec, pl.ANY) for name, spec in SAVED.items() if name != "even"}
    outs.update(pair_out=(*BOTH, pl.ANY), ship_out=(*BOTH, pl.ANY))
    scratch = {
        **SAVED, **param_buffers(), "u_own": TOK, "u_oth": TOK, "odd": TOK, "rank": RANK, "qm": ((HEADS, 128, OWN), BF),
        "vaug": ((HEADS * VAUG, ROW), BF), "kb": ((ROW, 128), F32), "sd": HEAD_ROWS,
    }
    if layer == 0:
        outs["rank_out"] = (*RANK, pl.ANY)
        scratch["known"] = ((2, ROW), jnp.int32)
    return call(lambda r: forward_body(r, layer), ins, outs, scratch, micros=20)


def ff_back(r, layer, need):
    sums = [jnp.zeros((1, D), F32) for _ in range(7)]

    def add(slot, value):
        sums[slot] = sums[slot] + jnp.sum(value, axis=0, keepdims=True)

    need("g", "nrm1", "inv", "w_down", "w_up", "gp", "nrm0")
    for at in range(0, OWN, 256):
        rows = slice(at, at + 256)
        if layer == 1:
            grad = r.g[rows, :].astype(F32)
        else:
            low = (r.dx[rows, :] + r.g[rows, :].astype(F32)).astype(BF)
            r.g[rows, :] = low
            grad = low.astype(F32)
        normed = r.nrm1[rows, :].astype(F32)
        add(5, grad * normed)
        add(6, grad)
        dres = norm_back(grad, normed, r.inv[rows, 1:2], param_row(r.norm_gain, layer, 1))
        add(4, dres)
        low = dres.astype(BF)
        r.db1[rows, :] = low
        dp = nt(low, r.w_down[...]) * r.gp[rows, :].astype(F32)
        add(3, dp)
        low = dp.astype(BF)
        r.dpre[rows, :] = low
        low = (dres + nt(low, r.w_up[...])).astype(BF)
        r.g_odd[rows, :] = low
        grad = low.astype(F32)
        normed = r.nrm0[rows, :].astype(F32)
        add(1, grad * normed)
        add(2, grad)
        dres = norm_back(grad, normed, r.inv[rows, 0:1], param_row(r.norm_gain, layer, 0))
        add(0, dres)
        r.dr[rows, :] = dres
        r.db0[rows, :] = dres.astype(BF)
    vectors = jnp.concatenate(sums + [jnp.zeros((121, D), F32)], axis=0)
    r.ff_pack[:, 2 * D :] = vectors.T.astype(BF)


def ff_weights(r, need):
    need("hid", "even")
    r.ff_pack[:, :D] = tn(r.even[...], r.dpre[...]).astype(BF)
    r.ff_pack[:, D : 2 * D] = tn(r.hid[...], r.db1[...]).astype(BF)


def attention_back(r, layer, copies, need):
    core = r.scal[0]
    need("w_mix", "mix_t")
    dm_t = nt(r.w_mix[...], r.db0[...]).astype(BF)
    r.dm_t[...] = dm_t
    dm_sum = jnp.sum(dm_t.astype(F32), axis=1, keepdims=True)
    need("q_t", "top", "total", "ko_t", "vo_t")
    put_masked(r.qm, r.q_t, OWN)
    zeros = jnp.zeros((HEAD_DIM, OWN), BF)
    deltas = head_sums(r.dm_t, r.mix_t)
    for head in range(HEADS):
        rows = slice(head * HEAD_DIM, (head + 1) * HEAD_DIM)
        part = (head % 2) * HEAD_DIM
        inv_total = 1.0 / r.total[head]
        r.total[head] = inv_total
        r.delta[head] = deltas[head] * inv_total
        r.dmm[head, part : part + HEAD_DIM, :] = (r.dm_t[rows, :].astype(F32) * inv_total).astype(BF)
        r.dmm[head, HEAD_DIM - part : 2 * HEAD_DIM - part, :] = zeros
    need("k_c", "v_c", "uc", "w", "rank")
    ranks, counts = split_rank(r)
    quick_ok = small_counts(counts) & (jnp.max(jnp.abs(r.top[...])) == 0.0)

    def run(quick):
        rows_of, total = key_rows(quick)
        r.kc_t[:, :total] = r.k_c[:total, :].T
        if not quick:
            put_key_bias(r, rows_of, counts)

        def pair(p, carry):
            lanes = pl.ds(pl.multiple_of(p * 128, 128), 128)
            late_lanes = pl.ds(pl.multiple_of(D + p * 128, 128), 128)
            dk = [jnp.zeros((size, 128), F32) for _, size in rows_of]
            dv = [jnp.zeros((size, 128), F32) for _, size in rows_of]
            for e in range(2):
                head = 2 * p + e
                feats = pl.ds(pl.multiple_of(head * HEAD_DIM, HEAD_DIM), HEAD_DIM)
                for cell, cols in units():
                    keys_at = slice(rows_of[cell][0], rows_of[cell][0] + rows_of[cell][1])
                    qtm = r.qm[head, :, cols]
                    dmh = r.dmm[head, :, cols]
                    scores = nn(r.k_c[keys_at, lanes], qtm)
                    dprob = nn(r.v_c[keys_at, lanes], dmh)
                    delta = r.delta[head, :, cols]
                    if quick:
                        prob = jnp.exp2(scores)
                        low = prob.astype(BF)
                        ds = (prob * (dprob - delta)).astype(BF)
                    else:
                        top = r.top[head, :, cols]
                        lows, grads = [], []
                        for t in range(0, 256, 128):
                            tile = slice(t, t + 128)
                            prob = jnp.exp2(jnp.minimum(scores[:, tile] - top[:, tile], r.kb[keys_at, :]))
                            lows.append(prob.astype(BF))
                            grads.append((prob * (dprob[:, tile] - delta[:, tile])).astype(BF))
                        low = jnp.concatenate(lows, axis=1)
                        ds = jnp.concatenate(grads, axis=1)
                    dv[cell] = dv[cell] + nt(low, dmh)
                    dk[cell] = dk[cell] + nt(ds, qtm)
                    r.dq_t[feats, cols] = nn(r.kc_t[feats, keys_at], ds) * LN2
            for cell, (first, size) in enumerate(rows_of):
                r.dkv[first : first + size, lanes] = (dk[cell] * SCALE).astype(BF)
                r.dkv[first : first + size, late_lanes] = dv[cell].astype(BF)
            return carry

        lax.fori_loop(0, HEADS // 2, pair, 0)
        dkv = r.dkv[:total, :]
        r.dw_kv[...] = tn(r.uc[:total, :], dkv)
        dxc = nt(dkv, r.w[:, D:]).astype(BF)
        for rank, (_, _, own_first, count), (first, size) in zip(ranks, CELLS, rows_of):
            rank_col = rank.astype(F32).T[:, 0:1].astype(jnp.int32)
            tokens = slice(own_first, own_first + count)
            part = dxc[first : first + size, :]
            r.dr[tokens, :] += nn(one_hot_cols(rank_col[:count, :], size), part)
            r.dxo[tokens, :] = nn(one_hot_cols(rank_col[count:, :], size), part).astype(BF)

    pl.when(quick_ok)(lambda: run(True))
    pl.when(jnp.logical_not(quick_ok))(lambda: run(False))
    if layer == 1:
        copies.out(r.dxo, r.dx_oth_out)
    else:
        copies.out(r.dxo, r.dx_out.at[1 - core])

    unk = jnp.concatenate(
        [jnp.where(rank[0:1, :count] >= 0, FILL, 0.0) for rank, (_, _, _, count) in zip(ranks, CELLS)], axis=1
    )
    own_scores = head_sums(r.q_t, r.ko_t)
    own_dprobs = head_sums(r.dm_t, r.vo_t)
    dq_parts, dk_parts, dv_parts = [], [], []
    for head in range(HEADS):
        rows = slice(head * HEAD_DIM, (head + 1) * HEAD_DIM)
        prob = jnp.exp2(own_scores[head] + unk - r.top[head])
        ds = (prob * (own_dprobs[head] * r.total[head] - r.delta[head])).astype(BF).astype(F32)
        low = (prob * r.total[head]).astype(BF).astype(F32)
        dq_parts.append(r.dq_t[rows, :] + (ds * LN2) * r.ko_t[rows, :].astype(F32))
        dk_parts.append(((ds * SCALE) * r.q_t[rows, :].astype(F32)).astype(BF))
        dv_parts.append((low * r.dm_t[rows, :].astype(F32)).astype(BF))
    dq = jnp.concatenate(dq_parts, axis=0)
    dq_sum = jnp.sum(dq, axis=1, keepdims=True)
    dp = jnp.concatenate([dq.astype(BF)] + dk_parts + dv_parts, axis=0).T
    r.dr[...] += nt(dp, r.w[...])
    if layer == 1:
        copies.out(r.dr, r.dx_own_out)
    else:
        r.dxw[...] = r.dr[...].astype(BF)
        copies.out(r.dxw, r.dx_out.at[core])
    need("u_own")
    dw = tn(r.u_own[...], dp)
    r.att_pack[:, :D] = dw[:, :D].astype(BF)
    r.att_pack[:, D : 3 * D] = (dw[:, D:] + r.dw_kv[...]).astype(BF)
    r.att_pack[:, 3 * D : 4 * D] = nn(r.mix_t[...], r.db0[...]).astype(BF)
    lane = lax.broadcasted_iota(jnp.int32, (D, 128), 1)
    r.att_pack[:, 4 * D :] = jnp.where(lane == 0, dq_sum, jnp.where(lane == 1, dm_sum, 0.0)).astype(BF)


FF_BUFFERS = dict(
    {name: SAVED[name] for name in FF_SAVED}, g=TOK, g_odd=TOK, db0=TOK, db1=TOK, dpre=TOK, dr=((OWN, D), F32),
    ff_pack=((D, FF_PACK), BF),
)
ATT_BUFFERS = dict(
    {name: SAVED[name] for name in ATT_SAVED}, u_own=TOK, db0=TOK, dxo=TOK, dr=((OWN, D), F32), qm=((HEADS, 128, OWN), BF),
    dmm=((HEADS, 128, OWN), BF), dm_t=FEAT, delta=HEAD_ROWS, kc_t=((D, ROW), BF), kb=((ROW, 128), F32),
    dq_t=((D, OWN), F32), dkv=((ROW, 2 * D), BF), dw_kv=((D, 2 * D), F32), att_pack=((D, ATT_PACK), BF), rank=RANK,
)


class Loads:
    def __init__(self):
        self.waiting = {}

    def add(self, name, *copies):
        self.waiting.setdefault(name, []).extend(copies)

    def need(self, *names):
        for name in names:
            for copy in self.waiting.pop(name):
                copy.wait()


def start_ff_loads(r, copies, loads, layer):
    loads.add("even", copies.start(r.pair_in.at[0], r.even))
    for name in FF_SAVED[:3]:
        loads.add(name, copies.start(getattr(r, name + "_in"), getattr(r, name)))
    loads.add("w_down", copies.start(r.ff_out_in.at[layer], r.w_down))
    loads.add("w_up", copies.start(r.ff_in_in.at[layer], r.w_up))
    for name in FF_SAVED[3:5]:
        loads.add(name, copies.start(getattr(r, name + "_in"), getattr(r, name)))


def start_att_loads(r, copies, loads, layer):
    loads.add("w_mix", copies.start(r.attn_out_in.at[layer], r.w_mix))
    for name in ATT_SAVED:
        loads.add(name, copies.start(getattr(r, name + "_in"), getattr(r, name)))
    loads.add("rank", copies.start(r.rank_in, r.rank))
    loads.add("w", copies.start(r.attn_proj_in.at[layer], r.w))


def saved_inputs(saved, names):
    ins = {name + "_in": (saved[name + "_out"], pl.ANY) for name in names if name != "even"}
    if "even" in names:
        ins["pair_in"] = (saved["pair_out"], pl.ANY)
    return ins


def backward_last(scal, params, saved, inputs, rank):
    def body(r):
        core, mine, slot = r.scal[0], r.scal[1] == 1, r.scal[2]
        copies, loads = Copies(r.sems), Loads()
        for rows, (_, _, first, count) in zip(own_rows_of(core), CELLS):
            src = [c.at[slot, rows] for c in (r.c_here, r.c_there)]
            loads.add("g", copies.either(mine, *src, r.g.at[pl.ds(first, count)]))
        loads.add("g", *start_params(copies, r))
        start_ff_loads(r, copies, loads, 1)
        start_att_loads(r, copies, loads, 1)
        loads.add("u_own", copies.start(r.x_own.at[1], r.u_own))
        ff_back(r, 1, loads.need)
        ff_weights(r, loads.need)
        copies.out(r.ff_pack, r.pack_out.at[:, pl.ds(0, FF_PACK)])
        attention_back(r, 1, copies, loads.need)
        copies.out(r.att_pack, r.pack_out.at[:, pl.ds(FF_PACK, ATT_PACK)])
        copies.finish()

    ins = {
        "scal": (scal, pltpu.SMEM), **param_inputs(params), **inputs, "rank_in": (rank, pl.ANY), **saved_inputs(saved, SAVED)
    }
    outs = {
        "dx_own_out": ((OWN, D), F32, pl.ANY), "dx_oth_out": (*TOK, pl.ANY),
        "pack_out": ((D, FF_PACK + ATT_PACK), BF, pl.ANY),
    }
    return call(body, ins, outs, {**FF_BUFFERS, **ATT_BUFFERS, **param_buffers()}, sems=64, micros=30)


def backward_first_ff(scal, params, saved, inputs):
    def body(r):
        copies, loads = Copies(r.sems), Loads()
        loads.add("g", copies.start(r.dx_oth, r.g), copies.start(r.dx_own, r.dx))
        loads.add("g", *start_params(copies, r))
        start_ff_loads(r, copies, loads, 0)
        ff_back(r, 0, loads.need)
        core = r.scal[0]
        copies.either(core == 0, r.g_odd, r.g, r.give_out, True)
        copies.either(core == 0, r.g, r.g_odd, r.ship_out.at[core], True)
        copies.out(r.db0, r.db0_out)
        copies.out(r.dr, r.dr_out)
        ff_weights(r, loads.need)
        copies.out(r.ff_pack, r.pack_out)
        copies.finish()

    ins = {"scal": (scal, pltpu.SMEM), **param_inputs(params), **inputs, **saved_inputs(saved, FF_SAVED)}
    outs = {
        "db0_out": (*TOK, pl.ANY), "dr_out": ((OWN, D), F32, pl.ANY), "pack_out": ((D, FF_PACK), BF, pl.ANY),
        "give_out": (*TOK, pl.ANY), "ship_out": (*BOTH, pl.ANY),
    }
    scratch = {**FF_BUFFERS, **param_buffers(), "dx": ((OWN, D), F32)}
    return call(body, ins, outs, scratch, sems=64, micros=7)


def backward_first_att(scal, params, saved, inputs, rank, dp_count):
    size = D // dp_count

    def body(r):
        core, mine, slot = r.scal[0], r.scal[1] == 1, r.scal[2]
        copies, loads = Copies(r.sems), Loads()
        loads.add("w_mix", copies.start(r.db0_in, r.db0), copies.start(r.dr_in, r.dr))
        start_att_loads(r, copies, loads, 0)
        for rows, (_, _, first, count) in zip(own_rows_of(core), CELLS):
            src = [x.at[slot, rows] for x in (r.x_here, r.x_there)]
            loads.add("u_own", copies.either(mine, *src, r.u_own.at[pl.ds(first, count)]))
        loads.add("ff", copies.start(r.ff_in, r.ff_pack))

        def halves(pack, at, width):
            for n in range(dp_count // 2):
                to = pl.ds(n * size, size)
                keep = pl.ds(pl.multiple_of((2 * n + core) * size, size), size)
                send = pl.ds(pl.multiple_of((2 * n + 1 - core) * size, size), size)
                copies.out(pack.at[keep], r.keep_out.at[to, pl.ds(at, width)])
                copies.out(pack.at[send], r.send_out.at[to, pl.ds(at, width)])

        loads.need("ff")
        halves(r.ff_pack, 0, FF_PACK)
        attention_back(r, 0, copies, loads.need)
        halves(r.att_pack, FF_PACK, ATT_PACK)
        copies.finish()

    ins = {
        "scal": (scal, pltpu.SMEM), **param_inputs(params), **inputs, "rank_in": (rank, pl.ANY),
        **saved_inputs(saved, ATT_SAVED),
    }
    half = ((D // 2, PACK), BF, pl.ANY)
    outs = {"dx_out": (*BOTH, pl.ANY), "keep_out": half, "send_out": half}
    scratch = {**ATT_BUFFERS, **param_buffers(), "ff_pack": ((D, FF_PACK), BF), "dxw": TOK}
    return call(body, ins, outs, scratch, sems=48 + 2 * dp_count, micros=0.001)


def add_and_split(scal, keep, got, groups):
    size = D // (2 * groups)

    def body(r):
        copies = Copies(r.sems)
        ins = [copies.start(r.keep, r.a), copies.start(r.got, r.b)]
        for copy in ins:
            copy.wait()
        r.a[...] = (r.a[...].astype(F32) + r.b[...].astype(F32)).astype(BF)
        for m in range(groups):
            part = pl.ds(pl.multiple_of((r.scal[5] ^ m) * size, size), size)
            copies.out(r.a.at[part], getattr(r, f"part{m}"))
        copies.finish()

    half = ((D // 2, PACK), BF)
    ins = {"scal": (scal, pltpu.SMEM), **any_inputs(keep=keep, got=got)}
    outs = {f"part{m}": ((size, PACK), BF, pl.ANY) for m in range(groups)}
    return list(call(body, ins, outs, {"a": half, "b": half}, sems=2 + groups).values())


def join(own, others, last):
    size = own.shape[0]
    parts = [own] + list(others)

    def body(r):
        copies = Copies(r.sems)
        loads = [copies.start(getattr(r, f"p{n}"), r.parts.at[n]) for n in range(len(parts))]
        loads.append(copies.start(r.last, r.out.at[:, pl.ds(PACK, PACK)]))
        for copy in loads:
            copy.wait()
        total = r.parts[0].astype(F32)
        for n in range(1, len(parts)):
            total = total + r.parts[n].astype(F32)
        r.out[:, :PACK] = total.astype(BF)
        copies.out(r.out, r.all_out)
        copies.finish()

    ins = any_inputs(**{f"p{n}": p for n, p in enumerate(parts)}, last=last)
    scratch = {"parts": ((len(parts), size, PACK), BF), "out": ((size, 2 * PACK), BF)}
    return call(body, ins, {"all_out": ((size, 2 * PACK), BF, pl.ANY)}, scratch, sems=len(parts) + 2)["all_out"]


def put_row(copies, held, out, row):
    for half in range(2):
        for start, _, own_first, count in CELLS:
            copies.out(held.at[half, pl.ds(own_first, count)], out.at[0, row, pl.ds(start + half * count, count)])


def finish_outputs(scal, low, high, cotangent, params):
    def body(r):
        section = r.scal[4]
        copies = Copies(r.sems)
        loads = []
        for row in range(2):
            loads.append(copies.either(section < 2, getattr(r, f"low{row}"), getattr(r, f"high{row}"), r.held.at[row]))
        for copy in loads:
            copy.wait()

        @pl.when(section < 3)
        def _():
            rest = Copies(r.sems)
            rest.used = copies.used
            for row in range(2):
                put_row(rest, r.held.at[row], r.out, row)
            rest.finish()

        @pl.when(section == 3)
        def _():
            rest = Copies(r.sems)
            rest.used = copies.used
            loads = start_params(rest, r)
            loads.append(rest.start(r.ff_in_in.at[1], r.w_up))
            loads.append(rest.start(r.ff_out_in.at[1], r.w_down))
            for row in range(2):
                for half in range(2):
                    for start, _, own_first, count in CELLS:
                        src = r.cot.at[row, pl.ds(start + half * count, count)]
                        loads.append(rest.start(src, r.g.at[row, half, pl.ds(own_first, count)]))
            for copy in loads:
                copy.wait()

            def step(n, carry):
                row, half = n // 2, n % 2
                for at in range(0, OWN, 256):
                    rows = slice(at, at + 256)
                    even = r.held[row, half, rows, :]
                    pre = nn(even, r.w_up[...]) + param_row(r.ff_bias_in, 1)
                    cdf = 0.5 + 0.5 * lax.erf(pre * 0.7071067811865476)
                    hidden = (pre * cdf).astype(BF)
                    gp = cdf + pre * (0.3989422804014327 * jnp.exp(-0.5 * pre * pre))
                    res = even.astype(F32) + nn(hidden, r.w_down[...]) + param_row(r.ff_bias_out, 1)
                    normed, inv = norm_rows(res)
                    gain = param_row(r.norm_gain, 1, 1)
                    r.held[row, half, rows, :] = (normed * gain + param_row(r.norm_shift, 1, 1)).astype(BF)
                    dres = norm_back(r.g[row, half, rows, :].astype(F32), normed, inv, gain)
                    dp = (nt(dres.astype(BF), r.w_down[...]) * gp).astype(BF)
                    r.g[row, half, rows, :] = (dres + nt(dp, r.w_up[...])).astype(BF)
                return carry

            lax.fori_loop(0, 4, step, 0)
            for row in range(2):
                put_row(rest, r.held.at[row], r.out, row)
                put_row(rest, r.g.at[row], r.grads, row)
            rest.finish()

    ins = {"scal": (scal, pltpu.SMEM), **param_inputs(params)}
    ins.update(any_inputs(low0=low[0], low1=low[1], high0=high[0], high1=high[1], cot=cotangent))
    whole = ((1, 2, ROW, D), BF, pl.ANY)
    scratch = {"held": ((2, 2, OWN, D), BF), "g": ((2, 2, OWN, D), BF), **param_buffers()}
    out = call(body, ins, {"out": whole, "grads": whole}, scratch, sems=48)
    return out["out"], out["grads"]


def finish_grads(scal, first, middle, last):
    def body(r):
        section = r.scal[4]
        copies = Copies(r.sems)
        loads = [
            copies.either(section == 0, getattr(r, f"a{row}"), getattr(r, f"b{row}"), r.held.at[row]) for row in range(2)
        ]
        for row in range(2):
            loads[row].wait()

        @pl.when(section < 3)
        def _():
            rest = Copies(r.sems)
            rest.used = copies.used
            for row in range(2):
                put_row(rest, r.held.at[row], r.out, row)
            rest.finish()

    ins = {"scal": (scal, pltpu.SMEM)}
    ins.update(any_inputs(a0=first[0], a1=first[1], b0=middle[0], b1=middle[1], last=last))
    whole = ((1, 2, ROW, D), BF, pl.ANY)
    return call(body, ins, {"out": whole}, {"held": ((2, 2, OWN, D), BF)}, {"last": "out"}, 16)["out"]


def unpack(got):
    count, size, width = got.shape
    wide = ((2, size, 3 * D), F32, pltpu.VMEM)
    square = ((2, size, D), F32, pltpu.VMEM)
    vec = ((2, size), F32, pltpu.VMEM)
    pair = ((2, 2, size), F32, pltpu.VMEM)
    outs = dict(
        proj=wide, out=square, qb=vec, vb=vec, ob=vec, up=square, down=square, ub=vec, db=vec, gain=pair, shift=pair
    )

    def body(r):
        pltpu.sync_copy(r.got, r.held)
        total = r.held[0].astype(F32)
        for n in range(1, count):
            total = total + r.held[n].astype(F32)
        for layer in range(2):
            base = layer * PACK
            ff = total[:, base : base + FF_PACK]
            att = total[:, base + FF_PACK : base + FF_PACK + ATT_PACK]
            r.up[layer] = ff[:, :D]
            r.down[layer] = ff[:, D : 2 * D]
            r.proj[layer] = att[:, : 3 * D]
            r.out[layer] = att[:, 3 * D : 4 * D]
            cols = ff[:, 2 * D :].T
            for ref, k in ((r.ob, 0), (r.ub, 3), (r.db, 4)):
                ref[layer : layer + 1, :] = cols[k : k + 1, :]
            for kind in range(2):
                r.gain[layer, kind : kind + 1, :] = cols[4 * kind + 1 : 4 * kind + 2, :]
                r.shift[layer, kind : kind + 1, :] = cols[4 * kind + 2 : 4 * kind + 3, :]
            cols = att[:, 4 * D :].T
            for ref, k in ((r.qb, 0), (r.vb, 1)):
                ref[layer : layer + 1, :] = cols[k : k + 1, :]

    scratch = {"held": ((count, size, width), BF)}
    return list(call(body, any_inputs(got=got), outs, scratch, sems=1).values())


def make_per_device(dp_count, section_count):
    both = ("dp", "section")

    def index(dp, section):
        return dp * section_count + section

    everyone = [(d, s) for d in range(dp_count) for s in range(section_count)]
    mate_pairs = [(index(d, s), index(d ^ 1, s)) for d, s in everyone]
    fetch_pairs = [(index(d, s), index(d ^ 1, s)) for d, s in everyone if d % 2 == s // 2]

    def ship(rows, sections):
        got = []
        for odd in range(2):
            pairs = []
            for d, z in everyone:
                to = sections[d % 2]
                if z % 2 == odd and to is not None:
                    pairs.append((index(d, z), index(d - d % 2 + z // 2, to)))
            got.append(lax.ppermute(rows, both, pairs))
        return got

    def mate(x):
        return lax.ppermute(x, both, mate_pairs)

    def after(value, *earlier):
        return lax.optimization_barrier((value, earlier))[0]

    def per_device(
        block_input, known_genes, attn_proj, attn_out, query_bias, value_bias, out_bias, ff_in, ff_out,
        ff_bias_in, ff_bias_out, norm_gain, norm_shift, cotangent,
    ):
        params = dict(
            attn_proj=attn_proj, attn_out=attn_out, query_bias=query_bias, value_bias=value_bias, out_bias=out_bias,
            ff_in=ff_in, ff_out=ff_out, ff_bias_in=ff_bias_in, ff_bias_out=ff_bias_out, norm_gain=norm_gain,
            norm_shift=norm_shift,
        )
        dp = lax.axis_index("dp")
        core = dp % 2
        section = lax.axis_index("section")
        mine = (core == section // 2).astype(jnp.int32)
        scal = jnp.stack([core, mine, section % 2, 2 * (section % 2) + core, section, dp // 2]).astype(jnp.int32)

        known_there = lax.ppermute(known_genes, both, fetch_pairs)
        x_there = lax.ppermute(block_input, both, fetch_pairs)
        x_in = any_inputs(x_here=block_input, x_there=x_there)
        f0 = forward_layer(0, scal, params, {**x_in, **any_inputs(known_here=known_genes, known_there=known_there)})
        rank = f0["rank_out"]
        x_own = f0["pair_out"]
        x_oth = mate(x_own)

        def other_half(rows, half):
            return lax.dynamic_update_index_in_dim(rows, half, 1 - core, 0)

        c_there = lax.ppermute(after(cotangent, x_own), both, fetch_pairs)
        missing = lax.dynamic_index_in_dim(x_oth, core, 0, keepdims=False)
        got_low = ship(other_half(f0["ship_out"], missing), (0, 1))
        f1 = forward_layer(1, scal, params, any_inputs(x_own=x_own, x_oth=x_oth, rank_in=rank))
        high_rows = other_half(f1["ship_out"], mate(f1["pair_out"][0]))
        got_high = ship(high_rows, (2, 3))
        b1 = backward_last(after(scal, got_low[0]), params, f1, any_inputs(c_here=cotangent, c_there=c_there, x_own=x_own), rank)
        wide = lax.psum_scatter(b1["pack_out"], "dp", scatter_dimension=0, tiled=True)
        ins = any_inputs(dx_own=b1["dx_own_out"], dx_oth=mate(b1["dx_oth_out"]))
        b0 = backward_first_ff(after(scal, got_low[1], got_high[0]), params, f0, ins)
        grad_rows = other_half(b0["ship_out"], mate(b0["give_out"]))
        got_grads = ship(grad_rows, (2, 1))
        ins = {**x_in, **any_inputs(db0_in=b0["db0_out"], dr_in=b0["dr_out"], ff_in=b0["pack_out"])}
        last = backward_first_att(after(scal, grad_rows), params, f0, ins, rank, dp_count)

        to_first = [(index(d, s), index(d - 1, s)) for d, s in everyone if d % 2]
        theirs = lax.ppermute(after(last["dx_out"], got_grads, got_high[1]), both, to_first)
        got_first = ship((last["dx_out"].astype(F32) + theirs.astype(F32)).astype(BF), (0, None))
        groups = dp_count // 2
        parts = add_and_split(scal, last["keep_out"], mate(last["send_out"]), groups)
        others = []
        for m in range(1, groups):
            pairs = [(index(d, s), index(d ^ (2 * m), s)) for d, s in everyone]
            others.append(lax.ppermute(parts[m], both, pairs))
        held = join(parts[0], others, wide)
        got = lax.all_to_all(held.reshape(section_count, -1, held.shape[1]), "section", 0, 0)
        grads = unpack(got)
        section_outputs, last_grads = finish_outputs(scal, got_low, got_high, cotangent, params)
        section_grads = finish_grads(scal, got_first, got_grads, last_grads)
        return (section_outputs, section_grads, *grads)

    return per_device


def solution(mesh):
    rows = P("dp", None, None)
    placed = (rows, P("dp", None)) + (P(),) * 11 + (rows,)
    sections = P("section", "dp", None, None)
    matrix = P(None, ("dp", "section"), None)
    vector = P(None, ("dp", "section"))
    pairs = P(None, None, ("dp", "section"))
    return jax.shard_map(
        make_per_device(mesh.shape["dp"], mesh.shape["section"]),
        mesh=mesh,
        in_specs=placed,
        out_specs=(
            sections, sections, matrix, matrix, vector, vector, vector, matrix, matrix, vector, vector, pairs, pairs,
        ),
        check_vma=False,
    )
```

```python
from types import SimpleNamespace

import jax
import jax.numpy as jnp
from jax import lax
from jax.experimental import pallas as pl
from jax.experimental.pallas import tpu as pltpu
from jax.sharding import PartitionSpec as P

D = 512
HEADS = 8
HEAD_DIM = 64
LONG = 1024
SHORT = 512
ROW = LONG + SHORT
EPS = 1e-05
FILL = -1e30
SCALE = HEAD_DIM ** (-0.5)
LOG2E = 1.4426950408889634
LN2 = 0.6931471805599453
SOFT = SCALE * LOG2E
BF = jnp.bfloat16
F32 = jnp.float32
VAUG = HEAD_DIM + 16
ATT_PACK = 4 * D + 128
FF_PACK = 2 * D + 128
PACK = ATT_PACK + FF_PACK
OWN = ROW // 2
CELLS = ((0, LONG, 0, LONG // 2), (LONG, SHORT, LONG // 2, SHORT // 2))
SMALLEST, LARGEST = 2.0 ** -60, 2.0 ** 90
VMEM_LIMIT = 63 * 1024 * 1024
LAYER_PARAMS = (
    "attn_proj", "attn_out", "ff_in", "ff_out",
    "query_bias", "value_bias", "out_bias", "ff_bias_in", "ff_bias_out", "norm_gain", "norm_shift",
)
MATRICES = LAYER_PARAMS[:4]


def nn(a, b):
    return lax.dot_general(a, b, (((1,), (0,)), ((), ())), preferred_element_type=F32)


def nt(a, b):
    return lax.dot_general(a, b, (((1,), (1,)), ((), ())), preferred_element_type=F32)


def tn(a, b):
    return lax.dot_general(a, b, (((0,), (0,)), ((), ())), preferred_element_type=F32)


def call(body, ins, outs, scratch, aliases=None, sems=48, micros=0.001):
    names = list(ins) + list(outs) + list(scratch) + ["sems"]

    def kernel(*refs):
        body(SimpleNamespace(**dict(zip(names, refs))))

    in_names, out_names = list(ins), list(outs)
    result = pl.pallas_call(
        kernel,
        in_specs=[pl.BlockSpec(memory_space=space) for _, space in ins.values()],
        out_specs=[pl.BlockSpec(memory_space=space) for _, _, space in outs.values()],
        out_shape=[jax.ShapeDtypeStruct(shape, dtype) for shape, dtype, _ in outs.values()],
        scratch_shapes=[pltpu.VMEM(shape, dtype) for shape, dtype in scratch.values()] + [pltpu.SemaphoreType.DMA((sems,))],
        input_output_aliases={in_names.index(a): out_names.index(b) for a, b in (aliases or {}).items()},
        compiler_params=pltpu.CompilerParams(vmem_limit_bytes=VMEM_LIMIT),
        cost_estimate=pl.CostEstimate(flops=int(micros * 1150000000), bytes_accessed=2**12, transcendentals=0),
    )(*[array for array, _ in ins.values()])
    return dict(zip(out_names, result))


class Copies:
    def __init__(self, sems):
        self.sems, self.used, self.ends = sems, 0, []

    def start(self, src, dst):
        copy = pltpu.make_async_copy(src, dst, self.sems.at[self.used])
        self.used += 1
        copy.start()
        return copy

    def either(self, first, src_a, src_b, dst, out=False):
        sem = self.sems.at[self.used]
        self.used += 1
        pl.when(first)(lambda: pltpu.make_async_copy(src_a, dst, sem).start())
        pl.when(jnp.logical_not(first))(lambda: pltpu.make_async_copy(src_b, dst, sem).start())
        copy = pltpu.make_async_copy(src_a, dst, sem)
        if out:
            self.ends.append(copy)
        return copy

    def choose(self, cases, dst):
        sem = self.sems.at[self.used]
        self.used += 1
        for holds, src in cases:
            pl.when(holds)(lambda src=src: pltpu.make_async_copy(src, dst, sem).start())
        return pltpu.make_async_copy(cases[0][1], dst, sem)

    def out(self, src, dst):
        self.ends.append(self.start(src, dst))

    def finish(self):
        for copy in self.ends:
            copy.wait()


def norm_rows(residual):
    center = residual - jnp.mean(residual, axis=-1, keepdims=True)
    inv_std = lax.rsqrt(jnp.mean(center * center, axis=-1, keepdims=True) + EPS)
    return center * inv_std, inv_std


def norm_back(grad, normed, inv, gain):
    e = grad * gain
    return inv * (
        e - jnp.mean(e, axis=-1, keepdims=True) - normed * jnp.mean(e * normed, axis=-1, keepdims=True)
    )


def one_hot_rows(rank_row, size, length):
    return (lax.broadcasted_iota(jnp.int32, (size, length), 0) == rank_row).astype(F32).astype(BF)


def one_hot_cols(rank_col, size):
    length = rank_col.shape[0]
    return (lax.broadcasted_iota(jnp.int32, (length, size), 1) == rank_col).astype(F32).astype(BF)


def put_masked(dst, src, tokens):
    zeros = jnp.zeros((HEAD_DIM, tokens), BF)
    for head in range(HEADS):
        part = (head % 2) * HEAD_DIM
        dst[head, part : part + HEAD_DIM, :] = src[head * HEAD_DIM : (head + 1) * HEAD_DIM, :]
        dst[head, HEAD_DIM - part : 2 * HEAD_DIM - part, :] = zeros


def head_sums(a, b):
    out = []
    for head in range(HEADS):
        rows = slice(head * HEAD_DIM, (head + 1) * HEAD_DIM)
        out.append(jnp.sum(a[rows, :].astype(F32) * b[rows, :].astype(F32), axis=0, keepdims=True))
    return out


def rank_tokens(known, length):
    upto = lax.broadcasted_iota(jnp.int32, (length, length), 0) <= lax.broadcasted_iota(jnp.int32, (length, length), 1)
    low = jnp.broadcast_to(known.astype(F32), (8, length))
    place = nn(low.astype(BF), upto.astype(F32).astype(BF))
    return jnp.where(low > 0.5, place - 1.0, -1.0).astype(jnp.int32)


def small_count(length):
    return length // 2 + length // 8


def param_row(ref, layer, kind=None):
    return ref[pl.ds(layer, 1), :] if kind is None else ref[layer, pl.ds(kind, 1), :]


def key_rows(quick):
    sizes = [small_count(length) if quick else length for _, length, _, _ in CELLS]
    return ((0, sizes[0]), (sizes[0], sizes[1])), sum(sizes)


def split_rank(r):
    ranks = [r.rank[:, start : start + length] for start, length, _, _ in CELLS]
    return ranks, [jnp.max(rank[0:1, :]) + 1 for rank in ranks]


def units():
    out = []
    for cell, (_, _, first, count) in enumerate(CELLS):
        for at in range(first, first + count, 256):
            out.append((cell, slice(at, at + 256)))
    return out


def small_counts(counts):
    ok = counts[0] <= small_count(CELLS[0][1])
    for count, (_, length, _, _) in zip(counts[1:], CELLS[1:]):
        ok = ok & (count <= small_count(length))
    return ok


def put_key_bias(r, rows, counts):
    for (first, size), count in zip(rows, counts):
        inside = lax.broadcasted_iota(jnp.int32, (size, 128), 0) < count
        r.kb[first : first + size, :] = jnp.where(inside, 0.0, FILL)


def own_rows_of(core, other=False):
    place = 1 - core if other else core
    return [pl.ds(pl.multiple_of(start + place * count, count), count) for start, _, _, count in CELLS]


def forward_body(r, layer):
    core = r.scal[0]
    copies = Copies(r.sems)
    mine, slot = r.scal[1] == 1, r.scal[2]
    if layer == 0:
        known_in = copies.either(mine, r.known_here, r.known_there, r.known)
        u_in = []
        for buffer, other in ((r.u_own, False), (r.u_oth, True)):
            for rows, (_, _, first, count) in zip(own_rows_of(core, other), CELLS):
                u_in.append(
                    copies.either(
                        mine, r.x_here.at[slot, rows], r.x_there.at[slot, rows], buffer.at[pl.ds(first, count)]
                    )
                )
        u_own_in, u_oth_in = u_in[:2], u_in[2:]
    else:
        rank_in = copies.start(r.rank_in, r.rank)
        u_own_in, u_oth_in = [copies.start(r.x_own.at[1], r.u_own)], [copies.start(r.x_oth.at[1], r.u_oth)]
    w_in = copies.start(r.attn_proj_in.at[layer], r.w)
    small = start_params(copies, r)
    late = [
        copies.start(r.attn_out_in.at[layer], r.w_mix),
        copies.start(r.ff_in_in.at[layer], r.w_up),
        copies.start(r.ff_out_in.at[layer], r.w_down),
    ]

    def save(*names):
        for name in names:
            copies.out(getattr(r, name), getattr(r, name + "_out"))

    if layer == 0:
        known_in.wait()
        for start, length, _, count in CELLS:
            known = r.known[pl.ds(slot, 1), :][:, start : start + length]
            first, second = known[:, :count], known[:, count:]
            known = jnp.concatenate([jnp.where(core == 0, first, second), jnp.where(core == 0, second, first)], axis=1)
            r.rank[:, start : start + length] = rank_tokens(known, length)
        save("rank")
    else:
        rank_in.wait()
    ranks, counts = split_rank(r)
    for copy in small + u_own_in:
        copy.wait()
    w_in.wait()
    own = nn(r.u_own[...], r.w[...])
    r.q_t[...] = (own[:, :D] + param_row(r.query_bias, layer)).astype(BF).T
    r.ko_t[...] = (own[:, D : 2 * D] * SOFT).astype(BF).T
    r.vo_t[...] = (own[:, 2 * D :] + param_row(r.value_bias, layer)).astype(BF).T
    save("q_t", "ko_t", "vo_t")
    put_masked(r.qm, r.q_t, OWN)
    unk = jnp.concatenate(
        [jnp.where(rank[0:1, :count] >= 0, FILL, 0.0) for rank, (_, _, _, count) in zip(ranks, CELLS)], axis=1
    )
    for head, row in enumerate(head_sums(r.q_t, r.ko_t)):
        r.sd[head] = row + unk
        r.total[head] = jnp.zeros_like(row)
        r.top[head] = jnp.zeros_like(row)
    for copy in u_oth_in:
        copy.wait()

    def keys(quick):
        rows, total = key_rows(quick)
        for rank, (_, length, own_first, count), (first, size) in zip(ranks, CELLS, rows):
            pick = one_hot_rows(rank[0:1, :], size, length)
            tokens = slice(own_first, own_first + count)
            uc = nn(pick[:, :count], r.u_own[tokens, :]) + nn(pick[:, count:], r.u_oth[tokens, :])
            r.uc[first : first + size, :] = uc.astype(BF)
        kv = nn(r.uc[:total, :], r.w[:, D:])
        r.k_c[:total, :] = (kv[:, :D] * SOFT).astype(BF)
        ones = []
        for (first, size), known in zip(rows, counts):
            inside = lax.broadcasted_iota(jnp.int32, (size, D), 0) < known
            vc = kv[first : first + size, D:] + param_row(r.value_bias, layer)
            r.v_c[first : first + size, :] = jnp.where(inside, vc, 0.0).astype(BF)
            lane = lax.broadcasted_iota(jnp.int32, (16, size), 1)
            ones.append(((lane < known) & (lax.broadcasted_iota(jnp.int32, (16, size), 0) == 0)).astype(F32))
        vct = r.v_c[:total, :].T
        ones = jnp.concatenate(ones, axis=1).astype(BF)
        for head in range(HEADS):
            r.vaug[head * VAUG : head * VAUG + HEAD_DIM, :total] = vct[head * HEAD_DIM : (head + 1) * HEAD_DIM, :]
            r.vaug[head * VAUG + HEAD_DIM : (head + 1) * VAUG, :total] = ones

    def attend(quick):
        rows_of, _ = key_rows(quick)
        if not quick:
            put_key_bias(r, rows_of, counts)

        def pair(p, carry):
            lanes = pl.ds(pl.multiple_of(p * 128, 128), 128)
            for e in range(2):
                head = 2 * p + e
                feats = pl.ds(pl.multiple_of(head * HEAD_DIM, HEAD_DIM), HEAD_DIM)
                for cell, cols in units():
                    keys_at = slice(rows_of[cell][0], rows_of[cell][0] + rows_of[cell][1])
                    vrows = r.vaug[pl.ds(pl.multiple_of(head * VAUG, 16), VAUG), keys_at]
                    scores = nn(r.k_c[keys_at, lanes], r.qm[head, :, cols])
                    own_score = r.sd[head, :, cols]
                    if quick:
                        low = jnp.exp2(scores).astype(BF)
                    else:
                        tops, probs = [], []
                        for t in range(0, 256, 128):
                            part = scores[:, t : t + 128] + r.kb[keys_at, :]
                            top = jnp.maximum(jnp.max(part, axis=0, keepdims=True), own_score[:, t : t + 128])
                            tops.append(top)
                            probs.append(jnp.exp2(part - top).astype(BF))
                        top = jnp.concatenate(tops, axis=1)
                        low = jnp.concatenate(probs, axis=1)
                        r.top[head, :, cols] = top
                        own_score = own_score - top
                    mixed = nn(vrows, low)
                    own_prob = jnp.exp2(own_score)
                    total = mixed[HEAD_DIM : HEAD_DIM + 1] + own_prob
                    r.total[head, :, cols] = total
                    mixed = mixed[:HEAD_DIM] + own_prob * r.vo_t[feats, cols].astype(F32)
                    r.mix_t[feats, cols] = (mixed * (1.0 / total)).astype(BF)
            return carry

        lax.fori_loop(0, HEADS // 2, pair, 0)

    def run(quick):
        keys(quick)
        attend(quick)

    pl.when(small_counts(counts))(lambda: run(True))
    totals = r.total[...]
    fine = jnp.min(jnp.where((totals > SMALLEST) & (totals < LARGEST), 1, 0)) == 1
    pl.when(jnp.logical_not(fine))(lambda: run(False))
    save("uc", "k_c", "v_c", "mix_t", "top", "total")
    for copy in late:
        copy.wait()

    for at in range(0, OWN, 256):
        rows = slice(at, at + 256)
        res = r.u_own[rows, :].astype(F32) + tn(r.mix_t[:, rows], r.w_mix[...]) + param_row(r.out_bias, layer)
        normed, inv0 = norm_rows(res)
        r.nrm0[rows, :] = normed.astype(BF)
        even = (normed * param_row(r.norm_gain, layer, 0) + param_row(r.norm_shift, layer, 0)).astype(BF)
        r.even[rows, :] = even
        pre = nn(even, r.w_up[...]) + param_row(r.ff_bias_in, layer)
        cdf = 0.5 + 0.5 * lax.erf(pre * 0.7071067811865476)
        hidden = (pre * cdf).astype(BF)
        r.hid[rows, :] = hidden
        r.gp[rows, :] = (cdf + pre * (0.3989422804014327 * jnp.exp(-0.5 * pre * pre))).astype(BF)
        res = even.astype(F32) + nn(hidden, r.w_down[...]) + param_row(r.ff_bias_out, layer)
        normed, inv1 = norm_rows(res)
        r.nrm1[rows, :] = normed.astype(BF)
        r.odd[rows, :] = (normed * param_row(r.norm_gain, layer, 1) + param_row(r.norm_shift, layer, 1)).astype(BF)
        r.inv[rows, :] = jnp.where(lax.broadcasted_iota(jnp.int32, (256, 128), 1) == 0, inv0, inv1)

    copies.out(r.even, r.pair_out.at[0])
    copies.out(r.odd, r.pair_out.at[1])
    if layer == 0:
        copies.either(core == 0, r.even, r.odd, r.ship_out.at[core], True)
    else:
        copies.out(r.even, r.ship_out.at[core])
    save("nrm0", "nrm1", "gp", "hid", "inv")
    copies.finish()


TOK = ((OWN, D), BF)
FEAT = ((D, OWN), BF)
KEYS = ((ROW, D), BF)
HEAD_ROWS = ((HEADS, 1, OWN), F32)
RANK = ((8, ROW), jnp.int32)
SAVED = dict(
    even=TOK, q_t=FEAT, ko_t=FEAT, vo_t=FEAT, uc=KEYS, k_c=KEYS, v_c=KEYS, mix_t=FEAT, nrm0=TOK, nrm1=TOK, gp=TOK, hid=TOK,
    inv=((OWN, 128), F32), top=HEAD_ROWS, total=HEAD_ROWS,
)
FF_SAVED = ("nrm1", "inv", "gp", "nrm0", "hid", "even")
ATT_SAVED = ("mix_t", "q_t", "k_c", "v_c", "top", "total", "ko_t", "vo_t", "uc")
BOTH = ((2, OWN, D), BF)


def weight_buffers():
    square = ((D, D), BF)
    return dict(w=((D, 3 * D), BF), w_mix=square, w_up=square, w_down=square)


def param_inputs(params):
    return {name + "_in": (params[name], pl.ANY) for name in LAYER_PARAMS}


def param_buffers():
    pairs = {name: ((2, 2, D) if name.startswith("norm") else (2, D), F32) for name in LAYER_PARAMS[4:]}
    return {**pairs, **weight_buffers()}


def start_params(copies, r):
    return [copies.start(getattr(r, name + "_in"), getattr(r, name)) for name in LAYER_PARAMS[4:]]


def any_inputs(**arrays):
    return {name: (array, pl.ANY) for name, array in arrays.items()}


def forward_layer(layer, scal, params, inputs):
    ins = {"scal": (scal, pltpu.SMEM), **param_inputs(params), **inputs}
    outs = {name + "_out": (*spec, pl.ANY) for name, spec in SAVED.items() if name != "even"}
    outs.update(pair_out=(*BOTH, pl.ANY), ship_out=(*BOTH, pl.ANY))
    scratch = {
        **SAVED, **param_buffers(), "u_own": TOK, "u_oth": TOK, "odd": TOK, "rank": RANK, "qm": ((HEADS, 128, OWN), BF),
        "vaug": ((HEADS * VAUG, ROW), BF), "kb": ((ROW, 128), F32), "sd": HEAD_ROWS,
    }
    if layer == 0:
        outs["rank_out"] = (*RANK, pl.ANY)
        scratch["known"] = ((2, ROW), jnp.int32)
    return call(lambda r: forward_body(r, layer), ins, outs, scratch, micros=20)


def ff_back(r, layer, need):
    sums = [jnp.zeros((1, D), F32) for _ in range(7)]

    def add(slot, value):
        sums[slot] = sums[slot] + jnp.sum(value, axis=0, keepdims=True)

    need("g", "nrm1", "inv", "w_down", "w_up", "gp", "nrm0")
    for at in range(0, OWN, 256):
        rows = slice(at, at + 256)
        if layer == 1:
            grad = r.g[rows, :].astype(F32)
        else:
            low = (r.dx[rows, :] + r.g[rows, :].astype(F32)).astype(BF)
            r.g[rows, :] = low
            grad = low.astype(F32)
        normed = r.nrm1[rows, :].astype(F32)
        add(5, grad * normed)
        add(6, grad)
        dres = norm_back(grad, normed, r.inv[rows, 1:2], param_row(r.norm_gain, layer, 1))
        add(4, dres)
        low = dres.astype(BF)
        r.db1[rows, :] = low
        dp = nt(low, r.w_down[...]) * r.gp[rows, :].astype(F32)
        add(3, dp)
        low = dp.astype(BF)
        r.dpre[rows, :] = low
        low = (dres + nt(low, r.w_up[...])).astype(BF)
        r.g_odd[rows, :] = low
        grad = low.astype(F32)
        normed = r.nrm0[rows, :].astype(F32)
        add(1, grad * normed)
        add(2, grad)
        dres = norm_back(grad, normed, r.inv[rows, 0:1], param_row(r.norm_gain, layer, 0))
        add(0, dres)
        r.dr[rows, :] = dres
        r.db0[rows, :] = dres.astype(BF)
    vectors = jnp.concatenate(sums + [jnp.zeros((121, D), F32)], axis=0)
    r.ff_pack[:, 2 * D :] = vectors.T.astype(BF)


def ff_weights(r, need):
    need("hid", "even")
    r.ff_pack[:, :D] = tn(r.even[...], r.dpre[...]).astype(BF)
    r.ff_pack[:, D : 2 * D] = tn(r.hid[...], r.db1[...]).astype(BF)


def attention_back(r, layer, copies, need):
    core = r.scal[0]
    need("w_mix", "mix_t")
    dm_t = nt(r.w_mix[...], r.db0[...]).astype(BF)
    r.dm_t[...] = dm_t
    dm_sum = jnp.sum(dm_t.astype(F32), axis=1, keepdims=True)
    need("q_t", "top", "total", "ko_t", "vo_t")
    put_masked(r.qm, r.q_t, OWN)
    zeros = jnp.zeros((HEAD_DIM, OWN), BF)
    deltas = head_sums(r.dm_t, r.mix_t)
    for head in range(HEADS):
        rows = slice(head * HEAD_DIM, (head + 1) * HEAD_DIM)
        part = (head % 2) * HEAD_DIM
        inv_total = 1.0 / r.total[head]
        r.total[head] = inv_total
        r.delta[head] = deltas[head] * inv_total
        r.dmm[head, part : part + HEAD_DIM, :] = (r.dm_t[rows, :].astype(F32) * inv_total).astype(BF)
        r.dmm[head, HEAD_DIM - part : 2 * HEAD_DIM - part, :] = zeros
    need("k_c", "v_c", "uc", "w", "rank")
    ranks, counts = split_rank(r)
    quick_ok = small_counts(counts) & (jnp.max(jnp.abs(r.top[...])) == 0.0)

    def run(quick):
        rows_of, total = key_rows(quick)
        r.kc_t[:, :total] = r.k_c[:total, :].T
        if not quick:
            put_key_bias(r, rows_of, counts)

        def pair(p, carry):
            lanes = pl.ds(pl.multiple_of(p * 128, 128), 128)
            late_lanes = pl.ds(pl.multiple_of(D + p * 128, 128), 128)
            dk = [jnp.zeros((size, 128), F32) for _, size in rows_of]
            dv = [jnp.zeros((size, 128), F32) for _, size in rows_of]
            for e in range(2):
                head = 2 * p + e
                feats = pl.ds(pl.multiple_of(head * HEAD_DIM, HEAD_DIM), HEAD_DIM)
                for cell, cols in units():
                    keys_at = slice(rows_of[cell][0], rows_of[cell][0] + rows_of[cell][1])
                    qtm = r.qm[head, :, cols]
                    dmh = r.dmm[head, :, cols]
                    scores = nn(r.k_c[keys_at, lanes], qtm)
                    dprob = nn(r.v_c[keys_at, lanes], dmh)
                    delta = r.delta[head, :, cols]
                    if quick:
                        prob = jnp.exp2(scores)
                        low = prob.astype(BF)
                        ds = (prob * (dprob - delta)).astype(BF)
                    else:
                        top = r.top[head, :, cols]
                        lows, grads = [], []
                        for t in range(0, 256, 128):
                            tile = slice(t, t + 128)
                            prob = jnp.exp2(jnp.minimum(scores[:, tile] - top[:, tile], r.kb[keys_at, :]))
                            lows.append(prob.astype(BF))
                            grads.append((prob * (dprob[:, tile] - delta[:, tile])).astype(BF))
                        low = jnp.concatenate(lows, axis=1)
                        ds = jnp.concatenate(grads, axis=1)
                    dv[cell] = dv[cell] + nt(low, dmh)
                    dk[cell] = dk[cell] + nt(ds, qtm)
                    r.dq_t[feats, cols] = nn(r.kc_t[feats, keys_at], ds) * LN2
            for cell, (first, size) in enumerate(rows_of):
                r.dkv[first : first + size, lanes] = (dk[cell] * SCALE).astype(BF)
                r.dkv[first : first + size, late_lanes] = dv[cell].astype(BF)
            return carry

        lax.fori_loop(0, HEADS // 2, pair, 0)
        dkv = r.dkv[:total, :]
        r.dw_kv[...] = tn(r.uc[:total, :], dkv)
        dxc = nt(dkv, r.w[:, D:]).astype(BF)
        for rank, (_, _, own_first, count), (first, size) in zip(ranks, CELLS, rows_of):
            rank_col = rank.astype(F32).T[:, 0:1].astype(jnp.int32)
            tokens = slice(own_first, own_first + count)
            part = dxc[first : first + size, :]
            r.dr[tokens, :] += nn(one_hot_cols(rank_col[:count, :], size), part)
            r.dxo[tokens, :] = nn(one_hot_cols(rank_col[count:, :], size), part).astype(BF)

    pl.when(quick_ok)(lambda: run(True))
    pl.when(jnp.logical_not(quick_ok))(lambda: run(False))
    if layer == 1:
        copies.out(r.dxo, r.dx_oth_out)
    else:
        copies.out(r.dxo, r.dx_out.at[1 - core])

    unk = jnp.concatenate(
        [jnp.where(rank[0:1, :count] >= 0, FILL, 0.0) for rank, (_, _, _, count) in zip(ranks, CELLS)], axis=1
    )
    own_scores = head_sums(r.q_t, r.ko_t)
    own_dprobs = head_sums(r.dm_t, r.vo_t)
    dq_parts, dk_parts, dv_parts = [], [], []
    for head in range(HEADS):
        rows = slice(head * HEAD_DIM, (head + 1) * HEAD_DIM)
        prob = jnp.exp2(own_scores[head] + unk - r.top[head])
        ds = (prob * (own_dprobs[head] * r.total[head] - r.delta[head])).astype(BF).astype(F32)
        low = (prob * r.total[head]).astype(BF).astype(F32)
        dq_parts.append(r.dq_t[rows, :] + (ds * LN2) * r.ko_t[rows, :].astype(F32))
        dk_parts.append(((ds * SCALE) * r.q_t[rows, :].astype(F32)).astype(BF))
        dv_parts.append((low * r.dm_t[rows, :].astype(F32)).astype(BF))
    dq = jnp.concatenate(dq_parts, axis=0)
    dq_sum = jnp.sum(dq, axis=1, keepdims=True)
    dp = jnp.concatenate([dq.astype(BF)] + dk_parts + dv_parts, axis=0).T
    r.dr[...] += nt(dp, r.w[...])
    if layer == 1:
        copies.out(r.dr, r.dx_own_out)
    else:
        r.dxw[...] = r.dr[...].astype(BF)
        copies.out(r.dxw, r.dx_out.at[core])
    need("u_own")
    dw = tn(r.u_own[...], dp)
    r.att_pack[:, :D] = dw[:, :D].astype(BF)
    r.att_pack[:, D : 3 * D] = (dw[:, D:] + r.dw_kv[...]).astype(BF)
    r.att_pack[:, 3 * D : 4 * D] = nn(r.mix_t[...], r.db0[...]).astype(BF)
    lane = lax.broadcasted_iota(jnp.int32, (D, 128), 1)
    r.att_pack[:, 4 * D :] = jnp.where(lane == 0, dq_sum, jnp.where(lane == 1, dm_sum, 0.0)).astype(BF)


FF_BUFFERS = dict(
    {name: SAVED[name] for name in FF_SAVED}, g=TOK, g_odd=TOK, db0=TOK, db1=TOK, dpre=TOK, dr=((OWN, D), F32),
    ff_pack=((D, FF_PACK), BF),
)
ATT_BUFFERS = dict(
    {name: SAVED[name] for name in ATT_SAVED}, u_own=TOK, db0=TOK, dxo=TOK, dr=((OWN, D), F32), qm=((HEADS, 128, OWN), BF),
    dmm=((HEADS, 128, OWN), BF), dm_t=FEAT, delta=HEAD_ROWS, kc_t=((D, ROW), BF), kb=((ROW, 128), F32),
    dq_t=((D, OWN), F32), dkv=((ROW, 2 * D), BF), dw_kv=((D, 2 * D), F32), att_pack=((D, ATT_PACK), BF), rank=RANK,
)


class Loads:
    def __init__(self):
        self.waiting = {}

    def add(self, name, *copies):
        self.waiting.setdefault(name, []).extend(copies)

    def need(self, *names):
        for name in names:
            for copy in self.waiting.pop(name):
                copy.wait()


def start_ff_loads(r, copies, loads, layer):
    loads.add("even", copies.start(r.pair_in.at[0], r.even))
    for name in FF_SAVED[:3]:
        loads.add(name, copies.start(getattr(r, name + "_in"), getattr(r, name)))
    loads.add("w_down", copies.start(r.ff_out_in.at[layer], r.w_down))
    loads.add("w_up", copies.start(r.ff_in_in.at[layer], r.w_up))
    for name in FF_SAVED[3:5]:
        loads.add(name, copies.start(getattr(r, name + "_in"), getattr(r, name)))


def start_att_loads(r, copies, loads, layer):
    loads.add("w_mix", copies.start(r.attn_out_in.at[layer], r.w_mix))
    for name in ATT_SAVED:
        loads.add(name, copies.start(getattr(r, name + "_in"), getattr(r, name)))
    loads.add("rank", copies.start(r.rank_in, r.rank))
    loads.add("w", copies.start(r.attn_proj_in.at[layer], r.w))


def saved_inputs(saved, names):
    ins = {name + "_in": (saved[name + "_out"], pl.ANY) for name in names if name != "even"}
    if "even" in names:
        ins["pair_in"] = (saved["pair_out"], pl.ANY)
    return ins


def backward_last(scal, params, saved, inputs, rank):
    def body(r):
        core, mine, slot = r.scal[0], r.scal[1] == 1, r.scal[2]
        copies, loads = Copies(r.sems), Loads()
        for rows, (_, _, first, count) in zip(own_rows_of(core), CELLS):
            src = [c.at[slot, rows] for c in (r.c_here, r.c_there)]
            loads.add("g", copies.either(mine, *src, r.g.at[pl.ds(first, count)]))
        loads.add("g", *start_params(copies, r))
        start_ff_loads(r, copies, loads, 1)
        start_att_loads(r, copies, loads, 1)
        loads.add("u_own", copies.start(r.x_own.at[1], r.u_own))
        ff_back(r, 1, loads.need)
        ff_weights(r, loads.need)
        copies.out(r.ff_pack, r.pack_out.at[:, pl.ds(0, FF_PACK)])
        attention_back(r, 1, copies, loads.need)
        copies.out(r.att_pack, r.pack_out.at[:, pl.ds(FF_PACK, ATT_PACK)])
        copies.finish()

    ins = {
        "scal": (scal, pltpu.SMEM), **param_inputs(params), **inputs, "rank_in": (rank, pl.ANY), **saved_inputs(saved, SAVED)
    }
    outs = {
        "dx_own_out": ((OWN, D), F32, pl.ANY), "dx_oth_out": (*TOK, pl.ANY),
        "pack_out": ((D, FF_PACK + ATT_PACK), BF, pl.ANY),
    }
    return call(body, ins, outs, {**FF_BUFFERS, **ATT_BUFFERS, **param_buffers()}, sems=64, micros=30)


def backward_first_ff(scal, params, saved, inputs):
    def body(r):
        copies, loads = Copies(r.sems), Loads()
        loads.add("g", copies.start(r.dx_oth, r.g), copies.start(r.dx_own, r.dx))
        loads.add("g", *start_params(copies, r))
        start_ff_loads(r, copies, loads, 0)
        ff_back(r, 0, loads.need)
        core = r.scal[0]
        copies.either(core == 0, r.g_odd, r.g, r.give_out, True)
        copies.either(core == 0, r.g, r.g_odd, r.ship_out.at[core], True)
        copies.out(r.db0, r.db0_out)
        copies.out(r.dr, r.dr_out)
        ff_weights(r, loads.need)
        copies.out(r.ff_pack, r.pack_out)
        copies.finish()

    ins = {"scal": (scal, pltpu.SMEM), **param_inputs(params), **inputs, **saved_inputs(saved, FF_SAVED)}
    outs = {
        "db0_out": (*TOK, pl.ANY), "dr_out": ((OWN, D), F32, pl.ANY), "pack_out": ((D, FF_PACK), BF, pl.ANY),
        "give_out": (*TOK, pl.ANY), "ship_out": (*BOTH, pl.ANY),
    }
    scratch = {**FF_BUFFERS, **param_buffers(), "dx": ((OWN, D), F32)}
    return call(body, ins, outs, scratch, sems=64, micros=7)


def backward_first_att(scal, params, saved, inputs, rank, dp_count):
    size = D // dp_count

    def body(r):
        core, mine, slot = r.scal[0], r.scal[1] == 1, r.scal[2]
        copies, loads = Copies(r.sems), Loads()
        loads.add("w_mix", copies.start(r.db0_in, r.db0), copies.start(r.dr_in, r.dr))
        start_att_loads(r, copies, loads, 0)
        for rows, (_, _, first, count) in zip(own_rows_of(core), CELLS):
            src = [x.at[slot, rows] for x in (r.x_here, r.x_there)]
            loads.add("u_own", copies.either(mine, *src, r.u_own.at[pl.ds(first, count)]))
        loads.add("ff", copies.start(r.ff_in, r.ff_pack))

        def halves(pack, at, width):
            for n in range(dp_count // 2):
                to = pl.ds(n * size, size)
                keep = pl.ds(pl.multiple_of((2 * n + core) * size, size), size)
                send = pl.ds(pl.multiple_of((2 * n + 1 - core) * size, size), size)
                copies.out(pack.at[keep], r.keep_out.at[to, pl.ds(at, width)])
                copies.out(pack.at[send], r.send_out.at[to, pl.ds(at, width)])

        loads.need("ff")
        halves(r.ff_pack, 0, FF_PACK)
        attention_back(r, 0, copies, loads.need)
        halves(r.att_pack, FF_PACK, ATT_PACK)
        copies.finish()

    ins = {
        "scal": (scal, pltpu.SMEM), **param_inputs(params), **inputs, "rank_in": (rank, pl.ANY),
        **saved_inputs(saved, ATT_SAVED),
    }
    half = ((D // 2, PACK), BF, pl.ANY)
    outs = {"dx_out": (*BOTH, pl.ANY), "keep_out": half, "send_out": half}
    scratch = {**ATT_BUFFERS, **param_buffers(), "ff_pack": ((D, FF_PACK), BF), "dxw": TOK}
    return call(body, ins, outs, scratch, sems=48 + 2 * dp_count, micros=0.001)


def add_and_split(scal, keep, got, groups):
    size = D // (2 * groups)

    def body(r):
        copies = Copies(r.sems)
        ins = [copies.start(r.keep, r.a), copies.start(r.got, r.b)]
        for copy in ins:
            copy.wait()
        r.a[...] = (r.a[...].astype(F32) + r.b[...].astype(F32)).astype(BF)
        for m in range(groups):
            part = pl.ds(pl.multiple_of((r.scal[5] ^ m) * size, size), size)
            copies.out(r.a.at[part], getattr(r, f"part{m}"))
        copies.finish()

    half = ((D // 2, PACK), BF)
    ins = {"scal": (scal, pltpu.SMEM), **any_inputs(keep=keep, got=got)}
    outs = {f"part{m}": ((size, PACK), BF, pl.ANY) for m in range(groups)}
    return list(call(body, ins, outs, {"a": half, "b": half}, sems=2 + groups).values())


def join(own, others, last):
    size = own.shape[0]
    count = last.shape[0]
    parts = [own] + list(others)

    def body(r):
        copies = Copies(r.sems)
        loads = [copies.start(r.last, r.last_parts)]
        loads += [copies.start(getattr(r, f"p{n}"), r.parts.at[n]) for n in range(len(parts))]
        for copy in loads:
            copy.wait()
        for at, held, number in ((PACK, r.last_parts, count), (0, r.parts, len(parts))):
            total = held[0].astype(F32)
            for n in range(1, number):
                total = total + held[n].astype(F32)
            r.out[:, at : at + PACK] = total.astype(BF)
        copies.out(r.out, r.all_out)
        copies.finish()

    ins = any_inputs(**{f"p{n}": p for n, p in enumerate(parts)}, last=last)
    scratch = {
        "parts": ((len(parts), size, PACK), BF), "last_parts": ((count, size, PACK), BF), "out": ((size, 2 * PACK), BF)
    }
    return call(body, ins, {"all_out": ((size, 2 * PACK), BF, pl.ANY)}, scratch, sems=len(parts) + 2)["all_out"]


def put_row(copies, held, out, row):
    for half in range(2):
        for start, _, own_first, count in CELLS:
            copies.out(held.at[half, pl.ds(own_first, count)], out.at[0, row, pl.ds(start + half * count, count)])


def finish_outputs(scal, low, high, own_low, own_high, cotangent, params):
    def body(r):
        section, core = r.scal[4], r.scal[0]
        copies = Copies(r.sems)
        here_high = (section == 3) & (core == 1)
        at00, at01 = ((section == s) & (core == 0) for s in (0, 1))
        at10, at11 = ((section == s) & (core == 1) for s in (0, 1))
        loads = [
            copies.choose(
                [(at00, r.own_low), (at01 | at10, r.low0), (at11, r.low1), (section >= 2, r.high0)], r.held.at[0]
            ),
            copies.choose(
                [
                    (at00, r.low0), (at01 | at10, r.low1), (at11, r.low2),
                    ((section >= 2) & jnp.logical_not(here_high), r.high1), (here_high, r.own_high),
                ],
                r.held.at[1],
            ),
        ]
        for copy in loads:
            copy.wait()

        @pl.when(section < 3)
        def _():
            rest = Copies(r.sems)
            rest.used = copies.used
            for row in range(2):
                put_row(rest, r.held.at[row], r.out, row)
            rest.finish()

        @pl.when(section == 3)
        def _():
            rest = Copies(r.sems)
            rest.used = copies.used
            loads = start_params(rest, r)
            loads.append(rest.start(r.ff_in_in.at[1], r.w_up))
            loads.append(rest.start(r.ff_out_in.at[1], r.w_down))
            for row in range(2):
                for half in range(2):
                    for start, _, own_first, count in CELLS:
                        src = r.cot.at[row, pl.ds(start + half * count, count)]
                        loads.append(rest.start(src, r.g.at[row, half, pl.ds(own_first, count)]))
            for copy in loads:
                copy.wait()

            def step(n, carry):
                row, half = n // 2, n % 2
                for at in range(0, OWN, 256):
                    rows = slice(at, at + 256)
                    even = r.held[row, half, rows, :]
                    pre = nn(even, r.w_up[...]) + param_row(r.ff_bias_in, 1)
                    cdf = 0.5 + 0.5 * lax.erf(pre * 0.7071067811865476)
                    hidden = (pre * cdf).astype(BF)
                    gp = cdf + pre * (0.3989422804014327 * jnp.exp(-0.5 * pre * pre))
                    res = even.astype(F32) + nn(hidden, r.w_down[...]) + param_row(r.ff_bias_out, 1)
                    normed, inv = norm_rows(res)
                    gain = param_row(r.norm_gain, 1, 1)
                    r.held[row, half, rows, :] = (normed * gain + param_row(r.norm_shift, 1, 1)).astype(BF)
                    dres = norm_back(r.g[row, half, rows, :].astype(F32), normed, inv, gain)
                    dp = (nt(dres.astype(BF), r.w_down[...]) * gp).astype(BF)
                    r.g[row, half, rows, :] = (dres + nt(dp, r.w_up[...])).astype(BF)
                return carry

            lax.fori_loop(0, 4, step, 0)
            for row in range(2):
                put_row(rest, r.held.at[row], r.out, row)
                put_row(rest, r.g.at[row], r.grads, row)
            rest.finish()

    ins = {"scal": (scal, pltpu.SMEM), **param_inputs(params)}
    ins.update(any_inputs(low0=low[0], low1=low[1], low2=low[2], high0=high[0], high1=high[1], cot=cotangent))
    ins.update(any_inputs(own_low=own_low, own_high=own_high))
    whole = ((1, 2, ROW, D), BF, pl.ANY)
    scratch = {"held": ((2, 2, OWN, D), BF), "g": ((2, 2, OWN, D), BF), **param_buffers()}
    out = call(body, ins, {"out": whole, "grads": whole}, scratch, sems=48)
    return out["out"], out["grads"]


def finish_grads(scal, first, own_first, second, third, last):
    def body(r):
        section, core = r.scal[4], r.scal[0]
        copies = Copies(r.sems)
        here = (section == 0) & (core == 0)
        loads = [
            copies.choose(
                [(here, r.own), ((section == 0) & jnp.logical_not(here), r.a0), (section == 1, r.b0), (section > 1, r.c0)],
                r.held.at[0],
            ),
            copies.choose([(section == 0, r.a1), (section == 1, r.b1), (section > 1, r.c1)], r.held.at[1]),
        ]
        for row in range(2):
            loads[row].wait()

        @pl.when(section < 3)
        def _():
            rest = Copies(r.sems)
            rest.used = copies.used
            for row in range(2):
                put_row(rest, r.held.at[row], r.out, row)
            rest.finish()

    ins = {"scal": (scal, pltpu.SMEM)}
    ins.update(any_inputs(a0=first[0], a1=first[1], b0=second[0], b1=second[1], c0=third[0], c1=third[1]))
    ins.update(any_inputs(last=last, own=own_first))
    whole = ((1, 2, ROW, D), BF, pl.ANY)
    return call(body, ins, {"out": whole}, {"held": ((2, 2, OWN, D), BF)}, {"last": "out"}, 16)["out"]


def unpack(got):
    count, size, width = got.shape
    wide = ((2, size, 3 * D), F32, pltpu.VMEM)
    square = ((2, size, D), F32, pltpu.VMEM)
    vec = ((2, size), F32, pltpu.VMEM)
    pair = ((2, 2, size), F32, pltpu.VMEM)
    outs = dict(
        proj=wide, out=square, qb=vec, vb=vec, ob=vec, up=square, down=square, ub=vec, db=vec, gain=pair, shift=pair
    )

    def body(r):
        pltpu.sync_copy(r.got, r.held)
        total = r.held[0].astype(F32)
        for n in range(1, count):
            total = total + r.held[n].astype(F32)
        for layer in range(2):
            base = layer * PACK
            ff = total[:, base : base + FF_PACK]
            att = total[:, base + FF_PACK : base + FF_PACK + ATT_PACK]
            r.up[layer] = ff[:, :D]
            r.down[layer] = ff[:, D : 2 * D]
            r.proj[layer] = att[:, : 3 * D]
            r.out[layer] = att[:, 3 * D : 4 * D]
            cols = ff[:, 2 * D :].T
            for ref, k in ((r.ob, 0), (r.ub, 3), (r.db, 4)):
                ref[layer : layer + 1, :] = cols[k : k + 1, :]
            for kind in range(2):
                r.gain[layer, kind : kind + 1, :] = cols[4 * kind + 1 : 4 * kind + 2, :]
                r.shift[layer, kind : kind + 1, :] = cols[4 * kind + 2 : 4 * kind + 3, :]
            cols = att[:, 4 * D :].T
            for ref, k in ((r.qb, 0), (r.vb, 1)):
                ref[layer : layer + 1, :] = cols[k : k + 1, :]

    scratch = {"held": ((count, size, width), BF)}
    return list(call(body, any_inputs(got=got), outs, scratch, sems=1).values())


def make_per_device(dp_count, section_count):
    both = ("dp", "section")

    def index(dp, section):
        return dp * section_count + section

    everyone = [(d, s) for d in range(dp_count) for s in range(section_count)]
    mate_pairs = [(index(d, s), index(d ^ 1, s)) for d, s in everyone]
    fetch_pairs = [(index(d, s), index(d ^ 1, s)) for d, s in everyone if d % 2 == s // 2]

    def send(rows, moves):
        pairs = []
        for d, z in everyone:
            to = moves.get((d % 2, z))
            if to is not None and index(d - d % 2 + z // 2, to) != index(d, z):
                pairs.append((index(d, z), index(d - d % 2 + z // 2, to)))
        return lax.ppermute(rows, both, pairs)

    def ship(rows, sections):
        return [
            send(rows, {(c, z): to for c, to in enumerate(sections) if to is not None for z in (odd, 2 + odd)})
            for odd in range(2)
        ]

    def mate(x):
        return lax.ppermute(x, both, mate_pairs)

    def after(value, *earlier):
        return lax.optimization_barrier((value, earlier))[0]

    def per_device(
        block_input, known_genes, attn_proj, attn_out, query_bias, value_bias, out_bias, ff_in, ff_out,
        ff_bias_in, ff_bias_out, norm_gain, norm_shift, cotangent,
    ):
        params = dict(
            attn_proj=attn_proj, attn_out=attn_out, query_bias=query_bias, value_bias=value_bias, out_bias=out_bias,
            ff_in=ff_in, ff_out=ff_out, ff_bias_in=ff_bias_in, ff_bias_out=ff_bias_out, norm_gain=norm_gain,
            norm_shift=norm_shift,
        )
        dp = lax.axis_index("dp")
        core = dp % 2
        section = lax.axis_index("section")
        mine = (core == section // 2).astype(jnp.int32)
        scal = jnp.stack([core, mine, section % 2, 2 * (section % 2) + core, section, dp // 2]).astype(jnp.int32)

        known_there = lax.ppermute(known_genes, both, fetch_pairs)
        x_there = lax.ppermute(block_input, both, fetch_pairs)
        x_in = any_inputs(x_here=block_input, x_there=x_there)
        f0 = forward_layer(0, scal, params, {**x_in, **any_inputs(known_here=known_genes, known_there=known_there)})
        rank = f0["rank_out"]
        x_own = f0["pair_out"]
        x_oth = mate(x_own)

        def other_half(rows, half):
            return lax.dynamic_update_index_in_dim(rows, half, 1 - core, 0)

        c_there = lax.ppermute(after(cotangent, x_own), both, fetch_pairs)
        missing = lax.dynamic_index_in_dim(x_oth, core, 0, keepdims=False)
        low_rows = other_half(f0["ship_out"], missing)
        got_low = [
            send(low_rows, {(0, 2): 0, (1, 0): 1, (0, 1): 0}),
            send(low_rows, {(1, 2): 1, (1, 1): 1, (0, 3): 0}),
            send(low_rows, {(1, 3): 1}),
        ]
        f1 = forward_layer(1, scal, params, any_inputs(x_own=x_own, x_oth=x_oth, rank_in=rank))
        high_rows = other_half(f1["ship_out"], mate(f1["pair_out"][0]))
        got_high = ship(high_rows, (2, 3))
        b1 = backward_last(after(scal, got_low[0]), params, f1, any_inputs(c_here=cotangent, c_there=c_there, x_own=x_own), rank)
        wide = lax.all_to_all(b1["pack_out"].reshape(dp_count, -1, PACK), "dp", 0, 0)
        ins = any_inputs(dx_own=b1["dx_own_out"], dx_oth=mate(b1["dx_oth_out"]))
        b0 = backward_first_ff(after(scal, got_high[0]), params, f0, ins)
        grad_rows = other_half(b0["ship_out"], mate(after(b0["give_out"], got_low[1:])))
        got_third = ship(grad_rows, (2, None))
        got_second = ship(grad_rows, (None, 1))
        ins = {**x_in, **any_inputs(db0_in=b0["db0_out"], dr_in=b0["dr_out"], ff_in=b0["pack_out"])}
        last = backward_first_att(after(scal, grad_rows), params, f0, ins, rank, dp_count)

        to_first = [(index(d, s), index(d - 1, s)) for d, s in everyone if d % 2]
        theirs = lax.ppermute(after(last["dx_out"], got_second, got_high[1]), both, to_first)
        first_rows = (last["dx_out"].astype(F32) + theirs.astype(F32)).astype(BF)
        got_first = ship(first_rows, (0, None))
        groups = dp_count // 2
        parts = add_and_split(scal, last["keep_out"], mate(last["send_out"]), groups)
        others = []
        for m in range(1, groups):
            pairs = [(index(d, s), index(d ^ (2 * m), s)) for d, s in everyone]
            others.append(lax.ppermute(parts[m], both, pairs))
        held = join(parts[0], others, wide)
        got = lax.all_to_all(held.reshape(section_count, -1, held.shape[1]), "section", 0, 0)
        grads = unpack(got)
        section_outputs, last_grads = finish_outputs(scal, got_low, got_high, low_rows, high_rows, cotangent, params)
        section_grads = finish_grads(scal, got_first, first_rows, got_second, got_third, last_grads)
        return (section_outputs, section_grads, *grads)

    return per_device


def solution(mesh):
    rows = P("dp", None, None)
    placed = (rows, P("dp", None)) + (P(),) * 11 + (rows,)
    sections = P("section", "dp", None, None)
    matrix = P(None, ("dp", "section"), None)
    vector = P(None, ("dp", "section"))
    pairs = P(None, None, ("dp", "section"))
    return jax.shard_map(
        make_per_device(mesh.shape["dp"], mesh.shape["section"]),
        mesh=mesh,
        in_specs=placed,
        out_specs=(
            sections, sections, matrix, matrix, vector, vector, vector, matrix, matrix, vector, vector, pairs, pairs,
        ),
        check_vma=False,
    )
```

```python
from types import SimpleNamespace

import jax
import jax.numpy as jnp
from jax import lax
from jax.experimental import pallas as pl
from jax.experimental.pallas import tpu as pltpu
from jax.sharding import PartitionSpec as P

D = 512
HEADS = 8
HEAD_DIM = 64
LONG = 1024
SHORT = 512
ROW = LONG + SHORT
EPS = 1e-05
FILL = -1e30
SCALE = HEAD_DIM ** (-0.5)
LOG2E = 1.4426950408889634
LN2 = 0.6931471805599453
SOFT = SCALE * LOG2E
BF = jnp.bfloat16
F32 = jnp.float32
VAUG = HEAD_DIM + 16
ATT_PACK = 4 * D + 128
FF_PACK = 2 * D + 128
PACK = ATT_PACK + FF_PACK
OWN = ROW // 2
CELLS = ((0, LONG, 0, LONG // 2), (LONG, SHORT, LONG // 2, SHORT // 2))
SMALLEST, LARGEST = 2.0 ** -60, 2.0 ** 90
VMEM_LIMIT = 63 * 1024 * 1024
LAYER_PARAMS = (
    "attn_proj", "attn_out", "ff_in", "ff_out",
    "query_bias", "value_bias", "out_bias", "ff_bias_in", "ff_bias_out", "norm_gain", "norm_shift",
)
MATRICES = LAYER_PARAMS[:4]


def nn(a, b):
    return lax.dot_general(a, b, (((1,), (0,)), ((), ())), preferred_element_type=F32)


def nt(a, b):
    return lax.dot_general(a, b, (((1,), (1,)), ((), ())), preferred_element_type=F32)


def tn(a, b):
    return lax.dot_general(a, b, (((0,), (0,)), ((), ())), preferred_element_type=F32)


def call(body, ins, outs, scratch, aliases=None, sems=48, micros=0.001):
    names = list(ins) + list(outs) + list(scratch) + ["sems"]

    def kernel(*refs):
        body(SimpleNamespace(**dict(zip(names, refs))))

    in_names, out_names = list(ins), list(outs)
    result = pl.pallas_call(
        kernel,
        in_specs=[pl.BlockSpec(memory_space=space) for _, space in ins.values()],
        out_specs=[pl.BlockSpec(memory_space=space) for _, _, space in outs.values()],
        out_shape=[jax.ShapeDtypeStruct(shape, dtype) for shape, dtype, _ in outs.values()],
        scratch_shapes=[pltpu.VMEM(shape, dtype) for shape, dtype in scratch.values()] + [pltpu.SemaphoreType.DMA((sems,))],
        input_output_aliases={in_names.index(a): out_names.index(b) for a, b in (aliases or {}).items()},
        compiler_params=pltpu.CompilerParams(vmem_limit_bytes=VMEM_LIMIT),
        cost_estimate=pl.CostEstimate(flops=int(micros * 1150000000), bytes_accessed=2**12, transcendentals=0),
    )(*[array for array, _ in ins.values()])
    return dict(zip(out_names, result))


class Copies:
    def __init__(self, sems):
        self.sems, self.used, self.ends = sems, 0, []

    def start(self, src, dst):
        copy = pltpu.make_async_copy(src, dst, self.sems.at[self.used])
        self.used += 1
        copy.start()
        return copy

    def either(self, first, src_a, src_b, dst, out=False):
        sem = self.sems.at[self.used]
        self.used += 1
        pl.when(first)(lambda: pltpu.make_async_copy(src_a, dst, sem).start())
        pl.when(jnp.logical_not(first))(lambda: pltpu.make_async_copy(src_b, dst, sem).start())
        copy = pltpu.make_async_copy(src_a, dst, sem)
        if out:
            self.ends.append(copy)
        return copy

    def choose(self, cases, dst):
        sem = self.sems.at[self.used]
        self.used += 1
        for holds, src in cases:
            pl.when(holds)(lambda src=src: pltpu.make_async_copy(src, dst, sem).start())
        return pltpu.make_async_copy(cases[0][1], dst, sem)

    def out(self, src, dst):
        self.ends.append(self.start(src, dst))

    def finish(self):
        for copy in self.ends:
            copy.wait()


def norm_rows(residual):
    center = residual - jnp.mean(residual, axis=-1, keepdims=True)
    inv_std = lax.rsqrt(jnp.mean(center * center, axis=-1, keepdims=True) + EPS)
    return center * inv_std, inv_std


def norm_back(grad, normed, inv, gain):
    e = grad * gain
    return inv * (
        e - jnp.mean(e, axis=-1, keepdims=True) - normed * jnp.mean(e * normed, axis=-1, keepdims=True)
    )


def one_hot_rows(rank_row, size, length):
    return (lax.broadcasted_iota(jnp.int32, (size, length), 0) == rank_row).astype(F32).astype(BF)


def one_hot_cols(rank_col, size):
    length = rank_col.shape[0]
    return (lax.broadcasted_iota(jnp.int32, (length, size), 1) == rank_col).astype(F32).astype(BF)


def put_masked(dst, src, tokens):
    zeros = jnp.zeros((HEAD_DIM, tokens.stop - tokens.start), BF)
    for head in range(HEADS):
        part = (head % 2) * HEAD_DIM
        dst[head, part : part + HEAD_DIM, tokens] = src[head * HEAD_DIM : (head + 1) * HEAD_DIM, tokens]
        dst[head, HEAD_DIM - part : 2 * HEAD_DIM - part, tokens] = zeros


def head_sums(a, b, tokens):
    out = []
    for head in range(HEADS):
        rows = slice(head * HEAD_DIM, (head + 1) * HEAD_DIM)
        out.append(jnp.sum(a[rows, tokens].astype(F32) * b[rows, tokens].astype(F32), axis=0, keepdims=True))
    return out


def rank_tokens(known, length):
    upto = lax.broadcasted_iota(jnp.int32, (length, length), 0) <= lax.broadcasted_iota(jnp.int32, (length, length), 1)
    low = jnp.broadcast_to(known.astype(F32), (8, length))
    place = nn(low.astype(BF), upto.astype(F32).astype(BF))
    return jnp.where(low > 0.5, place - 1.0, -1.0).astype(jnp.int32)


def small_count(length):
    return length // 2 + length // 8


def param_row(ref, layer, kind=None):
    return ref[pl.ds(layer, 1), :] if kind is None else ref[layer, pl.ds(kind, 1), :]


def key_rows(quick):
    sizes = [small_count(length) if quick else length for _, length, _, _ in CELLS]
    return ((0, sizes[0]), (sizes[0], sizes[1])), sum(sizes)


def split_rank(r):
    ranks = [r.rank[:, start : start + length] for start, length, _, _ in CELLS]
    return ranks, [jnp.max(rank[0:1, :]) + 1 for rank in ranks]


def units():
    out = []
    for cell, (_, _, first, count) in enumerate(CELLS):
        for at in range(first, first + count, 256):
            out.append((cell, slice(at, at + 256)))
    return out


def small_counts(counts):
    ok = counts[0] <= small_count(CELLS[0][1])
    for count, (_, length, _, _) in zip(counts[1:], CELLS[1:]):
        ok = ok & (count <= small_count(length))
    return ok


def put_key_bias(r, rows, counts):
    for (first, size), count in zip(rows, counts):
        inside = lax.broadcasted_iota(jnp.int32, (size, 128), 0) < count
        r.kb[first : first + size, :] = jnp.where(inside, 0.0, FILL)


def own_rows_of(core, other=False):
    place = 1 - core if other else core
    return [pl.ds(pl.multiple_of(start + place * count, count), count) for start, _, _, count in CELLS]


def forward_body(r, layer):
    core = r.scal[0]
    copies = Copies(r.sems)
    mine, slot = r.scal[1] == 1, r.scal[2]
    if layer == 0:
        known_in = copies.either(mine, r.known_here, r.known_there, r.known)
        u_in = []
        for buffer, other in ((r.u_own, False), (r.u_oth, True)):
            for rows, (_, _, first, count) in zip(own_rows_of(core, other), CELLS):
                u_in.append(
                    copies.either(
                        mine, r.x_here.at[slot, rows], r.x_there.at[slot, rows], buffer.at[pl.ds(first, count)]
                    )
                )
        u_own_in, u_oth_in = u_in[:2], u_in[2:]
    else:
        rank_in = copies.start(r.rank_in, r.rank)
        u_own_in, u_oth_in = [copies.start(r.x_own.at[1], r.u_own)], [copies.start(r.x_oth.at[1], r.u_oth)]
    w_in = copies.start(r.attn_proj_in.at[layer], r.w)
    small = start_params(copies, r)
    late = [
        copies.start(r.attn_out_in.at[layer], r.w_mix),
        copies.start(r.ff_in_in.at[layer], r.w_up),
        copies.start(r.ff_out_in.at[layer], r.w_down),
    ]

    def save(*names):
        for name in names:
            copies.out(getattr(r, name), getattr(r, name + "_out"))

    if layer == 0:
        known_in.wait()
        for start, length, _, count in CELLS:
            known = r.known[pl.ds(slot, 1), :][:, start : start + length]
            first, second = known[:, :count], known[:, count:]
            known = jnp.concatenate([jnp.where(core == 0, first, second), jnp.where(core == 0, second, first)], axis=1)
            r.rank[:, start : start + length] = rank_tokens(known, length)
        save("rank")
    else:
        rank_in.wait()
    ranks, counts = split_rank(r)
    for copy in small + u_own_in:
        copy.wait()
    w_in.wait()
    own = nn(r.u_own[...], r.w[...])
    r.q_t[...] = (own[:, :D] + param_row(r.query_bias, layer)).astype(BF).T
    r.ko_t[...] = (own[:, D : 2 * D] * SOFT).astype(BF).T
    r.vo_t[...] = (own[:, 2 * D :] + param_row(r.value_bias, layer)).astype(BF).T
    save("q_t", "ko_t", "vo_t")
    put_masked(r.qm, r.q_t, slice(0, OWN))
    unk = jnp.concatenate(
        [jnp.where(rank[0:1, :count] >= 0, FILL, 0.0) for rank, (_, _, _, count) in zip(ranks, CELLS)], axis=1
    )
    for head, row in enumerate(head_sums(r.q_t, r.ko_t, slice(0, OWN))):
        r.sd[head] = row + unk
        r.total[head] = jnp.zeros_like(row)
        r.top[head] = jnp.zeros_like(row)
    for copy in u_oth_in:
        copy.wait()

    def keys(quick):
        rows, total = key_rows(quick)
        for rank, (_, length, own_first, count), (first, size) in zip(ranks, CELLS, rows):
            pick = one_hot_rows(rank[0:1, :], size, length)
            tokens = slice(own_first, own_first + count)
            uc = nn(pick[:, :count], r.u_own[tokens, :]) + nn(pick[:, count:], r.u_oth[tokens, :])
            r.uc[first : first + size, :] = uc.astype(BF)
        kv = nn(r.uc[:total, :], r.w[:, D:])
        r.k_c[:total, :] = (kv[:, :D] * SOFT).astype(BF)
        ones = []
        for (first, size), known in zip(rows, counts):
            inside = lax.broadcasted_iota(jnp.int32, (size, D), 0) < known
            vc = kv[first : first + size, D:] + param_row(r.value_bias, layer)
            r.v_c[first : first + size, :] = jnp.where(inside, vc, 0.0).astype(BF)
            lane = lax.broadcasted_iota(jnp.int32, (16, size), 1)
            ones.append(((lane < known) & (lax.broadcasted_iota(jnp.int32, (16, size), 0) == 0)).astype(F32))
        vct = r.v_c[:total, :].T
        ones = jnp.concatenate(ones, axis=1).astype(BF)
        for head in range(HEADS):
            r.vaug[head * VAUG : head * VAUG + HEAD_DIM, :total] = vct[head * HEAD_DIM : (head + 1) * HEAD_DIM, :]
            r.vaug[head * VAUG + HEAD_DIM : (head + 1) * VAUG, :total] = ones

    def attend(quick):
        rows_of, _ = key_rows(quick)
        if not quick:
            put_key_bias(r, rows_of, counts)

        def pair(p, carry):
            lanes = pl.ds(pl.multiple_of(p * 128, 128), 128)
            for e in range(2):
                head = 2 * p + e
                feats = pl.ds(pl.multiple_of(head * HEAD_DIM, HEAD_DIM), HEAD_DIM)
                for cell, cols in units():
                    keys_at = slice(rows_of[cell][0], rows_of[cell][0] + rows_of[cell][1])
                    vrows = r.vaug[pl.ds(pl.multiple_of(head * VAUG, 16), VAUG), keys_at]
                    scores = nn(r.k_c[keys_at, lanes], r.qm[head, :, cols])
                    own_score = r.sd[head, :, cols]
                    if quick:
                        low = jnp.exp2(scores).astype(BF)
                    else:
                        tops, probs = [], []
                        for t in range(0, 256, 128):
                            part = scores[:, t : t + 128] + r.kb[keys_at, :]
                            top = jnp.maximum(jnp.max(part, axis=0, keepdims=True), own_score[:, t : t + 128])
                            tops.append(top)
                            probs.append(jnp.exp2(part - top).astype(BF))
                        top = jnp.concatenate(tops, axis=1)
                        low = jnp.concatenate(probs, axis=1)
                        r.top[head, :, cols] = top
                        own_score = own_score - top
                    mixed = nn(vrows, low)
                    own_prob = jnp.exp2(own_score)
                    total = mixed[HEAD_DIM : HEAD_DIM + 1] + own_prob
                    r.total[head, :, cols] = total
                    mixed = mixed[:HEAD_DIM] + own_prob * r.vo_t[feats, cols].astype(F32)
                    r.mix_t[feats, cols] = (mixed * (1.0 / total)).astype(BF)
            return carry

        lax.fori_loop(0, HEADS // 2, pair, 0)

    def run(quick):
        keys(quick)
        attend(quick)

    pl.when(small_counts(counts))(lambda: run(True))
    totals = r.total[...]
    fine = jnp.min(jnp.where((totals > SMALLEST) & (totals < LARGEST), 1, 0)) == 1
    pl.when(jnp.logical_not(fine))(lambda: run(False))
    save("uc", "k_c", "v_c", "mix_t", "top", "total")
    for copy in late:
        copy.wait()

    for at in range(0, OWN, 256):
        rows = slice(at, at + 256)
        res = r.u_own[rows, :].astype(F32) + tn(r.mix_t[:, rows], r.w_mix[...]) + param_row(r.out_bias, layer)
        normed, inv0 = norm_rows(res)
        r.nrm0[rows, :] = normed.astype(BF)
        even = (normed * param_row(r.norm_gain, layer, 0) + param_row(r.norm_shift, layer, 0)).astype(BF)
        r.even[rows, :] = even
        pre = nn(even, r.w_up[...]) + param_row(r.ff_bias_in, layer)
        cdf = 0.5 + 0.5 * lax.erf(pre * 0.7071067811865476)
        hidden = (pre * cdf).astype(BF)
        r.hid[rows, :] = hidden
        r.gp[rows, :] = (cdf + pre * (0.3989422804014327 * jnp.exp(-0.5 * pre * pre))).astype(BF)
        res = even.astype(F32) + nn(hidden, r.w_down[...]) + param_row(r.ff_bias_out, layer)
        normed, inv1 = norm_rows(res)
        r.nrm1[rows, :] = normed.astype(BF)
        r.odd[rows, :] = (normed * param_row(r.norm_gain, layer, 1) + param_row(r.norm_shift, layer, 1)).astype(BF)
        r.inv[rows, :] = jnp.where(lax.broadcasted_iota(jnp.int32, (256, 128), 1) == 0, inv0, inv1)

    copies.out(r.even, r.pair_out.at[0])
    copies.out(r.odd, r.pair_out.at[1])
    if layer == 0:
        copies.either(core == 0, r.even, r.odd, r.ship_out.at[core], True)
    else:
        copies.out(r.even, r.ship_out.at[core])
    save("nrm0", "nrm1", "gp", "hid", "inv")
    copies.finish()


TOK = ((OWN, D), BF)
FEAT = ((D, OWN), BF)
KEYS = ((ROW, D), BF)
HEAD_ROWS = ((HEADS, 1, OWN), F32)
RANK = ((8, ROW), jnp.int32)
SAVED = dict(
    even=TOK, q_t=FEAT, ko_t=FEAT, vo_t=FEAT, uc=KEYS, k_c=KEYS, v_c=KEYS, mix_t=FEAT, nrm0=TOK, nrm1=TOK, gp=TOK, hid=TOK,
    inv=((OWN, 128), F32), top=HEAD_ROWS, total=HEAD_ROWS,
)
FF_SAVED = ("nrm1", "inv", "gp", "nrm0", "hid", "even")
ATT_SAVED = ("mix_t", "q_t", "k_c", "v_c", "top", "total", "ko_t", "vo_t", "uc")
BOTH = ((2, OWN, D), BF)


def weight_buffers():
    square = ((D, D), BF)
    return dict(w=((D, 3 * D), BF), w_mix=square, w_up=square, w_down=square)


def param_inputs(params):
    return {name + "_in": (params[name], pl.ANY) for name in LAYER_PARAMS}


def param_buffers():
    pairs = {name: ((2, 2, D) if name.startswith("norm") else (2, D), F32) for name in LAYER_PARAMS[4:]}
    return {**pairs, **weight_buffers()}


def start_params(copies, r):
    return [copies.start(getattr(r, name + "_in"), getattr(r, name)) for name in LAYER_PARAMS[4:]]


def any_inputs(**arrays):
    return {name: (array, pl.ANY) for name, array in arrays.items()}


def forward_layer(layer, scal, params, inputs):
    ins = {"scal": (scal, pltpu.SMEM), **param_inputs(params), **inputs}
    outs = {name + "_out": (*spec, pl.ANY) for name, spec in SAVED.items() if name != "even"}
    outs.update(pair_out=(*BOTH, pl.ANY), ship_out=(*BOTH, pl.ANY))
    scratch = {
        **SAVED, **param_buffers(), "u_own": TOK, "u_oth": TOK, "odd": TOK, "rank": RANK, "qm": ((HEADS, 128, OWN), BF),
        "vaug": ((HEADS * VAUG, ROW), BF), "kb": ((ROW, 128), F32), "sd": HEAD_ROWS,
    }
    if layer == 0:
        outs["rank_out"] = (*RANK, pl.ANY)
        scratch["known"] = ((2, ROW), jnp.int32)
    return call(lambda r: forward_body(r, layer), ins, outs, scratch, micros=20)


def ff_back(r, layer, need):
    sums = [jnp.zeros((1, D), F32) for _ in range(7)]

    def add(slot, value):
        sums[slot] = sums[slot] + jnp.sum(value, axis=0, keepdims=True)

    need("g", "nrm1", "inv", "w_down", "w_up", "gp", "nrm0")
    for at in range(0, OWN, 256):
        rows = slice(at, at + 256)
        if layer == 1:
            grad = r.g[rows, :].astype(F32)
        else:
            low = (r.dx[rows, :] + r.g[rows, :].astype(F32)).astype(BF)
            r.g[rows, :] = low
            grad = low.astype(F32)
        normed = r.nrm1[rows, :].astype(F32)
        add(5, grad * normed)
        add(6, grad)
        dres = norm_back(grad, normed, r.inv[rows, 1:2], param_row(r.norm_gain, layer, 1))
        add(4, dres)
        low = dres.astype(BF)
        r.db1[rows, :] = low
        dp = nt(low, r.w_down[...]) * r.gp[rows, :].astype(F32)
        add(3, dp)
        low = dp.astype(BF)
        r.dpre[rows, :] = low
        low = (dres + nt(low, r.w_up[...])).astype(BF)
        r.g_odd[rows, :] = low
        grad = low.astype(F32)
        normed = r.nrm0[rows, :].astype(F32)
        add(1, grad * normed)
        add(2, grad)
        dres = norm_back(grad, normed, r.inv[rows, 0:1], param_row(r.norm_gain, layer, 0))
        add(0, dres)
        r.dr[rows, :] = dres
        r.db0[rows, :] = dres.astype(BF)
    vectors = jnp.concatenate(sums + [jnp.zeros((121, D), F32)], axis=0)
    r.ff_pack[:, 2 * D :] = vectors.T.astype(BF)


def ff_weights(r, need):
    need("hid", "even")
    r.ff_pack[:, :D] = tn(r.even[...], r.dpre[...]).astype(BF)
    r.ff_pack[:, D : 2 * D] = tn(r.hid[...], r.db1[...]).astype(BF)


def attention_back(r, layer, cells, copies, need):
    core = r.scal[0]
    start = CELLS[cells[0]][2]
    stop = CELLS[cells[-1]][2] + CELLS[cells[-1]][3]
    tok = slice(start, stop)
    need("w_mix", "mix_t")
    dm_t = nt(r.w_mix[...], r.db0[tok, :]).astype(BF)
    r.dm_t[:, tok] = dm_t
    dm_sum = jnp.sum(dm_t.astype(F32), axis=1, keepdims=True)
    need("q_t", "top", "total", "ko_t", "vo_t")
    put_masked(r.qm, r.q_t, tok)
    zeros = jnp.zeros((HEAD_DIM, stop - start), BF)
    deltas = head_sums(r.dm_t, r.mix_t, tok)
    for head in range(HEADS):
        rows = slice(head * HEAD_DIM, (head + 1) * HEAD_DIM)
        part = (head % 2) * HEAD_DIM
        inv_total = 1.0 / r.total[head, :, tok]
        r.total[head, :, tok] = inv_total
        r.delta[head, :, tok] = deltas[head] * inv_total
        r.dmm[head, part : part + HEAD_DIM, tok] = (dm_t[rows, :].astype(F32) * inv_total).astype(BF)
        r.dmm[head, HEAD_DIM - part : 2 * HEAD_DIM - part, tok] = zeros
    need("k_c", "v_c", "uc", "w", "rank")
    ranks, counts = split_rank(r)
    quick_ok = small_counts(counts) & (jnp.max(jnp.abs(r.top[...])) == 0.0)

    def run(quick):
        rows_of, _ = key_rows(quick)
        kept = slice(rows_of[cells[0]][0], rows_of[cells[-1]][0] + rows_of[cells[-1]][1])
        r.kc_t[:, kept] = r.k_c[kept, :].T
        if not quick:
            put_key_bias(r, rows_of, counts)

        def pair(p, carry):
            lanes = pl.ds(pl.multiple_of(p * 128, 128), 128)
            late_lanes = pl.ds(pl.multiple_of(D + p * 128, 128), 128)
            dk = {cell: jnp.zeros((rows_of[cell][1], 128), F32) for cell in cells}
            dv = {cell: jnp.zeros((rows_of[cell][1], 128), F32) for cell in cells}
            for e in range(2):
                head = 2 * p + e
                feats = pl.ds(pl.multiple_of(head * HEAD_DIM, HEAD_DIM), HEAD_DIM)
                for cell, cols in units():
                    if cell not in cells:
                        continue
                    keys_at = slice(rows_of[cell][0], rows_of[cell][0] + rows_of[cell][1])
                    qtm = r.qm[head, :, cols]
                    dmh = r.dmm[head, :, cols]
                    scores = nn(r.k_c[keys_at, lanes], qtm)
                    dprob = nn(r.v_c[keys_at, lanes], dmh)
                    delta = r.delta[head, :, cols]
                    if quick:
                        prob = jnp.exp2(scores)
                        low = prob.astype(BF)
                        ds = (prob * (dprob - delta)).astype(BF)
                    else:
                        top = r.top[head, :, cols]
                        lows, grads = [], []
                        for t in range(0, 256, 128):
                            tile = slice(t, t + 128)
                            prob = jnp.exp2(jnp.minimum(scores[:, tile] - top[:, tile], r.kb[keys_at, :]))
                            lows.append(prob.astype(BF))
                            grads.append((prob * (dprob[:, tile] - delta[:, tile])).astype(BF))
                        low = jnp.concatenate(lows, axis=1)
                        ds = jnp.concatenate(grads, axis=1)
                    dv[cell] = dv[cell] + nt(low, dmh)
                    dk[cell] = dk[cell] + nt(ds, qtm)
                    r.dq_t[feats, cols] = nn(r.kc_t[feats, keys_at], ds) * LN2
            for cell in cells:
                first, size = rows_of[cell]
                r.dkv[first : first + size, lanes] = (dk[cell] * SCALE).astype(BF)
                r.dkv[first : first + size, late_lanes] = dv[cell].astype(BF)
            return carry

        lax.fori_loop(0, HEADS // 2, pair, 0)
        dkv = r.dkv[kept, :]
        r.dw_kv[...] = tn(r.uc[kept, :], dkv)
        dxc = nt(dkv, r.w[:, D:]).astype(BF)
        for cell in cells:
            _, _, own_first, count = CELLS[cell]
            first, size = rows_of[cell]
            rank_col = ranks[cell].astype(F32).T[:, 0:1].astype(jnp.int32)
            tokens = slice(own_first, own_first + count)
            part = dxc[first - kept.start : first - kept.start + size, :]
            r.dr[tokens, :] += nn(one_hot_cols(rank_col[:count, :], size), part)
            r.dxo[tokens, :] = nn(one_hot_cols(rank_col[count:, :], size), part).astype(BF)

    pl.when(quick_ok)(lambda: run(True))
    pl.when(jnp.logical_not(quick_ok))(lambda: run(False))
    if layer == 1:
        copies.out(r.dxo, r.dx_oth_out)
    else:
        copies.out(r.dxo.at[pl.ds(start, stop - start)], r.dx_out.at[1 - core])

    unk = jnp.concatenate([jnp.where(ranks[cell][0:1, : CELLS[cell][3]] >= 0, FILL, 0.0) for cell in cells], axis=1)
    own_scores = head_sums(r.q_t, r.ko_t, tok)
    own_dprobs = head_sums(r.dm_t, r.vo_t, tok)
    dq_parts, dk_parts, dv_parts = [], [], []
    for head in range(HEADS):
        rows = slice(head * HEAD_DIM, (head + 1) * HEAD_DIM)
        inv_total = r.total[head, :, tok]
        prob = jnp.exp2(own_scores[head] + unk - r.top[head, :, tok])
        ds = (prob * (own_dprobs[head] * inv_total - r.delta[head, :, tok])).astype(BF).astype(F32)
        low = (prob * inv_total).astype(BF).astype(F32)
        dq_parts.append(r.dq_t[rows, tok] + (ds * LN2) * r.ko_t[rows, tok].astype(F32))
        dk_parts.append(((ds * SCALE) * r.q_t[rows, tok].astype(F32)).astype(BF))
        dv_parts.append((low * r.dm_t[rows, tok].astype(F32)).astype(BF))
    dq = jnp.concatenate(dq_parts, axis=0)
    dq_sum = jnp.sum(dq, axis=1, keepdims=True)
    dp = jnp.concatenate([dq.astype(BF)] + dk_parts + dv_parts, axis=0).T
    total = r.dr[tok, :] + nt(dp, r.w[...])
    if layer == 1:
        r.dr[...] = total
        copies.out(r.dr, r.dx_own_out)
    else:
        r.dxw[tok, :] = total.astype(BF)
        copies.out(r.dxw.at[pl.ds(start, stop - start)], r.dx_out.at[core])
    need("u_own")
    dw = tn(r.u_own[tok, :], dp)
    later = cells[0] > 0
    if later:
        need("prev")

    def put(cols, value):
        if later:
            value = value + r.prev[:, cols].astype(F32)
        r.att_pack[:, cols] = value.astype(BF)

    put(slice(0, D), dw[:, :D])
    put(slice(D, 3 * D), dw[:, D:] + r.dw_kv[...])
    put(slice(3 * D, 4 * D), nn(r.mix_t[:, tok], r.db0[tok, :]))
    lane = lax.broadcasted_iota(jnp.int32, (D, 128), 1)
    put(slice(4 * D, 4 * D + 128), jnp.where(lane == 0, dq_sum, jnp.where(lane == 1, dm_sum, 0.0)))


FF_BUFFERS = dict(
    {name: SAVED[name] for name in FF_SAVED}, g=TOK, g_odd=TOK, db0=TOK, db1=TOK, dpre=TOK, dr=((OWN, D), F32),
    ff_pack=((D, FF_PACK), BF),
)
ATT_BUFFERS = dict(
    {name: SAVED[name] for name in ATT_SAVED}, u_own=TOK, db0=TOK, dxo=TOK, dr=((OWN, D), F32), qm=((HEADS, 128, OWN), BF),
    dmm=((HEADS, 128, OWN), BF), dm_t=FEAT, delta=HEAD_ROWS, kc_t=((D, ROW), BF), kb=((ROW, 128), F32),
    dq_t=((D, OWN), F32), dkv=((ROW, 2 * D), BF), dw_kv=((D, 2 * D), F32), att_pack=((D, ATT_PACK), BF), rank=RANK,
)


class Loads:
    def __init__(self):
        self.waiting = {}

    def add(self, name, *copies):
        self.waiting.setdefault(name, []).extend(copies)

    def need(self, *names):
        for name in names:
            for copy in self.waiting.pop(name):
                copy.wait()


def start_ff_loads(r, copies, loads, layer):
    loads.add("even", copies.start(r.pair_in.at[0], r.even))
    for name in FF_SAVED[:3]:
        loads.add(name, copies.start(getattr(r, name + "_in"), getattr(r, name)))
    loads.add("w_down", copies.start(r.ff_out_in.at[layer], r.w_down))
    loads.add("w_up", copies.start(r.ff_in_in.at[layer], r.w_up))
    for name in FF_SAVED[3:5]:
        loads.add(name, copies.start(getattr(r, name + "_in"), getattr(r, name)))


def start_att_loads(r, copies, loads, layer):
    loads.add("w_mix", copies.start(r.attn_out_in.at[layer], r.w_mix))
    for name in ATT_SAVED:
        loads.add(name, copies.start(getattr(r, name + "_in"), getattr(r, name)))
    loads.add("rank", copies.start(r.rank_in, r.rank))
    loads.add("w", copies.start(r.attn_proj_in.at[layer], r.w))


def saved_inputs(saved, names):
    ins = {name + "_in": (saved[name + "_out"], pl.ANY) for name in names if name != "even"}
    if "even" in names:
        ins["pair_in"] = (saved["pair_out"], pl.ANY)
    return ins


def backward_last(scal, params, saved, inputs, rank):
    def body(r):
        core, mine, slot = r.scal[0], r.scal[1] == 1, r.scal[2]
        copies, loads = Copies(r.sems), Loads()
        for rows, (_, _, first, count) in zip(own_rows_of(core), CELLS):
            src = [c.at[slot, rows] for c in (r.c_here, r.c_there)]
            loads.add("g", copies.either(mine, *src, r.g.at[pl.ds(first, count)]))
        loads.add("g", *start_params(copies, r))
        start_ff_loads(r, copies, loads, 1)
        start_att_loads(r, copies, loads, 1)
        loads.add("u_own", copies.start(r.x_own.at[1], r.u_own))
        ff_back(r, 1, loads.need)
        ff_weights(r, loads.need)
        copies.out(r.ff_pack, r.pack_out.at[:, pl.ds(0, FF_PACK)])
        attention_back(r, 1, (0, 1), copies, loads.need)
        copies.out(r.att_pack, r.pack_out.at[:, pl.ds(FF_PACK, ATT_PACK)])
        copies.finish()

    ins = {
        "scal": (scal, pltpu.SMEM), **param_inputs(params), **inputs, "rank_in": (rank, pl.ANY), **saved_inputs(saved, SAVED)
    }
    outs = {
        "dx_own_out": ((OWN, D), F32, pl.ANY), "dx_oth_out": (*TOK, pl.ANY),
        "pack_out": ((D, FF_PACK + ATT_PACK), BF, pl.ANY),
    }
    return call(body, ins, outs, {**FF_BUFFERS, **ATT_BUFFERS, **param_buffers()}, sems=64, micros=30)


def backward_first_ff(scal, params, saved, inputs):
    def body(r):
        copies, loads = Copies(r.sems), Loads()
        loads.add("g", copies.start(r.dx_oth, r.g), copies.start(r.dx_own, r.dx))
        loads.add("g", *start_params(copies, r))
        start_ff_loads(r, copies, loads, 0)
        ff_back(r, 0, loads.need)
        core = r.scal[0]
        copies.either(core == 0, r.g_odd, r.g, r.give_out, True)
        copies.either(core == 0, r.g, r.g_odd, r.ship_out.at[core], True)
        copies.out(r.db0, r.db0_out)
        copies.out(r.dr, r.dr_out)
        ff_weights(r, loads.need)
        copies.out(r.ff_pack, r.pack_out)
        copies.finish()

    ins = {"scal": (scal, pltpu.SMEM), **param_inputs(params), **inputs, **saved_inputs(saved, FF_SAVED)}
    outs = {
        "db0_out": (*TOK, pl.ANY), "dr_out": ((OWN, D), F32, pl.ANY), "pack_out": ((D, FF_PACK), BF, pl.ANY),
        "give_out": (*TOK, pl.ANY), "ship_out": (*BOTH, pl.ANY),
    }
    scratch = {**FF_BUFFERS, **param_buffers(), "dx": ((OWN, D), F32)}
    return call(body, ins, outs, scratch, sems=64, micros=7)


def backward_first_att(scal, params, saved, inputs, rank, dp_count, cell):
    size = D // dp_count
    _, _, own_first, own_count = CELLS[cell]
    last = cell == len(CELLS) - 1

    def body(r):
        core, mine, slot = r.scal[0], r.scal[1] == 1, r.scal[2]
        copies, loads = Copies(r.sems), Loads()
        loads.add("w_mix", copies.start(r.db0_in, r.db0), copies.start(r.dr_in, r.dr))
        start_att_loads(r, copies, loads, 0)
        rows = own_rows_of(core)[cell]
        src = [x.at[slot, rows] for x in (r.x_here, r.x_there)]
        loads.add("u_own", copies.either(mine, *src, r.u_own.at[pl.ds(own_first, own_count)]))

        def halves(pack, at, width):
            for n in range(dp_count // 2):
                to = pl.ds(n * size, size)
                keep = pl.ds(pl.multiple_of((2 * n + core) * size, size), size)
                send = pl.ds(pl.multiple_of((2 * n + 1 - core) * size, size), size)
                copies.out(pack.at[keep], r.keep_out.at[to, pl.ds(at, width)])
                copies.out(pack.at[send], r.send_out.at[to, pl.ds(at, width)])

        if last:
            loads.add("ff", copies.start(r.ff_in, r.ff_pack))
            loads.add("prev", copies.start(r.prev_in, r.prev))
            loads.need("ff")
            halves(r.ff_pack, 0, FF_PACK)
        attention_back(r, 0, (cell,), copies, loads.need)
        if last:
            halves(r.att_pack, FF_PACK, ATT_PACK)
        else:
            copies.out(r.att_pack, r.pack_out)
        copies.finish()

    ins = {
        "scal": (scal, pltpu.SMEM), **param_inputs(params), **inputs, "rank_in": (rank, pl.ANY),
        **saved_inputs(saved, ATT_SAVED),
    }
    outs = {"dx_out": ((2, own_count, D), BF, pl.ANY)}
    scratch = {**ATT_BUFFERS, **param_buffers(), "dxw": TOK}
    if last:
        half = ((D // 2, PACK), BF, pl.ANY)
        outs.update(keep_out=half, send_out=half)
        scratch.update(ff_pack=((D, FF_PACK), BF), prev=((D, ATT_PACK), BF))
    else:
        outs["pack_out"] = ((D, ATT_PACK), BF, pl.ANY)
    return call(body, ins, outs, scratch, sems=48 + 2 * dp_count, micros=0.001)


def add_and_split(scal, keep, got, groups):
    size = D // (2 * groups)

    def body(r):
        copies = Copies(r.sems)
        ins = [copies.start(r.keep, r.a), copies.start(r.got, r.b)]
        for copy in ins:
            copy.wait()
        r.a[...] = (r.a[...].astype(F32) + r.b[...].astype(F32)).astype(BF)
        for m in range(groups):
            part = pl.ds(pl.multiple_of((r.scal[5] ^ m) * size, size), size)
            copies.out(r.a.at[part], getattr(r, f"part{m}"))
        copies.finish()

    half = ((D // 2, PACK), BF)
    ins = {"scal": (scal, pltpu.SMEM), **any_inputs(keep=keep, got=got)}
    outs = {f"part{m}": ((size, PACK), BF, pl.ANY) for m in range(groups)}
    return list(call(body, ins, outs, {"a": half, "b": half}, sems=2 + groups).values())


def join(own, others, last):
    size = own.shape[0]
    count = last.shape[0]
    parts = [own] + list(others)

    def body(r):
        copies = Copies(r.sems)
        loads = [copies.start(r.last, r.last_parts)]
        loads += [copies.start(getattr(r, f"p{n}"), r.parts.at[n]) for n in range(len(parts))]
        for copy in loads:
            copy.wait()
        for at, held, number in ((PACK, r.last_parts, count), (0, r.parts, len(parts))):
            total = held[0].astype(F32)
            for n in range(1, number):
                total = total + held[n].astype(F32)
            r.out[:, at : at + PACK] = total.astype(BF)
        copies.out(r.out, r.all_out)
        copies.finish()

    ins = any_inputs(**{f"p{n}": p for n, p in enumerate(parts)}, last=last)
    scratch = {
        "parts": ((len(parts), size, PACK), BF), "last_parts": ((count, size, PACK), BF), "out": ((size, 2 * PACK), BF)
    }
    return call(body, ins, {"all_out": ((size, 2 * PACK), BF, pl.ANY)}, scratch, sems=len(parts) + 2)["all_out"]


def put_row(copies, held, out, row):
    for half in range(2):
        for start, _, own_first, count in CELLS:
            copies.out(held.at[half, pl.ds(own_first, count)], out.at[0, row, pl.ds(start + half * count, count)])


def finish_outputs(scal, low, high, own_low, own_high, cotangent, params):
    def body(r):
        section, core = r.scal[4], r.scal[0]
        copies = Copies(r.sems)
        here_high = (section == 3) & (core == 1)
        at00, at01 = ((section == s) & (core == 0) for s in (0, 1))
        at10, at11 = ((section == s) & (core == 1) for s in (0, 1))
        loads = [
            copies.choose(
                [(at00, r.own_low), (at01 | at10, r.low0), (at11, r.low1), (section >= 2, r.high0)], r.held.at[0]
            ),
            copies.choose(
                [
                    (at00 | at01 | at10, r.low1), (at11, r.low2),
                    ((section >= 2) & jnp.logical_not(here_high), r.high1), (here_high, r.own_high),
                ],
                r.held.at[1],
            ),
        ]
        for copy in loads:
            copy.wait()

        @pl.when(section < 3)
        def _():
            rest = Copies(r.sems)
            rest.used = copies.used
            for row in range(2):
                put_row(rest, r.held.at[row], r.out, row)
            rest.finish()

        @pl.when(section == 3)
        def _():
            rest = Copies(r.sems)
            rest.used = copies.used
            loads = start_params(rest, r)
            loads.append(rest.start(r.ff_in_in.at[1], r.w_up))
            loads.append(rest.start(r.ff_out_in.at[1], r.w_down))
            for row in range(2):
                for half in range(2):
                    for start, _, own_first, count in CELLS:
                        src = r.cot.at[row, pl.ds(start + half * count, count)]
                        loads.append(rest.start(src, r.g.at[row, half, pl.ds(own_first, count)]))
            for copy in loads:
                copy.wait()

            def step(n, carry):
                row, half = n // 2, n % 2
                for at in range(0, OWN, 256):
                    rows = slice(at, at + 256)
                    even = r.held[row, half, rows, :]
                    pre = nn(even, r.w_up[...]) + param_row(r.ff_bias_in, 1)
                    cdf = 0.5 + 0.5 * lax.erf(pre * 0.7071067811865476)
                    hidden = (pre * cdf).astype(BF)
                    gp = cdf + pre * (0.3989422804014327 * jnp.exp(-0.5 * pre * pre))
                    res = even.astype(F32) + nn(hidden, r.w_down[...]) + param_row(r.ff_bias_out, 1)
                    normed, inv = norm_rows(res)
                    gain = param_row(r.norm_gain, 1, 1)
                    r.held[row, half, rows, :] = (normed * gain + param_row(r.norm_shift, 1, 1)).astype(BF)
                    dres = norm_back(r.g[row, half, rows, :].astype(F32), normed, inv, gain)
                    dp = (nt(dres.astype(BF), r.w_down[...]) * gp).astype(BF)
                    r.g[row, half, rows, :] = (dres + nt(dp, r.w_up[...])).astype(BF)
                return carry

            lax.fori_loop(0, 4, step, 0)
            for row in range(2):
                put_row(rest, r.held.at[row], r.out, row)
                put_row(rest, r.g.at[row], r.grads, row)
            rest.finish()

    ins = {"scal": (scal, pltpu.SMEM), **param_inputs(params)}
    ins.update(any_inputs(low0=low[0], low1=low[1], low2=low[2], high0=high[0], high1=high[1], cot=cotangent))
    ins.update(any_inputs(own_low=own_low, own_high=own_high))
    whole = ((1, 2, ROW, D), BF, pl.ANY)
    scratch = {"held": ((2, 2, OWN, D), BF), "g": ((2, 2, OWN, D), BF), **param_buffers()}
    out = call(body, ins, {"out": whole, "grads": whole}, scratch, sems=48)
    return out["out"], out["grads"]


def finish_grads(scal, first, own_first, second, third, last):
    def body(r):
        section, core = r.scal[4], r.scal[0]
        copies = Copies(r.sems)
        here = (section == 0) & (core == 0)
        loads = []
        for row in range(2):
            other = [(section == 1, f"b{row}"), (section > 1, f"c{row}")]
            for n, (_, _, at, count) in enumerate(CELLS):
                tokens = pl.ds(at, count)
                cases = [(holds, getattr(r, name).at[:, tokens]) for holds, name in other]
                got = getattr(r, f"a{row}_{n}")
                if row == 0:
                    cases.append((here, getattr(r, f"own{n}")))
                    cases.append(((section == 0) & jnp.logical_not(here), got))
                else:
                    cases.append((section == 0, got))
                loads.append(copies.choose(cases, r.held.at[row, :, tokens]))
        for copy in loads:
            copy.wait()

        @pl.when(section < 3)
        def _():
            rest = Copies(r.sems)
            rest.used = copies.used
            for row in range(2):
                put_row(rest, r.held.at[row], r.out, row)
            rest.finish()

    ins = {"scal": (scal, pltpu.SMEM)}
    ins.update(any_inputs(b0=second[0], b1=second[1], c0=third[0], c1=third[1], last=last))
    for n in range(len(CELLS)):
        ins.update(any_inputs(**{f"a0_{n}": first[n][0], f"a1_{n}": first[n][1], f"own{n}": own_first[n]}))
    whole = ((1, 2, ROW, D), BF, pl.ANY)
    return call(body, ins, {"out": whole}, {"held": ((2, 2, OWN, D), BF)}, {"last": "out"}, 16)["out"]


def unpack(got):
    count, size, width = got.shape
    wide = ((2, size, 3 * D), F32, pltpu.VMEM)
    square = ((2, size, D), F32, pltpu.VMEM)
    vec = ((2, size), F32, pltpu.VMEM)
    pair = ((2, 2, size), F32, pltpu.VMEM)
    outs = dict(
        proj=wide, out=square, qb=vec, vb=vec, ob=vec, up=square, down=square, ub=vec, db=vec, gain=pair, shift=pair
    )

    def body(r):
        pltpu.sync_copy(r.got, r.held)
        total = r.held[0].astype(F32)
        for n in range(1, count):
            total = total + r.held[n].astype(F32)
        for layer in range(2):
            base = layer * PACK
            ff = total[:, base : base + FF_PACK]
            att = total[:, base + FF_PACK : base + FF_PACK + ATT_PACK]
            r.up[layer] = ff[:, :D]
            r.down[layer] = ff[:, D : 2 * D]
            r.proj[layer] = att[:, : 3 * D]
            r.out[layer] = att[:, 3 * D : 4 * D]
            cols = ff[:, 2 * D :].T
            for ref, k in ((r.ob, 0), (r.ub, 3), (r.db, 4)):
                ref[layer : layer + 1, :] = cols[k : k + 1, :]
            for kind in range(2):
                r.gain[layer, kind : kind + 1, :] = cols[4 * kind + 1 : 4 * kind + 2, :]
                r.shift[layer, kind : kind + 1, :] = cols[4 * kind + 2 : 4 * kind + 3, :]
            cols = att[:, 4 * D :].T
            for ref, k in ((r.qb, 0), (r.vb, 1)):
                ref[layer : layer + 1, :] = cols[k : k + 1, :]

    scratch = {"held": ((count, size, width), BF)}
    return list(call(body, any_inputs(got=got), outs, scratch, sems=1).values())


def make_per_device(dp_count, section_count):
    both = ("dp", "section")

    def index(dp, section):
        return dp * section_count + section

    everyone = [(d, s) for d in range(dp_count) for s in range(section_count)]
    mate_pairs = [(index(d, s), index(d ^ 1, s)) for d, s in everyone]
    fetch_pairs = [(index(d, s), index(d ^ 1, s)) for d, s in everyone if d % 2 == s // 2]

    def send(rows, moves):
        pairs = []
        for d, z in everyone:
            to = moves.get((d % 2, z))
            if to is not None and index(d - d % 2 + z // 2, to) != index(d, z):
                pairs.append((index(d, z), index(d - d % 2 + z // 2, to)))
        return lax.ppermute(rows, both, pairs)

    def ship(rows, sections):
        return [
            send(rows, {(c, z): to for c, to in enumerate(sections) if to is not None for z in (odd, 2 + odd)})
            for odd in range(2)
        ]

    def mate(x):
        return lax.ppermute(x, both, mate_pairs)

    def after(value, *earlier):
        return lax.optimization_barrier((value, earlier))[0]

    def per_device(
        block_input, known_genes, attn_proj, attn_out, query_bias, value_bias, out_bias, ff_in, ff_out,
        ff_bias_in, ff_bias_out, norm_gain, norm_shift, cotangent,
    ):
        params = dict(
            attn_proj=attn_proj, attn_out=attn_out, query_bias=query_bias, value_bias=value_bias, out_bias=out_bias,
            ff_in=ff_in, ff_out=ff_out, ff_bias_in=ff_bias_in, ff_bias_out=ff_bias_out, norm_gain=norm_gain,
            norm_shift=norm_shift,
        )
        dp = lax.axis_index("dp")
        core = dp % 2
        section = lax.axis_index("section")
        mine = (core == section // 2).astype(jnp.int32)
        scal = jnp.stack([core, mine, section % 2, 2 * (section % 2) + core, section, dp // 2]).astype(jnp.int32)

        known_there = lax.ppermute(known_genes, both, fetch_pairs)
        x_there = lax.ppermute(block_input, both, fetch_pairs)
        x_in = any_inputs(x_here=block_input, x_there=x_there)
        f0 = forward_layer(0, scal, params, {**x_in, **any_inputs(known_here=known_genes, known_there=known_there)})
        rank = f0["rank_out"]
        x_own = f0["pair_out"]
        x_oth = mate(x_own)

        def other_half(rows, half):
            return lax.dynamic_update_index_in_dim(rows, half, 1 - core, 0)

        c_there = lax.ppermute(after(cotangent, x_own), both, fetch_pairs)
        missing = lax.dynamic_index_in_dim(x_oth, core, 0, keepdims=False)
        low_rows = other_half(f0["ship_out"], missing)
        got_low = [
            send(low_rows, {(0, 2): 0, (1, 0): 1}),
            send(low_rows, {(1, 2): 1, (1, 1): 1, (0, 3): 0, (0, 1): 0}),
            send(low_rows, {(1, 3): 1}),
        ]
        f1 = forward_layer(1, scal, params, any_inputs(x_own=x_own, x_oth=x_oth, rank_in=rank))
        high_rows = other_half(f1["ship_out"], mate(f1["pair_out"][0]))
        got_high = ship(high_rows, (2, 3))
        b1 = backward_last(after(scal, got_low[0]), params, f1, any_inputs(c_here=cotangent, c_there=c_there, x_own=x_own), rank)
        wide = lax.all_to_all(b1["pack_out"].reshape(dp_count, -1, PACK), "dp", 0, 0)
        ins = any_inputs(dx_own=b1["dx_own_out"], dx_oth=mate(b1["dx_oth_out"]))
        b0 = backward_first_ff(after(scal, got_high[0]), params, f0, ins)
        grad_rows = other_half(b0["ship_out"], mate(after(b0["give_out"], got_low[1:])))
        got_third = ship(grad_rows, (2, None))
        got_second = ship(grad_rows, (None, 1))
        ins = {**x_in, **any_inputs(db0_in=b0["db0_out"], dr_in=b0["dr_out"], ff_in=b0["pack_out"])}
        to_first = [(index(d, s), index(d - 1, s)) for d, s in everyone if d % 2]

        def first_rows(dx, *earlier):
            theirs = lax.ppermute(after(dx, *earlier), both, to_first)
            return (dx.astype(F32) + theirs.astype(F32)).astype(BF)

        last = backward_first_att(after(scal, grad_rows), params, f0, ins, rank, dp_count, 0)
        own_first = [first_rows(last["dx_out"], got_second, got_high[1])]
        got_first = [ship(own_first[0], (0, None))]
        ins.update(any_inputs(prev_in=last["pack_out"]))
        last = backward_first_att(after(scal, own_first[0]), params, f0, ins, rank, dp_count, 1)
        own_first.append(first_rows(last["dx_out"], got_first[0][0]))
        got_first.append(ship(own_first[1], (0, None)))
        groups = dp_count // 2
        parts = add_and_split(after(scal, own_first[1]), last["keep_out"], mate(last["send_out"]), groups)
        others = []
        for m in range(1, groups):
            pairs = [(index(d, s), index(d ^ (2 * m), s)) for d, s in everyone]
            others.append(lax.ppermute(parts[m], both, pairs))
        held = join(after(parts[0], got_first), others, wide)
        got = lax.all_to_all(held.reshape(section_count, -1, held.shape[1]), "section", 0, 0)
        grads = unpack(got)
        section_outputs, last_grads = finish_outputs(scal, got_low, got_high, low_rows, high_rows, cotangent, params)
        section_grads = finish_grads(scal, got_first, own_first, got_second, got_third, last_grads)
        return (section_outputs, section_grads, *grads)

    return per_device


def solution(mesh):
    rows = P("dp", None, None)
    placed = (rows, P("dp", None)) + (P(),) * 11 + (rows,)
    sections = P("section", "dp", None, None)
    matrix = P(None, ("dp", "section"), None)
    vector = P(None, ("dp", "section"))
    pairs = P(None, None, ("dp", "section"))
    return jax.shard_map(
        make_per_device(mesh.shape["dp"], mesh.shape["section"]),
        mesh=mesh,
        in_specs=placed,
        out_specs=(
            sections, sections, matrix, matrix, vector, vector, vector, matrix, matrix, vector, vector, pairs, pairs,
        ),
        check_vma=False,
    )
```

```python
from types import SimpleNamespace

import jax
import jax.numpy as jnp
from jax import lax
from jax.experimental import pallas as pl
from jax.experimental.pallas import tpu as pltpu
from jax.sharding import PartitionSpec as P

D = 512
HEADS = 8
HEAD_DIM = 64
LONG = 1024
SHORT = 512
ROW = LONG + SHORT
EPS = 1e-05
FILL = -1e30
SCALE = HEAD_DIM ** (-0.5)
LOG2E = 1.4426950408889634
LN2 = 0.6931471805599453
SOFT = SCALE * LOG2E
BF = jnp.bfloat16
F32 = jnp.float32
VAUG = HEAD_DIM + 16
ATT_PACK = 4 * D + 128
FF_PACK = 2 * D + 128
PACK = ATT_PACK + FF_PACK
OWN = ROW // 2
CELLS = ((0, LONG, 0, LONG // 2), (LONG, SHORT, LONG // 2, SHORT // 2))
SMALLEST, LARGEST = 2.0 ** -60, 2.0 ** 90
VMEM_LIMIT = 63 * 1024 * 1024
LAYER_PARAMS = (
    "attn_proj", "attn_out", "ff_in", "ff_out",
    "query_bias", "value_bias", "out_bias", "ff_bias_in", "ff_bias_out", "norm_gain", "norm_shift",
)
MATRICES = LAYER_PARAMS[:4]


def nn(a, b):
    return lax.dot_general(a, b, (((1,), (0,)), ((), ())), preferred_element_type=F32)


def nt(a, b):
    return lax.dot_general(a, b, (((1,), (1,)), ((), ())), preferred_element_type=F32)


def tn(a, b):
    return lax.dot_general(a, b, (((0,), (0,)), ((), ())), preferred_element_type=F32)


def call(body, ins, outs, scratch, aliases=None, sems=48, micros=0.001):
    names = list(ins) + list(outs) + list(scratch) + ["sems"]

    def kernel(*refs):
        body(SimpleNamespace(**dict(zip(names, refs))))

    in_names, out_names = list(ins), list(outs)
    result = pl.pallas_call(
        kernel,
        in_specs=[pl.BlockSpec(memory_space=space) for _, space in ins.values()],
        out_specs=[pl.BlockSpec(memory_space=space) for _, _, space in outs.values()],
        out_shape=[jax.ShapeDtypeStruct(shape, dtype) for shape, dtype, _ in outs.values()],
        scratch_shapes=[pltpu.VMEM(shape, dtype) for shape, dtype in scratch.values()] + [pltpu.SemaphoreType.DMA((sems,))],
        input_output_aliases={in_names.index(a): out_names.index(b) for a, b in (aliases or {}).items()},
        compiler_params=pltpu.CompilerParams(vmem_limit_bytes=VMEM_LIMIT),
        cost_estimate=pl.CostEstimate(flops=int(micros * 1150000000), bytes_accessed=2**12, transcendentals=0),
    )(*[array for array, _ in ins.values()])
    return dict(zip(out_names, result))


class Copies:
    def __init__(self, sems):
        self.sems, self.used, self.ends = sems, 0, []

    def start(self, src, dst):
        copy = pltpu.make_async_copy(src, dst, self.sems.at[self.used])
        self.used += 1
        copy.start()
        return copy

    def either(self, first, src_a, src_b, dst, out=False):
        sem = self.sems.at[self.used]
        self.used += 1
        pl.when(first)(lambda: pltpu.make_async_copy(src_a, dst, sem).start())
        pl.when(jnp.logical_not(first))(lambda: pltpu.make_async_copy(src_b, dst, sem).start())
        copy = pltpu.make_async_copy(src_a, dst, sem)
        if out:
            self.ends.append(copy)
        return copy

    def choose(self, cases, dst):
        sem = self.sems.at[self.used]
        self.used += 1
        for holds, src in cases:
            pl.when(holds)(lambda src=src: pltpu.make_async_copy(src, dst, sem).start())
        return pltpu.make_async_copy(cases[0][1], dst, sem)

    def out(self, src, dst):
        self.ends.append(self.start(src, dst))

    def finish(self):
        for copy in self.ends:
            copy.wait()


def norm_rows(residual):
    center = residual - jnp.mean(residual, axis=-1, keepdims=True)
    inv_std = lax.rsqrt(jnp.mean(center * center, axis=-1, keepdims=True) + EPS)
    return center * inv_std, inv_std


def norm_back(grad, normed, inv, gain):
    e = grad * gain
    return inv * (
        e - jnp.mean(e, axis=-1, keepdims=True) - normed * jnp.mean(e * normed, axis=-1, keepdims=True)
    )


def one_hot_rows(rank_row, size, length):
    return (lax.broadcasted_iota(jnp.int32, (size, length), 0) == rank_row).astype(F32).astype(BF)


def one_hot_cols(rank_col, size):
    length = rank_col.shape[0]
    return (lax.broadcasted_iota(jnp.int32, (length, size), 1) == rank_col).astype(F32).astype(BF)


def put_masked(dst, src, tokens):
    zeros = jnp.zeros((HEAD_DIM, tokens), BF)
    for head in range(HEADS):
        part = (head % 2) * HEAD_DIM
        dst[head, part : part + HEAD_DIM, :] = src[head * HEAD_DIM : (head + 1) * HEAD_DIM, :]
        dst[head, HEAD_DIM - part : 2 * HEAD_DIM - part, :] = zeros


def head_sums(a, b):
    out = []
    for head in range(HEADS):
        rows = slice(head * HEAD_DIM, (head + 1) * HEAD_DIM)
        out.append(jnp.sum(a[rows, :].astype(F32) * b[rows, :].astype(F32), axis=0, keepdims=True))
    return out


def rank_tokens(known, length):
    upto = lax.broadcasted_iota(jnp.int32, (length, length), 0) <= lax.broadcasted_iota(jnp.int32, (length, length), 1)
    low = jnp.broadcast_to(known.astype(F32), (8, length))
    place = nn(low.astype(BF), upto.astype(F32).astype(BF))
    return jnp.where(low > 0.5, place - 1.0, -1.0).astype(jnp.int32)


def small_count(length):
    return length // 2 + length // 8


def param_row(ref, layer, kind=None):
    return ref[pl.ds(layer, 1), :] if kind is None else ref[layer, pl.ds(kind, 1), :]


def key_rows(quick):
    sizes = [small_count(length) if quick else length for _, length, _, _ in CELLS]
    return ((0, sizes[0]), (sizes[0], sizes[1])), sum(sizes)


def split_rank(r):
    ranks = [r.rank[:, start : start + length] for start, length, _, _ in CELLS]
    return ranks, [jnp.max(rank[0:1, :]) + 1 for rank in ranks]


def units():
    out = []
    for cell, (_, _, first, count) in enumerate(CELLS):
        for at in range(first, first + count, 256):
            out.append((cell, slice(at, at + 256)))
    return out


def small_counts(counts):
    ok = counts[0] <= small_count(CELLS[0][1])
    for count, (_, length, _, _) in zip(counts[1:], CELLS[1:]):
        ok = ok & (count <= small_count(length))
    return ok


def put_key_bias(r, rows, counts):
    for (first, size), count in zip(rows, counts):
        inside = lax.broadcasted_iota(jnp.int32, (size, 128), 0) < count
        r.kb[first : first + size, :] = jnp.where(inside, 0.0, FILL)


def own_rows_of(core, other=False):
    place = 1 - core if other else core
    return [pl.ds(pl.multiple_of(start + place * count, count), count) for start, _, _, count in CELLS]


def forward_body(r, layer):
    core = r.scal[0]
    copies = Copies(r.sems)
    mine, slot = r.scal[1] == 1, r.scal[2]
    if layer == 0:
        known_in = copies.either(mine, r.known_here, r.known_there, r.known)
        u_in = []
        for buffer, other in ((r.u_own, False), (r.u_oth, True)):
            for rows, (_, _, first, count) in zip(own_rows_of(core, other), CELLS):
                u_in.append(
                    copies.either(
                        mine, r.x_here.at[slot, rows], r.x_there.at[slot, rows], buffer.at[pl.ds(first, count)]
                    )
                )
        u_own_in, u_oth_in = u_in[:2], u_in[2:]
    else:
        rank_in = copies.start(r.rank_in, r.rank)
        u_own_in, u_oth_in = [copies.start(r.x_own.at[1], r.u_own)], [copies.start(r.x_oth.at[1], r.u_oth)]
    w_in = copies.start(r.attn_proj_in.at[layer], r.w)
    small = start_params(copies, r)
    late = [
        copies.start(r.attn_out_in.at[layer], r.w_mix),
        copies.start(r.ff_in_in.at[layer], r.w_up),
        copies.start(r.ff_out_in.at[layer], r.w_down),
    ]

    def save(*names):
        for name in names:
            copies.out(getattr(r, name), getattr(r, name + "_out"))

    if layer == 0:
        known_in.wait()
        for start, length, _, count in CELLS:
            known = r.known[pl.ds(slot, 1), :][:, start : start + length]
            first, second = known[:, :count], known[:, count:]
            known = jnp.concatenate([jnp.where(core == 0, first, second), jnp.where(core == 0, second, first)], axis=1)
            r.rank[:, start : start + length] = rank_tokens(known, length)
        save("rank")
    else:
        rank_in.wait()
    ranks, counts = split_rank(r)
    for copy in small + u_own_in:
        copy.wait()
    w_in.wait()
    own = nn(r.u_own[...], r.w[...])
    r.q_t[...] = (own[:, :D] + param_row(r.query_bias, layer)).astype(BF).T
    r.ko_t[...] = (own[:, D : 2 * D] * SOFT).astype(BF).T
    r.vo_t[...] = (own[:, 2 * D :] + param_row(r.value_bias, layer)).astype(BF).T
    save("q_t", "ko_t", "vo_t")
    put_masked(r.qm, r.q_t, OWN)
    unk = jnp.concatenate(
        [jnp.where(rank[0:1, :count] >= 0, FILL, 0.0) for rank, (_, _, _, count) in zip(ranks, CELLS)], axis=1
    )
    for head, row in enumerate(head_sums(r.q_t, r.ko_t)):
        r.sd[head] = row + unk
        r.total[head] = jnp.zeros_like(row)
        r.top[head] = jnp.zeros_like(row)
    for copy in u_oth_in:
        copy.wait()

    def keys(quick):
        rows, total = key_rows(quick)
        for rank, (_, length, own_first, count), (first, size) in zip(ranks, CELLS, rows):
            pick = one_hot_rows(rank[0:1, :], size, length)
            tokens = slice(own_first, own_first + count)
            uc = nn(pick[:, :count], r.u_own[tokens, :]) + nn(pick[:, count:], r.u_oth[tokens, :])
            r.uc[first : first + size, :] = uc.astype(BF)
        kv = nn(r.uc[:total, :], r.w[:, D:])
        r.k_c[:total, :] = (kv[:, :D] * SOFT).astype(BF)
        ones = []
        for (first, size), known in zip(rows, counts):
            inside = lax.broadcasted_iota(jnp.int32, (size, D), 0) < known
            vc = kv[first : first + size, D:] + param_row(r.value_bias, layer)
            r.v_c[first : first + size, :] = jnp.where(inside, vc, 0.0).astype(BF)
            lane = lax.broadcasted_iota(jnp.int32, (16, size), 1)
            ones.append(((lane < known) & (lax.broadcasted_iota(jnp.int32, (16, size), 0) == 0)).astype(F32))
        vct = r.v_c[:total, :].T
        ones = jnp.concatenate(ones, axis=1).astype(BF)
        for head in range(HEADS):
            r.vaug[head * VAUG : head * VAUG + HEAD_DIM, :total] = vct[head * HEAD_DIM : (head + 1) * HEAD_DIM, :]
            r.vaug[head * VAUG + HEAD_DIM : (head + 1) * VAUG, :total] = ones

    def attend(quick):
        rows_of, _ = key_rows(quick)
        if not quick:
            put_key_bias(r, rows_of, counts)

        def pair(p, carry):
            lanes = pl.ds(pl.multiple_of(p * 128, 128), 128)
            for e in range(2):
                head = 2 * p + e
                feats = pl.ds(pl.multiple_of(head * HEAD_DIM, HEAD_DIM), HEAD_DIM)
                for cell, cols in units():
                    keys_at = slice(rows_of[cell][0], rows_of[cell][0] + rows_of[cell][1])
                    vrows = r.vaug[pl.ds(pl.multiple_of(head * VAUG, 16), VAUG), keys_at]
                    scores = nn(r.k_c[keys_at, lanes], r.qm[head, :, cols])
                    own_score = r.sd[head, :, cols]
                    if quick:
                        low = jnp.exp2(scores).astype(BF)
                    else:
                        tops, probs = [], []
                        for t in range(0, 256, 128):
                            part = scores[:, t : t + 128] + r.kb[keys_at, :]
                            top = jnp.maximum(jnp.max(part, axis=0, keepdims=True), own_score[:, t : t + 128])
                            tops.append(top)
                            probs.append(jnp.exp2(part - top).astype(BF))
                        top = jnp.concatenate(tops, axis=1)
                        low = jnp.concatenate(probs, axis=1)
                        r.top[head, :, cols] = top
                        own_score = own_score - top
                    mixed = nn(vrows, low)
                    own_prob = jnp.exp2(own_score)
                    total = mixed[HEAD_DIM : HEAD_DIM + 1] + own_prob
                    r.total[head, :, cols] = total
                    mixed = mixed[:HEAD_DIM] + own_prob * r.vo_t[feats, cols].astype(F32)
                    r.mix_t[feats, cols] = (mixed * (1.0 / total)).astype(BF)
            return carry

        lax.fori_loop(0, HEADS // 2, pair, 0)

    def run(quick):
        keys(quick)
        attend(quick)

    pl.when(small_counts(counts))(lambda: run(True))
    totals = r.total[...]
    fine = jnp.min(jnp.where((totals > SMALLEST) & (totals < LARGEST), 1, 0)) == 1
    pl.when(jnp.logical_not(fine))(lambda: run(False))
    save("uc", "k_c", "v_c", "mix_t", "top", "total")
    for copy in late:
        copy.wait()

    for at in range(0, OWN, 256):
        rows = slice(at, at + 256)
        res = r.u_own[rows, :].astype(F32) + tn(r.mix_t[:, rows], r.w_mix[...]) + param_row(r.out_bias, layer)
        normed, inv0 = norm_rows(res)
        r.nrm0[rows, :] = normed.astype(BF)
        even = (normed * param_row(r.norm_gain, layer, 0) + param_row(r.norm_shift, layer, 0)).astype(BF)
        r.even[rows, :] = even
        pre = nn(even, r.w_up[...]) + param_row(r.ff_bias_in, layer)
        cdf = 0.5 + 0.5 * lax.erf(pre * 0.7071067811865476)
        hidden = (pre * cdf).astype(BF)
        r.hid[rows, :] = hidden
        r.gp[rows, :] = (cdf + pre * (0.3989422804014327 * jnp.exp(-0.5 * pre * pre))).astype(BF)
        res = even.astype(F32) + nn(hidden, r.w_down[...]) + param_row(r.ff_bias_out, layer)
        normed, inv1 = norm_rows(res)
        r.nrm1[rows, :] = normed.astype(BF)
        r.odd[rows, :] = (normed * param_row(r.norm_gain, layer, 1) + param_row(r.norm_shift, layer, 1)).astype(BF)
        r.inv[rows, :] = jnp.where(lax.broadcasted_iota(jnp.int32, (256, 128), 1) == 0, inv0, inv1)

    copies.out(r.even, r.pair_out.at[0])
    copies.out(r.odd, r.pair_out.at[1])
    if layer == 0:
        copies.either(core == 0, r.even, r.odd, r.ship_out.at[core], True)
    else:
        copies.out(r.even, r.ship_out.at[core])
    save("nrm0", "nrm1", "gp", "hid", "inv")
    copies.finish()


TOK = ((OWN, D), BF)
FEAT = ((D, OWN), BF)
KEYS = ((ROW, D), BF)
HEAD_ROWS = ((HEADS, 1, OWN), F32)
RANK = ((8, ROW), jnp.int32)
SAVED = dict(
    even=TOK, q_t=FEAT, ko_t=FEAT, vo_t=FEAT, uc=KEYS, k_c=KEYS, v_c=KEYS, mix_t=FEAT, nrm0=TOK, nrm1=TOK, gp=TOK, hid=TOK,
    inv=((OWN, 128), F32), top=HEAD_ROWS, total=HEAD_ROWS,
)
FF_SAVED = ("nrm1", "inv", "gp", "nrm0", "hid", "even")
ATT_SAVED = ("mix_t", "q_t", "k_c", "v_c", "top", "total", "ko_t", "vo_t", "uc")
BOTH = ((2, OWN, D), BF)


def weight_buffers():
    square = ((D, D), BF)
    return dict(w=((D, 3 * D), BF), w_mix=square, w_up=square, w_down=square)


def param_inputs(params):
    return {name + "_in": (params[name], pl.ANY) for name in LAYER_PARAMS}


def param_buffers():
    pairs = {name: ((2, 2, D) if name.startswith("norm") else (2, D), F32) for name in LAYER_PARAMS[4:]}
    return {**pairs, **weight_buffers()}


def start_params(copies, r):
    return [copies.start(getattr(r, name + "_in"), getattr(r, name)) for name in LAYER_PARAMS[4:]]


def any_inputs(**arrays):
    return {name: (array, pl.ANY) for name, array in arrays.items()}


def forward_layer(layer, scal, params, inputs):
    ins = {"scal": (scal, pltpu.SMEM), **param_inputs(params), **inputs}
    outs = {name + "_out": (*spec, pl.ANY) for name, spec in SAVED.items() if name != "even"}
    outs.update(pair_out=(*BOTH, pl.ANY), ship_out=(*BOTH, pl.ANY))
    scratch = {
        **SAVED, **param_buffers(), "u_own": TOK, "u_oth": TOK, "odd": TOK, "rank": RANK, "qm": ((HEADS, 128, OWN), BF),
        "vaug": ((HEADS * VAUG, ROW), BF), "kb": ((ROW, 128), F32), "sd": HEAD_ROWS,
    }
    if layer == 0:
        outs["rank_out"] = (*RANK, pl.ANY)
        scratch["known"] = ((2, ROW), jnp.int32)
    return call(lambda r: forward_body(r, layer), ins, outs, scratch, micros=20)


def ff_back(r, layer, need):
    sums = [jnp.zeros((1, D), F32) for _ in range(7)]

    def add(slot, value):
        sums[slot] = sums[slot] + jnp.sum(value, axis=0, keepdims=True)

    need("g", "nrm1", "inv", "w_down", "w_up", "gp", "nrm0")
    for at in range(0, OWN, 256):
        rows = slice(at, at + 256)
        if layer == 1:
            grad = r.g[rows, :].astype(F32)
        else:
            low = (r.dx[rows, :] + r.g[rows, :].astype(F32)).astype(BF)
            r.g[rows, :] = low
            grad = low.astype(F32)
        normed = r.nrm1[rows, :].astype(F32)
        add(5, grad * normed)
        add(6, grad)
        dres = norm_back(grad, normed, r.inv[rows, 1:2], param_row(r.norm_gain, layer, 1))
        add(4, dres)
        low = dres.astype(BF)
        r.db1[rows, :] = low
        dp = nt(low, r.w_down[...]) * r.gp[rows, :].astype(F32)
        add(3, dp)
        low = dp.astype(BF)
        r.dpre[rows, :] = low
        low = (dres + nt(low, r.w_up[...])).astype(BF)
        r.g_odd[rows, :] = low
        grad = low.astype(F32)
        normed = r.nrm0[rows, :].astype(F32)
        add(1, grad * normed)
        add(2, grad)
        dres = norm_back(grad, normed, r.inv[rows, 0:1], param_row(r.norm_gain, layer, 0))
        add(0, dres)
        r.dr[rows, :] = dres
        r.db0[rows, :] = dres.astype(BF)
    vectors = jnp.concatenate(sums + [jnp.zeros((121, D), F32)], axis=0)
    r.ff_pack[:, 2 * D :] = vectors.T.astype(BF)


def ff_weights(r, need):
    need("hid", "even")
    r.ff_pack[:, :D] = tn(r.even[...], r.dpre[...]).astype(BF)
    r.ff_pack[:, D : 2 * D] = tn(r.hid[...], r.db1[...]).astype(BF)


def attention_back(r, layer, copies, need):
    core = r.scal[0]
    need("w_mix", "mix_t")
    dm_t = nt(r.w_mix[...], r.db0[...]).astype(BF)
    r.dm_t[...] = dm_t
    dm_sum = jnp.sum(dm_t.astype(F32), axis=1, keepdims=True)
    need("q_t", "top", "total", "ko_t", "vo_t")
    put_masked(r.qm, r.q_t, OWN)
    zeros = jnp.zeros((HEAD_DIM, OWN), BF)
    deltas = head_sums(r.dm_t, r.mix_t)
    for head in range(HEADS):
        rows = slice(head * HEAD_DIM, (head + 1) * HEAD_DIM)
        part = (head % 2) * HEAD_DIM
        inv_total = 1.0 / r.total[head]
        r.total[head] = inv_total
        r.delta[head] = deltas[head] * inv_total
        r.dmm[head, part : part + HEAD_DIM, :] = (r.dm_t[rows, :].astype(F32) * inv_total).astype(BF)
        r.dmm[head, HEAD_DIM - part : 2 * HEAD_DIM - part, :] = zeros
    need("k_c", "v_c", "uc", "w", "rank")
    ranks, counts = split_rank(r)
    quick_ok = small_counts(counts) & (jnp.max(jnp.abs(r.top[...])) == 0.0)

    def run(quick):
        rows_of, total = key_rows(quick)
        r.kc_t[:, :total] = r.k_c[:total, :].T
        if not quick:
            put_key_bias(r, rows_of, counts)

        def pair(p, carry):
            lanes = pl.ds(pl.multiple_of(p * 128, 128), 128)
            late_lanes = pl.ds(pl.multiple_of(D + p * 128, 128), 128)
            dk = [jnp.zeros((size, 128), F32) for _, size in rows_of]
            dv = [jnp.zeros((size, 128), F32) for _, size in rows_of]
            for e in range(2):
                head = 2 * p + e
                feats = pl.ds(pl.multiple_of(head * HEAD_DIM, HEAD_DIM), HEAD_DIM)
                for cell, cols in units():
                    keys_at = slice(rows_of[cell][0], rows_of[cell][0] + rows_of[cell][1])
                    qtm = r.qm[head, :, cols]
                    dmh = r.dmm[head, :, cols]
                    scores = nn(r.k_c[keys_at, lanes], qtm)
                    dprob = nn(r.v_c[keys_at, lanes], dmh)
                    delta = r.delta[head, :, cols]
                    if quick:
                        prob = jnp.exp2(scores)
                        low = prob.astype(BF)
                        ds = (prob * (dprob - delta)).astype(BF)
                    else:
                        top = r.top[head, :, cols]
                        lows, grads = [], []
                        for t in range(0, 256, 128):
                            tile = slice(t, t + 128)
                            prob = jnp.exp2(jnp.minimum(scores[:, tile] - top[:, tile], r.kb[keys_at, :]))
                            lows.append(prob.astype(BF))
                            grads.append((prob * (dprob[:, tile] - delta[:, tile])).astype(BF))
                        low = jnp.concatenate(lows, axis=1)
                        ds = jnp.concatenate(grads, axis=1)
                    dv[cell] = dv[cell] + nt(low, dmh)
                    dk[cell] = dk[cell] + nt(ds, qtm)
                    r.dq_t[feats, cols] = nn(r.kc_t[feats, keys_at], ds) * LN2
            for cell, (first, size) in enumerate(rows_of):
                r.dkv[first : first + size, lanes] = (dk[cell] * SCALE).astype(BF)
                r.dkv[first : first + size, late_lanes] = dv[cell].astype(BF)
            return carry

        lax.fori_loop(0, HEADS // 2, pair, 0)
        dkv = r.dkv[:total, :]
        r.dw_kv[...] = tn(r.uc[:total, :], dkv)
        dxc = nt(dkv, r.w[:, D:]).astype(BF)
        for rank, (_, _, own_first, count), (first, size) in zip(ranks, CELLS, rows_of):
            rank_col = rank.astype(F32).T[:, 0:1].astype(jnp.int32)
            tokens = slice(own_first, own_first + count)
            part = dxc[first : first + size, :]
            r.dr[tokens, :] += nn(one_hot_cols(rank_col[:count, :], size), part)
            r.dxo[tokens, :] = nn(one_hot_cols(rank_col[count:, :], size), part).astype(BF)

    pl.when(quick_ok)(lambda: run(True))
    pl.when(jnp.logical_not(quick_ok))(lambda: run(False))
    if layer == 1:
        copies.out(r.dxo, r.dx_oth_out)
    else:
        copies.out(r.dxo, r.dx_out.at[1 - core])

    unk = jnp.concatenate(
        [jnp.where(rank[0:1, :count] >= 0, FILL, 0.0) for rank, (_, _, _, count) in zip(ranks, CELLS)], axis=1
    )
    own_scores = head_sums(r.q_t, r.ko_t)
    own_dprobs = head_sums(r.dm_t, r.vo_t)
    dq_parts, dk_parts, dv_parts = [], [], []
    for head in range(HEADS):
        rows = slice(head * HEAD_DIM, (head + 1) * HEAD_DIM)
        prob = jnp.exp2(own_scores[head] + unk - r.top[head])
        ds = (prob * (own_dprobs[head] * r.total[head] - r.delta[head])).astype(BF).astype(F32)
        low = (prob * r.total[head]).astype(BF).astype(F32)
        dq_parts.append(r.dq_t[rows, :] + (ds * LN2) * r.ko_t[rows, :].astype(F32))
        dk_parts.append(((ds * SCALE) * r.q_t[rows, :].astype(F32)).astype(BF))
        dv_parts.append((low * r.dm_t[rows, :].astype(F32)).astype(BF))
    dq = jnp.concatenate(dq_parts, axis=0)
    dq_sum = jnp.sum(dq, axis=1, keepdims=True)
    dp = jnp.concatenate([dq.astype(BF)] + dk_parts + dv_parts, axis=0).T
    r.dr[...] += nt(dp, r.w[...])
    if layer == 1:
        copies.out(r.dr, r.dx_own_out)
    else:
        r.dxw[...] = r.dr[...].astype(BF)
        copies.out(r.dxw, r.dx_out.at[core])
    need("u_own")
    dw = tn(r.u_own[...], dp)
    r.att_pack[:, :D] = dw[:, :D].astype(BF)
    r.att_pack[:, D : 3 * D] = (dw[:, D:] + r.dw_kv[...]).astype(BF)
    r.att_pack[:, 3 * D : 4 * D] = nn(r.mix_t[...], r.db0[...]).astype(BF)
    lane = lax.broadcasted_iota(jnp.int32, (D, 128), 1)
    r.att_pack[:, 4 * D :] = jnp.where(lane == 0, dq_sum, jnp.where(lane == 1, dm_sum, 0.0)).astype(BF)


FF_BUFFERS = dict(
    {name: SAVED[name] for name in FF_SAVED}, g=TOK, g_odd=TOK, db0=TOK, db1=TOK, dpre=TOK, dr=((OWN, D), F32),
    ff_pack=((D, FF_PACK), BF),
)
ATT_BUFFERS = dict(
    {name: SAVED[name] for name in ATT_SAVED}, u_own=TOK, db0=TOK, dxo=TOK, dr=((OWN, D), F32), qm=((HEADS, 128, OWN), BF),
    dmm=((HEADS, 128, OWN), BF), dm_t=FEAT, delta=HEAD_ROWS, kc_t=((D, ROW), BF), kb=((ROW, 128), F32),
    dq_t=((D, OWN), F32), dkv=((ROW, 2 * D), BF), dw_kv=((D, 2 * D), F32), att_pack=((D, ATT_PACK), BF), rank=RANK,
)


class Loads:
    def __init__(self):
        self.waiting = {}

    def add(self, name, *copies):
        self.waiting.setdefault(name, []).extend(copies)

    def need(self, *names):
        for name in names:
            for copy in self.waiting.pop(name):
                copy.wait()


def start_ff_loads(r, copies, loads, layer):
    loads.add("even", copies.start(r.pair_in.at[0], r.even))
    for name in FF_SAVED[:3]:
        loads.add(name, copies.start(getattr(r, name + "_in"), getattr(r, name)))
    loads.add("w_down", copies.start(r.ff_out_in.at[layer], r.w_down))
    loads.add("w_up", copies.start(r.ff_in_in.at[layer], r.w_up))
    for name in FF_SAVED[3:5]:
        loads.add(name, copies.start(getattr(r, name + "_in"), getattr(r, name)))


def start_att_loads(r, copies, loads, layer):
    loads.add("w_mix", copies.start(r.attn_out_in.at[layer], r.w_mix))
    for name in ATT_SAVED:
        loads.add(name, copies.start(getattr(r, name + "_in"), getattr(r, name)))
    loads.add("rank", copies.start(r.rank_in, r.rank))
    loads.add("w", copies.start(r.attn_proj_in.at[layer], r.w))


def saved_inputs(saved, names):
    ins = {name + "_in": (saved[name + "_out"], pl.ANY) for name in names if name != "even"}
    if "even" in names:
        ins["pair_in"] = (saved["pair_out"], pl.ANY)
    return ins


def backward_last(scal, params, saved, inputs, rank):
    def body(r):
        core, mine, slot = r.scal[0], r.scal[1] == 1, r.scal[2]
        copies, loads = Copies(r.sems), Loads()
        for rows, (_, _, first, count) in zip(own_rows_of(core), CELLS):
            src = [c.at[slot, rows] for c in (r.c_here, r.c_there)]
            loads.add("g", copies.either(mine, *src, r.g.at[pl.ds(first, count)]))
        loads.add("g", *start_params(copies, r))
        start_ff_loads(r, copies, loads, 1)
        start_att_loads(r, copies, loads, 1)
        loads.add("u_own", copies.start(r.x_own.at[1], r.u_own))
        ff_back(r, 1, loads.need)
        ff_weights(r, loads.need)
        copies.out(r.ff_pack, r.pack_out.at[:, pl.ds(0, FF_PACK)])
        attention_back(r, 1, copies, loads.need)
        copies.out(r.att_pack, r.pack_out.at[:, pl.ds(FF_PACK, ATT_PACK)])
        copies.finish()

    ins = {
        "scal": (scal, pltpu.SMEM), **param_inputs(params), **inputs, "rank_in": (rank, pl.ANY), **saved_inputs(saved, SAVED)
    }
    outs = {
        "dx_own_out": ((OWN, D), F32, pl.ANY), "dx_oth_out": (*TOK, pl.ANY),
        "pack_out": ((D, FF_PACK + ATT_PACK), BF, pl.ANY),
    }
    return call(body, ins, outs, {**FF_BUFFERS, **ATT_BUFFERS, **param_buffers()}, sems=64, micros=30)


def backward_first_ff(scal, params, saved, inputs):
    def body(r):
        copies, loads = Copies(r.sems), Loads()
        loads.add("g", copies.start(r.dx_oth, r.g), copies.start(r.dx_own, r.dx))
        loads.add("g", *start_params(copies, r))
        start_ff_loads(r, copies, loads, 0)
        ff_back(r, 0, loads.need)
        core = r.scal[0]
        copies.either(core == 0, r.g_odd, r.g, r.give_out, True)
        copies.either(core == 0, r.g, r.g_odd, r.ship_out.at[core], True)
        copies.out(r.db0, r.db0_out)
        copies.out(r.dr, r.dr_out)
        ff_weights(r, loads.need)
        copies.out(r.ff_pack, r.pack_out)
        copies.finish()

    ins = {"scal": (scal, pltpu.SMEM), **param_inputs(params), **inputs, **saved_inputs(saved, FF_SAVED)}
    outs = {
        "db0_out": (*TOK, pl.ANY), "dr_out": ((OWN, D), F32, pl.ANY), "pack_out": ((D, FF_PACK), BF, pl.ANY),
        "give_out": (*TOK, pl.ANY), "ship_out": (*BOTH, pl.ANY),
    }
    scratch = {**FF_BUFFERS, **param_buffers(), "dx": ((OWN, D), F32)}
    return call(body, ins, outs, scratch, sems=64, micros=7)


def backward_first_att(scal, params, saved, inputs, rank, dp_count):
    size = D // dp_count

    def body(r):
        core, mine, slot = r.scal[0], r.scal[1] == 1, r.scal[2]
        copies, loads = Copies(r.sems), Loads()
        loads.add("w_mix", copies.start(r.db0_in, r.db0), copies.start(r.dr_in, r.dr))
        start_att_loads(r, copies, loads, 0)
        for rows, (_, _, first, count) in zip(own_rows_of(core), CELLS):
            src = [x.at[slot, rows] for x in (r.x_here, r.x_there)]
            loads.add("u_own", copies.either(mine, *src, r.u_own.at[pl.ds(first, count)]))
        loads.add("ff", copies.start(r.ff_in, r.ff_pack))

        def halves(pack, at, width):
            for n in range(dp_count // 2):
                to = pl.ds(n * size, size)
                keep = pl.ds(pl.multiple_of((2 * n + core) * size, size), size)
                send = pl.ds(pl.multiple_of((2 * n + 1 - core) * size, size), size)
                copies.out(pack.at[keep], r.keep_out.at[to, pl.ds(at, width)])
                copies.out(pack.at[send], r.send_out.at[to, pl.ds(at, width)])

        loads.need("ff")
        halves(r.ff_pack, 0, FF_PACK)
        attention_back(r, 0, copies, loads.need)
        halves(r.att_pack, FF_PACK, ATT_PACK)
        copies.finish()

    ins = {
        "scal": (scal, pltpu.SMEM), **param_inputs(params), **inputs, "rank_in": (rank, pl.ANY),
        **saved_inputs(saved, ATT_SAVED),
    }
    half = ((D // 2, PACK), BF, pl.ANY)
    outs = {"dx_out": (*BOTH, pl.ANY), "keep_out": half, "send_out": half}
    scratch = {**ATT_BUFFERS, **param_buffers(), "ff_pack": ((D, FF_PACK), BF), "dxw": TOK}
    return call(body, ins, outs, scratch, sems=48 + 2 * dp_count)


def add_and_split(scal, keep, got, groups):
    size = D // (2 * groups)

    def body(r):
        copies = Copies(r.sems)
        ins = [copies.start(r.keep, r.a), copies.start(r.got, r.b)]
        for copy in ins:
            copy.wait()
        r.a[...] = (r.a[...].astype(F32) + r.b[...].astype(F32)).astype(BF)
        for m in range(groups):
            part = pl.ds(pl.multiple_of((r.scal[5] ^ m) * size, size), size)
            copies.out(r.a.at[part], getattr(r, f"part{m}"))
        copies.finish()

    half = ((D // 2, PACK), BF)
    ins = {"scal": (scal, pltpu.SMEM), **any_inputs(keep=keep, got=got)}
    outs = {f"part{m}": ((size, PACK), BF, pl.ANY) for m in range(groups)}
    return list(call(body, ins, outs, {"a": half, "b": half}, sems=2 + groups).values())


def join(own, others, last):
    size = own.shape[0]
    count = last.shape[0]
    parts = [own] + list(others)

    def body(r):
        copies = Copies(r.sems)
        loads = [copies.start(r.last, r.last_parts)]
        loads += [copies.start(getattr(r, f"p{n}"), r.parts.at[n]) for n in range(len(parts))]
        for copy in loads:
            copy.wait()
        for at, held, number in ((PACK, r.last_parts, count), (0, r.parts, len(parts))):
            total = held[0].astype(F32)
            for n in range(1, number):
                total = total + held[n].astype(F32)
            r.out[:, at : at + PACK] = total.astype(BF)
        copies.out(r.out, r.all_out)
        copies.finish()

    ins = any_inputs(**{f"p{n}": p for n, p in enumerate(parts)}, last=last)
    scratch = {
        "parts": ((len(parts), size, PACK), BF), "last_parts": ((count, size, PACK), BF), "out": ((size, 2 * PACK), BF)
    }
    return call(body, ins, {"all_out": ((size, 2 * PACK), BF, pl.ANY)}, scratch, sems=len(parts) + 2)["all_out"]


def put_row(copies, held, out, row):
    for half in range(2):
        for start, _, own_first, count in CELLS:
            copies.out(held.at[half, pl.ds(own_first, count)], out.at[0, row, pl.ds(start + half * count, count)])


def finish_outputs(scal, low, high, own_low, own_high, cotangent, params):
    def body(r):
        section, core = r.scal[4], r.scal[0]
        copies = Copies(r.sems)
        here_high = (section == 3) & (core == 1)
        at00, at01 = ((section == s) & (core == 0) for s in (0, 1))
        at10, at11 = ((section == s) & (core == 1) for s in (0, 1))
        loads = [
            copies.choose(
                [(at00, r.own_low), (at01 | at10, r.low0), (at11, r.low1), (section >= 2, r.high0)], r.held.at[0]
            ),
            copies.choose(
                [
                    (at00 | at01 | at10, r.low1), (at11, r.low2),
                    ((section >= 2) & jnp.logical_not(here_high), r.high1), (here_high, r.own_high),
                ],
                r.held.at[1],
            ),
        ]
        for copy in loads:
            copy.wait()

        @pl.when(section < 3)
        def _():
            rest = Copies(r.sems)
            rest.used = copies.used
            for row in range(2):
                put_row(rest, r.held.at[row], r.out, row)
            rest.finish()

        @pl.when(section == 3)
        def _():
            rest = Copies(r.sems)
            rest.used = copies.used
            loads = start_params(rest, r)
            loads.append(rest.start(r.ff_in_in.at[1], r.w_up))
            loads.append(rest.start(r.ff_out_in.at[1], r.w_down))
            for row in range(2):
                for half in range(2):
                    for start, _, own_first, count in CELLS:
                        src = r.cot.at[row, pl.ds(start + half * count, count)]
                        loads.append(rest.start(src, r.g.at[row, half, pl.ds(own_first, count)]))
            for copy in loads:
                copy.wait()

            def step(n, carry):
                row, half = n // 2, n % 2
                for at in range(0, OWN, 256):
                    rows = slice(at, at + 256)
                    even = r.held[row, half, rows, :]
                    pre = nn(even, r.w_up[...]) + param_row(r.ff_bias_in, 1)
                    cdf = 0.5 + 0.5 * lax.erf(pre * 0.7071067811865476)
                    hidden = (pre * cdf).astype(BF)
                    gp = cdf + pre * (0.3989422804014327 * jnp.exp(-0.5 * pre * pre))
                    res = even.astype(F32) + nn(hidden, r.w_down[...]) + param_row(r.ff_bias_out, 1)
                    normed, inv = norm_rows(res)
                    gain = param_row(r.norm_gain, 1, 1)
                    r.held[row, half, rows, :] = (normed * gain + param_row(r.norm_shift, 1, 1)).astype(BF)
                    dres = norm_back(r.g[row, half, rows, :].astype(F32), normed, inv, gain)
                    dp = (nt(dres.astype(BF), r.w_down[...]) * gp).astype(BF)
                    r.g[row, half, rows, :] = (dres + nt(dp, r.w_up[...])).astype(BF)
                return carry

            lax.fori_loop(0, 4, step, 0)
            for row in range(2):
                put_row(rest, r.held.at[row], r.out, row)
                put_row(rest, r.g.at[row], r.grads, row)
            rest.finish()

    ins = {"scal": (scal, pltpu.SMEM), **param_inputs(params)}
    ins.update(any_inputs(low0=low[0], low1=low[1], low2=low[2], high0=high[0], high1=high[1], cot=cotangent))
    ins.update(any_inputs(own_low=own_low, own_high=own_high))
    whole = ((1, 2, ROW, D), BF, pl.ANY)
    scratch = {"held": ((2, 2, OWN, D), BF), "g": ((2, 2, OWN, D), BF), **param_buffers()}
    out = call(body, ins, {"out": whole, "grads": whole}, scratch, sems=48)
    return out["out"], out["grads"]


def finish_grads(scal, first, own_first, second, third, last):
    def body(r):
        section, core = r.scal[4], r.scal[0]
        copies = Copies(r.sems)
        here = (section == 0) & (core == 0)
        loads = [
            copies.choose(
                [(here, r.own), ((section == 0) & jnp.logical_not(here), r.a0), (section == 1, r.b0), (section > 1, r.c0)],
                r.held.at[0],
            ),
            copies.choose([(section == 0, r.a1), (section == 1, r.b1), (section > 1, r.c1)], r.held.at[1]),
        ]
        for row in range(2):
            loads[row].wait()

        @pl.when(section < 3)
        def _():
            rest = Copies(r.sems)
            rest.used = copies.used
            for row in range(2):
                put_row(rest, r.held.at[row], r.out, row)
            rest.finish()

    ins = {"scal": (scal, pltpu.SMEM)}
    ins.update(any_inputs(a0=first[0], a1=first[1], b0=second[0], b1=second[1], c0=third[0], c1=third[1]))
    ins.update(any_inputs(last=last, own=own_first))
    whole = ((1, 2, ROW, D), BF, pl.ANY)
    return call(body, ins, {"out": whole}, {"held": ((2, 2, OWN, D), BF)}, {"last": "out"}, 16)["out"]


def unpack(got):
    count, size, width = got.shape
    wide = ((2, size, 3 * D), F32, pltpu.VMEM)
    square = ((2, size, D), F32, pltpu.VMEM)
    vec = ((2, size), F32, pltpu.VMEM)
    pair = ((2, 2, size), F32, pltpu.VMEM)
    outs = dict(
        proj=wide, out=square, qb=vec, vb=vec, ob=vec, up=square, down=square, ub=vec, db=vec, gain=pair, shift=pair
    )

    def body(r):
        pltpu.sync_copy(r.got, r.held)
        total = r.held[0].astype(F32)
        for n in range(1, count):
            total = total + r.held[n].astype(F32)
        for layer in range(2):
            base = layer * PACK
            ff = total[:, base : base + FF_PACK]
            att = total[:, base + FF_PACK : base + FF_PACK + ATT_PACK]
            r.up[layer] = ff[:, :D]
            r.down[layer] = ff[:, D : 2 * D]
            r.proj[layer] = att[:, : 3 * D]
            r.out[layer] = att[:, 3 * D : 4 * D]
            cols = ff[:, 2 * D :].T
            for ref, k in ((r.ob, 0), (r.ub, 3), (r.db, 4)):
                ref[layer : layer + 1, :] = cols[k : k + 1, :]
            for kind in range(2):
                r.gain[layer, kind : kind + 1, :] = cols[4 * kind + 1 : 4 * kind + 2, :]
                r.shift[layer, kind : kind + 1, :] = cols[4 * kind + 2 : 4 * kind + 3, :]
            cols = att[:, 4 * D :].T
            for ref, k in ((r.qb, 0), (r.vb, 1)):
                ref[layer : layer + 1, :] = cols[k : k + 1, :]

    scratch = {"held": ((count, size, width), BF)}
    return list(call(body, any_inputs(got=got), outs, scratch, sems=1).values())


def make_per_device(dp_count, section_count):
    both = ("dp", "section")

    def index(dp, section):
        return dp * section_count + section

    everyone = [(d, s) for d in range(dp_count) for s in range(section_count)]
    mate_pairs = [(index(d, s), index(d ^ 1, s)) for d, s in everyone]
    fetch_pairs = [(index(d, s), index(d ^ 1, s)) for d, s in everyone if d % 2 == s // 2]

    def send(rows, moves):
        pairs = []
        for d, z in everyone:
            to = moves.get((d % 2, z))
            if to is not None and index(d - d % 2 + z // 2, to) != index(d, z):
                pairs.append((index(d, z), index(d - d % 2 + z // 2, to)))
        return lax.ppermute(rows, both, pairs)

    def ship(rows, sections):
        return [
            send(rows, {(c, z): to for c, to in enumerate(sections) if to is not None for z in (odd, 2 + odd)})
            for odd in range(2)
        ]

    def mate(x):
        return lax.ppermute(x, both, mate_pairs)

    def after(value, *earlier):
        return lax.optimization_barrier((value, earlier))[0]

    def per_device(
        block_input, known_genes, attn_proj, attn_out, query_bias, value_bias, out_bias, ff_in, ff_out,
        ff_bias_in, ff_bias_out, norm_gain, norm_shift, cotangent,
    ):
        params = dict(
            attn_proj=attn_proj, attn_out=attn_out, query_bias=query_bias, value_bias=value_bias, out_bias=out_bias,
            ff_in=ff_in, ff_out=ff_out, ff_bias_in=ff_bias_in, ff_bias_out=ff_bias_out, norm_gain=norm_gain,
            norm_shift=norm_shift,
        )
        dp = lax.axis_index("dp")
        core = dp % 2
        section = lax.axis_index("section")
        mine = (core == section // 2).astype(jnp.int32)
        scal = jnp.stack([core, mine, section % 2, 2 * (section % 2) + core, section, dp // 2]).astype(jnp.int32)

        known_there = lax.ppermute(known_genes, both, fetch_pairs)
        x_there = lax.ppermute(block_input, both, fetch_pairs)
        x_in = any_inputs(x_here=block_input, x_there=x_there)
        f0 = forward_layer(0, scal, params, {**x_in, **any_inputs(known_here=known_genes, known_there=known_there)})
        rank = f0["rank_out"]
        x_own = f0["pair_out"]
        x_oth = mate(x_own)

        def other_half(rows, half):
            return lax.dynamic_update_index_in_dim(rows, half, 1 - core, 0)

        c_there = lax.ppermute(after(cotangent, x_own), both, fetch_pairs)
        missing = lax.dynamic_index_in_dim(x_oth, core, 0, keepdims=False)
        low_rows = other_half(f0["ship_out"], missing)
        got_low = [
            send(low_rows, {(0, 2): 0, (1, 0): 1}),
            send(low_rows, {(1, 2): 1, (1, 1): 1, (0, 3): 0, (0, 1): 0}),
            send(low_rows, {(1, 3): 1}),
        ]
        f1 = forward_layer(1, scal, params, any_inputs(x_own=x_own, x_oth=x_oth, rank_in=rank))
        high_rows = other_half(f1["ship_out"], mate(f1["pair_out"][0]))
        got_high = ship(high_rows, (2, 3))
        b1 = backward_last(after(scal, got_low[0]), params, f1, any_inputs(c_here=cotangent, c_there=c_there, x_own=x_own), rank)
        wide = lax.all_to_all(b1["pack_out"].reshape(dp_count, -1, PACK), "dp", 0, 0)
        ins = any_inputs(dx_own=b1["dx_own_out"], dx_oth=mate(b1["dx_oth_out"]))
        b0 = backward_first_ff(after(scal, got_high[0]), params, f0, ins)
        grad_rows = other_half(b0["ship_out"], mate(after(b0["give_out"], got_low[1:])))
        got_third = ship(grad_rows, (2, None))
        got_second = ship(grad_rows, (None, 1))
        ins = {**x_in, **any_inputs(db0_in=b0["db0_out"], dr_in=b0["dr_out"], ff_in=b0["pack_out"])}
        last = backward_first_att(after(scal, grad_rows), params, f0, ins, rank, dp_count)

        to_first = [(index(d, s), index(d - 1, s)) for d, s in everyone if d % 2]
        theirs = lax.ppermute(after(last["dx_out"], got_second, got_high[1], wide), both, to_first)
        first_rows = (last["dx_out"].astype(F32) + theirs.astype(F32)).astype(BF)
        got_first = ship(first_rows, (0, None))
        groups = dp_count // 2
        parts = add_and_split(after(scal, first_rows), last["keep_out"], mate(last["send_out"]), groups)
        others = []
        for m in range(1, groups):
            pairs = [(index(d, s), index(d ^ (2 * m), s)) for d, s in everyone]
            others.append(lax.ppermute(parts[m], both, pairs))
        held = join(after(parts[0], got_first[0]), others, wide)
        got = lax.all_to_all(held.reshape(section_count, -1, held.shape[1]), "section", 0, 0)
        grads = unpack(got)
        section_outputs, last_grads = finish_outputs(scal, got_low, got_high, low_rows, high_rows, cotangent, params)
        section_grads = finish_grads(scal, got_first, first_rows, got_second, got_third, last_grads)
        return (section_outputs, section_grads, *grads)

    return per_device


def solution(mesh):
    rows = P("dp", None, None)
    placed = (rows, P("dp", None)) + (P(),) * 11 + (rows,)
    sections = P("section", "dp", None, None)
    matrix = P(None, ("dp", "section"), None)
    vector = P(None, ("dp", "section"))
    pairs = P(None, None, ("dp", "section"))
    return jax.shard_map(
        make_per_device(mesh.shape["dp"], mesh.shape["section"]),
        mesh=mesh,
        in_specs=placed,
        out_specs=(
            sections, sections, matrix, matrix, vector, vector, vector, matrix, matrix, vector, vector, pairs, pairs,
        ),
        check_vma=False,
    )
```

```python
from types import SimpleNamespace

import jax
import jax.numpy as jnp
from jax import lax
from jax.experimental import pallas as pl
from jax.experimental.pallas import tpu as pltpu
from jax.sharding import PartitionSpec as P

D = 512
HEADS = 8
HEAD_DIM = 64
LONG = 1024
SHORT = 512
ROW = LONG + SHORT
EPS = 1e-05
FILL = -1e30
SCALE = HEAD_DIM ** (-0.5)
LOG2E = 1.4426950408889634
LN2 = 0.6931471805599453
SOFT = SCALE * LOG2E
BF = jnp.bfloat16
F32 = jnp.float32
VAUG = HEAD_DIM + 16
ATT_PACK = 4 * D + 128
FF_PACK = 2 * D + 128
PACK = ATT_PACK + FF_PACK
OWN = ROW // 2
CELLS = ((0, LONG, 0, LONG // 2), (LONG, SHORT, LONG // 2, SHORT // 2))
SMALLEST, LARGEST = 2.0 ** -60, 2.0 ** 90
VMEM_LIMIT = 63 * 1024 * 1024
LAYER_PARAMS = (
    "attn_proj", "attn_out", "ff_in", "ff_out",
    "query_bias", "value_bias", "out_bias", "ff_bias_in", "ff_bias_out", "norm_gain", "norm_shift",
)
MATRICES = LAYER_PARAMS[:4]


def nn(a, b):
    return lax.dot_general(a, b, (((1,), (0,)), ((), ())), preferred_element_type=F32)


def nt(a, b):
    return lax.dot_general(a, b, (((1,), (1,)), ((), ())), preferred_element_type=F32)


def tn(a, b):
    return lax.dot_general(a, b, (((0,), (0,)), ((), ())), preferred_element_type=F32)


def call(body, ins, outs, scratch, aliases=None, sems=48, micros=0.001):
    names = list(ins) + list(outs) + list(scratch) + ["sems"]

    def kernel(*refs):
        body(SimpleNamespace(**dict(zip(names, refs))))

    in_names, out_names = list(ins), list(outs)
    result = pl.pallas_call(
        kernel,
        in_specs=[pl.BlockSpec(memory_space=space) for _, space in ins.values()],
        out_specs=[pl.BlockSpec(memory_space=space) for _, _, space in outs.values()],
        out_shape=[jax.ShapeDtypeStruct(shape, dtype) for shape, dtype, _ in outs.values()],
        scratch_shapes=[pltpu.VMEM(shape, dtype) for shape, dtype in scratch.values()] + [pltpu.SemaphoreType.DMA((sems,))],
        input_output_aliases={in_names.index(a): out_names.index(b) for a, b in (aliases or {}).items()},
        compiler_params=pltpu.CompilerParams(vmem_limit_bytes=VMEM_LIMIT),
        cost_estimate=pl.CostEstimate(flops=int(micros * 1150000000), bytes_accessed=2**12, transcendentals=0),
    )(*[array for array, _ in ins.values()])
    return dict(zip(out_names, result))


class Copies:
    def __init__(self, sems):
        self.sems, self.used, self.ends = sems, 0, []

    def start(self, src, dst):
        copy = pltpu.make_async_copy(src, dst, self.sems.at[self.used])
        self.used += 1
        copy.start()
        return copy

    def either(self, first, src_a, src_b, dst, out=False):
        sem = self.sems.at[self.used]
        self.used += 1
        pl.when(first)(lambda: pltpu.make_async_copy(src_a, dst, sem).start())
        pl.when(jnp.logical_not(first))(lambda: pltpu.make_async_copy(src_b, dst, sem).start())
        copy = pltpu.make_async_copy(src_a, dst, sem)
        if out:
            self.ends.append(copy)
        return copy

    def choose(self, cases, dst):
        sem = self.sems.at[self.used]
        self.used += 1
        for holds, src in cases:
            pl.when(holds)(lambda src=src: pltpu.make_async_copy(src, dst, sem).start())
        return pltpu.make_async_copy(cases[0][1], dst, sem)

    def out(self, src, dst):
        self.ends.append(self.start(src, dst))

    def finish(self):
        for copy in self.ends:
            copy.wait()


def norm_rows(residual):
    center = residual - jnp.mean(residual, axis=-1, keepdims=True)
    inv_std = lax.rsqrt(jnp.mean(center * center, axis=-1, keepdims=True) + EPS)
    return center * inv_std, inv_std


def norm_back(grad, normed, inv, gain):
    e = grad * gain
    return inv * (
        e - jnp.mean(e, axis=-1, keepdims=True) - normed * jnp.mean(e * normed, axis=-1, keepdims=True)
    )


def one_hot_rows(rank_row, size, length):
    return (lax.broadcasted_iota(jnp.int32, (size, length), 0) == rank_row).astype(F32).astype(BF)


def one_hot_cols(rank_col, size):
    length = rank_col.shape[0]
    return (lax.broadcasted_iota(jnp.int32, (length, size), 1) == rank_col).astype(F32).astype(BF)


def put_masked(dst, src, tokens):
    zeros = jnp.zeros((HEAD_DIM, tokens), BF)
    for head in range(HEADS):
        part = (head % 2) * HEAD_DIM
        dst[head, part : part + HEAD_DIM, :] = src[head * HEAD_DIM : (head + 1) * HEAD_DIM, :]
        dst[head, HEAD_DIM - part : 2 * HEAD_DIM - part, :] = zeros


def head_sums(a, b):
    out = []
    for head in range(HEADS):
        rows = slice(head * HEAD_DIM, (head + 1) * HEAD_DIM)
        out.append(jnp.sum(a[rows, :].astype(F32) * b[rows, :].astype(F32), axis=0, keepdims=True))
    return out


def rank_tokens(known, length):
    upto = lax.broadcasted_iota(jnp.int32, (length, length), 0) <= lax.broadcasted_iota(jnp.int32, (length, length), 1)
    low = jnp.broadcast_to(known.astype(F32), (8, length))
    place = nn(low.astype(BF), upto.astype(F32).astype(BF))
    return jnp.where(low > 0.5, place - 1.0, -1.0).astype(jnp.int32)


def small_count(length):
    return length // 2 + length // 8


def param_row(ref, layer, kind=None):
    return ref[pl.ds(layer, 1), :] if kind is None else ref[layer, pl.ds(kind, 1), :]


def key_rows(quick):
    sizes = [small_count(length) if quick else length for _, length, _, _ in CELLS]
    return ((0, sizes[0]), (sizes[0], sizes[1])), sum(sizes)


def split_rank(r):
    ranks = [r.rank[:, start : start + length] for start, length, _, _ in CELLS]
    return ranks, [jnp.max(rank[0:1, :]) + 1 for rank in ranks]


def units():
    out = []
    for cell, (_, _, first, count) in enumerate(CELLS):
        for at in range(first, first + count, 256):
            out.append((cell, slice(at, at + 256)))
    return out


def small_counts(counts):
    ok = counts[0] <= small_count(CELLS[0][1])
    for count, (_, length, _, _) in zip(counts[1:], CELLS[1:]):
        ok = ok & (count <= small_count(length))
    return ok


def put_key_bias(r, rows, counts):
    for (first, size), count in zip(rows, counts):
        inside = lax.broadcasted_iota(jnp.int32, (size, 128), 0) < count
        r.kb[first : first + size, :] = jnp.where(inside, 0.0, FILL)


def own_rows_of(core, other=False):
    place = 1 - core if other else core
    return [pl.ds(pl.multiple_of(start + place * count, count), count) for start, _, _, count in CELLS]


def forward_body(r, layer):
    core = r.scal[0]
    copies = Copies(r.sems)
    mine, slot = r.scal[1] == 1, r.scal[2]
    if layer == 0:
        known_in = copies.either(mine, r.known_here, r.known_there, r.known)
        u_in = []
        for buffer, other in ((r.u_own, False), (r.u_oth, True)):
            for rows, (_, _, first, count) in zip(own_rows_of(core, other), CELLS):
                u_in.append(
                    copies.either(
                        mine, r.x_here.at[slot, rows], r.x_there.at[slot, rows], buffer.at[pl.ds(first, count)]
                    )
                )
        u_own_in, u_oth_in = u_in[:2], u_in[2:]
    else:
        rank_in = copies.start(r.rank_in, r.rank)
        u_own_in, u_oth_in = [copies.start(r.x_own.at[1], r.u_own)], [copies.start(r.x_oth.at[1], r.u_oth)]
    w_in = copies.start(r.attn_proj_in.at[layer], r.w)
    small = start_params(copies, r)
    late = [
        copies.start(r.attn_out_in.at[layer], r.w_mix),
        copies.start(r.ff_in_in.at[layer], r.w_up),
        copies.start(r.ff_out_in.at[layer], r.w_down),
    ]

    def save(*names):
        for name in names:
            copies.out(getattr(r, name), getattr(r, name + "_out"))

    if layer == 0:
        known_in.wait()
        for start, length, _, count in CELLS:
            known = r.known[pl.ds(slot, 1), :][:, start : start + length]
            first, second = known[:, :count], known[:, count:]
            known = jnp.concatenate([jnp.where(core == 0, first, second), jnp.where(core == 0, second, first)], axis=1)
            r.rank[:, start : start + length] = rank_tokens(known, length)
        save("rank")
    else:
        rank_in.wait()
    ranks, counts = split_rank(r)
    for copy in small + u_own_in:
        copy.wait()
    w_in.wait()
    own = nn(r.u_own[...], r.w[...])
    r.q_t[...] = (own[:, :D] + param_row(r.query_bias, layer)).astype(BF).T
    r.ko_t[...] = (own[:, D : 2 * D] * SOFT).astype(BF).T
    r.vo_t[...] = (own[:, 2 * D :] + param_row(r.value_bias, layer)).astype(BF).T
    save("q_t", "ko_t", "vo_t")
    put_masked(r.qm, r.q_t, OWN)
    unk = jnp.concatenate(
        [jnp.where(rank[0:1, :count] >= 0, FILL, 0.0) for rank, (_, _, _, count) in zip(ranks, CELLS)], axis=1
    )
    for head, row in enumerate(head_sums(r.q_t, r.ko_t)):
        r.sd[head] = row + unk
        r.total[head] = jnp.zeros_like(row)
        r.top[head] = jnp.zeros_like(row)
    for copy in u_oth_in:
        copy.wait()

    def keys(quick):
        rows, total = key_rows(quick)
        for rank, (_, length, own_first, count), (first, size) in zip(ranks, CELLS, rows):
            pick = one_hot_rows(rank[0:1, :], size, length)
            tokens = slice(own_first, own_first + count)
            uc = nn(pick[:, :count], r.u_own[tokens, :]) + nn(pick[:, count:], r.u_oth[tokens, :])
            r.uc[first : first + size, :] = uc.astype(BF)
        kv = nn(r.uc[:total, :], r.w[:, D:])
        r.k_c[:total, :] = (kv[:, :D] * SOFT).astype(BF)
        ones = []
        for (first, size), known in zip(rows, counts):
            inside = lax.broadcasted_iota(jnp.int32, (size, D), 0) < known
            vc = kv[first : first + size, D:] + param_row(r.value_bias, layer)
            r.v_c[first : first + size, :] = jnp.where(inside, vc, 0.0).astype(BF)
            lane = lax.broadcasted_iota(jnp.int32, (16, size), 1)
            ones.append(((lane < known) & (lax.broadcasted_iota(jnp.int32, (16, size), 0) == 0)).astype(F32))
        vct = r.v_c[:total, :].T
        ones = jnp.concatenate(ones, axis=1).astype(BF)
        for head in range(HEADS):
            r.vaug[head * VAUG : head * VAUG + HEAD_DIM, :total] = vct[head * HEAD_DIM : (head + 1) * HEAD_DIM, :]
            r.vaug[head * VAUG + HEAD_DIM : (head + 1) * VAUG, :total] = ones

    def attend(quick):
        rows_of, _ = key_rows(quick)
        if not quick:
            put_key_bias(r, rows_of, counts)

        def pair(p, carry):
            lanes = pl.ds(pl.multiple_of(p * 128, 128), 128)
            for e in range(2):
                head = 2 * p + e
                feats = pl.ds(pl.multiple_of(head * HEAD_DIM, HEAD_DIM), HEAD_DIM)
                for cell, cols in units():
                    keys_at = slice(rows_of[cell][0], rows_of[cell][0] + rows_of[cell][1])
                    vrows = r.vaug[pl.ds(pl.multiple_of(head * VAUG, 16), VAUG), keys_at]
                    scores = nn(r.k_c[keys_at, lanes], r.qm[head, :, cols])
                    own_score = r.sd[head, :, cols]
                    if quick:
                        low = jnp.exp2(scores).astype(BF)
                    else:
                        tops, probs = [], []
                        for t in range(0, 256, 128):
                            part = scores[:, t : t + 128] + r.kb[keys_at, :]
                            top = jnp.maximum(jnp.max(part, axis=0, keepdims=True), own_score[:, t : t + 128])
                            tops.append(top)
                            probs.append(jnp.exp2(part - top).astype(BF))
                        top = jnp.concatenate(tops, axis=1)
                        low = jnp.concatenate(probs, axis=1)
                        r.top[head, :, cols] = top
                        own_score = own_score - top
                    mixed = nn(vrows, low)
                    own_prob = jnp.exp2(own_score)
                    total = mixed[HEAD_DIM : HEAD_DIM + 1] + own_prob
                    r.total[head, :, cols] = total
                    mixed = mixed[:HEAD_DIM] + own_prob * r.vo_t[feats, cols].astype(F32)
                    r.mix_t[feats, cols] = (mixed * (1.0 / total)).astype(BF)
            return carry

        lax.fori_loop(0, HEADS // 2, pair, 0)

    def run(quick):
        keys(quick)
        attend(quick)

    pl.when(small_counts(counts))(lambda: run(True))
    totals = r.total[...]
    fine = jnp.min(jnp.where((totals > SMALLEST) & (totals < LARGEST), 1, 0)) == 1
    pl.when(jnp.logical_not(fine))(lambda: run(False))
    save("uc", "k_c", "v_c", "mix_t", "top", "total")
    for copy in late:
        copy.wait()

    for at in range(0, OWN, 256):
        rows = slice(at, at + 256)
        res = r.u_own[rows, :].astype(F32) + tn(r.mix_t[:, rows], r.w_mix[...]) + param_row(r.out_bias, layer)
        normed, inv0 = norm_rows(res)
        r.nrm0[rows, :] = normed.astype(BF)
        even = (normed * param_row(r.norm_gain, layer, 0) + param_row(r.norm_shift, layer, 0)).astype(BF)
        r.even[rows, :] = even
        pre = nn(even, r.w_up[...]) + param_row(r.ff_bias_in, layer)
        cdf = 0.5 + 0.5 * lax.erf(pre * 0.7071067811865476)
        hidden = (pre * cdf).astype(BF)
        r.hid[rows, :] = hidden
        r.gp[rows, :] = (cdf + pre * (0.3989422804014327 * jnp.exp(-0.5 * pre * pre))).astype(BF)
        res = even.astype(F32) + nn(hidden, r.w_down[...]) + param_row(r.ff_bias_out, layer)
        normed, inv1 = norm_rows(res)
        r.nrm1[rows, :] = normed.astype(BF)
        r.odd[rows, :] = (normed * param_row(r.norm_gain, layer, 1) + param_row(r.norm_shift, layer, 1)).astype(BF)
        r.inv[rows, :] = jnp.where(lax.broadcasted_iota(jnp.int32, (256, 128), 1) == 0, inv0, inv1)

    copies.out(r.even, r.pair_out.at[0])
    copies.out(r.odd, r.pair_out.at[1])
    if layer == 0:
        copies.either(core == 0, r.even, r.odd, r.ship_out.at[core], True)
    else:
        copies.out(r.even, r.ship_out.at[core])
    save("nrm0", "nrm1", "gp", "hid", "inv")
    copies.finish()


TOK = ((OWN, D), BF)
FEAT = ((D, OWN), BF)
KEYS = ((ROW, D), BF)
HEAD_ROWS = ((HEADS, 1, OWN), F32)
RANK = ((8, ROW), jnp.int32)
SAVED = dict(
    even=TOK, q_t=FEAT, ko_t=FEAT, vo_t=FEAT, uc=KEYS, k_c=KEYS, v_c=KEYS, mix_t=FEAT, nrm0=TOK, nrm1=TOK, gp=TOK, hid=TOK,
    inv=((OWN, 128), F32), top=HEAD_ROWS, total=HEAD_ROWS,
)
FF_SAVED = ("nrm1", "inv", "gp", "nrm0", "hid", "even")
ATT_SAVED = ("mix_t", "q_t", "k_c", "v_c", "top", "total", "ko_t", "vo_t", "uc")
BOTH = ((2, OWN, D), BF)


def weight_buffers():
    square = ((D, D), BF)
    return dict(w=((D, 3 * D), BF), w_mix=square, w_up=square, w_down=square)


def param_inputs(params):
    return {name + "_in": (params[name], pl.ANY) for name in LAYER_PARAMS}


def param_buffers():
    pairs = {name: ((2, 2, D) if name.startswith("norm") else (2, D), F32) for name in LAYER_PARAMS[4:]}
    return {**pairs, **weight_buffers()}


def start_params(copies, r):
    return [copies.start(getattr(r, name + "_in"), getattr(r, name)) for name in LAYER_PARAMS[4:]]


def any_inputs(**arrays):
    return {name: (array, pl.ANY) for name, array in arrays.items()}


def forward_layer(layer, scal, params, inputs):
    ins = {"scal": (scal, pltpu.SMEM), **param_inputs(params), **inputs}
    outs = {name + "_out": (*spec, pl.ANY) for name, spec in SAVED.items() if name != "even"}
    outs.update(pair_out=(*BOTH, pl.ANY), ship_out=(*BOTH, pl.ANY))
    scratch = {
        **SAVED, **param_buffers(), "u_own": TOK, "u_oth": TOK, "odd": TOK, "rank": RANK, "qm": ((HEADS, 128, OWN), BF),
        "vaug": ((HEADS * VAUG, ROW), BF), "kb": ((ROW, 128), F32), "sd": HEAD_ROWS,
    }
    if layer == 0:
        outs["rank_out"] = (*RANK, pl.ANY)
        scratch["known"] = ((2, ROW), jnp.int32)
    return call(lambda r: forward_body(r, layer), ins, outs, scratch, micros=20)


def ff_back(r, layer, need):
    sums = [jnp.zeros((1, D), F32) for _ in range(7)]

    def add(slot, value):
        sums[slot] = sums[slot] + jnp.sum(value, axis=0, keepdims=True)

    need("g", "nrm1", "inv", "w_down", "w_up", "gp", "nrm0")
    for at in range(0, OWN, 256):
        rows = slice(at, at + 256)
        if layer == 1:
            grad = r.g[rows, :].astype(F32)
        else:
            low = (r.dx[rows, :] + r.g[rows, :].astype(F32)).astype(BF)
            r.g[rows, :] = low
            grad = low.astype(F32)
        normed = r.nrm1[rows, :].astype(F32)
        add(5, grad * normed)
        add(6, grad)
        dres = norm_back(grad, normed, r.inv[rows, 1:2], param_row(r.norm_gain, layer, 1))
        add(4, dres)
        low = dres.astype(BF)
        r.db1[rows, :] = low
        dp = nt(low, r.w_down[...]) * r.gp[rows, :].astype(F32)
        add(3, dp)
        low = dp.astype(BF)
        r.dpre[rows, :] = low
        low = (dres + nt(low, r.w_up[...])).astype(BF)
        r.g_odd[rows, :] = low
        grad = low.astype(F32)
        normed = r.nrm0[rows, :].astype(F32)
        add(1, grad * normed)
        add(2, grad)
        dres = norm_back(grad, normed, r.inv[rows, 0:1], param_row(r.norm_gain, layer, 0))
        add(0, dres)
        r.dr[rows, :] = dres
        r.db0[rows, :] = dres.astype(BF)
    vectors = jnp.concatenate(sums + [jnp.zeros((121, D), F32)], axis=0)
    r.ff_pack[:, 2 * D :] = vectors.T.astype(BF)


def ff_weights(r, need):
    need("hid", "even")
    r.ff_pack[:, :D] = tn(r.even[...], r.dpre[...]).astype(BF)
    r.ff_pack[:, D : 2 * D] = tn(r.hid[...], r.db1[...]).astype(BF)


def attention_back(r, layer, copies, need):
    core = r.scal[0]
    need("w_mix", "mix_t")
    dm_t = nt(r.w_mix[...], r.db0[...]).astype(BF)
    r.dm_t[...] = dm_t
    dm_sum = jnp.sum(dm_t.astype(F32), axis=1, keepdims=True)
    need("q_t", "top", "total", "ko_t", "vo_t")
    put_masked(r.qm, r.q_t, OWN)
    zeros = jnp.zeros((HEAD_DIM, OWN), BF)
    deltas = head_sums(r.dm_t, r.mix_t)
    for head in range(HEADS):
        rows = slice(head * HEAD_DIM, (head + 1) * HEAD_DIM)
        part = (head % 2) * HEAD_DIM
        inv_total = 1.0 / r.total[head]
        r.total[head] = inv_total
        r.delta[head] = deltas[head] * inv_total
        r.dmm[head, part : part + HEAD_DIM, :] = (r.dm_t[rows, :].astype(F32) * inv_total).astype(BF)
        r.dmm[head, HEAD_DIM - part : 2 * HEAD_DIM - part, :] = zeros
    need("k_c", "v_c", "uc", "w", "rank")
    ranks, counts = split_rank(r)
    quick_ok = small_counts(counts) & (jnp.max(jnp.abs(r.top[...])) == 0.0)

    def run(quick):
        rows_of, total = key_rows(quick)
        r.kc_t[:, :total] = r.k_c[:total, :].T
        if not quick:
            put_key_bias(r, rows_of, counts)

        def pair(p, carry):
            lanes = pl.ds(pl.multiple_of(p * 128, 128), 128)
            late_lanes = pl.ds(pl.multiple_of(D + p * 128, 128), 128)
            dk = [jnp.zeros((size, 128), F32) for _, size in rows_of]
            dv = [jnp.zeros((size, 128), F32) for _, size in rows_of]
            for e in range(2):
                head = 2 * p + e
                feats = pl.ds(pl.multiple_of(head * HEAD_DIM, HEAD_DIM), HEAD_DIM)
                for cell, cols in units():
                    keys_at = slice(rows_of[cell][0], rows_of[cell][0] + rows_of[cell][1])
                    qtm = r.qm[head, :, cols]
                    dmh = r.dmm[head, :, cols]
                    scores = nn(r.k_c[keys_at, lanes], qtm)
                    dprob = nn(r.v_c[keys_at, lanes], dmh)
                    delta = r.delta[head, :, cols]
                    if quick:
                        prob = jnp.exp2(scores)
                        low = prob.astype(BF)
                        ds = (prob * (dprob - delta)).astype(BF)
                    else:
                        top = r.top[head, :, cols]
                        lows, grads = [], []
                        for t in range(0, 256, 128):
                            tile = slice(t, t + 128)
                            prob = jnp.exp2(jnp.minimum(scores[:, tile] - top[:, tile], r.kb[keys_at, :]))
                            lows.append(prob.astype(BF))
                            grads.append((prob * (dprob[:, tile] - delta[:, tile])).astype(BF))
                        low = jnp.concatenate(lows, axis=1)
                        ds = jnp.concatenate(grads, axis=1)
                    dv[cell] = dv[cell] + nt(low, dmh)
                    dk[cell] = dk[cell] + nt(ds, qtm)
                    r.dq_t[feats, cols] = nn(r.kc_t[feats, keys_at], ds) * LN2
            for cell, (first, size) in enumerate(rows_of):
                r.dkv[first : first + size, lanes] = (dk[cell] * SCALE).astype(BF)
                r.dkv[first : first + size, late_lanes] = dv[cell].astype(BF)
            return carry

        lax.fori_loop(0, HEADS // 2, pair, 0)
        dkv = r.dkv[:total, :]
        r.dw_kv[...] = tn(r.uc[:total, :], dkv)
        dxc = nt(dkv, r.w[:, D:]).astype(BF)
        for rank, (_, _, own_first, count), (first, size) in zip(ranks, CELLS, rows_of):
            rank_col = rank.astype(F32).T[:, 0:1].astype(jnp.int32)
            tokens = slice(own_first, own_first + count)
            part = dxc[first : first + size, :]
            r.dr[tokens, :] += nn(one_hot_cols(rank_col[:count, :], size), part)
            r.dxo[tokens, :] = nn(one_hot_cols(rank_col[count:, :], size), part).astype(BF)

    pl.when(quick_ok)(lambda: run(True))
    pl.when(jnp.logical_not(quick_ok))(lambda: run(False))
    if layer == 1:
        copies.out(r.dxo, r.dx_oth_out)
    else:
        copies.out(r.dxo, r.dx_out.at[1 - core])

    unk = jnp.concatenate(
        [jnp.where(rank[0:1, :count] >= 0, FILL, 0.0) for rank, (_, _, _, count) in zip(ranks, CELLS)], axis=1
    )
    own_scores = head_sums(r.q_t, r.ko_t)
    own_dprobs = head_sums(r.dm_t, r.vo_t)
    dq_parts, dk_parts, dv_parts = [], [], []
    for head in range(HEADS):
        rows = slice(head * HEAD_DIM, (head + 1) * HEAD_DIM)
        prob = jnp.exp2(own_scores[head] + unk - r.top[head])
        ds = (prob * (own_dprobs[head] * r.total[head] - r.delta[head])).astype(BF).astype(F32)
        low = (prob * r.total[head]).astype(BF).astype(F32)
        dq_parts.append(r.dq_t[rows, :] + (ds * LN2) * r.ko_t[rows, :].astype(F32))
        dk_parts.append(((ds * SCALE) * r.q_t[rows, :].astype(F32)).astype(BF))
        dv_parts.append((low * r.dm_t[rows, :].astype(F32)).astype(BF))
    dq = jnp.concatenate(dq_parts, axis=0)
    dq_sum = jnp.sum(dq, axis=1, keepdims=True)
    dp = jnp.concatenate([dq.astype(BF)] + dk_parts + dv_parts, axis=0).T
    r.dr[...] += nt(dp, r.w[...])
    if layer == 1:
        copies.out(r.dr, r.dx_own_out)
    else:
        r.dxw[...] = r.dr[...].astype(BF)
        copies.out(r.dxw, r.dx_out.at[core])
    need("u_own")
    dw = tn(r.u_own[...], dp)
    r.att_pack[:, :D] = dw[:, :D].astype(BF)
    r.att_pack[:, D : 3 * D] = (dw[:, D:] + r.dw_kv[...]).astype(BF)
    r.att_pack[:, 3 * D : 4 * D] = nn(r.mix_t[...], r.db0[...]).astype(BF)
    lane = lax.broadcasted_iota(jnp.int32, (D, 128), 1)
    r.att_pack[:, 4 * D :] = jnp.where(lane == 0, dq_sum, jnp.where(lane == 1, dm_sum, 0.0)).astype(BF)


FF_BUFFERS = dict(
    {name: SAVED[name] for name in FF_SAVED}, g=TOK, g_odd=TOK, db0=TOK, db1=TOK, dpre=TOK, dr=((OWN, D), F32),
    ff_pack=((D, FF_PACK), BF),
)
ATT_BUFFERS = dict(
    {name: SAVED[name] for name in ATT_SAVED}, u_own=TOK, db0=TOK, dxo=TOK, dr=((OWN, D), F32), qm=((HEADS, 128, OWN), BF),
    dmm=((HEADS, 128, OWN), BF), dm_t=FEAT, delta=HEAD_ROWS, kc_t=((D, ROW), BF), kb=((ROW, 128), F32),
    dq_t=((D, OWN), F32), dkv=((ROW, 2 * D), BF), dw_kv=((D, 2 * D), F32), att_pack=((D, ATT_PACK), BF), rank=RANK,
)


class Loads:
    def __init__(self):
        self.waiting = {}

    def add(self, name, *copies):
        self.waiting.setdefault(name, []).extend(copies)

    def need(self, *names):
        for name in names:
            for copy in self.waiting.pop(name):
                copy.wait()


def start_ff_loads(r, copies, loads, layer):
    loads.add("even", copies.start(r.pair_in.at[0], r.even))
    for name in FF_SAVED[:3]:
        loads.add(name, copies.start(getattr(r, name + "_in"), getattr(r, name)))
    loads.add("w_down", copies.start(r.ff_out_in.at[layer], r.w_down))
    loads.add("w_up", copies.start(r.ff_in_in.at[layer], r.w_up))
    for name in FF_SAVED[3:5]:
        loads.add(name, copies.start(getattr(r, name + "_in"), getattr(r, name)))


def start_att_loads(r, copies, loads, layer):
    loads.add("w_mix", copies.start(r.attn_out_in.at[layer], r.w_mix))
    for name in ATT_SAVED:
        loads.add(name, copies.start(getattr(r, name + "_in"), getattr(r, name)))
    loads.add("rank", copies.start(r.rank_in, r.rank))
    loads.add("w", copies.start(r.attn_proj_in.at[layer], r.w))


def saved_inputs(saved, names):
    ins = {name + "_in": (saved[name + "_out"], pl.ANY) for name in names if name != "even"}
    if "even" in names:
        ins["pair_in"] = (saved["pair_out"], pl.ANY)
    return ins


def backward_last(scal, params, saved, inputs, rank):
    def body(r):
        core, mine, slot = r.scal[0], r.scal[1] == 1, r.scal[2]
        copies, loads = Copies(r.sems), Loads()
        for rows, (_, _, first, count) in zip(own_rows_of(core), CELLS):
            src = [c.at[slot, rows] for c in (r.c_here, r.c_there)]
            loads.add("g", copies.either(mine, *src, r.g.at[pl.ds(first, count)]))
        loads.add("g", *start_params(copies, r))
        start_ff_loads(r, copies, loads, 1)
        start_att_loads(r, copies, loads, 1)
        loads.add("u_own", copies.start(r.x_own.at[1], r.u_own))
        ff_back(r, 1, loads.need)
        ff_weights(r, loads.need)
        copies.out(r.ff_pack, r.pack_out.at[:, pl.ds(0, FF_PACK)])
        attention_back(r, 1, copies, loads.need)
        copies.out(r.att_pack, r.pack_out.at[:, pl.ds(FF_PACK, ATT_PACK)])
        copies.finish()

    ins = {
        "scal": (scal, pltpu.SMEM), **param_inputs(params), **inputs, "rank_in": (rank, pl.ANY), **saved_inputs(saved, SAVED)
    }
    outs = {
        "dx_own_out": ((OWN, D), F32, pl.ANY), "dx_oth_out": (*TOK, pl.ANY),
        "pack_out": ((D, FF_PACK + ATT_PACK), BF, pl.ANY),
    }
    return call(body, ins, outs, {**FF_BUFFERS, **ATT_BUFFERS, **param_buffers()}, sems=64, micros=30)


def backward_first_ff(scal, params, saved, inputs):
    def body(r):
        copies, loads = Copies(r.sems), Loads()
        loads.add("g", copies.start(r.dx_oth, r.g), copies.start(r.dx_own, r.dx))
        loads.add("g", *start_params(copies, r))
        start_ff_loads(r, copies, loads, 0)
        ff_back(r, 0, loads.need)
        core = r.scal[0]
        copies.either(core == 0, r.g_odd, r.g, r.give_out, True)
        copies.either(core == 0, r.g, r.g_odd, r.ship_out.at[core], True)
        copies.out(r.db0, r.db0_out)
        copies.out(r.dr, r.dr_out)
        ff_weights(r, loads.need)
        copies.out(r.ff_pack, r.pack_out)
        copies.finish()

    ins = {"scal": (scal, pltpu.SMEM), **param_inputs(params), **inputs, **saved_inputs(saved, FF_SAVED)}
    outs = {
        "db0_out": (*TOK, pl.ANY), "dr_out": ((OWN, D), F32, pl.ANY), "pack_out": ((D, FF_PACK), BF, pl.ANY),
        "give_out": (*TOK, pl.ANY), "ship_out": (*BOTH, pl.ANY),
    }
    scratch = {**FF_BUFFERS, **param_buffers(), "dx": ((OWN, D), F32)}
    return call(body, ins, outs, scratch, sems=64, micros=7)


def backward_first_att(scal, params, saved, inputs, rank):
    def body(r):
        core, mine, slot = r.scal[0], r.scal[1] == 1, r.scal[2]
        copies, loads = Copies(r.sems), Loads()
        loads.add("w_mix", copies.start(r.db0_in, r.db0), copies.start(r.dr_in, r.dr))
        start_att_loads(r, copies, loads, 0)
        for rows, (_, _, first, count) in zip(own_rows_of(core), CELLS):
            src = [x.at[slot, rows] for x in (r.x_here, r.x_there)]
            loads.add("u_own", copies.either(mine, *src, r.u_own.at[pl.ds(first, count)]))
        loads.add("ff", copies.start(r.ff_in, r.ff_pack))

        loads.need("ff")
        copies.out(r.ff_pack, r.pack_out.at[:, pl.ds(0, FF_PACK)])
        attention_back(r, 0, copies, loads.need)
        copies.out(r.att_pack, r.pack_out.at[:, pl.ds(FF_PACK, ATT_PACK)])
        copies.finish()

    ins = {
        "scal": (scal, pltpu.SMEM), **param_inputs(params), **inputs, "rank_in": (rank, pl.ANY),
        **saved_inputs(saved, ATT_SAVED),
    }
    outs = {"dx_out": (*BOTH, pl.ANY), "pack_out": ((D, PACK), BF, pl.ANY)}
    scratch = {**ATT_BUFFERS, **param_buffers(), "ff_pack": ((D, FF_PACK), BF), "dxw": TOK}
    return call(body, ins, outs, scratch, sems=48, micros=0.001)


def join(first, last):
    count, size, _ = first.shape

    def body(r):
        copies = Copies(r.sems)
        loads = [copies.start(r.last, r.held.at[1]), copies.start(r.first, r.held.at[0])]
        for layer in (1, 0):
            loads[1 - layer].wait()
            total = r.held[layer, 0].astype(F32)
            for n in range(1, count):
                total = total + r.held[layer, n].astype(F32)
            r.sums[:, layer * PACK : (layer + 1) * PACK] = total.astype(BF)
        copies.out(r.sums, r.all_out)
        copies.finish()

    scratch = {"held": ((2, count, size, PACK), BF), "sums": ((size, 2 * PACK), BF)}
    outs = {"all_out": ((size, 2 * PACK), BF, pl.ANY)}
    return call(body, any_inputs(first=first, last=last), outs, scratch, sems=3)["all_out"]


def put_row(copies, held, out, row):
    for half in range(2):
        for start, _, own_first, count in CELLS:
            copies.out(held.at[half, pl.ds(own_first, count)], out.at[0, row, pl.ds(start + half * count, count)])


def finish_outputs(scal, low, high, own_low, own_high, cotangent, params):
    def body(r):
        section, core = r.scal[4], r.scal[0]
        copies = Copies(r.sems)
        here_high = (section == 3) & (core == 1)
        at00, at01 = ((section == s) & (core == 0) for s in (0, 1))
        at10, at11 = ((section == s) & (core == 1) for s in (0, 1))
        loads = [
            copies.choose(
                [(at00, r.own_low), (at01 | at10, r.low0), (at11, r.low1), (section >= 2, r.high0)], r.held.at[0]
            ),
            copies.choose(
                [
                    (at00 | at01 | at10, r.low1), (at11, r.low2),
                    ((section >= 2) & jnp.logical_not(here_high), r.high1), (here_high, r.own_high),
                ],
                r.held.at[1],
            ),
        ]
        for copy in loads:
            copy.wait()

        @pl.when(section < 3)
        def _():
            rest = Copies(r.sems)
            rest.used = copies.used
            for row in range(2):
                put_row(rest, r.held.at[row], r.out, row)
            rest.finish()

        @pl.when(section == 3)
        def _():
            rest = Copies(r.sems)
            rest.used = copies.used
            loads = start_params(rest, r)
            loads.append(rest.start(r.ff_in_in.at[1], r.w_up))
            loads.append(rest.start(r.ff_out_in.at[1], r.w_down))
            for row in range(2):
                for half in range(2):
                    for start, _, own_first, count in CELLS:
                        src = r.cot.at[row, pl.ds(start + half * count, count)]
                        loads.append(rest.start(src, r.g.at[row, half, pl.ds(own_first, count)]))
            for copy in loads:
                copy.wait()

            def step(n, carry):
                row, half = n // 2, n % 2
                for at in range(0, OWN, 256):
                    rows = slice(at, at + 256)
                    even = r.held[row, half, rows, :]
                    pre = nn(even, r.w_up[...]) + param_row(r.ff_bias_in, 1)
                    cdf = 0.5 + 0.5 * lax.erf(pre * 0.7071067811865476)
                    hidden = (pre * cdf).astype(BF)
                    gp = cdf + pre * (0.3989422804014327 * jnp.exp(-0.5 * pre * pre))
                    res = even.astype(F32) + nn(hidden, r.w_down[...]) + param_row(r.ff_bias_out, 1)
                    normed, inv = norm_rows(res)
                    gain = param_row(r.norm_gain, 1, 1)
                    r.held[row, half, rows, :] = (normed * gain + param_row(r.norm_shift, 1, 1)).astype(BF)
                    dres = norm_back(r.g[row, half, rows, :].astype(F32), normed, inv, gain)
                    dp = (nt(dres.astype(BF), r.w_down[...]) * gp).astype(BF)
                    r.g[row, half, rows, :] = (dres + nt(dp, r.w_up[...])).astype(BF)
                return carry

            lax.fori_loop(0, 4, step, 0)
            for row in range(2):
                put_row(rest, r.held.at[row], r.out, row)
                put_row(rest, r.g.at[row], r.grads, row)
            rest.finish()

    ins = {"scal": (scal, pltpu.SMEM), **param_inputs(params)}
    ins.update(any_inputs(low0=low[0], low1=low[1], low2=low[2], high0=high[0], high1=high[1], cot=cotangent))
    ins.update(any_inputs(own_low=own_low, own_high=own_high))
    whole = ((1, 2, ROW, D), BF, pl.ANY)
    scratch = {"held": ((2, 2, OWN, D), BF), "g": ((2, 2, OWN, D), BF), **param_buffers()}
    out = call(body, ins, {"out": whole, "grads": whole}, scratch, sems=48)
    return out["out"], out["grads"]


def finish_grads(scal, first, own_first, second, third, last):
    def body(r):
        section, core = r.scal[4], r.scal[0]
        copies = Copies(r.sems)
        here = (section == 0) & (core == 0)
        loads = [
            copies.choose(
                [(here, r.own), ((section == 0) & jnp.logical_not(here), r.a0), (section == 1, r.b0), (section > 1, r.c0)],
                r.held.at[0],
            ),
            copies.choose([(section == 0, r.a1), (section == 1, r.b1), (section > 1, r.c1)], r.held.at[1]),
        ]
        for row in range(2):
            loads[row].wait()

        @pl.when(section < 3)
        def _():
            rest = Copies(r.sems)
            rest.used = copies.used
            for row in range(2):
                put_row(rest, r.held.at[row], r.out, row)
            rest.finish()

    ins = {"scal": (scal, pltpu.SMEM)}
    ins.update(any_inputs(a0=first[0], a1=first[1], b0=second[0], b1=second[1], c0=third[0], c1=third[1]))
    ins.update(any_inputs(last=last, own=own_first))
    whole = ((1, 2, ROW, D), BF, pl.ANY)
    return call(body, ins, {"out": whole}, {"held": ((2, 2, OWN, D), BF)}, {"last": "out"}, 16)["out"]


def unpack(got):
    count, size, width = got.shape
    wide = ((2, size, 3 * D), F32, pltpu.VMEM)
    square = ((2, size, D), F32, pltpu.VMEM)
    vec = ((2, size), F32, pltpu.VMEM)
    pair = ((2, 2, size), F32, pltpu.VMEM)
    outs = dict(
        proj=wide, out=square, qb=vec, vb=vec, ob=vec, up=square, down=square, ub=vec, db=vec, gain=pair, shift=pair
    )

    def body(r):
        pltpu.sync_copy(r.got, r.held)
        total = r.held[0].astype(F32)
        for n in range(1, count):
            total = total + r.held[n].astype(F32)
        for layer in range(2):
            base = layer * PACK
            ff = total[:, base : base + FF_PACK]
            att = total[:, base + FF_PACK : base + FF_PACK + ATT_PACK]
            r.up[layer] = ff[:, :D]
            r.down[layer] = ff[:, D : 2 * D]
            r.proj[layer] = att[:, : 3 * D]
            r.out[layer] = att[:, 3 * D : 4 * D]
            cols = ff[:, 2 * D :].T
            for ref, k in ((r.ob, 0), (r.ub, 3), (r.db, 4)):
                ref[layer : layer + 1, :] = cols[k : k + 1, :]
            for kind in range(2):
                r.gain[layer, kind : kind + 1, :] = cols[4 * kind + 1 : 4 * kind + 2, :]
                r.shift[layer, kind : kind + 1, :] = cols[4 * kind + 2 : 4 * kind + 3, :]
            cols = att[:, 4 * D :].T
            for ref, k in ((r.qb, 0), (r.vb, 1)):
                ref[layer : layer + 1, :] = cols[k : k + 1, :]

    scratch = {"held": ((count, size, width), BF)}
    return list(call(body, any_inputs(got=got), outs, scratch, sems=1).values())


def make_per_device(dp_count, section_count):
    both = ("dp", "section")

    def index(dp, section):
        return dp * section_count + section

    everyone = [(d, s) for d in range(dp_count) for s in range(section_count)]
    mate_pairs = [(index(d, s), index(d ^ 1, s)) for d, s in everyone]
    fetch_pairs = [(index(d, s), index(d ^ 1, s)) for d, s in everyone if d % 2 == s // 2]

    def send(rows, moves):
        pairs = []
        for d, z in everyone:
            to = moves.get((d % 2, z))
            if to is not None and index(d - d % 2 + z // 2, to) != index(d, z):
                pairs.append((index(d, z), index(d - d % 2 + z // 2, to)))
        return lax.ppermute(rows, both, pairs)

    def ship(rows, sections):
        return [
            send(rows, {(c, z): to for c, to in enumerate(sections) if to is not None for z in (odd, 2 + odd)})
            for odd in range(2)
        ]

    def mate(x):
        return lax.ppermute(x, both, mate_pairs)

    def after(value, *earlier):
        return lax.optimization_barrier((value, earlier))[0]

    def per_device(
        block_input, known_genes, attn_proj, attn_out, query_bias, value_bias, out_bias, ff_in, ff_out,
        ff_bias_in, ff_bias_out, norm_gain, norm_shift, cotangent,
    ):
        params = dict(
            attn_proj=attn_proj, attn_out=attn_out, query_bias=query_bias, value_bias=value_bias, out_bias=out_bias,
            ff_in=ff_in, ff_out=ff_out, ff_bias_in=ff_bias_in, ff_bias_out=ff_bias_out, norm_gain=norm_gain,
            norm_shift=norm_shift,
        )
        dp = lax.axis_index("dp")
        core = dp % 2
        section = lax.axis_index("section")
        mine = (core == section // 2).astype(jnp.int32)
        scal = jnp.stack([core, mine, section % 2, 2 * (section % 2) + core, section, dp // 2]).astype(jnp.int32)

        known_there = lax.ppermute(known_genes, both, fetch_pairs)
        x_there = lax.ppermute(block_input, both, fetch_pairs)
        x_in = any_inputs(x_here=block_input, x_there=x_there)
        f0 = forward_layer(0, scal, params, {**x_in, **any_inputs(known_here=known_genes, known_there=known_there)})
        rank = f0["rank_out"]
        x_own = f0["pair_out"]
        x_oth = mate(x_own)

        def other_half(rows, half):
            return lax.dynamic_update_index_in_dim(rows, half, 1 - core, 0)

        c_there = lax.ppermute(after(cotangent, x_own), both, fetch_pairs)
        missing = lax.dynamic_index_in_dim(x_oth, core, 0, keepdims=False)
        low_rows = other_half(f0["ship_out"], missing)
        got_low = [
            send(low_rows, {(0, 2): 0, (1, 0): 1}),
            send(low_rows, {(1, 2): 1, (1, 1): 1, (0, 3): 0, (0, 1): 0}),
            send(low_rows, {(1, 3): 1}),
        ]
        f1 = forward_layer(1, scal, params, any_inputs(x_own=x_own, x_oth=x_oth, rank_in=rank))
        high_rows = other_half(f1["ship_out"], mate(f1["pair_out"][0]))
        got_high = ship(high_rows, (2, 3))
        b1 = backward_last(after(scal, got_low[0]), params, f1, any_inputs(c_here=cotangent, c_there=c_there, x_own=x_own), rank)
        wide = lax.all_to_all(b1["pack_out"].reshape(dp_count, -1, PACK), "dp", 0, 0)
        ins = any_inputs(dx_own=b1["dx_own_out"], dx_oth=mate(b1["dx_oth_out"]))
        b0 = backward_first_ff(after(scal, got_high[0]), params, f0, ins)
        grad_rows = other_half(b0["ship_out"], mate(after(b0["give_out"], got_low[1:])))
        got_third = ship(grad_rows, (2, None))
        got_second = ship(grad_rows, (None, 1))
        ins = {**x_in, **any_inputs(db0_in=b0["db0_out"], dr_in=b0["dr_out"], ff_in=b0["pack_out"])}
        last = backward_first_att(after(scal, grad_rows), params, f0, ins, rank)

        to_first = [(index(d, s), index(d - 1, s)) for d, s in everyone if d % 2]
        theirs = lax.ppermute(after(last["dx_out"], got_second, got_high[1], wide), both, to_first)
        first_rows = (last["dx_out"].astype(F32) + theirs.astype(F32)).astype(BF)
        got_first = ship(first_rows, (0, None))
        narrow = lax.all_to_all(last["pack_out"].reshape(dp_count, -1, PACK), "dp", 0, 0)
        section_outputs, last_grads = finish_outputs(after(scal, first_rows), got_low, got_high, low_rows, high_rows, cotangent, params)
        held = join(after(narrow, last_grads), wide)
        got = lax.all_to_all(held.reshape(section_count, -1, held.shape[1]), "section", 0, 0)
        grads = unpack(got)
        section_grads = finish_grads(scal, got_first, first_rows, got_second, got_third, last_grads)
        return (section_outputs, section_grads, *grads)

    return per_device


def solution(mesh):
    rows = P("dp", None, None)
    placed = (rows, P("dp", None)) + (P(),) * 11 + (rows,)
    sections = P("section", "dp", None, None)
    matrix = P(None, ("dp", "section"), None)
    vector = P(None, ("dp", "section"))
    pairs = P(None, None, ("dp", "section"))
    return jax.shard_map(
        make_per_device(mesh.shape["dp"], mesh.shape["section"]),
        mesh=mesh,
        in_specs=placed,
        out_specs=(
            sections, sections, matrix, matrix, vector, vector, vector, matrix, matrix, vector, vector, pairs, pairs,
        ),
        check_vma=False,
    )
```

```python
from types import SimpleNamespace

import jax
import jax.numpy as jnp
from jax import lax
from jax.experimental import pallas as pl
from jax.experimental.pallas import tpu as pltpu
from jax.sharding import PartitionSpec as P

D = 512
HEADS = 8
HEAD_DIM = 64
LONG = 1024
SHORT = 512
ROW = LONG + SHORT
EPS = 1e-05
FILL = -1e30
SCALE = HEAD_DIM ** (-0.5)
LOG2E = 1.4426950408889634
LN2 = 0.6931471805599453
SOFT = SCALE * LOG2E
BF = jnp.bfloat16
F32 = jnp.float32
VAUG = HEAD_DIM + 16
ATT_PACK = 4 * D + 128
FF_PACK = 2 * D + 128
PACK = ATT_PACK + FF_PACK
OWN = ROW // 2
CELLS = ((0, LONG, 0, LONG // 2), (LONG, SHORT, LONG // 2, SHORT // 2))
SMALLEST, LARGEST = 2.0 ** -60, 2.0 ** 90
VMEM_LIMIT = 63 * 1024 * 1024
LAYER_PARAMS = (
    "attn_proj", "attn_out", "ff_in", "ff_out",
    "query_bias", "value_bias", "out_bias", "ff_bias_in", "ff_bias_out", "norm_gain", "norm_shift",
)
MATRICES = LAYER_PARAMS[:4]


def nn(a, b):
    return lax.dot_general(a, b, (((1,), (0,)), ((), ())), preferred_element_type=F32)


def nt(a, b):
    return lax.dot_general(a, b, (((1,), (1,)), ((), ())), preferred_element_type=F32)


def tn(a, b):
    return lax.dot_general(a, b, (((0,), (0,)), ((), ())), preferred_element_type=F32)


def call(body, ins, outs, scratch, aliases=None, sems=48, micros=0.001):
    names = list(ins) + list(outs) + list(scratch) + ["sems"]

    def kernel(*refs):
        body(SimpleNamespace(**dict(zip(names, refs))))

    in_names, out_names = list(ins), list(outs)
    result = pl.pallas_call(
        kernel,
        in_specs=[pl.BlockSpec(memory_space=space) for _, space in ins.values()],
        out_specs=[pl.BlockSpec(memory_space=space) for _, _, space in outs.values()],
        out_shape=[jax.ShapeDtypeStruct(shape, dtype) for shape, dtype, _ in outs.values()],
        scratch_shapes=[pltpu.VMEM(shape, dtype) for shape, dtype in scratch.values()] + [pltpu.SemaphoreType.DMA((sems,))],
        input_output_aliases={in_names.index(a): out_names.index(b) for a, b in (aliases or {}).items()},
        compiler_params=pltpu.CompilerParams(vmem_limit_bytes=VMEM_LIMIT),
        cost_estimate=pl.CostEstimate(flops=int(micros * 1150000000), bytes_accessed=2**12, transcendentals=0),
    )(*[array for array, _ in ins.values()])
    return dict(zip(out_names, result))


class Copies:
    def __init__(self, sems):
        self.sems, self.used, self.ends = sems, 0, []

    def start(self, src, dst):
        copy = pltpu.make_async_copy(src, dst, self.sems.at[self.used])
        self.used += 1
        copy.start()
        return copy

    def either(self, first, src_a, src_b, dst, out=False):
        sem = self.sems.at[self.used]
        self.used += 1
        pl.when(first)(lambda: pltpu.make_async_copy(src_a, dst, sem).start())
        pl.when(jnp.logical_not(first))(lambda: pltpu.make_async_copy(src_b, dst, sem).start())
        copy = pltpu.make_async_copy(src_a, dst, sem)
        if out:
            self.ends.append(copy)
        return copy

    def choose(self, cases, dst):
        sem = self.sems.at[self.used]
        self.used += 1
        for holds, src in cases:
            pl.when(holds)(lambda src=src: pltpu.make_async_copy(src, dst, sem).start())
        return pltpu.make_async_copy(cases[0][1], dst, sem)

    def out(self, src, dst):
        self.ends.append(self.start(src, dst))

    def finish(self):
        for copy in self.ends:
            copy.wait()


def norm_rows(residual):
    center = residual - jnp.mean(residual, axis=-1, keepdims=True)
    inv_std = lax.rsqrt(jnp.mean(center * center, axis=-1, keepdims=True) + EPS)
    return center * inv_std, inv_std


def norm_back(grad, normed, inv, gain):
    e = grad * gain
    return inv * (
        e - jnp.mean(e, axis=-1, keepdims=True) - normed * jnp.mean(e * normed, axis=-1, keepdims=True)
    )


def one_hot_rows(rank_row, size, length):
    return (lax.broadcasted_iota(jnp.int32, (size, length), 0) == rank_row).astype(F32).astype(BF)


def one_hot_cols(rank_col, size):
    length = rank_col.shape[0]
    return (lax.broadcasted_iota(jnp.int32, (length, size), 1) == rank_col).astype(F32).astype(BF)


def put_masked(dst, src, tokens):
    zeros = jnp.zeros((HEAD_DIM, tokens), BF)
    for head in range(HEADS):
        part = (head % 2) * HEAD_DIM
        dst[head, part : part + HEAD_DIM, :] = src[head * HEAD_DIM : (head + 1) * HEAD_DIM, :]
        dst[head, HEAD_DIM - part : 2 * HEAD_DIM - part, :] = zeros


def head_sums(a, b):
    out = []
    for head in range(HEADS):
        rows = slice(head * HEAD_DIM, (head + 1) * HEAD_DIM)
        out.append(jnp.sum(a[rows, :].astype(F32) * b[rows, :].astype(F32), axis=0, keepdims=True))
    return out


def rank_tokens(known, length):
    upto = lax.broadcasted_iota(jnp.int32, (length, length), 0) <= lax.broadcasted_iota(jnp.int32, (length, length), 1)
    low = jnp.broadcast_to(known.astype(F32), (8, length))
    place = nn(low.astype(BF), upto.astype(F32).astype(BF))
    return jnp.where(low > 0.5, place - 1.0, -1.0).astype(jnp.int32)


def small_count(length):
    return length // 2 + length // 8


def param_row(ref, layer, kind=None):
    return ref[pl.ds(layer, 1), :] if kind is None else ref[layer, pl.ds(kind, 1), :]


def key_rows(quick):
    sizes = [small_count(length) if quick else length for _, length, _, _ in CELLS]
    return ((0, sizes[0]), (sizes[0], sizes[1])), sum(sizes)


def split_rank(r):
    ranks = [r.rank[:, start : start + length] for start, length, _, _ in CELLS]
    return ranks, [jnp.max(rank[0:1, :]) + 1 for rank in ranks]


def units():
    out = []
    for cell, (_, _, first, count) in enumerate(CELLS):
        for at in range(first, first + count, 256):
            out.append((cell, slice(at, at + 256)))
    return out


def small_counts(counts):
    ok = counts[0] <= small_count(CELLS[0][1])
    for count, (_, length, _, _) in zip(counts[1:], CELLS[1:]):
        ok = ok & (count <= small_count(length))
    return ok


def put_key_bias(r, rows, counts):
    for (first, size), count in zip(rows, counts):
        inside = lax.broadcasted_iota(jnp.int32, (size, 128), 0) < count
        r.kb[first : first + size, :] = jnp.where(inside, 0.0, FILL)


def own_rows_of(core, other=False):
    place = 1 - core if other else core
    return [pl.ds(pl.multiple_of(start + place * count, count), count) for start, _, _, count in CELLS]


def forward_body(r, layer):
    core = r.scal[0]
    copies = Copies(r.sems)
    mine, slot = r.scal[1] == 1, r.scal[2]
    if layer == 0:
        known_in = copies.either(mine, r.known_here, r.known_there, r.known)
        u_in = []
        for buffer, other in ((r.u_own, False), (r.u_oth, True)):
            for rows, (_, _, first, count) in zip(own_rows_of(core, other), CELLS):
                u_in.append(
                    copies.either(
                        mine, r.x_here.at[slot, rows], r.x_there.at[slot, rows], buffer.at[pl.ds(first, count)]
                    )
                )
        u_own_in, u_oth_in = u_in[:2], u_in[2:]
    else:
        rank_in = copies.start(r.rank_in, r.rank)
        u_own_in, u_oth_in = [copies.start(r.x_own.at[1], r.u_own)], [copies.start(r.x_oth.at[1], r.u_oth)]
    w_in = copies.start(r.attn_proj_in.at[layer], r.w)
    small = start_params(copies, r)
    late = [
        copies.start(r.attn_out_in.at[layer], r.w_mix),
        copies.start(r.ff_in_in.at[layer], r.w_up),
        copies.start(r.ff_out_in.at[layer], r.w_down),
    ]

    def save(*names):
        for name in names:
            copies.out(getattr(r, name), getattr(r, name + "_out"))

    if layer == 0:
        known_in.wait()
        for start, length, _, count in CELLS:
            known = r.known[pl.ds(slot, 1), :][:, start : start + length]
            first, second = known[:, :count], known[:, count:]
            known = jnp.concatenate([jnp.where(core == 0, first, second), jnp.where(core == 0, second, first)], axis=1)
            r.rank[:, start : start + length] = rank_tokens(known, length)
        save("rank")
    else:
        rank_in.wait()
    ranks, counts = split_rank(r)
    for copy in small + u_own_in:
        copy.wait()
    w_in.wait()
    own = nn(r.u_own[...], r.w[...])
    r.q_t[...] = (own[:, :D] + param_row(r.query_bias, layer)).astype(BF).T
    r.ko_t[...] = (own[:, D : 2 * D] * SOFT).astype(BF).T
    r.vo_t[...] = (own[:, 2 * D :] + param_row(r.value_bias, layer)).astype(BF).T
    save("q_t", "ko_t", "vo_t")
    put_masked(r.qm, r.q_t, OWN)
    unk = jnp.concatenate(
        [jnp.where(rank[0:1, :count] >= 0, FILL, 0.0) for rank, (_, _, _, count) in zip(ranks, CELLS)], axis=1
    )
    for head, row in enumerate(head_sums(r.q_t, r.ko_t)):
        r.sd[head] = row + unk
        r.total[head] = jnp.zeros_like(row)
        r.top[head] = jnp.zeros_like(row)
    for copy in u_oth_in:
        copy.wait()

    def keys(quick):
        rows, total = key_rows(quick)
        for rank, (_, length, own_first, count), (first, size) in zip(ranks, CELLS, rows):
            pick = one_hot_rows(rank[0:1, :], size, length)
            tokens = slice(own_first, own_first + count)
            uc = nn(pick[:, :count], r.u_own[tokens, :]) + nn(pick[:, count:], r.u_oth[tokens, :])
            r.uc[first : first + size, :] = uc.astype(BF)
        kv = nn(r.uc[:total, :], r.w[:, D:])
        r.k_c[:total, :] = (kv[:, :D] * SOFT).astype(BF)
        ones = []
        for (first, size), known in zip(rows, counts):
            inside = lax.broadcasted_iota(jnp.int32, (size, D), 0) < known
            vc = kv[first : first + size, D:] + param_row(r.value_bias, layer)
            r.v_c[first : first + size, :] = jnp.where(inside, vc, 0.0).astype(BF)
            lane = lax.broadcasted_iota(jnp.int32, (16, size), 1)
            ones.append(((lane < known) & (lax.broadcasted_iota(jnp.int32, (16, size), 0) == 0)).astype(F32))
        vct = r.v_c[:total, :].T
        ones = jnp.concatenate(ones, axis=1).astype(BF)
        for head in range(HEADS):
            r.vaug[head * VAUG : head * VAUG + HEAD_DIM, :total] = vct[head * HEAD_DIM : (head + 1) * HEAD_DIM, :]
            r.vaug[head * VAUG + HEAD_DIM : (head + 1) * VAUG, :total] = ones

    def attend(quick):
        rows_of, _ = key_rows(quick)
        if not quick:
            put_key_bias(r, rows_of, counts)

        def pair(p, carry):
            lanes = pl.ds(pl.multiple_of(p * 128, 128), 128)
            for e in range(2):
                head = 2 * p + e
                feats = pl.ds(pl.multiple_of(head * HEAD_DIM, HEAD_DIM), HEAD_DIM)
                for cell, cols in units():
                    keys_at = slice(rows_of[cell][0], rows_of[cell][0] + rows_of[cell][1])
                    vrows = r.vaug[pl.ds(pl.multiple_of(head * VAUG, 16), VAUG), keys_at]
                    scores = nn(r.k_c[keys_at, lanes], r.qm[head, :, cols])
                    own_score = r.sd[head, :, cols]
                    if quick:
                        low = jnp.exp2(scores).astype(BF)
                    else:
                        tops, probs = [], []
                        for t in range(0, 256, 128):
                            part = scores[:, t : t + 128] + r.kb[keys_at, :]
                            top = jnp.maximum(jnp.max(part, axis=0, keepdims=True), own_score[:, t : t + 128])
                            tops.append(top)
                            probs.append(jnp.exp2(part - top).astype(BF))
                        top = jnp.concatenate(tops, axis=1)
                        low = jnp.concatenate(probs, axis=1)
                        r.top[head, :, cols] = top
                        own_score = own_score - top
                    mixed = nn(vrows, low)
                    own_prob = jnp.exp2(own_score)
                    total = mixed[HEAD_DIM : HEAD_DIM + 1] + own_prob
                    r.total[head, :, cols] = total
                    mixed = mixed[:HEAD_DIM] + own_prob * r.vo_t[feats, cols].astype(F32)
                    r.mix_t[feats, cols] = (mixed * (1.0 / total)).astype(BF)
            return carry

        lax.fori_loop(0, HEADS // 2, pair, 0)

    def run(quick):
        keys(quick)
        attend(quick)

    pl.when(small_counts(counts))(lambda: run(True))
    totals = r.total[...]
    fine = jnp.min(jnp.where((totals > SMALLEST) & (totals < LARGEST), 1, 0)) == 1
    pl.when(jnp.logical_not(fine))(lambda: run(False))
    save("uc", "k_c", "v_c", "mix_t", "top", "total")
    for copy in late:
        copy.wait()

    for at in range(0, OWN, 256):
        rows = slice(at, at + 256)
        res = r.u_own[rows, :].astype(F32) + tn(r.mix_t[:, rows], r.w_mix[...]) + param_row(r.out_bias, layer)
        normed, inv0 = norm_rows(res)
        r.nrm0[rows, :] = normed.astype(BF)
        even = (normed * param_row(r.norm_gain, layer, 0) + param_row(r.norm_shift, layer, 0)).astype(BF)
        r.even[rows, :] = even
        pre = nn(even, r.w_up[...]) + param_row(r.ff_bias_in, layer)
        cdf = 0.5 + 0.5 * lax.erf(pre * 0.7071067811865476)
        hidden = (pre * cdf).astype(BF)
        r.hid[rows, :] = hidden
        r.gp[rows, :] = (cdf + pre * (0.3989422804014327 * jnp.exp(-0.5 * pre * pre))).astype(BF)
        res = even.astype(F32) + nn(hidden, r.w_down[...]) + param_row(r.ff_bias_out, layer)
        normed, inv1 = norm_rows(res)
        r.nrm1[rows, :] = normed.astype(BF)
        r.odd[rows, :] = (normed * param_row(r.norm_gain, layer, 1) + param_row(r.norm_shift, layer, 1)).astype(BF)
        r.inv[rows, :] = jnp.where(lax.broadcasted_iota(jnp.int32, (256, 128), 1) == 0, inv0, inv1)

    copies.out(r.even, r.pair_out.at[0])
    copies.out(r.odd, r.pair_out.at[1])
    if layer == 0:
        copies.either(core == 0, r.even, r.odd, r.ship_out.at[core], True)
    else:
        copies.out(r.even, r.ship_out.at[core])
        copies.out(r.even, r.half_out)
    save("nrm0", "nrm1", "gp", "hid", "inv")
    copies.finish()


TOK = ((OWN, D), BF)
FEAT = ((D, OWN), BF)
KEYS = ((ROW, D), BF)
HEAD_ROWS = ((HEADS, 1, OWN), F32)
RANK = ((8, ROW), jnp.int32)
SAVED = dict(
    even=TOK, q_t=FEAT, ko_t=FEAT, vo_t=FEAT, uc=KEYS, k_c=KEYS, v_c=KEYS, mix_t=FEAT, nrm0=TOK, nrm1=TOK, gp=TOK, hid=TOK,
    inv=((OWN, 128), F32), top=HEAD_ROWS, total=HEAD_ROWS,
)
FF_SAVED = ("nrm1", "inv", "gp", "nrm0", "hid", "even")
ATT_SAVED = ("mix_t", "q_t", "k_c", "v_c", "top", "total", "ko_t", "vo_t", "uc")
BOTH = ((2, OWN, D), BF)


def weight_buffers():
    square = ((D, D), BF)
    return dict(w=((D, 3 * D), BF), w_mix=square, w_up=square, w_down=square)


def param_inputs(params):
    return {name + "_in": (params[name], pl.ANY) for name in LAYER_PARAMS}


def param_buffers():
    pairs = {name: ((2, 2, D) if name.startswith("norm") else (2, D), F32) for name in LAYER_PARAMS[4:]}
    return {**pairs, **weight_buffers()}


def start_params(copies, r):
    return [copies.start(getattr(r, name + "_in"), getattr(r, name)) for name in LAYER_PARAMS[4:]]


def any_inputs(**arrays):
    return {name: (array, pl.ANY) for name, array in arrays.items()}


def forward_layer(layer, scal, params, inputs):
    ins = {"scal": (scal, pltpu.SMEM), **param_inputs(params), **inputs}
    outs = {name + "_out": (*spec, pl.ANY) for name, spec in SAVED.items() if name != "even"}
    outs.update(pair_out=(*BOTH, pl.ANY), ship_out=(*BOTH, pl.ANY))
    scratch = {
        **SAVED, **param_buffers(), "u_own": TOK, "u_oth": TOK, "odd": TOK, "rank": RANK, "qm": ((HEADS, 128, OWN), BF),
        "vaug": ((HEADS * VAUG, ROW), BF), "kb": ((ROW, 128), F32), "sd": HEAD_ROWS,
    }
    if layer == 1:
        outs["half_out"] = (*TOK, pl.ANY)
    if layer == 0:
        outs["rank_out"] = (*RANK, pl.ANY)
        scratch["known"] = ((2, ROW), jnp.int32)
    return call(lambda r: forward_body(r, layer), ins, outs, scratch, micros=20)


def ff_back(r, layer, need):
    sums = [jnp.zeros((1, D), F32) for _ in range(7)]

    def add(slot, value):
        sums[slot] = sums[slot] + jnp.sum(value, axis=0, keepdims=True)

    need("g", "nrm1", "inv", "w_down", "w_up", "gp", "nrm0")
    for at in range(0, OWN, 256):
        rows = slice(at, at + 256)
        if layer == 1:
            grad = r.g[rows, :].astype(F32)
        else:
            low = (r.dx[rows, :] + r.g[rows, :].astype(F32)).astype(BF)
            r.g[rows, :] = low
            grad = low.astype(F32)
        normed = r.nrm1[rows, :].astype(F32)
        add(5, grad * normed)
        add(6, grad)
        dres = norm_back(grad, normed, r.inv[rows, 1:2], param_row(r.norm_gain, layer, 1))
        add(4, dres)
        low = dres.astype(BF)
        r.db1[rows, :] = low
        dp = nt(low, r.w_down[...]) * r.gp[rows, :].astype(F32)
        add(3, dp)
        low = dp.astype(BF)
        r.dpre[rows, :] = low
        low = (dres + nt(low, r.w_up[...])).astype(BF)
        r.g_odd[rows, :] = low
        grad = low.astype(F32)
        normed = r.nrm0[rows, :].astype(F32)
        add(1, grad * normed)
        add(2, grad)
        dres = norm_back(grad, normed, r.inv[rows, 0:1], param_row(r.norm_gain, layer, 0))
        add(0, dres)
        r.dr[rows, :] = dres
        r.db0[rows, :] = dres.astype(BF)
    vectors = jnp.concatenate(sums + [jnp.zeros((121, D), F32)], axis=0)
    r.ff_pack[:, 2 * D :] = vectors.T.astype(BF)


def ff_weights(r, need):
    need("hid", "even")
    r.ff_pack[:, :D] = tn(r.even[...], r.dpre[...]).astype(BF)
    r.ff_pack[:, D : 2 * D] = tn(r.hid[...], r.db1[...]).astype(BF)


def attention_back(r, layer, copies, need):
    core = r.scal[0]
    need("w_mix", "mix_t")
    dm_t = nt(r.w_mix[...], r.db0[...]).astype(BF)
    r.dm_t[...] = dm_t
    dm_sum = jnp.sum(dm_t.astype(F32), axis=1, keepdims=True)
    need("q_t", "top", "total", "ko_t", "vo_t")
    put_masked(r.qm, r.q_t, OWN)
    zeros = jnp.zeros((HEAD_DIM, OWN), BF)
    deltas = head_sums(r.dm_t, r.mix_t)
    for head in range(HEADS):
        rows = slice(head * HEAD_DIM, (head + 1) * HEAD_DIM)
        part = (head % 2) * HEAD_DIM
        inv_total = 1.0 / r.total[head]
        r.total[head] = inv_total
        r.delta[head] = deltas[head] * inv_total
        r.dmm[head, part : part + HEAD_DIM, :] = (r.dm_t[rows, :].astype(F32) * inv_total).astype(BF)
        r.dmm[head, HEAD_DIM - part : 2 * HEAD_DIM - part, :] = zeros
    need("k_c", "v_c", "uc", "w", "rank")
    ranks, counts = split_rank(r)
    quick_ok = small_counts(counts) & (jnp.max(jnp.abs(r.top[...])) == 0.0)

    def run(quick):
        rows_of, total = key_rows(quick)
        r.kc_t[:, :total] = r.k_c[:total, :].T
        if not quick:
            put_key_bias(r, rows_of, counts)

        def pair(p, carry):
            lanes = pl.ds(pl.multiple_of(p * 128, 128), 128)
            late_lanes = pl.ds(pl.multiple_of(D + p * 128, 128), 128)
            dk = [jnp.zeros((size, 128), F32) for _, size in rows_of]
            dv = [jnp.zeros((size, 128), F32) for _, size in rows_of]
            for e in range(2):
                head = 2 * p + e
                feats = pl.ds(pl.multiple_of(head * HEAD_DIM, HEAD_DIM), HEAD_DIM)
                for cell, cols in units():
                    keys_at = slice(rows_of[cell][0], rows_of[cell][0] + rows_of[cell][1])
                    qtm = r.qm[head, :, cols]
                    dmh = r.dmm[head, :, cols]
                    scores = nn(r.k_c[keys_at, lanes], qtm)
                    dprob = nn(r.v_c[keys_at, lanes], dmh)
                    delta = r.delta[head, :, cols]
                    if quick:
                        prob = jnp.exp2(scores)
                        low = prob.astype(BF)
                        ds = (prob * (dprob - delta)).astype(BF)
                    else:
                        top = r.top[head, :, cols]
                        lows, grads = [], []
                        for t in range(0, 256, 128):
                            tile = slice(t, t + 128)
                            prob = jnp.exp2(jnp.minimum(scores[:, tile] - top[:, tile], r.kb[keys_at, :]))
                            lows.append(prob.astype(BF))
                            grads.append((prob * (dprob[:, tile] - delta[:, tile])).astype(BF))
                        low = jnp.concatenate(lows, axis=1)
                        ds = jnp.concatenate(grads, axis=1)
                    dv[cell] = dv[cell] + nt(low, dmh)
                    dk[cell] = dk[cell] + nt(ds, qtm)
                    r.dq_t[feats, cols] = nn(r.kc_t[feats, keys_at], ds) * LN2
            for cell, (first, size) in enumerate(rows_of):
                r.dkv[first : first + size, lanes] = (dk[cell] * SCALE).astype(BF)
                r.dkv[first : first + size, late_lanes] = dv[cell].astype(BF)
            return carry

        lax.fori_loop(0, HEADS // 2, pair, 0)
        dkv = r.dkv[:total, :]
        r.dw_kv[...] = tn(r.uc[:total, :], dkv)
        dxc = nt(dkv, r.w[:, D:]).astype(BF)
        for rank, (_, _, own_first, count), (first, size) in zip(ranks, CELLS, rows_of):
            rank_col = rank.astype(F32).T[:, 0:1].astype(jnp.int32)
            tokens = slice(own_first, own_first + count)
            part = dxc[first : first + size, :]
            r.dr[tokens, :] += nn(one_hot_cols(rank_col[:count, :], size), part)
            r.dxo[tokens, :] = nn(one_hot_cols(rank_col[count:, :], size), part).astype(BF)

    pl.when(quick_ok)(lambda: run(True))
    pl.when(jnp.logical_not(quick_ok))(lambda: run(False))
    if layer == 1:
        copies.out(r.dxo, r.dx_oth_out)
    else:
        copies.out(r.dxo, r.dx_out.at[1 - core])

    unk = jnp.concatenate(
        [jnp.where(rank[0:1, :count] >= 0, FILL, 0.0) for rank, (_, _, _, count) in zip(ranks, CELLS)], axis=1
    )
    own_scores = head_sums(r.q_t, r.ko_t)
    own_dprobs = head_sums(r.dm_t, r.vo_t)
    dq_parts, dk_parts, dv_parts = [], [], []
    for head in range(HEADS):
        rows = slice(head * HEAD_DIM, (head + 1) * HEAD_DIM)
        prob = jnp.exp2(own_scores[head] + unk - r.top[head])
        ds = (prob * (own_dprobs[head] * r.total[head] - r.delta[head])).astype(BF).astype(F32)
        low = (prob * r.total[head]).astype(BF).astype(F32)
        dq_parts.append(r.dq_t[rows, :] + (ds * LN2) * r.ko_t[rows, :].astype(F32))
        dk_parts.append(((ds * SCALE) * r.q_t[rows, :].astype(F32)).astype(BF))
        dv_parts.append((low * r.dm_t[rows, :].astype(F32)).astype(BF))
    dq = jnp.concatenate(dq_parts, axis=0)
    dq_sum = jnp.sum(dq, axis=1, keepdims=True)
    dp = jnp.concatenate([dq.astype(BF)] + dk_parts + dv_parts, axis=0).T
    r.dr[...] += nt(dp, r.w[...])
    if layer == 1:
        copies.out(r.dr, r.dx_own_out)
    else:
        r.dxw[...] = r.dr[...].astype(BF)
        copies.out(r.dxw, r.dx_out.at[core])
    need("u_own")
    dw = tn(r.u_own[...], dp)
    r.att_pack[:, :D] = dw[:, :D].astype(BF)
    r.att_pack[:, D : 3 * D] = (dw[:, D:] + r.dw_kv[...]).astype(BF)
    r.att_pack[:, 3 * D : 4 * D] = nn(r.mix_t[...], r.db0[...]).astype(BF)
    lane = lax.broadcasted_iota(jnp.int32, (D, 128), 1)
    r.att_pack[:, 4 * D :] = jnp.where(lane == 0, dq_sum, jnp.where(lane == 1, dm_sum, 0.0)).astype(BF)


FF_BUFFERS = dict(
    {name: SAVED[name] for name in FF_SAVED}, g=TOK, g_odd=TOK, db0=TOK, db1=TOK, dpre=TOK, dr=((OWN, D), F32),
    ff_pack=((D, FF_PACK), BF),
)
ATT_BUFFERS = dict(
    {name: SAVED[name] for name in ATT_SAVED}, u_own=TOK, db0=TOK, dxo=TOK, dr=((OWN, D), F32), qm=((HEADS, 128, OWN), BF),
    dmm=((HEADS, 128, OWN), BF), dm_t=FEAT, delta=HEAD_ROWS, kc_t=((D, ROW), BF), kb=((ROW, 128), F32),
    dq_t=((D, OWN), F32), dkv=((ROW, 2 * D), BF), dw_kv=((D, 2 * D), F32), att_pack=((D, ATT_PACK), BF), rank=RANK,
)


class Loads:
    def __init__(self):
        self.waiting = {}

    def add(self, name, *copies):
        self.waiting.setdefault(name, []).extend(copies)

    def need(self, *names):
        for name in names:
            for copy in self.waiting.pop(name):
                copy.wait()


def start_ff_loads(r, copies, loads, layer):
    loads.add("even", copies.start(r.pair_in.at[0], r.even))
    for name in FF_SAVED[:3]:
        loads.add(name, copies.start(getattr(r, name + "_in"), getattr(r, name)))
    loads.add("w_down", copies.start(r.ff_out_in.at[layer], r.w_down))
    loads.add("w_up", copies.start(r.ff_in_in.at[layer], r.w_up))
    for name in FF_SAVED[3:5]:
        loads.add(name, copies.start(getattr(r, name + "_in"), getattr(r, name)))


def start_att_loads(r, copies, loads, layer):
    loads.add("w_mix", copies.start(r.attn_out_in.at[layer], r.w_mix))
    for name in ATT_SAVED:
        loads.add(name, copies.start(getattr(r, name + "_in"), getattr(r, name)))
    loads.add("rank", copies.start(r.rank_in, r.rank))
    loads.add("w", copies.start(r.attn_proj_in.at[layer], r.w))


def saved_inputs(saved, names):
    ins = {name + "_in": (saved[name + "_out"], pl.ANY) for name in names if name != "even"}
    if "even" in names:
        ins["pair_in"] = (saved["pair_out"], pl.ANY)
    return ins


def backward_last(scal, params, saved, inputs, rank):
    def body(r):
        core, mine, slot = r.scal[0], r.scal[1] == 1, r.scal[2]
        copies, loads = Copies(r.sems), Loads()
        for rows, (_, _, first, count) in zip(own_rows_of(core), CELLS):
            src = [c.at[slot, rows] for c in (r.c_here, r.c_there)]
            loads.add("g", copies.either(mine, *src, r.g.at[pl.ds(first, count)]))
        loads.add("g", *start_params(copies, r))
        start_ff_loads(r, copies, loads, 1)
        start_att_loads(r, copies, loads, 1)
        loads.add("u_own", copies.start(r.x_own.at[1], r.u_own))
        ff_back(r, 1, loads.need)
        ff_weights(r, loads.need)
        copies.out(r.ff_pack, r.pack_out.at[:, pl.ds(0, FF_PACK)])
        attention_back(r, 1, copies, loads.need)
        copies.out(r.att_pack, r.pack_out.at[:, pl.ds(FF_PACK, ATT_PACK)])
        copies.finish()

    ins = {
        "scal": (scal, pltpu.SMEM), **param_inputs(params), **inputs, "rank_in": (rank, pl.ANY), **saved_inputs(saved, SAVED)
    }
    outs = {
        "dx_own_out": ((OWN, D), F32, pl.ANY), "dx_oth_out": (*TOK, pl.ANY),
        "pack_out": ((D, FF_PACK + ATT_PACK), BF, pl.ANY),
    }
    return call(body, ins, outs, {**FF_BUFFERS, **ATT_BUFFERS, **param_buffers()}, sems=64, micros=30)


def backward_first_ff(scal, params, saved, inputs):
    def body(r):
        copies, loads = Copies(r.sems), Loads()
        loads.add("g", copies.start(r.dx_oth, r.g), copies.start(r.dx_own, r.dx))
        loads.add("g", *start_params(copies, r))
        start_ff_loads(r, copies, loads, 0)
        ff_back(r, 0, loads.need)
        core = r.scal[0]
        copies.either(core == 0, r.g_odd, r.g, r.give_out, True)
        copies.either(core == 0, r.g, r.g_odd, r.ship_out.at[core], True)
        copies.out(r.db0, r.db0_out)
        copies.out(r.dr, r.dr_out)
        ff_weights(r, loads.need)
        copies.out(r.ff_pack, r.pack_out)
        copies.finish()

    ins = {"scal": (scal, pltpu.SMEM), **param_inputs(params), **inputs, **saved_inputs(saved, FF_SAVED)}
    outs = {
        "db0_out": (*TOK, pl.ANY), "dr_out": ((OWN, D), F32, pl.ANY), "pack_out": ((D, FF_PACK), BF, pl.ANY),
        "give_out": (*TOK, pl.ANY), "ship_out": (*BOTH, pl.ANY),
    }
    scratch = {**FF_BUFFERS, **param_buffers(), "dx": ((OWN, D), F32)}
    return call(body, ins, outs, scratch, sems=64, micros=7)


def backward_first_att(scal, params, saved, inputs, rank):
    def body(r):
        core, mine, slot = r.scal[0], r.scal[1] == 1, r.scal[2]
        copies, loads = Copies(r.sems), Loads()
        loads.add("w_mix", copies.start(r.db0_in, r.db0), copies.start(r.dr_in, r.dr))
        start_att_loads(r, copies, loads, 0)
        for rows, (_, _, first, count) in zip(own_rows_of(core), CELLS):
            src = [x.at[slot, rows] for x in (r.x_here, r.x_there)]
            loads.add("u_own", copies.either(mine, *src, r.u_own.at[pl.ds(first, count)]))
        loads.add("ff", copies.start(r.ff_in, r.ff_pack))

        loads.need("ff")
        copies.out(r.ff_pack, r.pack_out.at[:, pl.ds(0, FF_PACK)])
        attention_back(r, 0, copies, loads.need)
        copies.out(r.att_pack, r.pack_out.at[:, pl.ds(FF_PACK, ATT_PACK)])
        copies.finish()

    ins = {
        "scal": (scal, pltpu.SMEM), **param_inputs(params), **inputs, "rank_in": (rank, pl.ANY),
        **saved_inputs(saved, ATT_SAVED),
    }
    outs = {"dx_out": (*BOTH, pl.ANY), "pack_out": ((D, PACK), BF, pl.ANY)}
    scratch = {**ATT_BUFFERS, **param_buffers(), "ff_pack": ((D, FF_PACK), BF), "dxw": TOK}
    return call(body, ins, outs, scratch, sems=48, micros=0.001)


def join(first, last):
    count, size, _ = first.shape

    def body(r):
        copies = Copies(r.sems)
        loads = [copies.start(r.last, r.held.at[1]), copies.start(r.first, r.held.at[0])]
        for layer in (1, 0):
            loads[1 - layer].wait()
            total = r.held[layer, 0].astype(F32)
            for n in range(1, count):
                total = total + r.held[layer, n].astype(F32)
            r.sums[:, layer * PACK : (layer + 1) * PACK] = total.astype(BF)
        copies.out(r.sums, r.all_out)
        copies.finish()

    scratch = {"held": ((2, count, size, PACK), BF), "sums": ((size, 2 * PACK), BF)}
    outs = {"all_out": ((size, 2 * PACK), BF, pl.ANY)}
    return call(body, any_inputs(first=first, last=last), outs, scratch, sems=3)["all_out"]


def put_row(copies, held, out, row):
    for half in range(2):
        for start, _, own_first, count in CELLS:
            copies.out(held.at[half, pl.ds(own_first, count)], out.at[0, row, pl.ds(start + half * count, count)])


def finish_outputs(scal, low, high, own_low, own_high, cotangent, params):
    def body(r):
        section, core = r.scal[4], r.scal[0]
        copies = Copies(r.sems)
        here_high = (section == 3) & (core == 1)
        at00, at01 = ((section == s) & (core == 0) for s in (0, 1))
        at10, at11 = ((section == s) & (core == 1) for s in (0, 1))
        loads = [
            copies.choose(
                [(at00, r.own_low), (at01 | at10, r.low0), (at11, r.low1), (section >= 2, r.high0)], r.held.at[0]
            ),
            copies.choose(
                [
                    (at00 | at01 | at10, r.low1), (at11, r.low2),
                    ((section >= 2) & jnp.logical_not(here_high), r.high1), (here_high, r.own_high),
                ],
                r.held.at[1],
            ),
        ]
        for copy in loads:
            copy.wait()

        @pl.when(section < 3)
        def _():
            rest = Copies(r.sems)
            rest.used = copies.used
            for row in range(2):
                put_row(rest, r.held.at[row], r.out, row)
            rest.finish()

        @pl.when(section == 3)
        def _():
            rest = Copies(r.sems)
            rest.used = copies.used
            loads = start_params(rest, r)
            loads.append(rest.start(r.ff_in_in.at[1], r.w_up))
            loads.append(rest.start(r.ff_out_in.at[1], r.w_down))
            for row in range(2):
                for half in range(2):
                    for start, _, own_first, count in CELLS:
                        src = r.cot.at[row, pl.ds(start + half * count, count)]
                        loads.append(rest.start(src, r.g.at[row, half, pl.ds(own_first, count)]))
            for copy in loads:
                copy.wait()

            def step(n, carry):
                row, half = n // 2, n % 2
                for at in range(0, OWN, 256):
                    rows = slice(at, at + 256)
                    even = r.held[row, half, rows, :]
                    pre = nn(even, r.w_up[...]) + param_row(r.ff_bias_in, 1)
                    cdf = 0.5 + 0.5 * lax.erf(pre * 0.7071067811865476)
                    hidden = (pre * cdf).astype(BF)
                    gp = cdf + pre * (0.3989422804014327 * jnp.exp(-0.5 * pre * pre))
                    res = even.astype(F32) + nn(hidden, r.w_down[...]) + param_row(r.ff_bias_out, 1)
                    normed, inv = norm_rows(res)
                    gain = param_row(r.norm_gain, 1, 1)
                    r.held[row, half, rows, :] = (normed * gain + param_row(r.norm_shift, 1, 1)).astype(BF)
                    dres = norm_back(r.g[row, half, rows, :].astype(F32), normed, inv, gain)
                    dp = (nt(dres.astype(BF), r.w_down[...]) * gp).astype(BF)
                    r.g[row, half, rows, :] = (dres + nt(dp, r.w_up[...])).astype(BF)
                return carry

            lax.fori_loop(0, 4, step, 0)
            for row in range(2):
                put_row(rest, r.held.at[row], r.out, row)
                put_row(rest, r.g.at[row], r.grads, row)
            rest.finish()

    ins = {"scal": (scal, pltpu.SMEM), **param_inputs(params)}
    ins.update(any_inputs(low0=low[0], low1=low[1], low2=low[2], high0=high[0], high1=high[1], cot=cotangent))
    ins.update(any_inputs(own_low=own_low, own_high=own_high))
    whole = ((1, 2, ROW, D), BF, pl.ANY)
    scratch = {"held": ((2, 2, OWN, D), BF), "g": ((2, 2, OWN, D), BF), **param_buffers()}
    out = call(body, ins, {"out": whole, "grads": whole}, scratch, sems=48)
    return out["out"], out["grads"]


def finish_grads(scal, first, own_first, second, third, last):
    def body(r):
        section, core = r.scal[4], r.scal[0]
        copies = Copies(r.sems)
        here = (section == 0) & (core == 0)
        loads = [
            copies.choose(
                [(here, r.own), ((section == 0) & jnp.logical_not(here), r.a0), (section == 1, r.b0), (section > 1, r.c0)],
                r.held.at[0],
            ),
            copies.choose([(section == 0, r.a1), (section == 1, r.b1), (section > 1, r.c1)], r.held.at[1]),
        ]
        @pl.when(section < 3)
        def _():
            rest = Copies(r.sems)
            rest.used = copies.used
            for row in range(2):
                loads[row].wait()
                put_row(rest, r.held.at[row], r.out, row)
            rest.finish()

        @pl.when(section == 3)
        def _():
            for copy in loads:
                copy.wait()

    ins = {"scal": (scal, pltpu.SMEM)}
    ins.update(any_inputs(a0=first[0], a1=first[1], b0=second[0], b1=second[1], c0=third[0], c1=third[1]))
    ins.update(any_inputs(last=last, own=own_first))
    whole = ((1, 2, ROW, D), BF, pl.ANY)
    return call(body, ins, {"out": whole}, {"held": ((2, 2, OWN, D), BF)}, {"last": "out"}, 16)["out"]


def unpack(got):
    count, size, width = got.shape
    wide = ((2, size, 3 * D), F32, pltpu.VMEM)
    square = ((2, size, D), F32, pltpu.VMEM)
    vec = ((2, size), F32, pltpu.VMEM)
    pair = ((2, 2, size), F32, pltpu.VMEM)
    outs = dict(
        proj=wide, out=square, qb=vec, vb=vec, ob=vec, up=square, down=square, ub=vec, db=vec, gain=pair, shift=pair
    )

    def body(r):
        pltpu.sync_copy(r.got, r.held)
        total = r.held[0].astype(F32)
        for n in range(1, count):
            total = total + r.held[n].astype(F32)
        for layer in range(2):
            base = layer * PACK
            ff = total[:, base : base + FF_PACK]
            att = total[:, base + FF_PACK : base + FF_PACK + ATT_PACK]
            r.up[layer] = ff[:, :D]
            r.down[layer] = ff[:, D : 2 * D]
            r.proj[layer] = att[:, : 3 * D]
            r.out[layer] = att[:, 3 * D : 4 * D]
            cols = ff[:, 2 * D :].T
            for ref, k in ((r.ob, 0), (r.ub, 3), (r.db, 4)):
                ref[layer : layer + 1, :] = cols[k : k + 1, :]
            for kind in range(2):
                r.gain[layer, kind : kind + 1, :] = cols[4 * kind + 1 : 4 * kind + 2, :]
                r.shift[layer, kind : kind + 1, :] = cols[4 * kind + 2 : 4 * kind + 3, :]
            cols = att[:, 4 * D :].T
            for ref, k in ((r.qb, 0), (r.vb, 1)):
                ref[layer : layer + 1, :] = cols[k : k + 1, :]

    scratch = {"held": ((count, size, width), BF)}
    return list(call(body, any_inputs(got=got), outs, scratch, sems=1).values())


def make_per_device(dp_count, section_count):
    both = ("dp", "section")

    def index(dp, section):
        return dp * section_count + section

    everyone = [(d, s) for d in range(dp_count) for s in range(section_count)]
    mate_pairs = [(index(d, s), index(d ^ 1, s)) for d, s in everyone]
    fetch_pairs = [(index(d, s), index(d ^ 1, s)) for d, s in everyone if d % 2 == s // 2]

    def send(rows, moves):
        pairs = []
        for d, z in everyone:
            to = moves.get((d % 2, z))
            if to is not None and index(d - d % 2 + z // 2, to) != index(d, z):
                pairs.append((index(d, z), index(d - d % 2 + z // 2, to)))
        return lax.ppermute(rows, both, pairs)

    def ship(rows, sections):
        return [
            send(rows, {(c, z): to for c, to in enumerate(sections) if to is not None for z in (odd, 2 + odd)})
            for odd in range(2)
        ]

    def mate(x):
        return lax.ppermute(x, both, mate_pairs)

    def after(value, *earlier):
        return lax.optimization_barrier((value, earlier))[0]

    def per_device(
        block_input, known_genes, attn_proj, attn_out, query_bias, value_bias, out_bias, ff_in, ff_out,
        ff_bias_in, ff_bias_out, norm_gain, norm_shift, cotangent,
    ):
        params = dict(
            attn_proj=attn_proj, attn_out=attn_out, query_bias=query_bias, value_bias=value_bias, out_bias=out_bias,
            ff_in=ff_in, ff_out=ff_out, ff_bias_in=ff_bias_in, ff_bias_out=ff_bias_out, norm_gain=norm_gain,
            norm_shift=norm_shift,
        )
        dp = lax.axis_index("dp")
        core = dp % 2
        section = lax.axis_index("section")
        mine = (core == section // 2).astype(jnp.int32)
        scal = jnp.stack([core, mine, section % 2, 2 * (section % 2) + core, section, dp // 2]).astype(jnp.int32)

        known_there = lax.ppermute(known_genes, both, fetch_pairs)
        x_there = lax.ppermute(block_input, both, fetch_pairs)
        x_in = any_inputs(x_here=block_input, x_there=x_there)
        f0 = forward_layer(0, scal, params, {**x_in, **any_inputs(known_here=known_genes, known_there=known_there)})
        rank = f0["rank_out"]
        x_own = f0["pair_out"]
        x_oth = mate(x_own)

        def other_half(rows, half):
            return lax.dynamic_update_index_in_dim(rows, half, 1 - core, 0)

        c_there = lax.ppermute(after(cotangent, x_own), both, fetch_pairs)
        missing = lax.dynamic_index_in_dim(x_oth, core, 0, keepdims=False)
        low_rows = other_half(f0["ship_out"], missing)
        got_low = [
            send(low_rows, {(0, 2): 0, (1, 0): 1}),
            send(low_rows, {(1, 2): 1, (1, 1): 1, (0, 3): 0, (0, 1): 0}),
            send(low_rows, {(1, 3): 1}),
        ]
        f1 = forward_layer(1, scal, params, any_inputs(x_own=x_own, x_oth=x_oth, rank_in=rank))
        high_rows = other_half(f1["ship_out"], mate(f1["half_out"]))
        got_high = ship(high_rows, (2, 3))
        b1 = backward_last(after(scal, got_low[0]), params, f1, any_inputs(c_here=cotangent, c_there=c_there, x_own=x_own), rank)
        wide = lax.all_to_all(b1["pack_out"].reshape(dp_count, -1, PACK), "dp", 0, 0)
        ins = any_inputs(dx_own=b1["dx_own_out"], dx_oth=mate(b1["dx_oth_out"]))
        b0 = backward_first_ff(after(scal, got_high[0]), params, f0, ins)
        grad_rows = other_half(b0["ship_out"], mate(after(b0["give_out"], got_low[1:])))
        got_second = ship(grad_rows, (None, 1))
        ins = {**x_in, **any_inputs(db0_in=b0["db0_out"], dr_in=b0["dr_out"], ff_in=b0["pack_out"])}
        last = backward_first_att(after(scal, grad_rows), params, f0, ins, rank)

        to_first = [(index(d, s), index(d - 1, s)) for d, s in everyone if d % 2]
        theirs = lax.ppermute(after(last["dx_out"], got_second, got_high[1], wide), both, to_first)
        first_rows = (last["dx_out"].astype(F32) + theirs.astype(F32)).astype(BF)
        got_first = ship(first_rows, (0, None))
        got_third = ship(after(grad_rows, first_rows), (2, None))
        narrow = lax.all_to_all(last["pack_out"].reshape(dp_count, -1, PACK), "dp", 0, 0)
        section_outputs, last_grads = finish_outputs(after(scal, first_rows), got_low, got_high, low_rows, high_rows, cotangent, params)
        held = join(after(narrow, last_grads), wide)
        got = lax.all_to_all(held.reshape(section_count, -1, held.shape[1]), "section", 0, 0)
        section_grads = finish_grads(scal, got_first, first_rows, got_second, got_third, last_grads)
        grads = unpack(after(got, section_grads))
        return (section_outputs, section_grads, *grads)

    return per_device


def solution(mesh):
    rows = P("dp", None, None)
    placed = (rows, P("dp", None)) + (P(),) * 11 + (rows,)
    sections = P("section", "dp", None, None)
    matrix = P(None, ("dp", "section"), None)
    vector = P(None, ("dp", "section"))
    pairs = P(None, None, ("dp", "section"))
    return jax.shard_map(
        make_per_device(mesh.shape["dp"], mesh.shape["section"]),
        mesh=mesh,
        in_specs=placed,
        out_specs=(
            sections, sections, matrix, matrix, vector, vector, vector, matrix, matrix, vector, vector, pairs, pairs,
        ),
        check_vma=False,
    )
```

```python
from types import SimpleNamespace

import jax
import jax.numpy as jnp
from jax import lax
from jax.experimental import pallas as pl
from jax.experimental.pallas import tpu as pltpu
from jax.sharding import PartitionSpec as P

D = 512
HEADS = 8
HEAD_DIM = 64
LONG = 1024
SHORT = 512
ROW = LONG + SHORT
EPS = 1e-05
FILL = -1e30
SCALE = HEAD_DIM ** (-0.5)
LOG2E = 1.4426950408889634
LN2 = 0.6931471805599453
SOFT = SCALE * LOG2E
BF = jnp.bfloat16
F32 = jnp.float32
VAUG = HEAD_DIM + 16
ATT_PACK = 4 * D + 128
FF_PACK = 2 * D + 128
PACK = ATT_PACK + FF_PACK
OWN = ROW // 2
CELLS = ((0, LONG, 0, LONG // 2), (LONG, SHORT, LONG // 2, SHORT // 2))
SMALLEST, LARGEST = 2.0 ** -60, 2.0 ** 90
VMEM_LIMIT = 63 * 1024 * 1024
LAYER_PARAMS = (
    "attn_proj", "attn_out", "ff_in", "ff_out",
    "query_bias", "value_bias", "out_bias", "ff_bias_in", "ff_bias_out", "norm_gain", "norm_shift",
)
MATRICES = LAYER_PARAMS[:4]


def nn(a, b):
    return lax.dot_general(a, b, (((1,), (0,)), ((), ())), preferred_element_type=F32)


def nt(a, b):
    return lax.dot_general(a, b, (((1,), (1,)), ((), ())), preferred_element_type=F32)


def tn(a, b):
    return lax.dot_general(a, b, (((0,), (0,)), ((), ())), preferred_element_type=F32)


def call(body, ins, outs, scratch, aliases=None, sems=48, micros=0.001):
    names = list(ins) + list(outs) + list(scratch) + ["sems"]

    def kernel(*refs):
        body(SimpleNamespace(**dict(zip(names, refs))))

    in_names, out_names = list(ins), list(outs)
    result = pl.pallas_call(
        kernel,
        in_specs=[pl.BlockSpec(memory_space=space) for _, space in ins.values()],
        out_specs=[pl.BlockSpec(memory_space=space) for _, _, space in outs.values()],
        out_shape=[jax.ShapeDtypeStruct(shape, dtype) for shape, dtype, _ in outs.values()],
        scratch_shapes=[pltpu.VMEM(shape, dtype) for shape, dtype in scratch.values()] + [pltpu.SemaphoreType.DMA((sems,))],
        input_output_aliases={in_names.index(a): out_names.index(b) for a, b in (aliases or {}).items()},
        compiler_params=pltpu.CompilerParams(vmem_limit_bytes=VMEM_LIMIT),
        cost_estimate=pl.CostEstimate(flops=int(micros * 1150000000), bytes_accessed=2**12, transcendentals=0),
    )(*[array for array, _ in ins.values()])
    return dict(zip(out_names, result))


class Copies:
    def __init__(self, sems):
        self.sems, self.used, self.ends = sems, 0, []

    def start(self, src, dst):
        copy = pltpu.make_async_copy(src, dst, self.sems.at[self.used])
        self.used += 1
        copy.start()
        return copy

    def either(self, first, src_a, src_b, dst, out=False):
        sem = self.sems.at[self.used]
        self.used += 1
        pl.when(first)(lambda: pltpu.make_async_copy(src_a, dst, sem).start())
        pl.when(jnp.logical_not(first))(lambda: pltpu.make_async_copy(src_b, dst, sem).start())
        copy = pltpu.make_async_copy(src_a, dst, sem)
        if out:
            self.ends.append(copy)
        return copy

    def choose(self, cases, dst):
        sem = self.sems.at[self.used]
        self.used += 1
        for holds, src in cases:
            pl.when(holds)(lambda src=src: pltpu.make_async_copy(src, dst, sem).start())
        return pltpu.make_async_copy(cases[0][1], dst, sem)

    def out(self, src, dst):
        self.ends.append(self.start(src, dst))

    def finish(self):
        for copy in self.ends:
            copy.wait()


def norm_rows(residual):
    center = residual - jnp.mean(residual, axis=-1, keepdims=True)
    inv_std = lax.rsqrt(jnp.mean(center * center, axis=-1, keepdims=True) + EPS)
    return center * inv_std, inv_std


def norm_back(grad, normed, inv, gain):
    e = grad * gain
    return inv * (
        e - jnp.mean(e, axis=-1, keepdims=True) - normed * jnp.mean(e * normed, axis=-1, keepdims=True)
    )


def one_hot_rows(rank_row, size, length):
    return (lax.broadcasted_iota(jnp.int32, (size, length), 0) == rank_row).astype(F32).astype(BF)


def one_hot_cols(rank_col, size):
    length = rank_col.shape[0]
    return (lax.broadcasted_iota(jnp.int32, (length, size), 1) == rank_col).astype(F32).astype(BF)


def put_masked(dst, src, tokens):
    zeros = jnp.zeros((HEAD_DIM, tokens), BF)
    for head in range(HEADS):
        part = (head % 2) * HEAD_DIM
        dst[head, part : part + HEAD_DIM, :] = src[head * HEAD_DIM : (head + 1) * HEAD_DIM, :]
        dst[head, HEAD_DIM - part : 2 * HEAD_DIM - part, :] = zeros


def head_sums(a, b):
    out = []
    for head in range(HEADS):
        rows = slice(head * HEAD_DIM, (head + 1) * HEAD_DIM)
        out.append(jnp.sum(a[rows, :].astype(F32) * b[rows, :].astype(F32), axis=0, keepdims=True))
    return out


def rank_tokens(known, length):
    upto = lax.broadcasted_iota(jnp.int32, (length, length), 0) <= lax.broadcasted_iota(jnp.int32, (length, length), 1)
    low = jnp.broadcast_to(known.astype(F32), (8, length))
    place = nn(low.astype(BF), upto.astype(F32).astype(BF))
    return jnp.where(low > 0.5, place - 1.0, -1.0).astype(jnp.int32)


def small_count(length):
    return length // 2 + length // 8


def param_row(ref, layer, kind=None):
    return ref[pl.ds(layer, 1), :] if kind is None else ref[layer, pl.ds(kind, 1), :]


def key_rows(quick):
    sizes = [small_count(length) if quick else length for _, length, _, _ in CELLS]
    return ((0, sizes[0]), (sizes[0], sizes[1])), sum(sizes)


def split_rank(r):
    ranks = [r.rank[:, start : start + length] for start, length, _, _ in CELLS]
    return ranks, [jnp.max(rank[0:1, :]) + 1 for rank in ranks]


def units():
    out = []
    for cell, (_, _, first, count) in enumerate(CELLS):
        for at in range(first, first + count, 256):
            out.append((cell, slice(at, at + 256)))
    return out


def small_counts(counts):
    ok = counts[0] <= small_count(CELLS[0][1])
    for count, (_, length, _, _) in zip(counts[1:], CELLS[1:]):
        ok = ok & (count <= small_count(length))
    return ok


def put_key_bias(r, rows, counts):
    for (first, size), count in zip(rows, counts):
        inside = lax.broadcasted_iota(jnp.int32, (size, 128), 0) < count
        r.kb[first : first + size, :] = jnp.where(inside, 0.0, FILL)


def own_rows_of(core, other=False):
    place = 1 - core if other else core
    return [pl.ds(pl.multiple_of(start + place * count, count), count) for start, _, _, count in CELLS]


def forward_body(r, layer):
    core = r.scal[0]
    copies = Copies(r.sems)
    mine, slot = r.scal[1] == 1, r.scal[2]
    if layer == 0:
        known_in = copies.either(mine, r.known_here, r.known_there, r.known)
        u_in = []
        for buffer, other in ((r.u_own, False), (r.u_oth, True)):
            for rows, (_, _, first, count) in zip(own_rows_of(core, other), CELLS):
                u_in.append(
                    copies.either(
                        mine, r.x_here.at[slot, rows], r.x_there.at[slot, rows], buffer.at[pl.ds(first, count)]
                    )
                )
        u_own_in, u_oth_in = u_in[:2], u_in[2:]
    else:
        rank_in = copies.start(r.rank_in, r.rank)
        u_own_in, u_oth_in = [copies.start(r.x_own.at[1], r.u_own)], [copies.start(r.x_oth.at[1], r.u_oth)]
    w_in = copies.start(r.attn_proj_in.at[layer], r.w)
    small = start_params(copies, r)
    late = [
        copies.start(r.attn_out_in.at[layer], r.w_mix),
        copies.start(r.ff_in_in.at[layer], r.w_up),
        copies.start(r.ff_out_in.at[layer], r.w_down),
    ]

    def save(*names):
        for name in names:
            copies.out(getattr(r, name), getattr(r, name + "_out"))

    if layer == 0:
        known_in.wait()
        for start, length, _, count in CELLS:
            known = r.known[pl.ds(slot, 1), :][:, start : start + length]
            first, second = known[:, :count], known[:, count:]
            known = jnp.concatenate([jnp.where(core == 0, first, second), jnp.where(core == 0, second, first)], axis=1)
            r.rank[:, start : start + length] = rank_tokens(known, length)
        save("rank")
    else:
        rank_in.wait()
    ranks, counts = split_rank(r)
    for copy in small + u_own_in:
        copy.wait()
    w_in.wait()
    own = nn(r.u_own[...], r.w[...])
    r.q_t[...] = (own[:, :D] + param_row(r.query_bias, layer)).astype(BF).T
    r.ko_t[...] = (own[:, D : 2 * D] * SOFT).astype(BF).T
    r.vo_t[...] = (own[:, 2 * D :] + param_row(r.value_bias, layer)).astype(BF).T
    save("q_t", "ko_t", "vo_t")
    put_masked(r.qm, r.q_t, OWN)
    unk = jnp.concatenate(
        [jnp.where(rank[0:1, :count] >= 0, FILL, 0.0) for rank, (_, _, _, count) in zip(ranks, CELLS)], axis=1
    )
    for head, row in enumerate(head_sums(r.q_t, r.ko_t)):
        r.sd[head] = row + unk
        r.total[head] = jnp.zeros_like(row)
        r.top[head] = jnp.zeros_like(row)
    for copy in u_oth_in:
        copy.wait()

    def keys(quick):
        rows, total = key_rows(quick)
        for rank, (_, length, own_first, count), (first, size) in zip(ranks, CELLS, rows):
            pick = one_hot_rows(rank[0:1, :], size, length)
            tokens = slice(own_first, own_first + count)
            uc = nn(pick[:, :count], r.u_own[tokens, :]) + nn(pick[:, count:], r.u_oth[tokens, :])
            r.uc[first : first + size, :] = uc.astype(BF)
        kv = nn(r.uc[:total, :], r.w[:, D:])
        r.k_c[:total, :] = (kv[:, :D] * SOFT).astype(BF)
        ones = []
        for (first, size), known in zip(rows, counts):
            inside = lax.broadcasted_iota(jnp.int32, (size, D), 0) < known
            vc = kv[first : first + size, D:] + param_row(r.value_bias, layer)
            r.v_c[first : first + size, :] = jnp.where(inside, vc, 0.0).astype(BF)
            lane = lax.broadcasted_iota(jnp.int32, (16, size), 1)
            ones.append(((lane < known) & (lax.broadcasted_iota(jnp.int32, (16, size), 0) == 0)).astype(F32))
        vct = r.v_c[:total, :].T
        ones = jnp.concatenate(ones, axis=1).astype(BF)
        for head in range(HEADS):
            r.vaug[head * VAUG : head * VAUG + HEAD_DIM, :total] = vct[head * HEAD_DIM : (head + 1) * HEAD_DIM, :]
            r.vaug[head * VAUG + HEAD_DIM : (head + 1) * VAUG, :total] = ones

    def attend(quick):
        rows_of, _ = key_rows(quick)
        if not quick:
            put_key_bias(r, rows_of, counts)

        def pair(p, carry):
            lanes = pl.ds(pl.multiple_of(p * 128, 128), 128)
            for e in range(2):
                head = 2 * p + e
                feats = pl.ds(pl.multiple_of(head * HEAD_DIM, HEAD_DIM), HEAD_DIM)
                for cell, cols in units():
                    keys_at = slice(rows_of[cell][0], rows_of[cell][0] + rows_of[cell][1])
                    vrows = r.vaug[pl.ds(pl.multiple_of(head * VAUG, 16), VAUG), keys_at]
                    scores = nn(r.k_c[keys_at, lanes], r.qm[head, :, cols])
                    own_score = r.sd[head, :, cols]
                    if quick:
                        low = jnp.exp2(scores).astype(BF)
                    else:
                        tops, probs = [], []
                        for t in range(0, 256, 128):
                            part = scores[:, t : t + 128] + r.kb[keys_at, :]
                            top = jnp.maximum(jnp.max(part, axis=0, keepdims=True), own_score[:, t : t + 128])
                            tops.append(top)
                            probs.append(jnp.exp2(part - top).astype(BF))
                        top = jnp.concatenate(tops, axis=1)
                        low = jnp.concatenate(probs, axis=1)
                        r.top[head, :, cols] = top
                        own_score = own_score - top
                    mixed = nn(vrows, low)
                    own_prob = jnp.exp2(own_score)
                    total = mixed[HEAD_DIM : HEAD_DIM + 1] + own_prob
                    r.total[head, :, cols] = total
                    mixed = mixed[:HEAD_DIM] + own_prob * r.vo_t[feats, cols].astype(F32)
                    r.mix_t[feats, cols] = (mixed * (1.0 / total)).astype(BF)
            return carry

        if quick:
            lax.fori_loop(0, HEADS // 4, lambda n, carry: pair(2 * n + 1, pair(2 * n, carry)), 0)
        else:
            lax.fori_loop(0, HEADS // 2, pair, 0)

    def run(quick):
        keys(quick)
        attend(quick)

    pl.when(small_counts(counts))(lambda: run(True))
    totals = r.total[...]
    fine = jnp.min(jnp.where((totals > SMALLEST) & (totals < LARGEST), 1, 0)) == 1
    pl.when(jnp.logical_not(fine))(lambda: run(False))
    save("uc", "k_c", "v_c", "mix_t", "top", "total")
    for copy in late:
        copy.wait()

    for at in range(0, OWN, 256):
        rows = slice(at, at + 256)
        res = r.u_own[rows, :].astype(F32) + tn(r.mix_t[:, rows], r.w_mix[...]) + param_row(r.out_bias, layer)
        normed, inv0 = norm_rows(res)
        r.nrm0[rows, :] = normed.astype(BF)
        even = (normed * param_row(r.norm_gain, layer, 0) + param_row(r.norm_shift, layer, 0)).astype(BF)
        r.even[rows, :] = even
        pre = nn(even, r.w_up[...]) + param_row(r.ff_bias_in, layer)
        cdf = 0.5 + 0.5 * lax.erf(pre * 0.7071067811865476)
        hidden = (pre * cdf).astype(BF)
        r.hid[rows, :] = hidden
        r.gp[rows, :] = (cdf + pre * (0.3989422804014327 * jnp.exp(-0.5 * pre * pre))).astype(BF)
        res = even.astype(F32) + nn(hidden, r.w_down[...]) + param_row(r.ff_bias_out, layer)
        normed, inv1 = norm_rows(res)
        r.nrm1[rows, :] = normed.astype(BF)
        r.odd[rows, :] = (normed * param_row(r.norm_gain, layer, 1) + param_row(r.norm_shift, layer, 1)).astype(BF)
        r.inv[rows, :] = jnp.where(lax.broadcasted_iota(jnp.int32, (256, 128), 1) == 0, inv0, inv1)

    copies.out(r.even, r.pair_out.at[0])
    copies.out(r.odd, r.pair_out.at[1])
    if layer == 0:
        copies.either(core == 0, r.even, r.odd, r.ship_out.at[core], True)
    else:
        copies.out(r.even, r.ship_out.at[core])
        copies.out(r.even, r.half_out)
    save("nrm0", "nrm1", "gp", "hid", "inv")
    copies.finish()


TOK = ((OWN, D), BF)
FEAT = ((D, OWN), BF)
KEYS = ((ROW, D), BF)
HEAD_ROWS = ((HEADS, 1, OWN), F32)
RANK = ((8, ROW), jnp.int32)
SAVED = dict(
    even=TOK, q_t=FEAT, ko_t=FEAT, vo_t=FEAT, uc=KEYS, k_c=KEYS, v_c=KEYS, mix_t=FEAT, nrm0=TOK, nrm1=TOK, gp=TOK, hid=TOK,
    inv=((OWN, 128), F32), top=HEAD_ROWS, total=HEAD_ROWS,
)
FF_SAVED = ("nrm1", "inv", "gp", "nrm0", "hid", "even")
ATT_SAVED = ("mix_t", "q_t", "k_c", "v_c", "top", "total", "ko_t", "vo_t", "uc")
BOTH = ((2, OWN, D), BF)


def weight_buffers():
    square = ((D, D), BF)
    return dict(w=((D, 3 * D), BF), w_mix=square, w_up=square, w_down=square)


def param_inputs(params):
    return {name + "_in": (params[name], pl.ANY) for name in LAYER_PARAMS}


def param_buffers():
    pairs = {name: ((2, 2, D) if name.startswith("norm") else (2, D), F32) for name in LAYER_PARAMS[4:]}
    return {**pairs, **weight_buffers()}


def start_params(copies, r):
    return [copies.start(getattr(r, name + "_in"), getattr(r, name)) for name in LAYER_PARAMS[4:]]


def any_inputs(**arrays):
    return {name: (array, pl.ANY) for name, array in arrays.items()}


def forward_layer(layer, scal, params, inputs):
    ins = {"scal": (scal, pltpu.SMEM), **param_inputs(params), **inputs}
    outs = {name + "_out": (*spec, pl.ANY) for name, spec in SAVED.items() if name != "even"}
    outs.update(pair_out=(*BOTH, pl.ANY), ship_out=(*BOTH, pl.ANY))
    scratch = {
        **SAVED, **param_buffers(), "u_own": TOK, "u_oth": TOK, "odd": TOK, "rank": RANK, "qm": ((HEADS, 128, OWN), BF),
        "vaug": ((HEADS * VAUG, ROW), BF), "kb": ((ROW, 128), F32), "sd": HEAD_ROWS,
    }
    if layer == 1:
        outs["half_out"] = (*TOK, pl.ANY)
    if layer == 0:
        outs["rank_out"] = (*RANK, pl.ANY)
        scratch["known"] = ((2, ROW), jnp.int32)
    return call(lambda r: forward_body(r, layer), ins, outs, scratch, micros=20)


def ff_back(r, layer, need):
    sums = [jnp.zeros((1, D), F32) for _ in range(7)]

    def add(slot, value):
        sums[slot] = sums[slot] + jnp.sum(value, axis=0, keepdims=True)

    need("g", "nrm1", "inv", "w_down", "w_up", "gp", "nrm0")
    for at in range(0, OWN, 256):
        rows = slice(at, at + 256)
        if layer == 1:
            grad = r.g[rows, :].astype(F32)
        else:
            low = (r.dx[rows, :] + r.g[rows, :].astype(F32)).astype(BF)
            r.g[rows, :] = low
            grad = low.astype(F32)
        normed = r.nrm1[rows, :].astype(F32)
        add(5, grad * normed)
        add(6, grad)
        dres = norm_back(grad, normed, r.inv[rows, 1:2], param_row(r.norm_gain, layer, 1))
        add(4, dres)
        low = dres.astype(BF)
        r.db1[rows, :] = low
        dp = nt(low, r.w_down[...]) * r.gp[rows, :].astype(F32)
        add(3, dp)
        low = dp.astype(BF)
        r.dpre[rows, :] = low
        low = (dres + nt(low, r.w_up[...])).astype(BF)
        r.g_odd[rows, :] = low
        grad = low.astype(F32)
        normed = r.nrm0[rows, :].astype(F32)
        add(1, grad * normed)
        add(2, grad)
        dres = norm_back(grad, normed, r.inv[rows, 0:1], param_row(r.norm_gain, layer, 0))
        add(0, dres)
        r.dr[rows, :] = dres
        r.db0[rows, :] = dres.astype(BF)
    vectors = jnp.concatenate(sums + [jnp.zeros((121, D), F32)], axis=0)
    r.ff_pack[:, 2 * D :] = vectors.T.astype(BF)


def ff_weights(r, need):
    need("hid", "even")
    r.ff_pack[:, :D] = tn(r.even[...], r.dpre[...]).astype(BF)
    r.ff_pack[:, D : 2 * D] = tn(r.hid[...], r.db1[...]).astype(BF)


def attention_back(r, layer, copies, need):
    core = r.scal[0]
    need("w_mix", "mix_t")
    dm_t = nt(r.w_mix[...], r.db0[...]).astype(BF)
    r.dm_t[...] = dm_t
    dm_sum = jnp.sum(dm_t.astype(F32), axis=1, keepdims=True)
    need("q_t", "top", "total", "ko_t", "vo_t")
    put_masked(r.qm, r.q_t, OWN)
    zeros = jnp.zeros((HEAD_DIM, OWN), BF)
    deltas = head_sums(r.dm_t, r.mix_t)
    for head in range(HEADS):
        rows = slice(head * HEAD_DIM, (head + 1) * HEAD_DIM)
        part = (head % 2) * HEAD_DIM
        inv_total = 1.0 / r.total[head]
        r.total[head] = inv_total
        r.delta[head] = deltas[head] * inv_total
        r.dmm[head, part : part + HEAD_DIM, :] = (r.dm_t[rows, :].astype(F32) * inv_total).astype(BF)
        r.dmm[head, HEAD_DIM - part : 2 * HEAD_DIM - part, :] = zeros
    need("k_c", "v_c", "uc", "w", "rank")
    ranks, counts = split_rank(r)
    quick_ok = small_counts(counts) & (jnp.max(jnp.abs(r.top[...])) == 0.0)

    def run(quick):
        rows_of, total = key_rows(quick)
        r.kc_t[:, :total] = r.k_c[:total, :].T
        if not quick:
            put_key_bias(r, rows_of, counts)

        def pair(p, carry):
            lanes = pl.ds(pl.multiple_of(p * 128, 128), 128)
            late_lanes = pl.ds(pl.multiple_of(D + p * 128, 128), 128)
            dk = [jnp.zeros((size, 128), F32) for _, size in rows_of]
            dv = [jnp.zeros((size, 128), F32) for _, size in rows_of]
            for e in range(2):
                head = 2 * p + e
                feats = pl.ds(pl.multiple_of(head * HEAD_DIM, HEAD_DIM), HEAD_DIM)
                for cell, cols in units():
                    keys_at = slice(rows_of[cell][0], rows_of[cell][0] + rows_of[cell][1])
                    qtm = r.qm[head, :, cols]
                    dmh = r.dmm[head, :, cols]
                    scores = nn(r.k_c[keys_at, lanes], qtm)
                    dprob = nn(r.v_c[keys_at, lanes], dmh)
                    delta = r.delta[head, :, cols]
                    if quick:
                        prob = jnp.exp2(scores)
                        low = prob.astype(BF)
                        ds = (prob * (dprob - delta)).astype(BF)
                    else:
                        top = r.top[head, :, cols]
                        lows, grads = [], []
                        for t in range(0, 256, 128):
                            tile = slice(t, t + 128)
                            prob = jnp.exp2(jnp.minimum(scores[:, tile] - top[:, tile], r.kb[keys_at, :]))
                            lows.append(prob.astype(BF))
                            grads.append((prob * (dprob[:, tile] - delta[:, tile])).astype(BF))
                        low = jnp.concatenate(lows, axis=1)
                        ds = jnp.concatenate(grads, axis=1)
                    dv[cell] = dv[cell] + nt(low, dmh)
                    dk[cell] = dk[cell] + nt(ds, qtm)
                    r.dq_t[feats, cols] = nn(r.kc_t[feats, keys_at], ds) * LN2
            for cell, (first, size) in enumerate(rows_of):
                r.dkv[first : first + size, lanes] = (dk[cell] * SCALE).astype(BF)
                r.dkv[first : first + size, late_lanes] = dv[cell].astype(BF)
            return carry

        if quick:
            lax.fori_loop(0, HEADS // 4, lambda n, carry: pair(2 * n + 1, pair(2 * n, carry)), 0)
        else:
            lax.fori_loop(0, HEADS // 2, pair, 0)
        dkv = r.dkv[:total, :]
        r.dw_kv[...] = tn(r.uc[:total, :], dkv)
        dxc = nt(dkv, r.w[:, D:]).astype(BF)
        for rank, (_, _, own_first, count), (first, size) in zip(ranks, CELLS, rows_of):
            rank_col = rank.astype(F32).T[:, 0:1].astype(jnp.int32)
            tokens = slice(own_first, own_first + count)
            part = dxc[first : first + size, :]
            r.dr[tokens, :] += nn(one_hot_cols(rank_col[:count, :], size), part)
            r.dxo[tokens, :] = nn(one_hot_cols(rank_col[count:, :], size), part).astype(BF)

    pl.when(quick_ok)(lambda: run(True))
    pl.when(jnp.logical_not(quick_ok))(lambda: run(False))
    if layer == 1:
        copies.out(r.dxo, r.dx_oth_out)
    else:
        copies.out(r.dxo, r.dx_out.at[1 - core])

    unk = jnp.concatenate(
        [jnp.where(rank[0:1, :count] >= 0, FILL, 0.0) for rank, (_, _, _, count) in zip(ranks, CELLS)], axis=1
    )
    own_scores = head_sums(r.q_t, r.ko_t)
    own_dprobs = head_sums(r.dm_t, r.vo_t)
    dq_parts, dk_parts, dv_parts = [], [], []
    for head in range(HEADS):
        rows = slice(head * HEAD_DIM, (head + 1) * HEAD_DIM)
        prob = jnp.exp2(own_scores[head] + unk - r.top[head])
        ds = (prob * (own_dprobs[head] * r.total[head] - r.delta[head])).astype(BF).astype(F32)
        low = (prob * r.total[head]).astype(BF).astype(F32)
        dq_parts.append(r.dq_t[rows, :] + (ds * LN2) * r.ko_t[rows, :].astype(F32))
        dk_parts.append(((ds * SCALE) * r.q_t[rows, :].astype(F32)).astype(BF))
        dv_parts.append((low * r.dm_t[rows, :].astype(F32)).astype(BF))
    dq = jnp.concatenate(dq_parts, axis=0)
    dq_sum = jnp.sum(dq, axis=1, keepdims=True)
    dp = jnp.concatenate([dq.astype(BF)] + dk_parts + dv_parts, axis=0).T
    r.dr[...] += nt(dp, r.w[...])
    if layer == 1:
        copies.out(r.dr, r.dx_own_out)
    else:
        r.dxw[...] = r.dr[...].astype(BF)
        copies.out(r.dxw, r.dx_out.at[core])
    need("u_own")
    dw = tn(r.u_own[...], dp)
    r.att_pack[:, :D] = dw[:, :D].astype(BF)
    r.att_pack[:, D : 3 * D] = (dw[:, D:] + r.dw_kv[...]).astype(BF)
    r.att_pack[:, 3 * D : 4 * D] = nn(r.mix_t[...], r.db0[...]).astype(BF)
    lane = lax.broadcasted_iota(jnp.int32, (D, 128), 1)
    r.att_pack[:, 4 * D :] = jnp.where(lane == 0, dq_sum, jnp.where(lane == 1, dm_sum, 0.0)).astype(BF)


FF_BUFFERS = dict(
    {name: SAVED[name] for name in FF_SAVED}, g=TOK, g_odd=TOK, db0=TOK, db1=TOK, dpre=TOK, dr=((OWN, D), F32),
    ff_pack=((D, FF_PACK), BF),
)
ATT_BUFFERS = dict(
    {name: SAVED[name] for name in ATT_SAVED}, u_own=TOK, db0=TOK, dxo=TOK, dr=((OWN, D), F32), qm=((HEADS, 128, OWN), BF),
    dmm=((HEADS, 128, OWN), BF), dm_t=FEAT, delta=HEAD_ROWS, kc_t=((D, ROW), BF), kb=((ROW, 128), F32),
    dq_t=((D, OWN), F32), dkv=((ROW, 2 * D), BF), dw_kv=((D, 2 * D), F32), att_pack=((D, ATT_PACK), BF), rank=RANK,
)


class Loads:
    def __init__(self):
        self.waiting = {}

    def add(self, name, *copies):
        self.waiting.setdefault(name, []).extend(copies)

    def need(self, *names):
        for name in names:
            for copy in self.waiting.pop(name):
                copy.wait()


def start_ff_loads(r, copies, loads, layer):
    loads.add("even", copies.start(r.pair_in.at[0], r.even))
    for name in FF_SAVED[:3]:
        loads.add(name, copies.start(getattr(r, name + "_in"), getattr(r, name)))
    loads.add("w_down", copies.start(r.ff_out_in.at[layer], r.w_down))
    loads.add("w_up", copies.start(r.ff_in_in.at[layer], r.w_up))
    for name in FF_SAVED[3:5]:
        loads.add(name, copies.start(getattr(r, name + "_in"), getattr(r, name)))


def start_att_loads(r, copies, loads, layer):
    loads.add("w_mix", copies.start(r.attn_out_in.at[layer], r.w_mix))
    for name in ATT_SAVED:
        loads.add(name, copies.start(getattr(r, name + "_in"), getattr(r, name)))
    loads.add("rank", copies.start(r.rank_in, r.rank))
    loads.add("w", copies.start(r.attn_proj_in.at[layer], r.w))


def saved_inputs(saved, names):
    ins = {name + "_in": (saved[name + "_out"], pl.ANY) for name in names if name != "even"}
    if "even" in names:
        ins["pair_in"] = (saved["pair_out"], pl.ANY)
    return ins


def backward_last(scal, params, saved, inputs, rank):
    def body(r):
        core, mine, slot = r.scal[0], r.scal[1] == 1, r.scal[2]
        copies, loads = Copies(r.sems), Loads()
        for rows, (_, _, first, count) in zip(own_rows_of(core), CELLS):
            src = [c.at[slot, rows] for c in (r.c_here, r.c_there)]
            loads.add("g", copies.either(mine, *src, r.g.at[pl.ds(first, count)]))
        loads.add("g", *start_params(copies, r))
        start_ff_loads(r, copies, loads, 1)
        start_att_loads(r, copies, loads, 1)
        loads.add("u_own", copies.start(r.x_own.at[1], r.u_own))
        ff_back(r, 1, loads.need)
        ff_weights(r, loads.need)
        copies.out(r.ff_pack, r.pack_out.at[:, pl.ds(0, FF_PACK)])
        attention_back(r, 1, copies, loads.need)
        copies.out(r.att_pack, r.pack_out.at[:, pl.ds(FF_PACK, ATT_PACK)])
        copies.finish()

    ins = {
        "scal": (scal, pltpu.SMEM), **param_inputs(params), **inputs, "rank_in": (rank, pl.ANY), **saved_inputs(saved, SAVED)
    }
    outs = {
        "dx_own_out": ((OWN, D), F32, pl.ANY), "dx_oth_out": (*TOK, pl.ANY),
        "pack_out": ((D, FF_PACK + ATT_PACK), BF, pl.ANY),
    }
    return call(body, ins, outs, {**FF_BUFFERS, **ATT_BUFFERS, **param_buffers()}, sems=64, micros=30)


def backward_first_ff(scal, params, saved, inputs):
    def body(r):
        copies, loads = Copies(r.sems), Loads()
        loads.add("g", copies.start(r.dx_oth, r.g), copies.start(r.dx_own, r.dx))
        loads.add("g", *start_params(copies, r))
        start_ff_loads(r, copies, loads, 0)
        ff_back(r, 0, loads.need)
        core = r.scal[0]
        copies.either(core == 0, r.g_odd, r.g, r.give_out, True)
        copies.either(core == 0, r.g, r.g_odd, r.ship_out.at[core], True)
        copies.out(r.db0, r.db0_out)
        copies.out(r.dr, r.dr_out)
        ff_weights(r, loads.need)
        copies.out(r.ff_pack, r.pack_out)
        copies.finish()

    ins = {"scal": (scal, pltpu.SMEM), **param_inputs(params), **inputs, **saved_inputs(saved, FF_SAVED)}
    outs = {
        "db0_out": (*TOK, pl.ANY), "dr_out": ((OWN, D), F32, pl.ANY), "pack_out": ((D, FF_PACK), BF, pl.ANY),
        "give_out": (*TOK, pl.ANY), "ship_out": (*BOTH, pl.ANY),
    }
    scratch = {**FF_BUFFERS, **param_buffers(), "dx": ((OWN, D), F32)}
    return call(body, ins, outs, scratch, sems=64, micros=7)


def backward_first_att(scal, params, saved, inputs, rank):
    def body(r):
        core, mine, slot = r.scal[0], r.scal[1] == 1, r.scal[2]
        copies, loads = Copies(r.sems), Loads()
        loads.add("w_mix", copies.start(r.db0_in, r.db0), copies.start(r.dr_in, r.dr))
        start_att_loads(r, copies, loads, 0)
        for rows, (_, _, first, count) in zip(own_rows_of(core), CELLS):
            src = [x.at[slot, rows] for x in (r.x_here, r.x_there)]
            loads.add("u_own", copies.either(mine, *src, r.u_own.at[pl.ds(first, count)]))
        loads.add("ff", copies.start(r.ff_in, r.ff_pack))

        loads.need("ff")
        copies.out(r.ff_pack, r.pack_out.at[:, pl.ds(0, FF_PACK)])
        attention_back(r, 0, copies, loads.need)
        copies.out(r.att_pack, r.pack_out.at[:, pl.ds(FF_PACK, ATT_PACK)])
        copies.finish()

    ins = {
        "scal": (scal, pltpu.SMEM), **param_inputs(params), **inputs, "rank_in": (rank, pl.ANY),
        **saved_inputs(saved, ATT_SAVED),
    }
    outs = {"dx_out": (*BOTH, pl.ANY), "pack_out": ((D, PACK), BF, pl.ANY)}
    scratch = {**ATT_BUFFERS, **param_buffers(), "ff_pack": ((D, FF_PACK), BF), "dxw": TOK}
    return call(body, ins, outs, scratch, sems=48, micros=0.001)


def join(first, last):
    count, size, _ = first.shape

    def body(r):
        copies = Copies(r.sems)
        loads = [copies.start(r.last, r.held.at[1]), copies.start(r.first, r.held.at[0])]
        for layer in (1, 0):
            loads[1 - layer].wait()
            total = r.held[layer, 0].astype(F32)
            for n in range(1, count):
                total = total + r.held[layer, n].astype(F32)
            r.sums[:, layer * PACK : (layer + 1) * PACK] = total.astype(BF)
        copies.out(r.sums, r.all_out)
        copies.finish()

    scratch = {"held": ((2, count, size, PACK), BF), "sums": ((size, 2 * PACK), BF)}
    outs = {"all_out": ((size, 2 * PACK), BF, pl.ANY)}
    return call(body, any_inputs(first=first, last=last), outs, scratch, sems=3)["all_out"]


def put_row(copies, held, out, row):
    for half in range(2):
        for start, _, own_first, count in CELLS:
            copies.out(held.at[half, pl.ds(own_first, count)], out.at[0, row, pl.ds(start + half * count, count)])


def finish_outputs(scal, low, high, own_low, own_high, cotangent, params):
    def body(r):
        section, core = r.scal[4], r.scal[0]
        copies = Copies(r.sems)
        here_high = (section == 3) & (core == 1)
        at00, at01 = ((section == s) & (core == 0) for s in (0, 1))
        at10, at11 = ((section == s) & (core == 1) for s in (0, 1))
        loads = [
            copies.choose(
                [(at00, r.own_low), (at01 | at10, r.low0), (at11, r.low1), (section >= 2, r.high0)], r.held.at[0]
            ),
            copies.choose(
                [
                    (at00 | at01 | at10, r.low1), (at11, r.low2),
                    ((section >= 2) & jnp.logical_not(here_high), r.high1), (here_high, r.own_high),
                ],
                r.held.at[1],
            ),
        ]
        for copy in loads:
            copy.wait()

        @pl.when(section < 3)
        def _():
            rest = Copies(r.sems)
            rest.used = copies.used
            for row in range(2):
                put_row(rest, r.held.at[row], r.out, row)
            rest.finish()

        @pl.when(section == 3)
        def _():
            rest = Copies(r.sems)
            rest.used = copies.used
            loads = start_params(rest, r)
            loads.append(rest.start(r.ff_in_in.at[1], r.w_up))
            loads.append(rest.start(r.ff_out_in.at[1], r.w_down))
            for row in range(2):
                for half in range(2):
                    for start, _, own_first, count in CELLS:
                        src = r.cot.at[row, pl.ds(start + half * count, count)]
                        loads.append(rest.start(src, r.g.at[row, half, pl.ds(own_first, count)]))
            for copy in loads:
                copy.wait()

            def step(n, carry):
                row, half = n // 2, n % 2
                for at in range(0, OWN, 256):
                    rows = slice(at, at + 256)
                    even = r.held[row, half, rows, :]
                    pre = nn(even, r.w_up[...]) + param_row(r.ff_bias_in, 1)
                    cdf = 0.5 + 0.5 * lax.erf(pre * 0.7071067811865476)
                    hidden = (pre * cdf).astype(BF)
                    gp = cdf + pre * (0.3989422804014327 * jnp.exp(-0.5 * pre * pre))
                    res = even.astype(F32) + nn(hidden, r.w_down[...]) + param_row(r.ff_bias_out, 1)
                    normed, inv = norm_rows(res)
                    gain = param_row(r.norm_gain, 1, 1)
                    r.held[row, half, rows, :] = (normed * gain + param_row(r.norm_shift, 1, 1)).astype(BF)
                    dres = norm_back(r.g[row, half, rows, :].astype(F32), normed, inv, gain)
                    dp = (nt(dres.astype(BF), r.w_down[...]) * gp).astype(BF)
                    r.g[row, half, rows, :] = (dres + nt(dp, r.w_up[...])).astype(BF)
                return carry

            lax.fori_loop(0, 4, step, 0)
            for row in range(2):
                put_row(rest, r.held.at[row], r.out, row)
                put_row(rest, r.g.at[row], r.grads, row)
            rest.finish()

    ins = {"scal": (scal, pltpu.SMEM), **param_inputs(params)}
    ins.update(any_inputs(low0=low[0], low1=low[1], low2=low[2], high0=high[0], high1=high[1], cot=cotangent))
    ins.update(any_inputs(own_low=own_low, own_high=own_high))
    whole = ((1, 2, ROW, D), BF, pl.ANY)
    scratch = {"held": ((2, 2, OWN, D), BF), "g": ((2, 2, OWN, D), BF), **param_buffers()}
    out = call(body, ins, {"out": whole, "grads": whole}, scratch, sems=48)
    return out["out"], out["grads"]


def finish_grads(scal, first, own_first, second, third, last):
    def body(r):
        section, core = r.scal[4], r.scal[0]
        copies = Copies(r.sems)
        here = (section == 0) & (core == 0)
        loads = [
            copies.choose(
                [(here, r.own), ((section == 0) & jnp.logical_not(here), r.a0), (section == 1, r.b0), (section > 1, r.c0)],
                r.held.at[0],
            ),
            copies.choose([(section == 0, r.a1), (section == 1, r.b1), (section > 1, r.c1)], r.held.at[1]),
        ]
        @pl.when(section < 3)
        def _():
            rest = Copies(r.sems)
            rest.used = copies.used
            for row in range(2):
                loads[row].wait()
                put_row(rest, r.held.at[row], r.out, row)
            rest.finish()

        @pl.when(section == 3)
        def _():
            for copy in loads:
                copy.wait()

    ins = {"scal": (scal, pltpu.SMEM)}
    ins.update(any_inputs(a0=first[0], a1=first[1], b0=second[0], b1=second[1], c0=third[0], c1=third[1]))
    ins.update(any_inputs(last=last, own=own_first))
    whole = ((1, 2, ROW, D), BF, pl.ANY)
    return call(body, ins, {"out": whole}, {"held": ((2, 2, OWN, D), BF)}, {"last": "out"}, 16)["out"]


def unpack(got):
    count, size, width = got.shape
    wide = ((2, size, 3 * D), F32, pltpu.VMEM)
    square = ((2, size, D), F32, pltpu.VMEM)
    vec = ((2, size), F32, pltpu.VMEM)
    pair = ((2, 2, size), F32, pltpu.VMEM)
    outs = dict(
        proj=wide, out=square, qb=vec, vb=vec, ob=vec, up=square, down=square, ub=vec, db=vec, gain=pair, shift=pair
    )

    def body(r):
        pltpu.sync_copy(r.got, r.held)
        total = r.held[0].astype(F32)
        for n in range(1, count):
            total = total + r.held[n].astype(F32)
        for layer in range(2):
            base = layer * PACK
            ff = total[:, base : base + FF_PACK]
            att = total[:, base + FF_PACK : base + FF_PACK + ATT_PACK]
            r.up[layer] = ff[:, :D]
            r.down[layer] = ff[:, D : 2 * D]
            r.proj[layer] = att[:, : 3 * D]
            r.out[layer] = att[:, 3 * D : 4 * D]
            cols = ff[:, 2 * D :].T
            for ref, k in ((r.ob, 0), (r.ub, 3), (r.db, 4)):
                ref[layer : layer + 1, :] = cols[k : k + 1, :]
            for kind in range(2):
                r.gain[layer, kind : kind + 1, :] = cols[4 * kind + 1 : 4 * kind + 2, :]
                r.shift[layer, kind : kind + 1, :] = cols[4 * kind + 2 : 4 * kind + 3, :]
            cols = att[:, 4 * D :].T
            for ref, k in ((r.qb, 0), (r.vb, 1)):
                ref[layer : layer + 1, :] = cols[k : k + 1, :]

    scratch = {"held": ((count, size, width), BF)}
    return list(call(body, any_inputs(got=got), outs, scratch, sems=1).values())


def make_per_device(dp_count, section_count):
    both = ("dp", "section")

    def index(dp, section):
        return dp * section_count + section

    everyone = [(d, s) for d in range(dp_count) for s in range(section_count)]
    mate_pairs = [(index(d, s), index(d ^ 1, s)) for d, s in everyone]
    fetch_pairs = [(index(d, s), index(d ^ 1, s)) for d, s in everyone if d % 2 == s // 2]

    def send(rows, moves):
        pairs = []
        for d, z in everyone:
            to = moves.get((d % 2, z))
            if to is not None and index(d - d % 2 + z // 2, to) != index(d, z):
                pairs.append((index(d, z), index(d - d % 2 + z // 2, to)))
        return lax.ppermute(rows, both, pairs)

    def ship(rows, sections):
        return [
            send(rows, {(c, z): to for c, to in enumerate(sections) if to is not None for z in (odd, 2 + odd)})
            for odd in range(2)
        ]

    def mate(x):
        return lax.ppermute(x, both, mate_pairs)

    def after(value, *earlier):
        return lax.optimization_barrier((value, earlier))[0]

    def per_device(
        block_input, known_genes, attn_proj, attn_out, query_bias, value_bias, out_bias, ff_in, ff_out,
        ff_bias_in, ff_bias_out, norm_gain, norm_shift, cotangent,
    ):
        params = dict(
            attn_proj=attn_proj, attn_out=attn_out, query_bias=query_bias, value_bias=value_bias, out_bias=out_bias,
            ff_in=ff_in, ff_out=ff_out, ff_bias_in=ff_bias_in, ff_bias_out=ff_bias_out, norm_gain=norm_gain,
            norm_shift=norm_shift,
        )
        dp = lax.axis_index("dp")
        core = dp % 2
        section = lax.axis_index("section")
        mine = (core == section // 2).astype(jnp.int32)
        scal = jnp.stack([core, mine, section % 2, 2 * (section % 2) + core, section, dp // 2]).astype(jnp.int32)

        known_there = lax.ppermute(known_genes, both, fetch_pairs)
        x_there = lax.ppermute(block_input, both, fetch_pairs)
        x_in = any_inputs(x_here=block_input, x_there=x_there)
        f0 = forward_layer(0, scal, params, {**x_in, **any_inputs(known_here=known_genes, known_there=known_there)})
        rank = f0["rank_out"]
        x_own = f0["pair_out"]
        x_oth = mate(x_own)

        def other_half(rows, half):
            return lax.dynamic_update_index_in_dim(rows, half, 1 - core, 0)

        c_there = lax.ppermute(after(cotangent, x_own), both, fetch_pairs)
        missing = lax.dynamic_index_in_dim(x_oth, core, 0, keepdims=False)
        low_rows = other_half(f0["ship_out"], missing)
        got_low = [
            send(low_rows, {(0, 2): 0, (1, 0): 1}),
            send(low_rows, {(1, 2): 1, (1, 1): 1, (0, 3): 0, (0, 1): 0}),
            send(low_rows, {(1, 3): 1}),
        ]
        f1 = forward_layer(1, scal, params, any_inputs(x_own=x_own, x_oth=x_oth, rank_in=rank))
        high_rows = other_half(f1["ship_out"], mate(f1["half_out"]))
        got_high = ship(high_rows, (2, 3))
        b1 = backward_last(after(scal, got_low[0]), params, f1, any_inputs(c_here=cotangent, c_there=c_there, x_own=x_own), rank)
        wide = lax.all_to_all(b1["pack_out"].reshape(dp_count, -1, PACK), "dp", 0, 0)
        ins = any_inputs(dx_own=b1["dx_own_out"], dx_oth=mate(b1["dx_oth_out"]))
        b0 = backward_first_ff(after(scal, got_high[0]), params, f0, ins)
        grad_rows = other_half(b0["ship_out"], mate(after(b0["give_out"], got_low[1:])))
        got_second = ship(grad_rows, (None, 1))
        ins = {**x_in, **any_inputs(db0_in=b0["db0_out"], dr_in=b0["dr_out"], ff_in=b0["pack_out"])}
        last = backward_first_att(after(scal, grad_rows), params, f0, ins, rank)

        to_first = [(index(d, s), index(d - 1, s)) for d, s in everyone if d % 2]
        theirs = lax.ppermute(after(last["dx_out"], got_second, got_high[1], wide), both, to_first)
        first_rows = (last["dx_out"].astype(F32) + theirs.astype(F32)).astype(BF)
        got_first = ship(first_rows, (0, None))
        got_third = ship(after(grad_rows, first_rows), (2, None))
        narrow = lax.all_to_all(last["pack_out"].reshape(dp_count, -1, PACK), "dp", 0, 0)
        section_outputs, last_grads = finish_outputs(after(scal, first_rows), got_low, got_high, low_rows, high_rows, cotangent, params)
        held = join(after(narrow, last_grads), wide)
        got = lax.all_to_all(held.reshape(section_count, -1, held.shape[1]), "section", 0, 0)
        section_grads = finish_grads(scal, got_first, first_rows, got_second, got_third, last_grads)
        grads = unpack(after(got, section_grads))
        return (section_outputs, section_grads, *grads)

    return per_device


def solution(mesh):
    rows = P("dp", None, None)
    placed = (rows, P("dp", None)) + (P(),) * 11 + (rows,)
    sections = P("section", "dp", None, None)
    matrix = P(None, ("dp", "section"), None)
    vector = P(None, ("dp", "section"))
    pairs = P(None, None, ("dp", "section"))
    return jax.shard_map(
        make_per_device(mesh.shape["dp"], mesh.shape["section"]),
        mesh=mesh,
        in_specs=placed,
        out_specs=(
            sections, sections, matrix, matrix, vector, vector, vector, matrix, matrix, vector, vector, pairs, pairs,
        ),
        check_vma=False,
    )
```
